32 devices in a mesh: seq: 16 (over z, y, x), tile: 2 (over core).
Axes of the slice: x: 2, y: 2, z: 4, core: 2. Of those that a mesh axis runs over, the one named last changes fastest.
Arguments:
- tokens: bfloat16 [2, 8192, 1024], P('tile', 'seq'), may hold values from -6 to 6
- cotangent: bfloat16 [2, 8192, 1024], P('tile', 'seq'), may hold values from -6 to 6
- clip_big: int32 [10], replicated, may hold values from 0 to 1, as said below
- actions: int32 [160], replicated, may hold values from 0 to 7
- action_table: float32 [8, 1024], replicated, may hold values from -3 to 3
- norm_gain: float32 [3, 1024], replicated, may hold values from 0.25 to 1.75
- norm_bias: float32 [3, 1024], replicated, may hold values from -3 to 3
- spatial_q: bfloat16 [1024, 1024], replicated, may hold values from -0.1875 to 0.1875
- spatial_k: bfloat16 [1024, 1024], replicated, may hold values from -0.1875 to 0.1875
- spatial_v: bfloat16 [1024, 1024], replicated, may hold values from -0.1875 to 0.1875
- spatial_o: bfloat16 [1024, 1024], replicated, may hold values from -2 to 2
- temporal_q: bfloat16 [1024, 1024], replicated, may hold values from -0.1875 to 0.1875
- temporal_k: bfloat16 [1024, 1024], replicated, may hold values from -0.1875 to 0.1875
- temporal_v: bfloat16 [1024, 1024], replicated, may hold values from -0.1875 to 0.1875
- temporal_o: bfloat16 [1024, 1024], replicated, may hold values from -0.75 to 0.75
- ffn_in: bfloat16 [1024, 4096], replicated, may hold values from -0.1875 to 0.1875
- ffn_bias_in: float32 [1, 4096], replicated, may hold values from -3 to 3
- ffn_out: bfloat16 [4096, 1024], replicated, may hold values from -0.09375 to 0.09375
- ffn_bias_out: float32 [1, 1024], replicated, may hold values from -3 to 3
Outputs:
- mixed: bfloat16 [2, 8192, 1024], P('tile', 'seq')
- token_grad: bfloat16 [2, 8192, 1024], P('tile', 'seq')
- table_grad: float32 [8, 1024], P(None, 'seq')
- gain_grad: float32 [3, 1024], P(None, 'seq')
- norm_bias_grad: float32 [3, 1024], P(None, 'seq')
- spatial_q_grad: float32 [1024, 1024], P(None, 'seq')
- spatial_k_grad: float32 [1024, 1024], P(None, 'seq')
- spatial_v_grad: float32 [1024, 1024], P(None, 'seq')
- spatial_o_grad: float32 [1024, 1024], P(None, 'seq')
- temporal_q_grad: float32 [1024, 1024], P(None, 'seq')
- temporal_k_grad: float32 [1024, 1024], P(None, 'seq')
- temporal_v_grad: float32 [1024, 1024], P(None, 'seq')
- temporal_o_grad: float32 [1024, 1024], P(None, 'seq')
- ffn_in_grad: float32 [1024, 4096], P(None, 'seq')
- ffn_bias_in_grad: float32 [1, 4096], P(None, 'seq')
- ffn_out_grad: float32 [4096, 1024], P(None, 'seq')
- ffn_bias_out_grad: float32 [1, 1024], P(None, 'seq')
The draws below stay inside these ranges and needn't reach their ends.
Inputs may be any that keep to these rules, and one draw needn't show every extreme that they name: `clip_big`: exactly 2 entries are 1, the others 0.
All inputs are finite; a program needn't handle non-finite values.
Results may differ from the reference program's by a relative error of at most 0.019.
Values may be sent and summed in bfloat16 or wider, within the bound.
A program may use at most 256 MiB of HBM per device.

```python
import jax
import jax.numpy as jnp
from jax import lax

D = 1024
HEAD_DIM = 64
FF = 4096
ACTIONS = 8
FRAMES = 16
GRID_BIG = 16
GRID_SMALL = 8
BAND_BIG = 128
BAND_SMALL = 32
SPAN = 4
ROWS_DEV = 512
BIG_CLIPS = 2
CLIPS = 10
CLIP_FRAMES = 160
POSITIONS = 8192
N_TILE = 2


def draw_clip_big(key, part):
    key = jax.random.fold_in(key, 11)
    order = jax.random.permutation(key, CLIPS)
    return (order < BIG_CLIPS).astype(jnp.int32)


def with_ends(array, own_key, least, top_value):
    shape = array.shape
    index_at = [jax.random.randint(jax.random.fold_in(own_key, axis), (), 0, shape[axis]) for axis in range(len(shape))]
    array = array.at[tuple(index_at)].set(least)
    longest = shape.index(max(shape))
    index_at[longest] = (index_at[longest] + 1) % shape[longest]
    return array.at[tuple(index_at)].set(top_value)


def shard_levels(key, dims, cuts, low, largest):
    level, own = 1.0, jax.random.fold_in(key, 6)
    for dim, shards_of in cuts:
        steps = jnp.exp(jax.random.uniform(jax.random.fold_in(own, dim), (shards_of,), jnp.float32, low / len(cuts), largest / len(cuts)))
        level = level * jnp.repeat(steps, dims[dim] // shards_of).reshape([-1 if axis == dim else 1 for axis in range(len(dims))])
    return level


def centred(own_key, extent, deviation, most, split=(), kind=jnp.bfloat16):
    drawn = jax.random.normal(own_key, extent, jnp.float32) * deviation
    if len(split) > 0:
        drawn = shard_levels(own_key, extent, split, -0.22, 0.18) * drawn
    return jnp.clip(drawn, min=-most, max=most).astype(kind)


def setup_inputs(seed: int = 0) -> dict:
    seeds = jax.random.split(jax.random.key(seed), 20)
    tokens = centred(seeds[0], (N_TILE, POSITIONS, D), 1.0, 6.0, ((0, 2), (1, 16)))
    cotangent = centred(seeds[1], (N_TILE, POSITIONS, D), 1.0, 6.0, ((0, 2), (1, 16)))
    clip_big = draw_clip_big(jax.random.fold_in(seeds[19], 71), 0)
    actions = with_ends(jax.random.randint(seeds[3], (CLIP_FRAMES,), 0, ACTIONS), jax.random.fold_in(seeds[3], 1), 0, ACTIONS - 1).astype(jnp.int32)
    action_table = centred(seeds[4], (ACTIONS, D), 0.5, 3.0, (), jnp.float32)
    norm_gain = jnp.clip(1.0 + 0.15 * jax.random.normal(seeds[5], (3, D), jnp.float32), 0.25, 1.75)
    norm_bias = centred(seeds[6], (3, D), 0.3, 3.0, (), jnp.float32)
    spatial_q = centred(seeds[7], (D, D), D ** -0.5, 0.1875)
    spatial_k = centred(seeds[8], (D, D), D ** -0.5, 0.1875)
    spatial_v = centred(seeds[9], (D, D), D ** -0.5, 0.1875)
    spatial_o = centred(seeds[10], (D, D), (D // (GRID_BIG * GRID_SMALL)) ** -0.5, 2.0)
    temporal_q = centred(seeds[11], (D, D), D ** -0.5, 0.1875)
    temporal_k = centred(seeds[12], (D, D), D ** -0.5, 0.1875)
    temporal_v = centred(seeds[13], (D, D), D ** -0.5, 0.1875)
    temporal_o = centred(seeds[14], (D, D), (D // FRAMES) ** -0.5, 0.75)
    ffn_in = centred(seeds[15], (D, FF), D ** -0.5, 0.1875)
    ffn_bias_in = centred(seeds[16], (1, FF), 0.3, 3.0, (), jnp.float32)
    ffn_out = centred(seeds[17], (FF, D), FF ** -0.5, 0.09375)
    ffn_bias_out = centred(seeds[18], (1, D), 0.3, 3.0, (), jnp.float32)
    return dict(tokens=tokens, cotangent=cotangent, clip_big=clip_big, actions=actions, action_table=action_table, norm_gain=norm_gain, norm_bias=norm_bias, spatial_q=spatial_q, spatial_k=spatial_k, spatial_v=spatial_v, spatial_o=spatial_o, temporal_q=temporal_q, temporal_k=temporal_k, temporal_v=temporal_v, temporal_o=temporal_o, ffn_in=ffn_in, ffn_bias_in=ffn_bias_in, ffn_out=ffn_out, ffn_bias_out=ffn_bias_out)


@jax.custom_vjp
def low(v):
    return lax.optimization_barrier(v.astype(jnp.bfloat16)).astype(jnp.float32)

@jax.custom_vjp
def low_back(v):
    return v

def low_keep(v):
    return (low(v), None)

def low_pass(kept, grad):
    return (grad,)

def back_keep(v):
    return (v, None)

def back_low(kept, grad):
    return (low(grad),)
low.defvjp(low_keep, low_pass)
low_back.defvjp(back_keep, back_low)
precise = lax.Precision.HIGHEST

def layout(clip_big, places, band_big, band_small, frame_count):
    lengths = jnp.where(clip_big == 1, frame_count * band_big, frame_count * band_small).astype(jnp.int32)
    band_size = jnp.where(clip_big == 1, band_big, band_small).astype(jnp.int32)
    starts = (jnp.cumsum(lengths) - lengths).astype(jnp.int32)
    inside = (places[:, None] >= starts[None, :]) & (places[:, None] < (starts + lengths)[None, :])
    number = jnp.arange(clip_big.shape[0], dtype=jnp.int32)
    clip_id = lax.optimization_barrier(jnp.sum(jnp.where(inside, number[None, :], 0), axis=1)).astype(jnp.int32)
    clip_start = lax.optimization_barrier(jnp.sum(jnp.where(inside, starts[None, :], 0), axis=1)).astype(jnp.int32)
    band_of = jnp.maximum(lax.optimization_barrier(jnp.sum(jnp.where(inside, band_size[None, :], 0), axis=1)), 1).astype(jnp.int32)
    is_valid = jnp.any(inside, axis=1)
    offset = places - clip_start
    moment = offset // band_of
    spot_id = offset % band_of
    frame_id = clip_id * frame_count + moment
    return (clip_id, moment, spot_id, frame_id, is_valid)

def layer_norm(values, gain, shift):
    centre = values - lax.optimization_barrier(jnp.mean(values, axis=-1, keepdims=True))
    spread = lax.optimization_barrier(jnp.mean(centre * centre, axis=-1, keepdims=True))
    return centre * lax.rsqrt(spread + 1e-05) * gain + shift

def project(values, weight):
    return jnp.dot(values, weight, precision=precise)

def attention(queries, keys, values, key_mask):
    factor = HEAD_DIM ** (-0.5)
    query_head = queries.reshape(queries.shape[0], -1, HEAD_DIM)
    key_head = keys.reshape(keys.shape[0], -1, HEAD_DIM)
    value_head = values.reshape(values.shape[0], -1, HEAD_DIM)
    scores = low_back(jnp.einsum('qhd,khd->hqk', query_head, key_head, precision=precise) * factor)
    scores = jnp.where(key_mask[None], scores, -1e+30)
    row_top = lax.optimization_barrier(jnp.max(scores, axis=2, keepdims=True))
    row_exp = jnp.exp(scores - row_top)
    prob_low = low(row_exp / lax.optimization_barrier(jnp.sum(row_exp, axis=2, keepdims=True)))
    result = jnp.einsum('hqk,khd->qhd', prob_low, value_head, precision=precise)
    return result.reshape(queries.shape[0], -1)

def spatial(query, key, value, frame_id):
    blocks = frame_id.shape[0] // ROWS_DEV

    def regroup(values):
        return values.reshape(N_TILE, blocks, ROWS_DEV, -1).transpose(1, 0, 2, 3).reshape(blocks, N_TILE * ROWS_DEV, -1)

    def one_block(pieces):
        query_b, key_b, value_b, frame_b = pieces
        wide_frames = jnp.tile(frame_b, N_TILE)
        return attention(query_b, key_b, value_b, wide_frames[:, None] == wide_frames[None, :])
    result = lax.map(jax.checkpoint(one_block), (regroup(query), regroup(key), regroup(value), frame_id.reshape(blocks, ROWS_DEV)))
    return result.reshape(blocks, N_TILE, ROWS_DEV, -1).transpose(1, 0, 2, 3).reshape(N_TILE, blocks * ROWS_DEV, -1)

def temporal(query, key, value, clip_big):
    reach_back = SPAN - 1
    blocks = query.shape[1] // ROWS_DEV
    padding = jnp.zeros((N_TILE, reach_back * ROWS_DEV, key.shape[2]), jnp.float32)
    key_pad = jnp.concatenate([padding, key], axis=1)
    value_pad = jnp.concatenate([padding, value], axis=1)

    def one_block(block_at):
        first_row = block_at * ROWS_DEV
        query_b = lax.dynamic_slice_in_dim(query, first_row, ROWS_DEV, 1)
        key_b = lax.dynamic_slice_in_dim(key_pad, first_row, (reach_back + 1) * ROWS_DEV, 1)
        value_b = lax.dynamic_slice_in_dim(value_pad, first_row, (reach_back + 1) * ROWS_DEV, 1)
        query_places = first_row + jnp.arange(ROWS_DEV, dtype=jnp.int32)
        key_places = first_row - reach_back * ROWS_DEV + jnp.arange((reach_back + 1) * ROWS_DEV, dtype=jnp.int32)
        clip_q, moment_q, spot_q, frame_q, valid_q = layout(clip_big, query_places, BAND_BIG, BAND_SMALL, FRAMES)
        clip_k, moment_k, spot_k, frame_k, valid_k = layout(clip_big, key_places, BAND_BIG, BAND_SMALL, FRAMES)
        key_mask = valid_k[None, :] & (clip_q[:, None] == clip_k[None, :]) & (spot_q[:, None] == spot_k[None, :]) & (moment_k[None, :] <= moment_q[:, None])
        return jax.vmap(attention, in_axes=(0, 0, 0, None))(query_b, key_b, value_b, key_mask)
    result = lax.map(jax.checkpoint(one_block), jnp.arange(blocks, dtype=jnp.int32))
    return result.transpose(1, 0, 2, 3).reshape(N_TILE, blocks * ROWS_DEV, -1)

def reference(tokens, cotangent, clip_big, actions, action_table, norm_gain, norm_bias, spatial_q, spatial_k, spatial_v, spatial_o, temporal_q, temporal_k, temporal_v, temporal_o, ffn_in, ffn_bias_in, ffn_out, ffn_bias_out):
    places = jnp.arange(POSITIONS, dtype=jnp.int32)
    clip_id, moment, spot_id, frame_id, is_valid = layout(clip_big, places, BAND_BIG, BAND_SMALL, FRAMES)
    frame_all = jnp.arange(CLIP_FRAMES, dtype=jnp.int32)
    action_id = lax.optimization_barrier(jnp.sum(jnp.where(frame_id[:, None] == frame_all[None, :], actions[None, :], 0), axis=1))
    action_hot = (action_id[:, None] == jnp.arange(ACTIONS, dtype=jnp.int32)[None, :]).astype(jnp.float32)

    def forward(tokens_f, table, gains, shifts, s_query, s_key, s_value, s_out, t_query, t_key, t_value, t_out, w_in, b_in, w_out, b_out):
        first_sum = tokens_f + jnp.dot(action_hot, table, precision=precise)[None]
        normed_one = low(layer_norm(first_sum, gains[0], shifts[0]))
        query_one = low(low_back(project(normed_one, s_query)))
        key_one = low(low_back(project(normed_one, s_key)))
        value_one = low(low_back(project(normed_one, s_value)))
        mixed_one = low(low_back(spatial(query_one, key_one, value_one, frame_id)))
        second_sum = first_sum + low_back(project(mixed_one, s_out))
        normed_two = low(layer_norm(second_sum, gains[1], shifts[1]))
        query_two = low(low_back(project(normed_two, t_query)))
        key_two = low(low_back(project(normed_two, t_key)))
        value_two = low(low_back(project(normed_two, t_value)))
        mixed_two = low(low_back(temporal(query_two, key_two, value_two, clip_big)))
        third_sum = second_sum + low_back(project(mixed_two, t_out))
        normed_three = low(layer_norm(third_sum, gains[2], shifts[2]))
        inner_act = low_back(project(normed_three, w_in) + b_in)
        active = low(jax.nn.gelu(inner_act))
        return third_sum + low_back(project(active, w_out) + b_out)
    floats = (tokens.astype(jnp.float32), action_table.astype(jnp.float32), norm_gain.astype(jnp.float32), norm_bias.astype(jnp.float32), spatial_q.astype(jnp.float32), spatial_k.astype(jnp.float32), spatial_v.astype(jnp.float32), spatial_o.astype(jnp.float32), temporal_q.astype(jnp.float32), temporal_k.astype(jnp.float32), temporal_v.astype(jnp.float32), temporal_o.astype(jnp.float32), ffn_in.astype(jnp.float32), ffn_bias_in.astype(jnp.float32), ffn_out.astype(jnp.float32), ffn_bias_out.astype(jnp.float32))
    mixed, pullback = jax.vjp(forward, *floats)
    grads = pullback(cotangent.astype(jnp.float32))
    return (mixed.astype(jnp.bfloat16), grads[0].astype(jnp.bfloat16), grads[1], grads[2], grads[3], grads[4], grads[5], grads[6], grads[7], grads[8], grads[9], grads[10], grads[11], grads[12], grads[13], grads[14], grads[15])
```

```python
import functools

import jax
import jax.numpy as jnp
from jax import lax
from jax.experimental import pallas as pl
from jax.experimental.pallas import tpu as pltpu
from jax.sharding import PartitionSpec as P

HEAD_DIM = 64
FRAMES = 16
GRID_BIG = 16
GRID_SMALL = 8
WIDE = 128
KEYS = 256
CHUNK = 512
VMEM_BYTES = 58 * 2**20
FACTOR = HEAD_DIM**-0.5
ROOT = (2.0 / 3.141592653589793) ** 0.5

F32 = jnp.float32
BF16 = jnp.bfloat16
WHOLE = pl.BlockSpec(memory_space=pltpu.VMEM)
IN_HBM = pl.BlockSpec(memory_space=pl.ANY)
MESH = pl.DeviceIdType.MESH
IN_SMEM = pl.BlockSpec(memory_space=pltpu.SMEM)


def shape_of(dims, kind):
    return jax.ShapeDtypeStruct(dims, kind)


def params(**more):
    return pltpu.CompilerParams(vmem_limit_bytes=VMEM_BYTES, **more)


def dot(left, right):
    return jnp.dot(left, right, preferred_element_type=F32)


def dot_nt(left, right):
    return lax.dot_general(left, right, (((1,), (1,)), ((), ())), preferred_element_type=F32)


def dot_tn(left, right):
    return lax.dot_general(left, right, (((0,), (0,)), ((), ())), preferred_element_type=F32)


def normalise(values):
    centre = values - jnp.mean(values, axis=-1, keepdims=True)
    rate = lax.rsqrt(jnp.mean(centre * centre, axis=-1, keepdims=True) + 1e-05)
    return centre * rate, rate


def norm_backward(grad, hat, rate, gain):
    inner = grad * gain
    level = jnp.mean(inner, axis=-1, keepdims=True)
    slope = jnp.mean(inner * hat, axis=-1, keepdims=True)
    return rate * (inner - level - hat * slope)


def head_halves(block):
    lane = lax.broadcasted_iota(jnp.int32, block.shape, 1)
    zero = jnp.zeros_like(block)
    first = lane < HEAD_DIM
    return jnp.concatenate([jnp.where(first, block, zero), jnp.where(first, zero, block)], axis=0)


def join_halves(both):
    rows = both.shape[0] // 2
    lane = lax.broadcasted_iota(jnp.int32, (rows, both.shape[1]), 1)
    return jnp.where(lane < HEAD_DIM, both[:rows], both[rows:])


def attend(query, key, value, bias):
    scores = dot_nt(head_halves(query) * FACTOR, key) + bias
    top = jnp.max(scores, axis=1, keepdims=True)
    powers = jnp.exp(scores - top)
    prob = (powers * (1.0 / jnp.sum(powers, axis=1, keepdims=True))).astype(BF16)
    return prob, join_halves(dot(prob, value))


def attend_backward(prob, query, key, value, grad):
    grad_two = head_halves(grad)
    grad_prob = dot_nt(grad_two, value)
    prob_f = prob.astype(F32)
    delta = jnp.sum(prob_f * grad_prob, axis=1, keepdims=True)
    grad_score = (prob_f * (grad_prob - delta)).astype(BF16)
    grad_query = join_halves(dot(grad_score, key)) * FACTOR
    grad_key = dot_tn(grad_score, head_halves(query)) * FACTOR
    grad_value = dot_tn(prob, grad_two)
    return grad_query, grad_key, grad_value


def spatial_bias(is_big, rows):
    row = lax.broadcasted_iota(jnp.int32, (rows, KEYS), 0)
    column = lax.broadcasted_iota(jnp.int32, (rows, KEYS), 1)
    same = lax.rem(row, WIDE) // 32 == lax.rem(column, WIDE) // 32
    return jnp.where(same | (is_big == 1), 0.0, -1e30).astype(F32)


def temporal_bias(rows):
    row = lax.rem(lax.broadcasted_iota(jnp.int32, (rows, KEYS), 0), KEYS)
    column = lax.broadcasted_iota(jnp.int32, (rows, KEYS), 1)
    fits = (lax.rem(row, 16) == lax.rem(column, 16)) & (column <= row)
    return jnp.where(fits, 0.0, -1e30).astype(F32)


def columns_of(index):
    return pl.ds(pl.multiple_of(index * WIDE, WIDE), WIDE)


def project_kernel(tok, hot, table, gain, shift, wq, wk, wv, normed, query, key, value, held, sems):
    copies = [
        pltpu.make_async_copy(source, held.at[at], sems.at[at])
        for at, source in enumerate((wq, wk, wv))
    ]
    for copy in copies:
        copy.start()
    rows = tok.shape[0]

    def norm_rows(at, _):
        here = pl.ds(pl.multiple_of(at * 128, 128), 128)
        first = tok[here, :].astype(F32) + dot(hot[here, :], table[...])
        hat, _rate = normalise(first)
        normed[here, :] = (hat * gain[...] + shift[...]).astype(BF16)
        return 0

    lax.fori_loop(0, rows // 128, norm_rows, 0)
    for at, (copy, target) in enumerate(zip(copies, (query, key, value))):
        copy.wait()
        for part in range(4):
            side = pl.ds(part * 256, 256)
            target[:, side] = dot(normed[...], held[at, :, side]).astype(BF16)


def project(tok, hot, table, gain, shift, wq, wk, wv):
    rows, width = tok.shape
    out = shape_of((rows, width), BF16)
    return pl.pallas_call(
        project_kernel,
        out_shape=[out] * 4,
        in_specs=[WHOLE] * 5 + [IN_HBM] * 3,
        out_specs=[WHOLE] * 4,
        scratch_shapes=[pltpu.VMEM((3, width, width), BF16), pltpu.SemaphoreType.DMA((3,))],
        compiler_params=params(),
        cost_estimate=pl.CostEstimate(
            flops=6 * rows * width * width, bytes_accessed=12 * 2**20, transcendentals=0
        ),
    )(tok, hot, table, gain, shift, wq, wk, wv)


def spatial_kernel(meta, query, key, value, pair, tok, hot, table, wo, mixed, probs, second, kept, held, sem):
    at = pl.program_id(0)
    copy = pltpu.make_async_copy(wo, held, sem)

    @pl.when(at == 0)
    def _():
        copy.start()

    bias = spatial_bias(meta[0], 2 * WIDE)
    here = pl.ds(pl.multiple_of(at * WIDE, WIDE), WIDE)
    for two in range(8):
        side = pl.ds(two * WIDE, WIDE)
        keys = jnp.concatenate([key[:, side], pair[0, :, side]], axis=0)
        values = jnp.concatenate([value[:, side], pair[1, :, side]], axis=0)
        prob, out = attend(query[:, side], keys, values, bias)
        probs[0, two] = prob
        out = out.astype(BF16)
        mixed[:, side] = out
        kept[here, side] = out

    @pl.when(at == pl.num_programs(0) - 1)
    def _():
        copy.wait()
        for part in range(4):
            side = pl.ds(part * 256, 256)
            first = tok[:, side].astype(F32) + dot(hot[...], table[:, side])
            second[:, side] = (first + dot(kept[...], held[:, side])).astype(BF16)


def spatial(meta, query, key, value, pair, tok, hot, table, wo):
    rows, width = tok.shape
    block = pl.BlockSpec((WIDE, width), lambda i: (i, 0))

    def fixed(array):
        return pl.BlockSpec(array.shape, lambda i: (0,) * array.ndim)

    return pl.pallas_call(
        spatial_kernel,
        grid=(rows // WIDE,),
        out_shape=[
            shape_of((rows, width), BF16),
            shape_of((rows // WIDE, 8, 2 * WIDE, KEYS), BF16),
            shape_of((rows, width), BF16),
        ],
        in_specs=[
            IN_SMEM,
            block,
            block,
            block,
            pl.BlockSpec((2, WIDE, width), lambda i: (0, i, 0)),
            fixed(tok),
            fixed(hot),
            fixed(table),
            IN_HBM,
        ],
        out_specs=[
            block,
            pl.BlockSpec((1, 8, 2 * WIDE, KEYS), lambda i: (i, 0, 0, 0)),
            pl.BlockSpec((rows, width), lambda i: (0, 0)),
        ],
        scratch_shapes=[
            pltpu.VMEM((rows, width), BF16),
            pltpu.VMEM((width, width), BF16),
            pltpu.SemaphoreType.DMA,
        ],
        compiler_params=params(),
        cost_estimate=pl.CostEstimate(
            flops=8 * rows * width * width, bytes_accessed=14 * 2**20, transcendentals=0
        ),
    )(meta, query, key, value, pair, tok, hot, table, wo)


def temporal_kernel(
    second, gain, shift, wq, wk, wv, wo, normed, query, key, value, probs, mixed, third, held, sems
):
    copies = [
        pltpu.make_async_copy(source, held.at[at], sems.at[at])
        for at, source in enumerate((wq, wk, wv, wo))
    ]
    for copy in copies:
        copy.start()
    rows = second.shape[0]

    def norm_rows(at, _):
        here = pl.ds(pl.multiple_of(at * 128, 128), 128)
        hat, _rate = normalise(second[here, :].astype(F32))
        normed[here, :] = (hat * gain[...] + shift[...]).astype(BF16)
        return 0

    lax.fori_loop(0, rows // 128, norm_rows, 0)
    for at, target in enumerate((query, key, value)):
        copies[at].wait()
        for part in range(4):
            side = pl.ds(part * 256, 256)
            target[:, side] = dot(normed[...], held[at, :, side]).astype(BF16)
    bias = temporal_bias(2 * KEYS)

    def group(at, _):
        here = pl.ds(pl.multiple_of(at * KEYS, KEYS), KEYS)
        for two in range(8):
            side = pl.ds(two * WIDE, WIDE)
            prob, out = attend(query[here, side], key[here, side], value[here, side], bias)
            probs[at, two] = prob
            mixed[here, side] = out.astype(BF16)
        return 0

    lax.fori_loop(0, rows // KEYS, group, 0)
    copies[3].wait()
    for part in range(4):
        side = pl.ds(part * 256, 256)
        third[:, side] = second[:, side].astype(F32) + dot(mixed[...], held[3, :, side])


def temporal(second, gain, shift, wq, wk, wv, wo):
    rows, width = second.shape
    out = shape_of((rows, width), BF16)
    return pl.pallas_call(
        temporal_kernel,
        out_shape=[
            out,
            out,
            out,
            out,
            shape_of((rows // KEYS, 8, 2 * KEYS, KEYS), BF16),
            out,
            shape_of((rows, width), F32),
        ],
        in_specs=[WHOLE] * 3 + [IN_HBM] * 4,
        out_specs=[WHOLE] * 7,
        scratch_shapes=[pltpu.VMEM((4, width, width), BF16), pltpu.SemaphoreType.DMA((4,))],
        compiler_params=params(),
        cost_estimate=pl.CostEstimate(
            flops=14 * rows * width * width, bytes_accessed=20 * 2**20, transcendentals=0
        ),
    )(second, gain, shift, wq, wk, wv, wo)


def ffn_kernel(
    third, cot, gain, shift, win, bin_, wout, bout,
    mixed, grad_third, d_in, d_out, d_bin, d_norm, d_bout,
    normed, normed_t, cot_t, total, grad_normed,
):
    at = pl.program_id(0)
    rows = third.shape[0]

    @pl.when(at == 0)
    def _():
        def norm_rows(step, _):
            here = pl.ds(pl.multiple_of(step * 128, 128), 128)
            hat, _rate = normalise(third[here, :])
            normed[here, :] = (hat * gain[...] + shift[...]).astype(BF16)
            return 0

        lax.fori_loop(0, rows // 128, norm_rows, 0)
        normed_t[...] = normed[...].T
        cot_t[...] = cot[...].T
        d_bout[...] = jnp.sum(cot[...].astype(F32), axis=0, keepdims=True)
        total[...] = third[...] + bout[...]
        grad_normed[...] = jnp.zeros_like(grad_normed)

    half = CHUNK // 2
    for part in range(2):
        side = pl.ds(part * half, half)
        inner = dot(normed[...], win[:, side]) + bin_[:, side]
        square = inner * inner
        curve = jnp.tanh(ROOT * (inner + 0.044715 * inner * square))
        active = (0.5 * inner * (1.0 + curve)).astype(BF16)
        slope = 0.5 * (1.0 + curve) + (0.5 * ROOT) * inner * (1.0 - curve * curve) * (
            1.0 + (3 * 0.044715) * square
        )
        wide = slope * dot_nt(cot[...], wout[side, :])
        grad_inner = wide.astype(BF16)
        d_bin[:, side] = jnp.sum(grad_inner.astype(F32), axis=0, keepdims=True)
        total[...] += dot(active, wout[side, :])
        grad_normed[...] += dot_nt(grad_inner, win[:, side])
        d_out[0, :, side] = dot(cot_t[...], active).astype(BF16)
        for which in range(2):
            top = pl.ds(which * 512, 512)
            d_in[which, part] = dot(normed_t[top, :], grad_inner).astype(BF16)

    @pl.when(at == pl.num_programs(0) - 1)
    def _():
        mixed[...] = total[...].astype(BF16)

        def back_rows(step, carry):
            here = pl.ds(pl.multiple_of(step * 128, 128), 128)
            hat, rate = normalise(third[here, :])
            grad = grad_normed[here, :]
            grad_third[here, :] = cot[here, :].astype(F32) + norm_backward(
                grad, hat, rate, gain[...]
            )
            return (
                carry[0] + jnp.sum(grad * hat, axis=0, keepdims=True),
                carry[1] + jnp.sum(grad, axis=0, keepdims=True),
            )

        zero = jnp.zeros((1, third.shape[1]), F32)
        sums = lax.fori_loop(0, rows // 128, back_rows, (zero, zero))
        d_norm[0:1, :] = sums[0]
        d_norm[1:2, :] = sums[1]


def ffn(third, cot, gain, shift, win, bin_, wout, bout):
    rows, width = third.shape
    hidden = win.shape[1]
    steps = hidden // CHUNK

    def fixed(*dims):
        return pl.BlockSpec(dims, lambda i: (0,) * len(dims))

    return pl.pallas_call(
        ffn_kernel,
        grid=(steps,),
        out_shape=[
            shape_of((rows, width), BF16),
            shape_of((rows, width), F32),
            shape_of((2, 16, width // 2, hidden // 16), BF16),
            shape_of((2, width, hidden // 2), BF16),
            shape_of((1, hidden), F32),
            shape_of((2, width), F32),
            shape_of((1, width), F32),
        ],
        in_specs=[
            fixed(rows, width),
            fixed(rows, width),
            fixed(1, width),
            fixed(1, width),
            pl.BlockSpec((width, CHUNK), lambda i: (0, i)),
            pl.BlockSpec((1, CHUNK), lambda i: (0, i)),
            pl.BlockSpec((CHUNK, width), lambda i: (i, 0)),
            fixed(1, width),
        ],
        out_specs=[
            fixed(rows, width),
            fixed(rows, width),
            pl.BlockSpec((2, 2, width // 2, hidden // 16), lambda i: (0, i, 0, 0)),
            pl.BlockSpec((1, width, CHUNK), lambda i: (i // 4, 0, lax.rem(i, 4))),
            pl.BlockSpec((1, CHUNK), lambda i: (0, i)),
            fixed(2, width),
            fixed(1, width),
        ],
        scratch_shapes=[
            pltpu.VMEM((rows, width), BF16),
            pltpu.VMEM((width, rows), BF16),
            pltpu.VMEM((width, rows), BF16),
            pltpu.VMEM((rows, width), F32),
            pltpu.VMEM((rows, width), F32),
        ],
        compiler_params=params(),
        cost_estimate=pl.CostEstimate(
            flops=12 * rows * width * hidden, bytes_accessed=40 * 2**20, transcendentals=0
        ),
    )(third, cot, gain, shift, win, bin_, wout, bout)


def weight_grad(target, at, grad, normed):
    grad_t = grad.T
    count, _rows, width = target.shape[1:]
    part = grad_t.shape[0] // count
    for which in range(2):
        block = dot(grad_t, normed[:, which * width : (which + 1) * width]).astype(BF16)
        target[which, :, at * part : (at + 1) * part, :] = block.reshape(count, part, width)


def temporal_back_kernel(
    grad_third, second, mixed, query, key, value, normed, probs, gain, wq, wk, wv, wo,
    grad_second, d_weights, d_norm,
    held, low, grad_mixed, d_query, d_key, d_value, sems,
):
    copies = [
        pltpu.make_async_copy(source, held.at[at], sems.at[at])
        for at, source in enumerate((wo, wq, wk, wv))
    ]
    for copy in copies:
        copy.start()
    rows = second.shape[0]
    low[...] = grad_third[...].astype(BF16)
    weight_grad(d_weights, 0, low[...], mixed[...])
    copies[0].wait()
    for part in range(4):
        side = pl.ds(part * 256, 256)
        grad_mixed[:, side] = dot_nt(low[...], held[0, side, :]).astype(BF16)

    def group(at, _):
        here = pl.ds(pl.multiple_of(at * KEYS, KEYS), KEYS)
        for two in range(8):
            side = pl.ds(two * WIDE, WIDE)
            grads = attend_backward(
                probs[at, two], query[here, side], key[here, side], value[here, side],
                grad_mixed[here, side],
            )
            for target, grad in zip((d_query, d_key, d_value), grads):
                target[here, side] = grad.astype(BF16)
        return 0

    lax.fori_loop(0, rows // KEYS, group, 0)
    for at, grad in enumerate((d_query, d_key, d_value)):
        weight_grad(d_weights, at + 1, grad[...], normed[...])
    for at in range(3):
        copies[at + 1].wait()

    def back_rows(step, carry):
        here = pl.ds(pl.multiple_of(step * 256, 256), 256)
        grad = (
            dot_nt(d_query[here, :], held[1])
            + dot_nt(d_key[here, :], held[2])
            + dot_nt(d_value[here, :], held[3])
        )
        hat, rate = normalise(second[here, :].astype(F32))
        grad_second[here, :] = (
            grad_third[here, :] + norm_backward(grad, hat, rate, gain[...])
        ).astype(BF16)
        return (
            carry[0] + jnp.sum(grad * hat, axis=0, keepdims=True),
            carry[1] + jnp.sum(grad, axis=0, keepdims=True),
        )

    zero = jnp.zeros((1, second.shape[1]), F32)
    sums = lax.fori_loop(0, rows // 256, back_rows, (zero, zero))
    d_norm[0:1, :] = sums[0]
    d_norm[1:2, :] = sums[1]


def temporal_back(grad_third, second, mixed, query, key, value, normed, probs, gain, wq, wk, wv, wo):
    rows, width = second.shape
    count = lax.axis_size("seq")
    return pl.pallas_call(
        temporal_back_kernel,
        out_shape=[
            shape_of((rows, width), BF16),
            shape_of((2, count, 4 * width // count, width // 2), BF16),
            shape_of((2, width), F32),
        ],
        in_specs=[WHOLE] * 9 + [IN_HBM] * 4,
        out_specs=[WHOLE] * 3,
        scratch_shapes=[pltpu.VMEM((4, width, width), BF16)]
        + [pltpu.VMEM((rows, width), BF16)] * 5
        + [pltpu.SemaphoreType.DMA((4,))],
        compiler_params=params(),
        cost_estimate=pl.CostEstimate(
            flops=24 * rows * width * width, bytes_accessed=30 * 2**20, transcendentals=0
        ),
    )(grad_third, second, mixed, query, key, value, normed, probs, gain, wq, wk, wv, wo)


def spatial_back_kernel(
    grad_second, mixed, query, key, value, pair, probs, wo,
    d_query, d_pair, d_away, d_wo,
    held, grad_mixed, sem,
):
    copy = pltpu.make_async_copy(wo, held, sem)
    copy.start()
    rows = query.shape[0]
    weight_grad(d_wo, 0, grad_second[...], mixed[...])
    copy.wait()
    for part in range(4):
        side = pl.ds(part * 256, 256)
        grad_mixed[:, side] = dot_nt(grad_second[...], held[side, :]).astype(BF16)

    def group(at, _):
        here = pl.ds(pl.multiple_of(at * WIDE, WIDE), WIDE)
        for two in range(8):
            side = pl.ds(two * WIDE, WIDE)
            keys = jnp.concatenate([key[here, side], pair[0, here, side]], axis=0)
            values = jnp.concatenate([value[here, side], pair[1, here, side]], axis=0)
            grad_query, grad_key, grad_value = attend_backward(
                probs[at, two], query[here, side], keys, values, grad_mixed[here, side]
            )
            d_query[here, side] = grad_query.astype(BF16)
            d_pair[0, here, side] = grad_key[:WIDE]
            d_pair[1, here, side] = grad_value[:WIDE]
            d_away[0, here, side] = grad_key[WIDE:].astype(BF16)
            d_away[1, here, side] = grad_value[WIDE:].astype(BF16)
        return 0

    lax.fori_loop(0, rows // WIDE, group, 0)


def spatial_back(grad_second, mixed, query, key, value, pair, probs, wo):
    rows, width = query.shape
    count = lax.axis_size("seq")
    return pl.pallas_call(
        spatial_back_kernel,
        out_shape=[
            shape_of((rows, width), BF16),
            shape_of((2, rows, width), F32),
            shape_of((2, rows, width), BF16),
            shape_of((2, count, width // count, width // 2), BF16),
        ],
        in_specs=[WHOLE] * 7 + [IN_HBM],
        out_specs=[WHOLE] * 4,
        scratch_shapes=[
            pltpu.VMEM((width, width), BF16),
            pltpu.VMEM((rows, width), BF16),
            pltpu.SemaphoreType.DMA,
        ],
        compiler_params=params(),
        cost_estimate=pl.CostEstimate(
            flops=12 * rows * width * width, bytes_accessed=24 * 2**20, transcendentals=0
        ),
    )(grad_second, mixed, query, key, value, pair, probs, wo)


def spatial_weights_kernel(d_query, d_pair, came, normed, d_weights, d_key, d_value):
    d_key[...] = (d_pair[0] + came[0].astype(F32)).astype(BF16)
    d_value[...] = (d_pair[1] + came[1].astype(F32)).astype(BF16)
    for at, grad in enumerate((d_query, d_key, d_value)):
        weight_grad(d_weights, at, grad[...], normed[...])


def spatial_weights(d_query, d_pair, came, normed):
    rows, width = d_query.shape
    count = lax.axis_size("seq")
    out = shape_of((rows, width), BF16)
    return pl.pallas_call(
        spatial_weights_kernel,
        out_shape=[shape_of((2, count, 3 * width // count, width // 2), BF16), out, out],
        in_specs=[WHOLE] * 4,
        out_specs=[WHOLE] * 3,
        compiler_params=params(),
        cost_estimate=pl.CostEstimate(
            flops=6 * rows * width * width, bytes_accessed=16 * 2**20, transcendentals=0
        ),
    )(d_query, d_pair, came, normed)


def first_kernel(
    grad_second, d_query, d_key, d_value, tok, hot, table, gain, wq, wk, wv,
    token_grad, d_norm, d_table,
    held, sems,
):
    copies = [
        pltpu.make_async_copy(source, held.at[at], sems.at[at])
        for at, source in enumerate((wq, wk, wv))
    ]
    for copy in copies:
        copy.start()
    for copy in copies:
        copy.wait()
    rows = tok.shape[0]
    width = tok.shape[1]

    def back_rows(step, carry):
        here = pl.ds(pl.multiple_of(step * 256, 256), 256)
        grad = (
            dot_nt(d_query[here, :], held[0])
            + dot_nt(d_key[here, :], held[1])
            + dot_nt(d_value[here, :], held[2])
        )
        first = tok[here, :].astype(F32) + dot(hot[here, :], table[...])
        hat, rate = normalise(first)
        total = grad_second[here, :].astype(F32) + norm_backward(grad, hat, rate, gain[...])
        token_grad[here, :] = total.astype(BF16)
        high = total.astype(BF16)
        rest = (total - high.astype(F32)).astype(BF16)
        chosen = hot[here, :]
        return (
            carry[0] + jnp.sum(grad * hat, axis=0, keepdims=True),
            carry[1] + jnp.sum(grad, axis=0, keepdims=True),
            carry[2] + dot_tn(chosen, high)[:8] + dot_tn(chosen, rest)[:8],
        )

    zero = jnp.zeros((1, width), F32)
    sums = lax.fori_loop(0, rows // 256, back_rows, (zero, zero, jnp.zeros((8, width), F32)))
    d_norm[0:1, :] = sums[0]
    d_norm[1:2, :] = sums[1]
    d_table[...] = sums[2]


def first_grad(grad_second, d_query, d_key, d_value, tok, hot, table, gain, wq, wk, wv):
    rows, width = tok.shape
    return pl.pallas_call(
        first_kernel,
        out_shape=[
            shape_of((rows, width), BF16),
            shape_of((2, width), F32),
            shape_of((8, width), F32),
        ],
        in_specs=[WHOLE] * 8 + [IN_HBM] * 3,
        out_specs=[WHOLE] * 3,
        scratch_shapes=[pltpu.VMEM((3, width, width), BF16), pltpu.SemaphoreType.DMA((3,))],
        compiler_params=params(),
        cost_estimate=pl.CostEstimate(
            flops=6 * rows * width * width, bytes_accessed=14 * 2**20, transcendentals=0
        ),
    )(grad_second, d_query, d_key, d_value, tok, hot, table, gain, wq, wk, wv)


def exchange_kernel(to_time, meta, source, target, staged, came, send_sems, recv_sems):
    me = lax.axis_index("seq")
    count = lax.axis_size("seq")
    tile = lax.axis_index("tile")
    reach = 3
    offset = meta[1]
    steps = [step for step in range(reach, -reach - 1, -1) if step != 0]

    def peer(step):
        return (me + step, tile)

    def present(step):
        return (me + step >= 0) & (me + step < count)

    barrier = pltpu.get_barrier_semaphore()
    for step in steps:
        @pl.when(present(step))
        def _(step=step):
            pl.semaphore_signal(barrier, inc=1, device_id=peer(step), device_id_type=MESH)
    pl.semaphore_wait(barrier, jnp.minimum(me, reach) + jnp.minimum(count - 1 - me, reach))

    def copy(step):
        slot = reach - step
        return pltpu.make_async_remote_copy(
            src_ref=staged.at[slot],
            dst_ref=came.at[slot],
            send_sem=send_sems.at[slot],
            recv_sem=recv_sems.at[slot],
            device_id=peer(step),
            device_id_type=MESH,
        )

    for step in steps + [0]:
        slot = reach - step
        which = jnp.clip(offset + step, 0, reach)
        if to_time:
            block = jnp.swapaxes(source[:, pl.ds(which, 1)][:, 0], 0, 1)
        else:
            block = source[:, pl.ds(which, 1)][:, 0]
        if step == 0:
            came[slot] = block
        else:
            staged[slot] = block

            @pl.when(present(step))
            def _(step=step):
                copy(step).start()

    for step in steps:
        @pl.when(present(step))
        def _(step=step):
            copy(step).wait_send()

        @pl.when(present(-step))
        def _(step=step):
            copy(step).wait_recv()

    is_big = jnp.full(came.shape[1:], meta[0], jnp.int32) == 1
    for at in range(reach + 1):
        moved = came[pl.ds(reach - offset + at, 1)][0]
        if to_time:
            mine = jnp.swapaxes(source[at], 0, 1)
            target[:, at] = jnp.where(is_big, moved, mine)
        else:
            pass
    if not to_time:
        for at in range(reach + 1):
            for frame in range(4):
                moved = came[pl.ds(reach - offset + at, 1), :, frame][0]
                mine = source[:, frame, at]
                target[frame, at] = jnp.where(is_big[:, 0], moved, mine)


def exchange(meta, values, to_time, number):
    rows, width = values.shape
    spatial_dims, time_dims = (4, 4, 2, 16, width), (2, 4, 4, 16, width)
    block = (2, 4, 16, width)
    out = pl.pallas_call(
        functools.partial(exchange_kernel, to_time),
        out_shape=shape_of(time_dims if to_time else spatial_dims, BF16),
        in_specs=[IN_SMEM, WHOLE],
        out_specs=WHOLE,
        scratch_shapes=[
            pltpu.VMEM((7,) + block, BF16),
            pltpu.VMEM((7,) + block, BF16),
            pltpu.SemaphoreType.DMA((7,)),
            pltpu.SemaphoreType.DMA((7,)),
        ],
        compiler_params=params(collective_id=number, has_side_effects=True),
    )(meta, values.reshape(spatial_dims if to_time else time_dims))
    return out.reshape(rows, width)


def across(value):
    return lax.ppermute(value, "tile", [(0, 1), (1, 0)])


def seq_dims(count):
    return {16: (4, 2, 2), 64: (4, 4, 4)}.get(count, (1, 1, count))


ORDERS = ((2, 1, 0), (1, 2, 0))


class Grid:
    def __init__(self):
        self.count = lax.axis_size("seq")
        self.dims = seq_dims(self.count)
        self.me = lax.axis_index("seq")
        self.tile = lax.axis_index("tile")
        self.strides = (self.dims[1] * self.dims[2], self.dims[2], 1)
        self.places = [
            lax.rem(self.me // stride, size) for stride, size in zip(self.strides, self.dims)
        ]

    def along(self, axis, step):
        place = self.places[axis]
        there = lax.rem(place + step, self.dims[axis])
        return there, (self.me + (there - place) * self.strides[axis], self.tile)

    def other(self):
        return (self.me, 1 - self.tile)

    def meet(self):
        barrier = pltpu.get_barrier_semaphore()
        peers = [self.other()]
        for axis in range(3):
            peers += [self.along(axis, step)[1] for step in range(1, self.dims[axis])]
        for peer in peers:
            pl.semaphore_signal(barrier, inc=1, device_id=peer, device_id_type=MESH)
        pl.semaphore_wait(barrier, len(peers))


def remote(source, target, send_sem, recv_sem, device):
    return pltpu.make_async_remote_copy(
        src_ref=source,
        dst_ref=target,
        send_sem=send_sem,
        recv_sem=recv_sem,
        device_id=device,
        device_id_type=MESH,
    )


class Unit:
    def __init__(self, grid, order, rows, halves, out, bufs, sems, number, whole=False):
        self.grid, self.order, self.rows, self.whole = grid, order, rows, whole
        self.halves, self.out = halves, out
        self.kept, self.came = bufs[0], bufs[1:]
        self.sems, self.number = sems, number

    def source(self, phase, there):
        if phase == 1:
            where = [slice(None)] * 3
            where[self.order[0]] = there
            return self.came[0].at[tuple(where)]
        if phase == 2:
            rest = [axis for axis in range(3) if axis != self.order[0]]
            where = [slice(None)] * 2
            where[rest.index(self.order[1])] = there
            return self.came[1].at[(0,) + tuple(where)]
        return self.came[2].at[0, there]

    def copies(self, phase):
        sends, recvs = self.sems
        axis = self.order[phase - 1]
        out = []
        for step in range(1, self.grid.dims[axis]):
            there, device = self.grid.along(axis, step)
            out.append(
                remote(
                    self.source(phase, there),
                    self.came[phase].at[step - 1],
                    sends.at[self.number, phase, step - 1],
                    recvs.at[self.number, phase, step - 1],
                    device,
                )
            )
        return out

    def first(self):
        sends, recvs = self.sems
        count, dims = self.grid.count, self.grid.dims
        if self.whole:
            there = here = self.halves
        else:
            there = self.halves.at[1 - self.grid.tile, :, :, :, self.rows]
            here = self.halves.at[self.grid.tile, :, :, :, self.rows]
        return (
            remote(there, self.came[0], sends.at[self.number, 0, 0], recvs.at[self.number, 0, 0], self.grid.other()),
            pltpu.make_async_copy(here, self.kept, sends.at[self.number, 0, 1]),
        )

    def last(self):
        sends, recvs = self.sems
        mine = self.out.at[self.grid.tile, self.rows]
        return remote(mine, mine, sends.at[self.number, 4, 0], recvs.at[self.number, 4, 0], self.grid.other())

    def start(self, phase):
        if phase == 0:
            for copy in self.first():
                copy.start()
        elif phase == 4:
            self.last().start()
        else:
            for copy in self.copies(phase):
                copy.start()

    def wait(self, phase):
        if phase == 0:
            for copy in self.first():
                copy.wait()
        elif phase == 4:
            self.last().wait()
        else:
            for copy in self.copies(phase):
                copy.wait()

    def add(self, phase):
        grid, dims = self.grid, self.grid.dims
        if phase == 0:
            def step(at, _):
                where = (at // (dims[1] * dims[2]), lax.rem(at // dims[2], dims[1]), lax.rem(at, dims[2]))
                self.came[0][where] = self.came[0][where] + self.kept[where]
                return 0

            lax.fori_loop(0, grid.count, step, 0)
            return
        axis = self.order[phase - 1]
        mine = self.source(phase, grid.places[axis])
        came = self.came[phase]
        size = dims[axis]
        if phase == 3:
            total = mine[...].astype(F32)
            for at in range(size - 1):
                total = total + came[at].astype(F32)
            if self.whole:
                self.out[...] = total
            else:
                self.out[grid.tile, self.rows] = total.astype(BF16)
            return
        extent = mine.shape[:-2]
        steps = 1
        for dim in extent:
            steps *= dim

        def step(at, _):
            where = (at,) if len(extent) == 1 else (at // extent[1], lax.rem(at, extent[1]))
            total = mine[where]
            for other in range(size - 1):
                total = total + came[(other,) + where]
            came[(0,) + where] = total
            return 0

        lax.fori_loop(0, steps, step, 0)

    def turn(self, phase):
        self.wait(phase)
        self.add(phase)
        if phase < 3 or not self.whole:
            self.start(phase + 1)


def unit_scratch(rows, width, order, dims, kind=BF16):
    kept = pltpu.VMEM(dims + (rows, width), kind)
    first = pltpu.VMEM(dims + (rows, width), kind)
    rest = tuple(dims[axis] for axis in range(3) if axis != order[0])
    second = pltpu.VMEM((max(dims[order[0]] - 1, 1),) + rest + (rows, width), kind)
    third = pltpu.VMEM((max(dims[order[1]] - 1, 1), dims[0], rows, width), kind)
    fourth = pltpu.VMEM((max(dims[0] - 1, 1), rows, width), kind)
    return [kept, first, second, third, fourth]


def scatter_kernel(groups, *refs):
    halves, outs = refs[:groups], refs[groups : 2 * groups]
    bufs = refs[2 * groups : -2]
    grid = Grid()
    grid.meet()
    units = []
    for group in range(groups - 1):
        rows = halves[group].shape[4] // 2
        for which in range(2):
            number = len(units)
            units.append(
                Unit(
                    grid, ORDERS[which], pl.ds(which * rows, rows), halves[group], outs[group],
                    bufs[5 * number : 5 * number + 5], refs[-2:], number,
                )
            )
    number = len(units)
    units.append(
        Unit(
            grid, ORDERS[0], None, halves[-1], outs[-1], bufs[5 * number : 5 * number + 5],
            refs[-2:], number, True,
        )
    )
    for unit in units:
        unit.start(0)
    for phase in range(4):
        for unit in units:
            unit.turn(phase)
    for unit in units[:-1]:
        unit.wait(4)


def reduce_scatter(groups, small, number):
    count = lax.axis_size("seq")
    dims = seq_dims(count)
    outs, scratch = [], []
    for group in groups:
        rows, width = group.shape[2:]
        outs.append(shape_of((2, rows, width), BF16))
        for order in ORDERS:
            scratch += unit_scratch(rows // 2, width, order, dims)
    outs.append(shape_of(small.shape[1:], F32))
    scratch += unit_scratch(small.shape[1], small.shape[2], ORDERS[0], dims, F32)
    sems = pltpu.SemaphoreType.DMA((2 * len(groups) + 1, 5, max(max(dims) - 1, 2)))
    return pl.pallas_call(
        functools.partial(scatter_kernel, len(groups) + 1),
        out_shape=outs,
        in_specs=[IN_HBM] * (len(groups) + 1),
        out_specs=[WHOLE] * (len(groups) + 1),
        scratch_shapes=scratch + [sems, sems],
        compiler_params=params(collective_id=number, has_side_effects=True),
    )(
        *[group.reshape((2,) + dims + group.shape[2:]) for group in groups],
        small.reshape(dims + small.shape[1:]),
    )


def split_three(values):
    high = values.astype(BF16)
    rest = values - high.astype(F32)
    middle = rest.astype(BF16)
    return high, middle, (rest - middle.astype(F32)).astype(BF16)


def on_device(
    tokens,
    cotangent,
    clip_big,
    actions,
    action_table,
    norm_gain,
    norm_bias,
    spatial_q,
    spatial_k,
    spatial_v,
    spatial_o,
    temporal_q,
    temporal_k,
    temporal_v,
    temporal_o,
    ffn_in,
    ffn_bias_in,
    ffn_out,
    ffn_bias_out,
):
    tok = tokens[0]
    rows, width = tok.shape
    span = (GRID_BIG // GRID_SMALL) ** 2
    me = lax.axis_index("seq")
    tile = lax.axis_index("tile")
    count = lax.axis_size("seq")
    sizes = jnp.where(clip_big == 1, span, 1).astype(jnp.int32)
    ends = jnp.cumsum(sizes)
    clip = jnp.sum((ends <= me).astype(jnp.int32))
    chosen = jnp.arange(clip_big.shape[0], dtype=jnp.int32) == clip
    is_big = jnp.sum(jnp.where(chosen, clip_big, 0))
    offset = jnp.where(is_big == 1, me - jnp.sum(jnp.where(chosen, ends - sizes, 0)), 0)
    frame = clip * FRAMES + offset * (FRAMES // span)
    meta = jnp.stack([is_big, offset]).astype(jnp.int32)
    row = jnp.arange(rows, dtype=jnp.int32)
    frame_of = frame + jnp.where(is_big == 1, row // 128, row // 32)
    action = jnp.sum(
        jnp.where(
            frame_of[:, None] == jnp.arange(actions.shape[0], dtype=jnp.int32)[None, :],
            actions[None, :],
            0,
        ),
        axis=1,
    )
    lane = jnp.arange(WIDE, dtype=jnp.int32)
    hot = ((action[:, None] == (lane % 8)[None, :]) & (lane < 24)[None, :]).astype(BF16)
    table = jnp.concatenate(
        list(split_three(action_table)) + [jnp.zeros((WIDE - 24, width), BF16)], axis=0
    )
    gains = [norm_gain[at : at + 1] for at in range(3)]
    shifts = [norm_bias[at : at + 1] for at in range(3)]

    normed_one, query_one, key_one, value_one = project(
        tok, hot, table, gains[0], shifts[0], spatial_q, spatial_k, spatial_v
    )
    pair_one = across(jnp.stack([key_one, value_one]))
    cot = exchange(meta, cotangent[0], True, 1)
    mixed_one, probs_one, second_low = spatial(
        meta, query_one, key_one, value_one, pair_one, tok, hot, table, spatial_o
    )
    second = exchange(meta, second_low, True, 2)
    normed_two, query_two, key_two, value_two, probs_two, mixed_two, third = temporal(
        second, gains[1], shifts[1], temporal_q, temporal_k, temporal_v, temporal_o
    )
    mixed, grad_third, d_in, d_out, d_bin, d_norm_three, d_bout = ffn(
        third, cot, gains[2], shifts[2], ffn_in, ffn_bias_in, ffn_out, ffn_bias_out
    )
    mixed = exchange(meta, mixed, False, 3)
    finer = count // d_in.shape[1]
    d_in = d_in.reshape(2, -1, width // 2, finer, d_in.shape[3] // finer).transpose(0, 1, 3, 2, 4)
    d_in = d_in.reshape(2, count, -1, max(d_in.shape[-1], WIDE))
    d_out = d_out.reshape(2, count, max(width // count, 32), -1)
    grad_second, d_temporal, d_norm_two = temporal_back(
        grad_third, second, mixed_two, query_two, key_two, value_two, normed_two, probs_two,
        gains[1], temporal_q, temporal_k, temporal_v, temporal_o,
    )
    grad_second = exchange(meta, grad_second, False, 4)

    d_query, d_pair, d_away, d_wo = spatial_back(
        grad_second, mixed_one, query_one, key_one, value_one, pair_one, probs_one, spatial_o
    )
    came = across(d_away)
    d_spatial, d_key, d_value = spatial_weights(d_query, d_pair, came, normed_one)
    token_grad, d_norm_one, d_table = first_grad(
        grad_second, d_query, d_key, d_value, tok, hot, table, gains[0],
        spatial_q, spatial_k, spatial_v,
    )

    part = width // count
    pieces = d_bin.shape[1] // width
    small = jnp.concatenate(
        [
            d_table,
            jnp.stack([d_norm_one[0], d_norm_two[0], d_norm_three[0]]),
            jnp.stack([d_norm_one[1], d_norm_two[1], d_norm_three[1]]),
            d_bout,
            d_bin.reshape(count, pieces, part).transpose(1, 0, 2).reshape(pieces, width),
        ],
        axis=0,
    )
    short = small.shape[0]
    small = jnp.pad(small.reshape(short, count, part).transpose(1, 0, 2), ((0, 0), (0, 13), (0, 0)))
    small = small.reshape(count, -1, WIDE)

    sum_out, sum_in, sum_temporal, sum_spatial, small = reduce_scatter(
        [d_out, d_in, d_temporal, jnp.concatenate([d_wo, d_spatial], axis=2)], small, 5
    )
    small = small.reshape(short + 13, part)
    ffn_in_grad = sum_in.reshape(width, -1).astype(F32)
    sum_out = sum_out.reshape(2, part, -1)
    ffn_out_grad = jnp.concatenate([sum_out[0], sum_out[1]], axis=1).T.astype(F32)

    def finish(summed):
        joined = jnp.concatenate([summed[0], summed[1]], axis=1).T.astype(F32)
        return [joined[:, at * part : (at + 1) * part] for at in range(4)]

    temporal_o_grad, temporal_q_grad, temporal_k_grad, temporal_v_grad = finish(sum_temporal)
    spatial_o_grad, spatial_q_grad, spatial_k_grad, spatial_v_grad = finish(sum_spatial)
    return (
        mixed[None],
        token_grad[None],
        small[0:8],
        small[8:11],
        small[11:14],
        spatial_q_grad,
        spatial_k_grad,
        spatial_v_grad,
        spatial_o_grad,
        temporal_q_grad,
        temporal_k_grad,
        temporal_v_grad,
        temporal_o_grad,
        ffn_in_grad,
        small[15:19].reshape(1, -1),
        ffn_out_grad,
        small[14:15],
    )


def solution(mesh):
    placed = (P("tile", "seq", None),) * 2 + (P(),) * 17
    return jax.shard_map(
        on_device,
        mesh=mesh,
        in_specs=placed,
        out_specs=(P("tile", "seq", None),) * 2 + (P(None, "seq"),) * 15,
        check_vma=False,
    )
```

```python
import functools

import jax
import jax.numpy as jnp
from jax import lax
from jax.experimental import pallas as pl
from jax.experimental.pallas import tpu as pltpu
from jax.sharding import PartitionSpec as P

HEAD_DIM = 64
FRAMES = 16
GRID_BIG = 16
GRID_SMALL = 8
WIDE = 128
KEYS = 256
CHUNK = 512
VMEM_BYTES = 62 * 2**20
FACTOR = HEAD_DIM**-0.5
ROOT = (2.0 / 3.141592653589793) ** 0.5

F32 = jnp.float32
BF16 = jnp.bfloat16
WHOLE = pl.BlockSpec(memory_space=pltpu.VMEM)
IN_HBM = pl.BlockSpec(memory_space=pl.ANY)
MESH = pl.DeviceIdType.MESH
IN_SMEM = pl.BlockSpec(memory_space=pltpu.SMEM)


def shape_of(dims, kind):
    return jax.ShapeDtypeStruct(dims, kind)


def params(**more):
    return pltpu.CompilerParams(vmem_limit_bytes=VMEM_BYTES, **more)


def dot(left, right):
    return jnp.dot(left, right, preferred_element_type=F32)


def dot_nt(left, right):
    return lax.dot_general(left, right, (((1,), (1,)), ((), ())), preferred_element_type=F32)


def dot_tn(left, right):
    return lax.dot_general(left, right, (((0,), (0,)), ((), ())), preferred_element_type=F32)


def normalise(values):
    centre = values - jnp.mean(values, axis=-1, keepdims=True)
    rate = lax.rsqrt(jnp.mean(centre * centre, axis=-1, keepdims=True) + 1e-05)
    return centre * rate, rate


def norm_backward(grad, hat, rate, gain):
    inner = grad * gain
    level = jnp.mean(inner, axis=-1, keepdims=True)
    slope = jnp.mean(inner * hat, axis=-1, keepdims=True)
    return rate * (inner - level - hat * slope)


def head_halves(block):
    lane = lax.broadcasted_iota(jnp.int32, block.shape, 1)
    zero = jnp.zeros_like(block)
    first = lane < HEAD_DIM
    return jnp.concatenate([jnp.where(first, block, zero), jnp.where(first, zero, block)], axis=0)


def join_halves(both):
    rows = both.shape[0] // 2
    lane = lax.broadcasted_iota(jnp.int32, (rows, both.shape[1]), 1)
    return jnp.where(lane < HEAD_DIM, both[:rows], both[rows:])


def attend(query, key, value, bias):
    scores = dot_nt(head_halves(query) * FACTOR, key) + bias
    top = jnp.max(scores, axis=1, keepdims=True)
    powers = jnp.exp(scores - top)
    prob = (powers * (1.0 / jnp.sum(powers, axis=1, keepdims=True))).astype(BF16)
    return prob, join_halves(dot(prob, value))


def attend_backward(prob, query, key, value, grad):
    grad_two = head_halves(grad)
    grad_prob = dot_nt(grad_two, value)
    prob_f = prob.astype(F32)
    delta = jnp.sum(prob_f * grad_prob, axis=1, keepdims=True)
    grad_score = (prob_f * (grad_prob - delta)).astype(BF16)
    grad_query = join_halves(dot(grad_score, key)) * FACTOR
    grad_key = dot_tn(grad_score, head_halves(query)) * FACTOR
    grad_value = dot_tn(prob, grad_two)
    return grad_query, grad_key, grad_value


def spatial_bias(is_big, rows):
    row = lax.broadcasted_iota(jnp.int32, (rows, KEYS), 0)
    column = lax.broadcasted_iota(jnp.int32, (rows, KEYS), 1)
    same = lax.rem(row, WIDE) // 32 == lax.rem(column, WIDE) // 32
    return jnp.where(same | (is_big == 1), 0.0, -1e30).astype(F32)


def temporal_bias(rows):
    row = lax.rem(lax.broadcasted_iota(jnp.int32, (rows, KEYS), 0), KEYS)
    column = lax.broadcasted_iota(jnp.int32, (rows, KEYS), 1)
    fits = (lax.rem(row, 16) == lax.rem(column, 16)) & (column <= row)
    return jnp.where(fits, 0.0, -1e30).astype(F32)


def columns_of(index):
    return pl.ds(pl.multiple_of(index * WIDE, WIDE), WIDE)


def project_kernel(tok, hot, table, gain, shift, wq, wk, wv, normed, query, key, value, held, sems):
    copies = [
        pltpu.make_async_copy(source, held.at[at], sems.at[at])
        for at, source in enumerate((wq, wk, wv))
    ]
    for copy in copies:
        copy.start()
    rows = tok.shape[0]

    def norm_rows(at, _):
        here = pl.ds(pl.multiple_of(at * 128, 128), 128)
        first = tok[here, :].astype(F32) + dot(hot[here, :], table[...])
        hat, _rate = normalise(first)
        normed[here, :] = (hat * gain[...] + shift[...]).astype(BF16)
        return 0

    lax.fori_loop(0, rows // 128, norm_rows, 0)
    for at, (copy, target) in enumerate(zip(copies, (query, key, value))):
        copy.wait()
        for part in range(4):
            side = pl.ds(part * 256, 256)
            target[:, side] = dot(normed[...], held[at, :, side]).astype(BF16)


def project(tok, hot, table, gain, shift, wq, wk, wv):
    rows, width = tok.shape
    out = shape_of((rows, width), BF16)
    return pl.pallas_call(
        project_kernel,
        out_shape=[out] * 4,
        in_specs=[WHOLE] * 5 + [IN_HBM] * 3,
        out_specs=[WHOLE] * 4,
        scratch_shapes=[pltpu.VMEM((3, width, width), BF16), pltpu.SemaphoreType.DMA((3,))],
        compiler_params=params(),
        cost_estimate=pl.CostEstimate(
            flops=6 * rows * width * width, bytes_accessed=12 * 2**20, transcendentals=0
        ),
    )(tok, hot, table, gain, shift, wq, wk, wv)


def spatial_kernel(meta, query, key, value, pair, tok, hot, table, wo, mixed, probs, second, kept, held, sem):
    at = pl.program_id(0)
    copy = pltpu.make_async_copy(wo, held, sem)

    @pl.when(at == 0)
    def _():
        copy.start()

    bias = spatial_bias(meta[0], 2 * WIDE)
    here = pl.ds(pl.multiple_of(at * WIDE, WIDE), WIDE)
    for two in range(8):
        side = pl.ds(two * WIDE, WIDE)
        keys = jnp.concatenate([key[:, side], pair[0, :, side]], axis=0)
        values = jnp.concatenate([value[:, side], pair[1, :, side]], axis=0)
        prob, out = attend(query[:, side], keys, values, bias)
        probs[0, two] = prob
        out = out.astype(BF16)
        mixed[:, side] = out
        kept[here, side] = out

    @pl.when(at == pl.num_programs(0) - 1)
    def _():
        copy.wait()
        for part in range(4):
            side = pl.ds(part * 256, 256)
            first = tok[:, side].astype(F32) + dot(hot[...], table[:, side])
            second[:, side] = (first + dot(kept[...], held[:, side])).astype(BF16)


def spatial(meta, query, key, value, pair, tok, hot, table, wo):
    rows, width = tok.shape
    block = pl.BlockSpec((WIDE, width), lambda i: (i, 0))

    def fixed(array):
        return pl.BlockSpec(array.shape, lambda i: (0,) * array.ndim)

    return pl.pallas_call(
        spatial_kernel,
        grid=(rows // WIDE,),
        out_shape=[
            shape_of((rows, width), BF16),
            shape_of((rows // WIDE, 8, 2 * WIDE, KEYS), BF16),
            shape_of((rows, width), BF16),
        ],
        in_specs=[
            IN_SMEM,
            block,
            block,
            block,
            pl.BlockSpec((2, WIDE, width), lambda i: (0, i, 0)),
            fixed(tok),
            fixed(hot),
            fixed(table),
            IN_HBM,
        ],
        out_specs=[
            block,
            pl.BlockSpec((1, 8, 2 * WIDE, KEYS), lambda i: (i, 0, 0, 0)),
            pl.BlockSpec((rows, width), lambda i: (0, 0)),
        ],
        scratch_shapes=[
            pltpu.VMEM((rows, width), BF16),
            pltpu.VMEM((width, width), BF16),
            pltpu.SemaphoreType.DMA,
        ],
        compiler_params=params(),
        cost_estimate=pl.CostEstimate(
            flops=8 * rows * width * width, bytes_accessed=14 * 2**20, transcendentals=0
        ),
    )(meta, query, key, value, pair, tok, hot, table, wo)


def temporal_kernel(
    second, gain, shift, wq, wk, wv, wo, normed, query, key, value, probs, mixed, third, held, sems
):
    copies = [
        pltpu.make_async_copy(source, held.at[at], sems.at[at])
        for at, source in enumerate((wq, wk, wv, wo))
    ]
    for copy in copies:
        copy.start()
    rows = second.shape[0]

    def norm_rows(at, _):
        here = pl.ds(pl.multiple_of(at * 128, 128), 128)
        hat, _rate = normalise(second[here, :].astype(F32))
        normed[here, :] = (hat * gain[...] + shift[...]).astype(BF16)
        return 0

    lax.fori_loop(0, rows // 128, norm_rows, 0)
    for at, target in enumerate((query, key, value)):
        copies[at].wait()
        for part in range(4):
            side = pl.ds(part * 256, 256)
            target[:, side] = dot(normed[...], held[at, :, side]).astype(BF16)
    bias = temporal_bias(2 * KEYS)

    def group(at, _):
        here = pl.ds(pl.multiple_of(at * KEYS, KEYS), KEYS)
        for two in range(8):
            side = pl.ds(two * WIDE, WIDE)
            prob, out = attend(query[here, side], key[here, side], value[here, side], bias)
            probs[at, two] = prob
            mixed[here, side] = out.astype(BF16)
        return 0

    lax.fori_loop(0, rows // KEYS, group, 0)
    copies[3].wait()
    for part in range(4):
        side = pl.ds(part * 256, 256)
        third[:, side] = second[:, side].astype(F32) + dot(mixed[...], held[3, :, side])


def temporal(second, gain, shift, wq, wk, wv, wo):
    rows, width = second.shape
    out = shape_of((rows, width), BF16)
    return pl.pallas_call(
        temporal_kernel,
        out_shape=[
            out,
            out,
            out,
            out,
            shape_of((rows // KEYS, 8, 2 * KEYS, KEYS), BF16),
            out,
            shape_of((rows, width), F32),
        ],
        in_specs=[WHOLE] * 3 + [IN_HBM] * 4,
        out_specs=[WHOLE] * 7,
        scratch_shapes=[pltpu.VMEM((4, width, width), BF16), pltpu.SemaphoreType.DMA((4,))],
        compiler_params=params(),
        cost_estimate=pl.CostEstimate(
            flops=14 * rows * width * width, bytes_accessed=20 * 2**20, transcendentals=0
        ),
    )(second, gain, shift, wq, wk, wv, wo)


def ffn_kernel(
    third, cot, gain, shift, win, bin_, wout, bout,
    mixed, grad_third, d_in, d_out, d_bin, d_norm, d_bout,
    normed, normed_t, cot_t, total, grad_normed,
):
    at = pl.program_id(0)
    rows = third.shape[0]

    @pl.when(at == 0)
    def _():
        def norm_rows(step, _):
            here = pl.ds(pl.multiple_of(step * 128, 128), 128)
            hat, _rate = normalise(third[here, :])
            normed[here, :] = (hat * gain[...] + shift[...]).astype(BF16)
            return 0

        lax.fori_loop(0, rows // 128, norm_rows, 0)
        normed_t[...] = normed[...].T
        cot_t[...] = cot[...].T
        d_bout[...] = jnp.sum(cot[...].astype(F32), axis=0, keepdims=True)
        total[...] = third[...] + bout[...]
        grad_normed[...] = jnp.zeros_like(grad_normed)

    half = CHUNK // 2
    for part in range(2):
        side = pl.ds(part * half, half)
        inner = dot(normed[...], win[:, side]) + bin_[:, side]
        square = inner * inner
        curve = jnp.tanh(ROOT * (inner + 0.044715 * inner * square))
        active = (0.5 * inner * (1.0 + curve)).astype(BF16)
        slope = 0.5 * (1.0 + curve) + (0.5 * ROOT) * inner * (1.0 - curve * curve) * (
            1.0 + (3 * 0.044715) * square
        )
        wide = slope * dot_nt(cot[...], wout[side, :])
        grad_inner = wide.astype(BF16)
        d_bin[:, side] = jnp.sum(grad_inner.astype(F32), axis=0, keepdims=True)
        total[...] += dot(active, wout[side, :])
        grad_normed[...] += dot_nt(grad_inner, win[:, side])
        count, share = d_out.shape[1], d_out.shape[2]
        d_out[0, :, :, side] = dot(cot_t[...], active).astype(BF16).reshape(count, share, half)
        for top in range(4):
            block = dot(normed_t[top * 256 : (top + 1) * 256, :], grad_inner)
            d_in[top // 2, part, :, (top % 2) * half : (top % 2 + 1) * half] = block.astype(BF16)

    @pl.when(at == pl.num_programs(0) - 1)
    def _():
        mixed[...] = total[...].astype(BF16)

        def back_rows(step, carry):
            here = pl.ds(pl.multiple_of(step * 128, 128), 128)
            hat, rate = normalise(third[here, :])
            grad = grad_normed[here, :]
            grad_third[here, :] = (
                cot[here, :].astype(F32) + norm_backward(grad, hat, rate, gain[...])
            ).astype(BF16)
            return (
                carry[0] + jnp.sum(grad * hat, axis=0, keepdims=True),
                carry[1] + jnp.sum(grad, axis=0, keepdims=True),
            )

        zero = jnp.zeros((1, third.shape[1]), F32)
        sums = lax.fori_loop(0, rows // 128, back_rows, (zero, zero))
        d_norm[0:1, :] = sums[0]
        d_norm[1:2, :] = sums[1]


def ffn(third, cot, gain, shift, win, bin_, wout, bout):
    rows, width = third.shape
    hidden = win.shape[1]
    steps = hidden // CHUNK
    count = lax.axis_size("seq")
    share = width // count

    def fixed(*dims):
        return pl.BlockSpec(dims, lambda i: (0,) * len(dims))

    return pl.pallas_call(
        ffn_kernel,
        grid=(steps,),
        out_shape=[
            shape_of((rows, width), BF16),
            shape_of((rows, width), BF16),
            shape_of((2, hidden // KEYS, width // 4, 2 * KEYS), BF16),
            shape_of((2, count, 4 * share, CHUNK), BF16),
            shape_of((1, hidden), F32),
            shape_of((2, width), F32),
            shape_of((1, width), F32),
        ],
        in_specs=[
            fixed(rows, width),
            fixed(rows, width),
            fixed(1, width),
            fixed(1, width),
            pl.BlockSpec((width, CHUNK), lambda i: (0, i)),
            pl.BlockSpec((1, CHUNK), lambda i: (0, i)),
            pl.BlockSpec((CHUNK, width), lambda i: (i, 0)),
            fixed(1, width),
        ],
        out_specs=[
            fixed(rows, width),
            fixed(rows, width),
            pl.BlockSpec((2, 2, width // 4, 2 * KEYS), lambda i: (0, i, 0, 0)),
            pl.BlockSpec((1, count, share, CHUNK), lambda i: (i // 4, 0, lax.rem(i, 4), 0)),
            pl.BlockSpec((1, CHUNK), lambda i: (0, i)),
            fixed(2, width),
            fixed(1, width),
        ],
        scratch_shapes=[
            pltpu.VMEM((rows, width), BF16),
            pltpu.VMEM((width, rows), BF16),
            pltpu.VMEM((width, rows), BF16),
            pltpu.VMEM((rows, width), F32),
            pltpu.VMEM((rows, width), F32),
        ],
        compiler_params=params(),
        cost_estimate=pl.CostEstimate(
            flops=12 * rows * width * hidden, bytes_accessed=40 * 2**20, transcendentals=0
        ),
    )(third, cot, gain, shift, win, bin_, wout, bout)


def weight_grad(target, at, grad, normed):
    grad_t = grad.T
    count, _rows, width = target.shape[1:]
    part = grad_t.shape[0] // count
    for which in range(2):
        block = dot(grad_t, normed[:, which * width : (which + 1) * width]).astype(BF16)
        target[which, :, at * part : (at + 1) * part, :] = block.reshape(count, part, width)


REACH = 3
STEPS = tuple(step for step in range(REACH, -REACH - 1, -1) if step != 0)


class Swap:
    def __init__(self, to_time, offset, is_big, source, staged, came, sems):
        self.me, self.tile = lax.axis_index("seq"), lax.axis_index("tile")
        self.count = lax.axis_size("seq")
        self.to_time, self.offset, self.is_big = to_time, offset, is_big
        self.source, self.staged, self.came, self.sems = source, staged, came, sems

    def peer(self, step):
        return (self.me + step, self.tile)

    def present(self, step):
        return (self.me + step >= 0) & (self.me + step < self.count)

    def greet(self, barrier):
        for step in STEPS:
            @pl.when(self.present(step))
            def _(step=step):
                pl.semaphore_signal(
                    barrier, inc=1, device_id=self.peer(step), device_id_type=MESH
                )
        return jnp.minimum(self.me, REACH) + jnp.minimum(self.count - 1 - self.me, REACH)

    def copy(self, step):
        slot = REACH - step
        return remote(
            self.staged.at[slot], self.came.at[slot], self.sems[0].at[slot], self.sems[1].at[slot],
            self.peer(step),
        )

    def stage(self, step):
        which = jnp.clip(self.offset + step, 0, REACH)
        target = self.came if step == 0 else self.staged
        slot = REACH - step
        for side in range(2):
            if self.to_time:
                for frame in range(4):
                    target[slot, side * 64 + frame * 16 : side * 64 + frame * 16 + 16] = self.source[
                        pl.ds(which * 2 + (frame * 8 + side), 1)
                    ][0]
            else:
                block = self.source[pl.ds(which * 4 + side * 16, 4)]
                target[slot, side * 64 : side * 64 + 64] = block.reshape(64, block.shape[2])

    def send(self):
        for step in STEPS:
            self.stage(step)

            @pl.when(self.present(step))
            def _(step=step):
                self.copy(step).start()

        self.stage(0)

    def wait(self):
        for step in STEPS:
            @pl.when(self.present(step))
            def _(step=step):
                self.copy(step).wait_send()

            @pl.when(self.present(-step))
            def _(step=step):
                self.copy(step).wait_recv()

    def place(self, target):
        width = target.shape[-1]
        chosen = jnp.full((16, width), self.is_big, jnp.int32) == 1
        for at in range(REACH + 1):
            slot = REACH - self.offset + at
            for side in range(2):
                for frame in range(4):
                    low = side * 64 + frame * 16
                    moved = self.came[pl.ds(slot, 1), low : low + 16][0]
                    if self.to_time:
                        here, mine = side * 256 + at * 64 + frame * 16, at * 8 + frame * 2 + side
                    else:
                        here, mine = frame * 128 + at * 32 + side * 16, side * 16 + frame * 4 + at
                    target[here : here + 16] = jnp.where(chosen, moved, self.source[mine])


def exchange_kernel(to_time, meta, source, target, staged, came, send_sems, recv_sems):
    swap = Swap(to_time, meta[1], meta[0], source, staged, came, (send_sems, recv_sems))
    barrier = pltpu.get_barrier_semaphore()
    pl.semaphore_wait(barrier, swap.greet(barrier))
    swap.send()
    swap.wait()
    swap.place(target)


def exchange(meta, values, to_time, number):
    rows, width = values.shape
    return pl.pallas_call(
        functools.partial(exchange_kernel, to_time),
        out_shape=shape_of((rows, width), BF16),
        in_specs=[IN_SMEM, WHOLE],
        out_specs=WHOLE,
        scratch_shapes=[
            pltpu.VMEM((7, 128, width), BF16),
            pltpu.VMEM((7, 128, width), BF16),
            pltpu.SemaphoreType.DMA((7,)),
            pltpu.SemaphoreType.DMA((7,)),
        ],
        compiler_params=params(collective_id=number, has_side_effects=True),
    )(meta, values.reshape(rows // 16, 16, width))


def across(value):
    return lax.ppermute(value, "tile", [(0, 1), (1, 0)])


def seq_dims(count):
    return {16: (4, 2, 2), 64: (4, 4, 4)}.get(count, (1, 1, count))


ORDERS = ((2, 1, 0), (1, 2, 0))


class Grid:
    def __init__(self):
        self.count = lax.axis_size("seq")
        self.dims = seq_dims(self.count)
        self.me = lax.axis_index("seq")
        self.tile = lax.axis_index("tile")
        self.strides = (self.dims[1] * self.dims[2], self.dims[2], 1)
        self.places = [
            lax.rem(self.me // stride, size) for stride, size in zip(self.strides, self.dims)
        ]

    def along(self, axis, step):
        place = self.places[axis]
        there = lax.rem(place + step, self.dims[axis])
        return there, (self.me + (there - place) * self.strides[axis], self.tile)

    def other(self):
        return (self.me, 1 - self.tile)

    def peers(self, phase, order):
        if phase == 0:
            return [self.other()]
        axis = order[phase - 1]
        return [self.along(axis, step)[1] for step in range(1, self.dims[axis])]

    def greet(self, barrier):
        peers = [self.other()]
        for axis in range(3):
            peers += [self.along(axis, step)[1] for step in range(1, self.dims[axis])]
        for peer in peers:
            pl.semaphore_signal(barrier, inc=1, device_id=peer, device_id_type=MESH)
        return len(peers)


def remote(source, target, send_sem, recv_sem, device):
    return pltpu.make_async_remote_copy(
        src_ref=source,
        dst_ref=target,
        send_sem=send_sem,
        recv_sem=recv_sem,
        device_id=device,
        device_id_type=MESH,
    )


class Unit:
    def __init__(self, grid, which, group, halves, kept, out, bufs, sems, free, number):
        self.grid, self.order = grid, ORDERS[which]
        rows = halves.shape[4] // 2
        self.rows = pl.ds(which * rows, rows)
        self.halves, self.kept, self.out, self.came = halves, kept, out, bufs
        self.sends, self.recvs = sems
        self.number = number
        self.free, self.slot, self.again = free, number % 4, group >= 2

    def source(self, phase, there):
        if phase == 1:
            where = [slice(None)] * 3
            where[self.order[0]] = there
            return self.came[0].at[tuple(where)]
        if phase == 2:
            rest = [axis for axis in range(3) if axis != self.order[0]]
            where = [slice(None)] * 2
            where[rest.index(self.order[1])] = there
            return self.came[1].at[(0,) + tuple(where)]
        return self.came[2].at[0, there]

    def copies(self, phase):
        number = self.number
        if phase == 0:
            away = self.halves.at[1 - self.grid.tile, :, :, :, self.rows]
            return [
                remote(
                    away, self.came[0], self.sends.at[number, 0, 0], self.recvs.at[number, 0, 0],
                    self.grid.other(),
                )
            ]
        if phase == 4:
            mine = self.out.at[self.grid.tile, self.rows]
            return [
                remote(
                    mine, mine, self.sends.at[number, 4, 0], self.recvs.at[number, 4, 0],
                    self.grid.other(),
                )
            ]
        axis = self.order[phase - 1]
        out = []
        for step in range(1, self.grid.dims[axis]):
            there, device = self.grid.along(axis, step)
            out.append(
                remote(
                    self.source(phase, there), self.came[phase].at[step - 1],
                    self.sends.at[number, phase, step - 1], self.recvs.at[number, phase, step - 1],
                    device,
                )
            )
        return out

    def fetch(self, part):
        half = self.grid.dims[0] // 2
        here = self.halves.at[self.grid.tile, pl.ds(part * half, half), :, :, self.rows]
        return pltpu.make_async_copy(here, self.kept, self.sends.at[self.number, 0, 1])

    def start(self, phase):
        if self.again and phase < 4:
            amount = len(self.grid.peers(phase, self.order))
            pl.semaphore_wait(self.free.at[self.slot, phase], amount)
        for copy in self.copies(phase):
            copy.start()

    def release(self, phase):
        if not self.again:
            for peer in self.grid.peers(phase, self.order):
                pl.semaphore_signal(
                    self.free.at[self.slot, phase], inc=1, device_id=peer, device_id_type=MESH
                )

    def wait(self, phase):
        for copy in self.copies(phase):
            copy.wait()

    def turn(self, phase):
        self.wait(phase)
        grid, dims = self.grid, self.grid.dims
        if phase == 0:
            def place(at):
                return (at // (dims[1] * dims[2]), lax.rem(at // dims[2], dims[1]), lax.rem(at, dims[2]))

            def step(at, _):
                where = place(at)
                self.came[0][where] = self.came[0][where] + self.halves[(grid.tile,) + where + (self.rows,)]
                return 0

            def step_kept(base, at, _):
                where = place(at)
                there = (where[0] + base,) + where[1:]
                self.came[0][there] = self.came[0][there] + self.kept[where]
                return 0

            if self.kept is None:
                lax.fori_loop(0, grid.count, step, 0)
                return
            for part in range(2):
                copy = self.fetch(part)
                copy.start()
                copy.wait()
                lax.fori_loop(0, grid.count // 2, functools.partial(step_kept, part * dims[0] // 2), 0)
            return
        axis = self.order[phase - 1]
        own = self.source(phase, grid.places[axis])
        came = self.came[phase]
        size = dims[axis]
        if phase == 3:
            total = own[...].astype(F32)
            for at in range(size - 1):
                total = total + came[at].astype(F32)
            self.out[grid.tile, self.rows] = total.astype(BF16)
            self.release(2)
            self.release(3)
            return
        extent = own.shape[:-2]
        steps = 1
        for dim in extent:
            steps *= dim

        def step(at, _):
            where = (at,) if len(extent) == 1 else (at // extent[1], lax.rem(at, extent[1]))
            total = own[where]
            for other in range(size - 1):
                total = total + came[(other,) + where]
            came[(0,) + where] = total
            return 0

        lax.fori_loop(0, steps, step, 0)
        self.release(phase - 1)


class Pair:
    def __init__(self, *units):
        self.units = units

    def start(self, phase):
        for unit in self.units:
            unit.start(phase)

    def turn(self, phase):
        for unit in self.units:
            unit.turn(phase)

    def on(self, phase):
        for unit in self.units:
            unit.turn(phase)
            unit.start(phase + 1)

    def wait(self, phase):
        for unit in self.units:
            unit.wait(phase)


class Total:
    def __init__(self, grid, value, came, sends, recvs):
        self.grid, self.value, self.came, self.sends, self.recvs = grid, value, came, sends, recvs

    def copies(self, phase):
        first = sum(len(self.grid.peers(before, (2, 1, 0))) for before in range(phase))
        return [
            remote(
                self.value.at[phase], self.came.at[first + at], self.sends.at[first + at],
                self.recvs.at[first + at], peer,
            )
            for at, peer in enumerate(self.grid.peers(phase, (2, 1, 0)))
        ]

    def start(self, phase):
        for copy in self.copies(phase):
            copy.start()

    def on(self, phase):
        copies = self.copies(phase)
        for copy in copies:
            copy.wait()
        total = self.value[phase]
        first = sum(len(self.grid.peers(before, (2, 1, 0))) for before in range(phase))
        for at in range(len(copies)):
            total = total + self.came[first + at]
        self.value[phase + 1] = total
        if phase < 3:
            self.start(phase + 1)


def unit_scratch(rows, width, order, dims):
    rest = tuple(dims[axis] for axis in range(3) if axis != order[0])
    return [
        pltpu.VMEM(dims + (rows, width), BF16),
        pltpu.VMEM((max(dims[order[0]] - 1, 1),) + rest + (rows, width), BF16),
        pltpu.VMEM((max(dims[order[1]] - 1, 1), dims[0], rows, width), BF16),
        pltpu.VMEM((max(dims[0] - 1, 1), rows, width), BF16),
    ]


def back_kernel(
    meta, d_out, d_in, third, second, mixed_t, query_t, key_t, value_t, normed_t, probs_t,
    wq_t, wk_t, wv_t, wo_t, mixed_s, query_s, key_s, value_s, pair, normed_s, probs_s,
    wq_s, wk_s, wv_s, wo_s, tok, hot, table, gain_one, gain_two, small_ffn,
    token_grad, sum_out, sum_in, sum_time, sum_space, small,
    pool, turned, held, probs, d_weights, kept, came_key, came_value, swapped, *rest,
):
    unit_bufs, rest = rest[:16], rest[16:]
    (totals, total_came, loads, unit_sends, unit_recvs, free, swap_sends, swap_recvs,
     total_sends, total_recvs, pair_sems) = rest
    rows, width = 512, pool.shape[2]
    grid = Grid()
    swap = Swap(
        False, meta[1], meta[0], turned, _Slots(pool, 8), swapped, (swap_sends, swap_recvs)
    )
    barrier = pltpu.get_barrier_semaphore()
    pl.semaphore_wait(barrier, grid.greet(barrier) + swap.greet(barrier))

    used = [0]

    def load(source, target):
        copy = pltpu.make_async_copy(source, target, loads.at[used[0]])
        used[0] += 1
        copy.start()
        return copy

    sums = (sum_out, sum_in, sum_time, sum_space)
    sources = (d_out, d_in, d_weights, d_weights)
    pairs = []
    for group in range(4):
        bufs = unit_bufs[8 * (group % 2) : 8 * (group % 2) + 8]
        pairs.append(
            Pair(
                *[
                    Unit(
                        grid, which, group, sources[group], kept if group < 2 else None,
                        sums[group], bufs[4 * which : 4 * which + 4], (unit_sends, unit_recvs), free,
                        2 * group + which,
                    )
                    for which in range(2)
                ]
            )
        )
    p0, p1, p2, p3 = pairs
    p0.start(0)
    p1.start(0)

    in_low = load(third, pool.at[0])
    in_mixed = load(mixed_t, pool.at[2])
    weights = [load(source, held.at[at]) for at, source in enumerate((wo_t, wq_t, wk_t, wv_t))]
    ins = [load(source, pool.at[3 + at]) for at, source in enumerate((query_t, key_t, value_t))]
    ins += [load(probs_t.at[at], probs.at[at]) for at in range(2)]
    late = [load(second, pool.at[1]), load(normed_t, pool.at[6])]
    in_low.wait()
    in_mixed.wait()
    flat_weights = d_weights.reshape(2, grid.count, d_weights.shape[4], d_weights.shape[5])
    weight_grad(flat_weights, 0, pool[0], pool.at[2])
    weights[0].wait()

    def mix_back(grad, target):
        for part in range(4):
            side = slice(part * 256, (part + 1) * 256)
            pool[target, :, side] = dot_nt(pool[grad], held[0, side, :]).astype(BF16)

    mix_back(0, 7)
    weights.append(load(wo_s, held.at[0]))
    p0.on(0)
    for copy in ins:
        copy.wait()

    def time_group(at, _):
        here = pl.ds(pl.multiple_of(at * KEYS, KEYS), KEYS)
        for two in range(8):
            side = pl.ds(two * WIDE, WIDE)
            grads = attend_backward(
                probs[at, two], pool[3, here, side], pool[4, here, side], pool[5, here, side],
                pool[7, here, side],
            )
            for target, grad in enumerate(grads):
                pool[8 + target, here, side] = grad.astype(BF16)
        return 0

    lax.fori_loop(0, rows // KEYS, time_group, 0)
    ins = [
        load(source, pool.at[target])
        for source, target in (
            (query_s, 2), (key_s, 3), (value_s, 4), (pair.at[0], 5), (pair.at[1], 7)
        )
    ]
    ins += [
        load(probs_s.at[at], probs.at[at // 2, :, pl.ds(at % 2 * 2 * WIDE, 2 * WIDE)])
        for at in range(4)
    ]
    for copy in late:
        copy.wait()
    for at in range(3):
        weight_grad(flat_weights, at + 1, pool[8 + at], pool.at[6])
    for at in range(3):
        weights[at + 1].wait()

    def time_rows(step, carry):
        here = pl.ds(pl.multiple_of(step * 256, 256), 256)
        grad = (
            dot_nt(pool[8, here, :], held[1])
            + dot_nt(pool[9, here, :], held[2])
            + dot_nt(pool[10, here, :], held[3])
        )
        hat, rate = normalise(pool[1, here, :].astype(F32))
        total = pool[0, here, :].astype(F32) + norm_backward(grad, hat, rate, gain_two[...])
        turned[pl.ds(step * 16, 16)] = total.astype(BF16).reshape(16, 16, width)
        return (
            carry[0] + jnp.sum(grad * hat, axis=0, keepdims=True),
            carry[1] + jnp.sum(grad, axis=0, keepdims=True),
        )

    zero = jnp.zeros((1, width), F32)
    time_norm = lax.fori_loop(0, rows // 256, time_rows, (zero, zero))
    weights += [load(source, held.at[at + 1]) for at, source in enumerate((wq_s, wk_s, wv_s))]
    in_mixed = load(mixed_s, pool.at[6])
    swap.send()
    p0.on(1)
    p1.on(0)
    p2.start(0)
    swap.wait()
    swap.place(pool.at[1])
    in_normed = load(normed_s, pool.at[0])
    p2.turn(0)

    in_mixed.wait()
    weight_grad(flat_weights, 0, pool[1], pool.at[6])
    weights[4].wait()
    mix_back(1, 8)
    p0.on(2)
    p2.start(1)
    for copy in ins:
        copy.wait()

    def space_group(at, _):
        here = pl.ds(pl.multiple_of(at * WIDE, WIDE), WIDE)
        lower = pl.ds(pl.multiple_of(lax.rem(at, 2) * 2 * WIDE, 2 * WIDE), 2 * WIDE)
        for two in range(8):
            side = pl.ds(two * WIDE, WIDE)
            keys = jnp.concatenate([pool[3, here, side], pool[5, here, side]], axis=0)
            values = jnp.concatenate([pool[4, here, side], pool[7, here, side]], axis=0)
            grad_query, grad_key, grad_value = attend_backward(
                probs[at // 2, two, lower], pool[2, here, side], keys, values, pool[8, here, side]
            )
            pool[9, here, side] = grad_query.astype(BF16)
            pool[10, here, side] = grad_key[:WIDE].astype(BF16)
            pool[11, here, side] = grad_value[:WIDE].astype(BF16)
            pool[6, here, side] = grad_key[WIDE:].astype(BF16)
            turned[pl.ds(at * 8, 8), :, side] = grad_value[WIDE:].astype(BF16).reshape(8, 16, WIDE)
        return 0

    lax.fori_loop(0, rows // (2 * WIDE), space_group, 0)
    p1.on(1)
    lax.fori_loop(rows // (2 * WIDE), rows // WIDE, space_group, 0)
    across = [
        remote(
            source, target, pair_sems.at[0, at], pair_sems.at[1, at], grid.other(),
        )
        for at, (source, target) in enumerate(((pool.at[6], came_key), (turned, came_value)))
    ]
    for copy in across:
        copy.start()
    in_tok = load(tok, pool.at[2])
    in_normed.wait()
    weight_grad(flat_weights, 1, pool[9], pool.at[0])
    for at, copy in enumerate(across):
        copy.wait()
        came = (came_key, came_value)[at][...].reshape(rows, width)
        pool[10 + at] = pool[10 + at] + came
        weight_grad(flat_weights, 2 + at, pool[10 + at], pool.at[0])
    p0.on(3)
    p1.on(2)
    p3.start(0)
    p2.on(1)
    for at in range(3):
        weights[5 + at].wait()
    in_tok.wait()

    def space_rows(step, carry):
        here = pl.ds(pl.multiple_of(step * 256, 256), 256)
        grad = (
            dot_nt(pool[9, here, :], held[1])
            + dot_nt(pool[10, here, :], held[2])
            + dot_nt(pool[11, here, :], held[3])
        )
        first = pool[2, here, :].astype(F32) + dot(hot[here, :], table[...])
        hat, rate = normalise(first)
        total = pool[1, here, :].astype(F32) + norm_backward(grad, hat, rate, gain_one[...])
        high = total.astype(BF16)
        pool[1, here, :] = high
        rest = (total - high.astype(F32)).astype(BF16)
        chosen = hot[here, :]
        return (
            carry[0] + jnp.sum(grad * hat, axis=0, keepdims=True),
            carry[1] + jnp.sum(grad, axis=0, keepdims=True),
            carry[2] + dot_tn(chosen, high)[:8] + dot_tn(chosen, rest)[:8],
        )

    p3.on(0)
    space_norm = lax.fori_loop(0, rows // 256, space_rows, (zero, zero, jnp.zeros((8, width), F32)))
    out_grad = load(pool.at[1], token_grad)
    totals[0, 0:8] = space_norm[2]
    totals[0, 8:16] = jnp.concatenate(
        [space_norm[0], time_norm[0], space_norm[1], time_norm[1], jnp.zeros((4, width), F32)], axis=0
    )
    totals[0, 16:24] = small_ffn[...]
    total = Total(grid, totals, total_came, total_sends, total_recvs)
    total.start(0)
    p1.on(3)
    p2.on(2)
    total.on(0)
    p3.on(1)
    total.on(1)
    p2.on(3)
    total.on(2)
    p3.on(2)
    total.on(3)
    small[...] = totals[4]
    p3.on(3)
    for pair_of in pairs:
        pair_of.wait(4)
    out_grad.wait()


class _Slots:
    def __init__(self, pool, first):
        self.pool, self.first = pool, first

    class _At:
        def __init__(self, slots):
            self.slots = slots

        def __getitem__(self, slot):
            return self.slots.pool.at[
                self.slots.first + slot // 4, pl.ds(slot % 4 * 128, 128)
            ]

    @property
    def at(self):
        return _Slots._At(self)

    def __setitem__(self, where, value):
        slot, rows = where
        first = slot % 4 * 128
        self.pool[self.first + slot // 4, first + rows.start : first + rows.stop] = value


def back(args, number):
    (meta, d_out, d_in) = args[:3]
    tok = args[26]
    rows, width = tok.shape
    count = lax.axis_size("seq")
    dims = seq_dims(count)
    share = d_out.shape[2]
    group = d_out.shape[3]
    halves = (2,) + dims + (share, group)
    scratch = [
        pltpu.VMEM((12, rows, width), BF16),
        pltpu.VMEM((rows // 16, 16, width), BF16),
        pltpu.VMEM((4, width, width), BF16),
        pltpu.VMEM((2, 8, 2 * KEYS, KEYS), BF16),
        pltpu.VMEM(halves, BF16),
        pltpu.VMEM((dims[0] // 2,) + dims[1:] + (share // 2, group), BF16),
        pltpu.VMEM((rows, width), BF16),
        pltpu.VMEM((rows // 16, 16, width), BF16),
        pltpu.VMEM((7, 128, width), BF16),
    ]
    for _ in range(2):
        for order in ORDERS:
            scratch += unit_scratch(share // 2, group, order, dims)
    most = max(max(dims) - 1, 2)
    dma = pltpu.SemaphoreType.DMA
    scratch += [
        pltpu.VMEM((5, 24, width), F32),
        pltpu.VMEM((sum(dims) - 2, 24, width), F32),
        dma((40,)),
        dma((8, 5, most)),
        dma((8, 5, most)),
        pltpu.SemaphoreType.REGULAR((4, 4)),
        dma((7,)),
        dma((7,)),
        dma((sum(dims) - 2,)),
        dma((sum(dims) - 2,)),
        dma((2, 2)),
    ]
    args = list(args)
    args[1], args[2] = d_out.reshape(halves), d_in.reshape(halves)
    final = shape_of((2, share, group), BF16)
    return pl.pallas_call(
        back_kernel,
        out_shape=[shape_of((rows, width), BF16)] + [final] * 4 + [shape_of((24, width), F32)],
        in_specs=[IN_SMEM] + [IN_HBM] * 26 + [WHOLE] * 5,
        out_specs=[IN_HBM] + [WHOLE] * 5,
        scratch_shapes=scratch,
        compiler_params=params(collective_id=number, has_side_effects=True),
    )(*args)


def split_three(values):
    high = values.astype(BF16)
    rest = values - high.astype(F32)
    middle = rest.astype(BF16)
    return high, middle, (rest - middle.astype(F32)).astype(BF16)


def on_device(
    tokens,
    cotangent,
    clip_big,
    actions,
    action_table,
    norm_gain,
    norm_bias,
    spatial_q,
    spatial_k,
    spatial_v,
    spatial_o,
    temporal_q,
    temporal_k,
    temporal_v,
    temporal_o,
    ffn_in,
    ffn_bias_in,
    ffn_out,
    ffn_bias_out,
):
    tok = tokens[0]
    rows, width = tok.shape
    span = (GRID_BIG // GRID_SMALL) ** 2
    me = lax.axis_index("seq")
    tile = lax.axis_index("tile")
    count = lax.axis_size("seq")
    sizes = jnp.where(clip_big == 1, span, 1).astype(jnp.int32)
    ends = jnp.cumsum(sizes)
    clip = jnp.sum((ends <= me).astype(jnp.int32))
    chosen = jnp.arange(clip_big.shape[0], dtype=jnp.int32) == clip
    is_big = jnp.sum(jnp.where(chosen, clip_big, 0))
    offset = jnp.where(is_big == 1, me - jnp.sum(jnp.where(chosen, ends - sizes, 0)), 0)
    frame = clip * FRAMES + offset * (FRAMES // span)
    meta = jnp.stack([is_big, offset]).astype(jnp.int32)
    row = jnp.arange(rows, dtype=jnp.int32)
    frame_of = frame + jnp.where(is_big == 1, row // 128, row // 32)
    action = jnp.sum(
        jnp.where(
            frame_of[:, None] == jnp.arange(actions.shape[0], dtype=jnp.int32)[None, :],
            actions[None, :],
            0,
        ),
        axis=1,
    )
    lane = jnp.arange(WIDE, dtype=jnp.int32)
    hot = ((action[:, None] == (lane % 8)[None, :]) & (lane < 24)[None, :]).astype(BF16)
    table = jnp.concatenate(
        list(split_three(action_table)) + [jnp.zeros((WIDE - 24, width), BF16)], axis=0
    )
    gains = [norm_gain[at : at + 1] for at in range(3)]
    shifts = [norm_bias[at : at + 1] for at in range(3)]

    normed_one, query_one, key_one, value_one = project(
        tok, hot, table, gains[0], shifts[0], spatial_q, spatial_k, spatial_v
    )
    pair_one = across(jnp.stack([key_one, value_one]))
    cot = exchange(meta, cotangent[0], True, 1)
    mixed_one, probs_one, second_low = spatial(
        meta, query_one, key_one, value_one, pair_one, tok, hot, table, spatial_o
    )
    second = exchange(meta, second_low, True, 2)
    normed_two, query_two, key_two, value_two, probs_two, mixed_two, third = temporal(
        second, gains[1], shifts[1], temporal_q, temporal_k, temporal_v, temporal_o
    )
    mixed, grad_third, d_in, d_out, d_bin, d_norm_three, d_bout = ffn(
        third, cot, gains[2], shifts[2], ffn_in, ffn_bias_in, ffn_out, ffn_bias_out
    )
    mixed = exchange(meta, mixed, False, 3)
    part = width // count
    if count != d_in.shape[1]:
        finer = count // d_in.shape[1]
        d_in = d_in.reshape(2, d_in.shape[1], KEYS, 2, finer, KEYS // finer)
        d_in = d_in.transpose(0, 1, 4, 2, 3, 5).reshape(d_out.shape)
    pieces = d_bin.shape[1] // width
    small_ffn = jnp.concatenate(
        [d_norm_three, d_bout, d_bin.reshape(pieces, width), jnp.zeros((5 - pieces, width), F32)], axis=0
    )
    token_grad, sum_out, sum_in, sum_temporal, sum_spatial, small = back(
        [
            meta, d_out, d_in, grad_third, second, mixed_two, query_two, key_two, value_two,
            normed_two, probs_two, temporal_q, temporal_k, temporal_v, temporal_o, mixed_one,
            query_one, key_one, value_one, pair_one, normed_one, probs_one, spatial_q, spatial_k,
            spatial_v, spatial_o, tok, hot, table, gains[0], gains[1], small_ffn,
        ],
        5,
    )
    hidden = ffn_in.shape[1]
    ffn_in_grad = (
        sum_in.reshape(2, KEYS, 2, hidden // count).transpose(0, 2, 1, 3).reshape(width, -1).astype(F32)
    )
    ffn_out_grad = (
        sum_out.reshape(2, 4, part, CHUNK).transpose(0, 1, 3, 2).reshape(hidden, part).astype(F32)
    )

    def finish(summed):
        joined = summed.reshape(2, 4, part, width // 2).transpose(0, 3, 1, 2).astype(F32)
        joined = joined.reshape(width, 4, part)
        return [joined[:, at] for at in range(4)]

    temporal_o_grad, temporal_q_grad, temporal_k_grad, temporal_v_grad = finish(sum_temporal)
    spatial_o_grad, spatial_q_grad, spatial_k_grad, spatial_v_grad = finish(sum_spatial)

    def mine(values):
        return lax.dynamic_slice_in_dim(values, me * part, part, 1)

    bias_in = small[19 : 19 + pieces].reshape(1, hidden)
    bias_in = lax.dynamic_slice_in_dim(bias_in, me * (hidden // count), hidden // count, 1)
    return (
        mixed[None],
        token_grad[None],
        mine(small[0:8]),
        mine(jnp.concatenate([small[8:10], small[16:17]], axis=0)),
        mine(jnp.concatenate([small[10:12], small[17:18]], axis=0)),
        spatial_q_grad,
        spatial_k_grad,
        spatial_v_grad,
        spatial_o_grad,
        temporal_q_grad,
        temporal_k_grad,
        temporal_v_grad,
        temporal_o_grad,
        ffn_in_grad,
        bias_in,
        ffn_out_grad,
        mine(small[18:19]),
    )


def solution(mesh):
    placed = (P("tile", "seq", None),) * 2 + (P(),) * 17
    return jax.shard_map(
        on_device,
        mesh=mesh,
        in_specs=placed,
        out_specs=(P("tile", "seq", None),) * 2 + (P(None, "seq"),) * 15,
        check_vma=False,
    )
```

```python
import functools

import jax
import jax.numpy as jnp
from jax import lax
from jax.experimental import pallas as pl
from jax.experimental.pallas import tpu as pltpu
from jax.sharding import PartitionSpec as P

HEAD_DIM = 64
FRAMES = 16
GRID_BIG = 16
GRID_SMALL = 8
WIDE = 128
KEYS = 256
CHUNK = 512
VMEM_BYTES = 62 * 2**20
FACTOR = HEAD_DIM**-0.5
ROOT = (2.0 / 3.141592653589793) ** 0.5

F32 = jnp.float32
BF16 = jnp.bfloat16
WHOLE = pl.BlockSpec(memory_space=pltpu.VMEM)
IN_HBM = pl.BlockSpec(memory_space=pl.ANY)
MESH = pl.DeviceIdType.MESH
IN_SMEM = pl.BlockSpec(memory_space=pltpu.SMEM)


def shape_of(dims, kind):
    return jax.ShapeDtypeStruct(dims, kind)


def params(**more):
    return pltpu.CompilerParams(vmem_limit_bytes=VMEM_BYTES, **more)


def dot(left, right):
    return jnp.dot(left, right, preferred_element_type=F32)


def dot_nt(left, right):
    return lax.dot_general(left, right, (((1,), (1,)), ((), ())), preferred_element_type=F32)


def dot_tn(left, right):
    return lax.dot_general(left, right, (((0,), (0,)), ((), ())), preferred_element_type=F32)


def normalise(values):
    centre = values - jnp.mean(values, axis=-1, keepdims=True)
    rate = lax.rsqrt(jnp.mean(centre * centre, axis=-1, keepdims=True) + 1e-05)
    return centre * rate, rate


def norm_backward(grad, hat, rate, gain):
    inner = grad * gain
    level = jnp.mean(inner, axis=-1, keepdims=True)
    slope = jnp.mean(inner * hat, axis=-1, keepdims=True)
    return rate * (inner - level - hat * slope)


def head_halves(block):
    lane = lax.broadcasted_iota(jnp.int32, block.shape, 1)
    zero = jnp.zeros_like(block)
    first = lane < HEAD_DIM
    return jnp.concatenate([jnp.where(first, block, zero), jnp.where(first, zero, block)], axis=0)


def join_halves(both):
    rows = both.shape[0] // 2
    lane = lax.broadcasted_iota(jnp.int32, (rows, both.shape[1]), 1)
    return jnp.where(lane < HEAD_DIM, both[:rows], both[rows:])


def attend(query, key, value, bias):
    scores = dot_nt(head_halves(query) * FACTOR, key) + bias
    top = jnp.max(scores, axis=1, keepdims=True)
    powers = jnp.exp(scores - top)
    prob = (powers * (1.0 / jnp.sum(powers, axis=1, keepdims=True))).astype(BF16)
    return prob, join_halves(dot(prob, value))


def attend_backward(prob, query, key, value, grad):
    grad_two = head_halves(grad)
    grad_prob = dot_nt(grad_two, value)
    prob_f = prob.astype(F32)
    delta = jnp.sum(prob_f * grad_prob, axis=1, keepdims=True)
    grad_score = (prob_f * (grad_prob - delta)).astype(BF16)
    grad_query = join_halves(dot(grad_score, key)) * FACTOR
    grad_key = dot_tn(grad_score, head_halves(query)) * FACTOR
    grad_value = dot_tn(prob, grad_two)
    return grad_query, grad_key, grad_value


def spatial_bias(is_big, rows):
    row = lax.broadcasted_iota(jnp.int32, (rows, KEYS), 0)
    column = lax.broadcasted_iota(jnp.int32, (rows, KEYS), 1)
    same = lax.rem(row, WIDE) // 32 == lax.rem(column, WIDE) // 32
    return jnp.where(same | (is_big == 1), 0.0, -1e30).astype(F32)


def temporal_bias(rows):
    row = lax.rem(lax.broadcasted_iota(jnp.int32, (rows, KEYS), 0), KEYS)
    column = lax.broadcasted_iota(jnp.int32, (rows, KEYS), 1)
    fits = (lax.rem(row, 16) == lax.rem(column, 16)) & (column <= row)
    return jnp.where(fits, 0.0, -1e30).astype(F32)


def weight_grad(target, at, grad, normed):
    grad_t = grad.T
    count, _rows, width = target.shape[1:]
    part = grad_t.shape[0] // count
    for which in range(2):
        block = dot(grad_t, normed[:, which * width : (which + 1) * width]).astype(BF16)
        target[which, :, at * part : (at + 1) * part, :] = block.reshape(count, part, width)


REACH = 3
STEPS = tuple(step for step in range(REACH, -REACH - 1, -1) if step != 0)


class Swap:
    def __init__(self, to_time, offset, is_big, source, staged, came, sems, parts=1):
        self.me, self.tile = lax.axis_index("seq"), lax.axis_index("tile")
        self.count = lax.axis_size("seq")
        self.to_time, self.offset, self.is_big = to_time, offset, is_big
        self.source, self.staged, self.came, self.sems = source, staged, came, sems
        self.parts = parts

    def peer(self, step):
        return (self.me + step, self.tile)

    def present(self, step):
        return (self.me + step >= 0) & (self.me + step < self.count)

    def greet(self, barrier):
        for step in STEPS:
            @pl.when(self.present(step))
            def _(step=step):
                pl.semaphore_signal(
                    barrier, inc=1, device_id=self.peer(step), device_id_type=MESH
                )
        return jnp.minimum(self.me, REACH) + jnp.minimum(self.count - 1 - self.me, REACH)

    def copy(self, step, part):
        slot, sem = REACH - step, (REACH - step) * self.parts + part
        source, target = self.staged.at[slot], self.came.at[slot]
        if self.parts > 1:
            rows = pl.ds(part * (128 // self.parts), 128 // self.parts)
            source, target = source.at[rows], target.at[rows]
        return remote(source, target, self.sems[0].at[sem], self.sems[1].at[sem], self.peer(step))

    def stage(self, step, part):
        which = jnp.clip(self.offset + step, 0, REACH)
        target = self.came if step == 0 else self.staged
        slot = REACH - step
        if self.to_time:
            frames = 4 // self.parts
            for frame in range(part * frames, (part + 1) * frames):
                block = self.source[pl.ds(which * 2 + frame * 8, 2)]
                target[slot, frame * 32 : frame * 32 + 32] = block.reshape(32, block.shape[2])
            return
        for side in range(2):
            block = self.source[pl.ds(which * 4 + side * 16, 4)]
            target[slot, side * 64 : side * 64 + 64] = block.reshape(64, block.shape[2])

    def send(self, part=0):
        for step in STEPS:
            self.stage(step, part)

            @pl.when(self.present(step))
            def _(step=step):
                self.copy(step, part).start()

        self.stage(0, part)

    def wait(self):
        for part in range(self.parts):
            for step in STEPS:
                @pl.when(self.present(step))
                def _(step=step, part=part):
                    self.copy(step, part).wait_send()

                @pl.when(self.present(-step))
                def _(step=step, part=part):
                    self.copy(step, part).wait_recv()

    def place(self, target):
        width = target.shape[-1]
        chosen = jnp.full((16, width), self.is_big, jnp.int32) == 1
        for at in range(REACH + 1):
            slot = REACH - self.offset + at
            for side in range(2):
                for frame in range(4):
                    low = frame * 32 + side * 16 if self.to_time else side * 64 + frame * 16
                    moved = self.came[pl.ds(slot, 1), low : low + 16][0]
                    if self.to_time:
                        here, mine = side * 256 + at * 64 + frame * 16, at * 8 + frame * 2 + side
                    else:
                        here, mine = frame * 128 + at * 32 + side * 16, side * 16 + frame * 4 + at
                    target[here : here + 16] = jnp.where(chosen, moved, self.source[mine])


def seq_dims(count):
    return {16: (4, 2, 2), 64: (4, 4, 4)}.get(count, (1, 1, count))


ORDERS = ((2, 1, 0), (1, 2, 0))


class Grid:
    def __init__(self):
        self.count = lax.axis_size("seq")
        self.dims = seq_dims(self.count)
        self.me = lax.axis_index("seq")
        self.tile = lax.axis_index("tile")
        self.strides = (self.dims[1] * self.dims[2], self.dims[2], 1)
        self.places = [
            lax.rem(self.me // stride, size) for stride, size in zip(self.strides, self.dims)
        ]

    def along(self, axis, step):
        place = self.places[axis]
        there = lax.rem(place + step, self.dims[axis])
        return there, (self.me + (there - place) * self.strides[axis], self.tile)

    def other(self):
        return (self.me, 1 - self.tile)

    def peers(self, phase, order):
        if phase == 0:
            return [self.other()]
        axis = order[phase - 1]
        return [self.along(axis, step)[1] for step in range(1, self.dims[axis])]

    def greet(self, barrier):
        peers = [self.other()]
        for axis in range(3):
            peers += [self.along(axis, step)[1] for step in range(1, self.dims[axis])]
        for peer in peers:
            pl.semaphore_signal(barrier, inc=1, device_id=peer, device_id_type=MESH)
        return len(peers)


def remote(source, target, send_sem, recv_sem, device):
    return pltpu.make_async_remote_copy(
        src_ref=source,
        dst_ref=target,
        send_sem=send_sem,
        recv_sem=recv_sem,
        device_id=device,
        device_id_type=MESH,
    )


class Unit:
    def __init__(self, grid, which, group, halves, kept, out, bufs, sems, free, number):
        self.grid, self.order = grid, ORDERS[which]
        rows = halves.shape[4] // 2
        self.rows = pl.ds(which * rows, rows)
        self.halves, self.kept, self.out, self.came = halves, kept, out, bufs
        self.sends, self.recvs = sems
        self.number = number
        self.free, self.slot, self.again = free, number % 4, group >= 2

    def source(self, phase, there):
        if phase == 1:
            where = [slice(None)] * 3
            where[self.order[0]] = there
            return self.came[0].at[tuple(where)]
        if phase == 2:
            rest = [axis for axis in range(3) if axis != self.order[0]]
            where = [slice(None)] * 2
            where[rest.index(self.order[1])] = there
            return self.came[1].at[(0,) + tuple(where)]
        return self.came[2].at[0, there]

    def copies(self, phase):
        number = self.number
        if phase == 0:
            away = self.halves.at[1 - self.grid.tile, :, :, :, self.rows]
            return [
                remote(
                    away, self.came[0], self.sends.at[number, 0, 0], self.recvs.at[number, 0, 0],
                    self.grid.other(),
                )
            ]
        if phase == 4:
            mine = self.out.at[self.grid.tile, self.rows]
            return [
                remote(
                    mine, mine, self.sends.at[number, 4, 0], self.recvs.at[number, 4, 0],
                    self.grid.other(),
                )
            ]
        axis = self.order[phase - 1]
        out = []
        for step in range(1, self.grid.dims[axis]):
            there, device = self.grid.along(axis, step)
            out.append(
                remote(
                    self.source(phase, there), self.came[phase].at[step - 1],
                    self.sends.at[number, phase, step - 1], self.recvs.at[number, phase, step - 1],
                    device,
                )
            )
        return out

    def fetch(self, part):
        half = self.grid.dims[0] // 2
        here = self.halves.at[self.grid.tile, pl.ds(part * half, half), :, :, self.rows]
        return pltpu.make_async_copy(here, self.kept, self.sends.at[self.number, 0, 1])

    def start(self, phase):
        if self.again and phase < 4:
            amount = len(self.grid.peers(phase, self.order))
            pl.semaphore_wait(self.free.at[self.slot, phase], amount)
        for copy in self.copies(phase):
            copy.start()

    def release(self, phase):
        if not self.again:
            for peer in self.grid.peers(phase, self.order):
                pl.semaphore_signal(
                    self.free.at[self.slot, phase], inc=1, device_id=peer, device_id_type=MESH
                )

    def wait(self, phase):
        for copy in self.copies(phase):
            copy.wait()

    def turn(self, phase):
        self.wait(phase)
        grid, dims = self.grid, self.grid.dims
        if phase == 0:
            def place(at):
                return (at // (dims[1] * dims[2]), lax.rem(at // dims[2], dims[1]), lax.rem(at, dims[2]))

            def step(at, _):
                where = place(at)
                self.came[0][where] = self.came[0][where] + self.halves[(grid.tile,) + where + (self.rows,)]
                return 0

            def step_kept(base, at, _):
                where = place(at)
                there = (where[0] + base,) + where[1:]
                self.came[0][there] = self.came[0][there] + self.kept[where]
                return 0

            if self.kept is None:
                lax.fori_loop(0, grid.count, step, 0)
                return
            for part in range(2):
                copy = self.fetch(part)
                copy.start()
                copy.wait()
                lax.fori_loop(0, grid.count // 2, functools.partial(step_kept, part * dims[0] // 2), 0)
            return
        axis = self.order[phase - 1]
        own = self.source(phase, grid.places[axis])
        came = self.came[phase]
        size = dims[axis]
        if phase == 3:
            total = own[...].astype(F32)
            for at in range(size - 1):
                total = total + came[at].astype(F32)
            self.out[grid.tile, self.rows] = total.astype(BF16)
            self.release(2)
            self.release(3)
            return
        extent = own.shape[:-2]
        steps = 1
        for dim in extent:
            steps *= dim

        def step(at, _):
            where = (at,) if len(extent) == 1 else (at // extent[1], lax.rem(at, extent[1]))
            total = own[where]
            for other in range(size - 1):
                total = total + came[(other,) + where]
            came[(0,) + where] = total
            return 0

        lax.fori_loop(0, steps, step, 0)
        self.release(phase - 1)


class Pair:
    def __init__(self, *units):
        self.units = units

    def start(self, phase):
        for unit in self.units:
            unit.start(phase)

    def turn(self, phase):
        for unit in self.units:
            unit.turn(phase)

    def on(self, phase):
        for unit in self.units:
            unit.turn(phase)
            unit.start(phase + 1)

    def wait(self, phase):
        for unit in self.units:
            unit.wait(phase)


class Total:
    def __init__(self, grid, value, came, sends, recvs):
        self.grid, self.value, self.came, self.sends, self.recvs = grid, value, came, sends, recvs

    def copies(self, phase):
        first = sum(len(self.grid.peers(before, (2, 1, 0))) for before in range(phase))
        return [
            remote(
                self.value.at[phase], self.came.at[first + at], self.sends.at[first + at],
                self.recvs.at[first + at], peer,
            )
            for at, peer in enumerate(self.grid.peers(phase, (2, 1, 0)))
        ]

    def start(self, phase):
        for copy in self.copies(phase):
            copy.start()

    def on(self, phase):
        copies = self.copies(phase)
        for copy in copies:
            copy.wait()
        total = self.value[phase]
        first = sum(len(self.grid.peers(before, (2, 1, 0))) for before in range(phase))
        for at in range(len(copies)):
            total = total + self.came[first + at]
        self.value[phase + 1] = total
        if phase < 3:
            self.start(phase + 1)


def unit_scratch(rows, width, order, dims):
    rest = tuple(dims[axis] for axis in range(3) if axis != order[0])
    return [
        pltpu.VMEM(dims + (rows, width), BF16),
        pltpu.VMEM((max(dims[order[0]] - 1, 1),) + rest + (rows, width), BF16),
        pltpu.VMEM((max(dims[order[1]] - 1, 1), dims[0], rows, width), BF16),
        pltpu.VMEM((max(dims[0] - 1, 1), rows, width), BF16),
    ]


def back_kernel(
    clip_big, d_out, d_in, third, second, mixed_t, query_t, key_t, value_t, normed_t, probs_t,
    wq_t, wk_t, wv_t, wo_t, mixed_s, query_s, key_s, value_s, pair, normed_s, probs_s,
    wq_s, wk_s, wv_s, wo_s, tok, hot, table, gain_one, gain_two, small_ffn,
    token_grad, sum_out, sum_in, sum_time, sum_space, small,
    pool, turned, held, probs, d_weights, kept, came_key, came_value, swapped, *rest,
):
    unit_bufs, rest = rest[:16], rest[16:]
    (totals, total_came, loads, unit_sends, unit_recvs, free, swap_sends, swap_recvs,
     total_sends, total_recvs, pair_sems) = rest
    rows, width = pool.shape[1:]
    _clip, offset, is_big = where_am_i(clip_big)
    grid = Grid()
    swap = Swap(
        False, offset, is_big, turned, _Slots(pool, 8), swapped, (swap_sends, swap_recvs)
    )
    barrier = pltpu.get_barrier_semaphore()
    pl.semaphore_wait(barrier, grid.greet(barrier) + swap.greet(barrier))

    used = [0]

    def load(source, target):
        copy = pltpu.make_async_copy(source, target, loads.at[used[0]])
        used[0] += 1
        copy.start()
        return copy

    sums = (sum_out, sum_in, sum_time, sum_space)
    sources = (d_out, d_in, d_weights, d_weights)
    pairs = []
    for group in range(4):
        bufs = unit_bufs[8 * (group % 2) : 8 * (group % 2) + 8]
        pairs.append(
            Pair(
                *[
                    Unit(
                        grid, which, group, sources[group], kept if group < 2 else None,
                        sums[group], bufs[4 * which : 4 * which + 4], (unit_sends, unit_recvs), free,
                        2 * group + which,
                    )
                    for which in range(2)
                ]
            )
        )
    p0, p1, p2, p3 = pairs
    p0.start(0)
    p1.start(0)

    in_low = load(third, pool.at[0])
    in_mixed = load(mixed_t, pool.at[2])
    weights = [load(source, held.at[at]) for at, source in enumerate((wo_t, wq_t, wk_t, wv_t))]
    ins = [load(source, pool.at[3 + at]) for at, source in enumerate((query_t, key_t, value_t))]
    ins += [load(probs_t.at[at], probs.at[at]) for at in range(2)]
    late = [load(second, pool.at[1]), load(normed_t, pool.at[6])]
    in_low.wait()
    in_mixed.wait()
    flat_weights = d_weights.reshape(2, grid.count, d_weights.shape[4], d_weights.shape[5])
    weight_grad(flat_weights, 0, pool[0], pool.at[2])
    weights[0].wait()

    def mix_back(grad, target):
        for part in range(4):
            side = slice(part * 256, (part + 1) * 256)
            pool[target, :, side] = dot_nt(pool[grad], held[0, side, :]).astype(BF16)

    mix_back(0, 7)
    weights.append(load(wo_s, held.at[0]))
    p0.on(0)
    for copy in ins:
        copy.wait()

    def time_group(at, _):
        here = pl.ds(pl.multiple_of(at * KEYS, KEYS), KEYS)
        for two in range(8):
            side = pl.ds(two * WIDE, WIDE)
            grads = attend_backward(
                probs[at, two], pool[3, here, side], pool[4, here, side], pool[5, here, side],
                pool[7, here, side],
            )
            for target, grad in enumerate(grads):
                pool[8 + target, here, side] = grad.astype(BF16)
        return 0

    lax.fori_loop(0, rows // KEYS, time_group, 0)
    ins = [
        load(source, pool.at[target])
        for source, target in (
            (query_s, 2), (key_s, 3), (value_s, 4), (pair.at[0], 5), (pair.at[1], 7)
        )
    ]
    ins += [
        load(probs_s.at[at], probs.at[at // 2, :, pl.ds(at % 2 * 2 * WIDE, 2 * WIDE)])
        for at in range(4)
    ]
    for copy in late:
        copy.wait()
    for at in range(3):
        weight_grad(flat_weights, at + 1, pool[8 + at], pool.at[6])
    for at in range(3):
        weights[at + 1].wait()

    def time_rows(step, carry):
        here = pl.ds(pl.multiple_of(step * 256, 256), 256)
        grad = (
            dot_nt(pool[8, here, :], held[1])
            + dot_nt(pool[9, here, :], held[2])
            + dot_nt(pool[10, here, :], held[3])
        )
        hat, rate = normalise(pool[1, here, :].astype(F32))
        total = pool[0, here, :].astype(F32) + norm_backward(grad, hat, rate, gain_two[...])
        turned[pl.ds(step * 16, 16)] = total.astype(BF16).reshape(16, 16, width)
        return (
            carry[0] + jnp.sum(grad * hat, axis=0, keepdims=True),
            carry[1] + jnp.sum(grad, axis=0, keepdims=True),
        )

    zero = jnp.zeros((1, width), F32)
    time_norm = lax.fori_loop(0, rows // 256, time_rows, (zero, zero))
    weights += [load(source, held.at[at + 1]) for at, source in enumerate((wq_s, wk_s, wv_s))]
    in_mixed = load(mixed_s, pool.at[6])
    swap.send()
    p0.on(1)
    p1.on(0)
    p2.start(0)
    swap.wait()
    swap.place(pool.at[1])
    in_normed = load(normed_s, pool.at[0])
    p2.turn(0)

    in_mixed.wait()
    weight_grad(flat_weights, 0, pool[1], pool.at[6])
    weights[4].wait()
    mix_back(1, 8)
    p0.on(2)
    p2.start(1)
    for copy in ins:
        copy.wait()

    def space_group(at, _):
        here = pl.ds(pl.multiple_of(at * WIDE, WIDE), WIDE)
        lower = pl.ds(pl.multiple_of(lax.rem(at, 2) * 2 * WIDE, 2 * WIDE), 2 * WIDE)
        for two in range(8):
            side = pl.ds(two * WIDE, WIDE)
            keys = jnp.concatenate([pool[3, here, side], pool[5, here, side]], axis=0)
            values = jnp.concatenate([pool[4, here, side], pool[7, here, side]], axis=0)
            grad_query, grad_key, grad_value = attend_backward(
                probs[at // 2, two, lower], pool[2, here, side], keys, values, pool[8, here, side]
            )
            pool[9, here, side] = grad_query.astype(BF16)
            pool[10, here, side] = grad_key[:WIDE].astype(BF16)
            pool[11, here, side] = grad_value[:WIDE].astype(BF16)
            pool[6, here, side] = grad_key[WIDE:].astype(BF16)
            turned[pl.ds(at * 8, 8), :, side] = grad_value[WIDE:].astype(BF16).reshape(8, 16, WIDE)
        return 0

    lax.fori_loop(0, rows // (2 * WIDE), space_group, 0)
    p1.on(1)
    lax.fori_loop(rows // (2 * WIDE), rows // WIDE, space_group, 0)
    across = [
        remote(
            source, target, pair_sems.at[0, at], pair_sems.at[1, at], grid.other(),
        )
        for at, (source, target) in enumerate(((pool.at[6], came_key), (turned, came_value)))
    ]
    for copy in across:
        copy.start()
    in_tok = load(tok, pool.at[2])
    in_normed.wait()
    weight_grad(flat_weights, 1, pool[9], pool.at[0])
    for at, copy in enumerate(across):
        copy.wait()
        came = (came_key, came_value)[at][...].reshape(rows, width)
        pool[10 + at] = pool[10 + at] + came
        weight_grad(flat_weights, 2 + at, pool[10 + at], pool.at[0])
    p0.on(3)
    p1.on(2)
    p3.start(0)
    p2.on(1)
    for at in range(3):
        weights[5 + at].wait()
    in_tok.wait()

    def space_rows(step, carry):
        here = pl.ds(pl.multiple_of(step * 256, 256), 256)
        grad = (
            dot_nt(pool[9, here, :], held[1])
            + dot_nt(pool[10, here, :], held[2])
            + dot_nt(pool[11, here, :], held[3])
        )
        first = pool[2, here, :].astype(F32) + dot(hot[here, :], table[...])
        hat, rate = normalise(first)
        total = pool[1, here, :].astype(F32) + norm_backward(grad, hat, rate, gain_one[...])
        high = total.astype(BF16)
        pool[1, here, :] = high
        rest = (total - high.astype(F32)).astype(BF16)
        chosen = hot[here, :]
        return (
            carry[0] + jnp.sum(grad * hat, axis=0, keepdims=True),
            carry[1] + jnp.sum(grad, axis=0, keepdims=True),
            carry[2] + dot_tn(chosen, high)[:8] + dot_tn(chosen, rest)[:8],
        )

    p3.on(0)
    space_norm = lax.fori_loop(0, rows // 256, space_rows, (zero, zero, jnp.zeros((8, width), F32)))
    out_grad = load(pool.at[1], token_grad)
    totals[0, 0:8] = space_norm[2]
    totals[0, 8:16] = jnp.concatenate(
        [space_norm[0], time_norm[0], space_norm[1], time_norm[1], jnp.zeros((4, width), F32)], axis=0
    )
    totals[0, 16:24] = small_ffn[...]
    total = Total(grid, totals, total_came, total_sends, total_recvs)
    total.start(0)
    p1.on(3)
    p2.on(2)
    total.on(0)
    p3.on(1)
    total.on(1)
    p2.on(3)
    total.on(2)
    p3.on(2)
    total.on(3)
    small[...] = totals[4]
    p3.on(3)
    for pair_of in pairs:
        pair_of.wait(4)
    out_grad.wait()


class _Slots:
    def __init__(self, pool, first):
        self.pool, self.first = pool, first

    class _At:
        def __init__(self, slots):
            self.slots = slots

        def __getitem__(self, slot):
            return self.slots.pool.at[
                self.slots.first + slot // 4, pl.ds(slot % 4 * 128, 128)
            ]

    @property
    def at(self):
        return _Slots._At(self)

    def __setitem__(self, where, value):
        slot, rows = where
        first = slot % 4 * 128
        self.pool[self.first + slot // 4, first + rows.start : first + rows.stop] = value


def back(args, number):
    d_out, d_in = args[1:3]
    tok = args[26]
    rows, width = tok.shape
    count = lax.axis_size("seq")
    dims = seq_dims(count)
    share = d_out.shape[2]
    group = d_out.shape[3]
    halves = (2,) + dims + (share, group)
    scratch = [
        pltpu.VMEM((12, rows, width), BF16),
        pltpu.VMEM((rows // 16, 16, width), BF16),
        pltpu.VMEM((4, width, width), BF16),
        pltpu.VMEM((2, 8, 2 * KEYS, KEYS), BF16),
        pltpu.VMEM(halves, BF16),
        pltpu.VMEM((dims[0] // 2,) + dims[1:] + (share // 2, group), BF16),
        pltpu.VMEM((rows, width), BF16),
        pltpu.VMEM((rows // 16, 16, width), BF16),
        pltpu.VMEM((7, 128, width), BF16),
    ]
    for _ in range(2):
        for order in ORDERS:
            scratch += unit_scratch(share // 2, group, order, dims)
    most = max(max(dims) - 1, 2)
    dma = pltpu.SemaphoreType.DMA
    scratch += [
        pltpu.VMEM((5, 24, width), F32),
        pltpu.VMEM((sum(dims) - 2, 24, width), F32),
        dma((40,)),
        dma((8, 5, most)),
        dma((8, 5, most)),
        pltpu.SemaphoreType.REGULAR((4, 4)),
        dma((7,)),
        dma((7,)),
        dma((sum(dims) - 2,)),
        dma((sum(dims) - 2,)),
        dma((2, 2)),
    ]
    args = list(args)
    args[1], args[2] = d_out.reshape(halves), d_in.reshape(halves)
    final = shape_of((2, share, group), BF16)
    return pl.pallas_call(
        back_kernel,
        out_shape=[shape_of((rows, width), BF16)] + [final] * 4 + [shape_of((24, width), F32)],
        in_specs=[IN_SMEM] + [IN_HBM] * 26 + [WHOLE] * 5,
        out_specs=[IN_HBM] + [WHOLE] * 5,
        scratch_shapes=scratch,
        compiler_params=params(collective_id=number, has_side_effects=True),
    )(*args)


def where_am_i(clip_big):
    me = lax.axis_index("seq")
    span = (GRID_BIG // GRID_SMALL) ** 2
    start, clip, offset, is_big = jnp.int32(0), jnp.int32(0), jnp.int32(0), jnp.int32(0)
    for at in range(clip_big.shape[0]):
        big = clip_big[at]
        size = jnp.where(big == 1, span, 1)
        inside = (me >= start) & (me < start + size)
        clip = jnp.where(inside, at, clip)
        offset = jnp.where(inside, me - start, offset)
        is_big = jnp.where(inside, big, is_big)
        start = start + size
    return clip, offset, is_big


class Loads:
    def __init__(self, sems):
        self.sems, self.used = sems, 0

    def __call__(self, source, target):
        copy = pltpu.make_async_copy(source, target, self.sems.at[self.used])
        self.used += 1
        copy.start()
        return copy


def first_kernel(
    clip_big, actions, tok, action_table, gain, shift, wq, wk, wv, wo,
    normed_out, query_out, key_out, value_out, pair_out, mixed_out, probs_out, second_out, hot, table,
    held, normed, query, key, value, pair, mixed, probs, second, turned, staged, came,
    loads, pair_sems, swap_sends, swap_recvs,
):
    rows, width = tok.shape
    clip, offset, is_big = where_am_i(clip_big)
    grid = Grid()
    swap = Swap(True, offset, is_big, turned, staged, came, (swap_sends, swap_recvs), 2)
    barrier = pltpu.get_barrier_semaphore()
    pl.semaphore_signal(barrier, inc=1, device_id=grid.other(), device_id_type=MESH)
    peers = 1 + swap.greet(barrier)
    load = Loads(loads)
    weights = [load(source, held.at[at]) for at, source in enumerate((wk, wv, wq, wo))]

    last = actions.shape[0] - 1
    base = clip * FRAMES + offset * (FRAMES // (REACH + 1))
    row = lax.broadcasted_iota(jnp.int32, (rows, WIDE), 0)
    frame_of = jnp.where(jnp.full((rows, WIDE), is_big, jnp.int32) == 1, row // WIDE, row // 32)
    action = jnp.zeros((rows, WIDE), jnp.int32)
    for frame in range(FRAMES):
        action = jnp.where(frame_of == frame, actions[jnp.minimum(base + frame, last)], action)
    lane = lax.broadcasted_iota(jnp.int32, (rows, WIDE), 1)
    hot[...] = jnp.where((action == lax.rem(lane, 8)) & (lane < 24), 1.0, 0.0).astype(BF16)
    exact = action_table[...]
    high = exact.astype(BF16)
    left = exact - high.astype(F32)
    middle = left.astype(BF16)
    low = left - middle.astype(F32)
    table[...] = jnp.concatenate(
        [high.astype(F32), middle.astype(F32), low, jnp.zeros((WIDE - 24, width), F32)], axis=0
    ).astype(BF16)

    def norm_rows(at, _):
        here = pl.ds(pl.multiple_of(at * 128, 128), 128)
        hat, _rate = normalise(tok[here, :].astype(F32) + dot(hot[here, :], table[...]))
        normed[here, :] = (hat * gain[...] + shift[...]).astype(BF16)
        return 0

    lax.fori_loop(0, rows // 128, norm_rows, 0)
    outs = [load(normed, normed_out)]
    across = []
    for at, (target, out) in enumerate(((key, key_out), (value, value_out), (query, query_out))):
        weights[at].wait()
        for part in range(4):
            side = pl.ds(part * 256, 256)
            target[:, side] = dot(normed[...], held[at, :, side]).astype(BF16)
        if at == 0:
            pl.semaphore_wait(barrier, peers)
        if at < 2:
            copy = remote(
                target, pair.at[at], pair_sems.at[0, at], pair_sems.at[1, at], grid.other()
            )
            copy.start()
            across.append(copy)
        outs.append(load(target, out))
    for copy in across:
        copy.wait()
    outs.append(load(pair, pair_out))
    weights[3].wait()
    bias = spatial_bias(is_big, 2 * WIDE)

    def group(at, _):
        here = pl.ds(pl.multiple_of(at * WIDE, WIDE), WIDE)
        for two in range(8):
            side = pl.ds(two * WIDE, WIDE)
            keys = jnp.concatenate([key[here, side], pair[0, here, side]], axis=0)
            values = jnp.concatenate([value[here, side], pair[1, here, side]], axis=0)
            prob, out = attend(query[here, side], keys, values, bias)
            probs[at, two] = prob
            mixed[here, side] = out.astype(BF16)
        return 0

    for half in range(2):
        lax.fori_loop(2 * half, 2 * half + 2, group, 0)
        here = slice(half * KEYS, (half + 1) * KEYS)
        blocks = slice(half * 16, (half + 1) * 16)
        for part in range(4):
            side = slice(part * 256, (part + 1) * 256)
            first = tok[here, side].astype(F32) + dot(hot[here, :], table[:, side])
            total = first + dot(mixed[here, :], held[3, :, side])
            turned[blocks, :, side] = total.astype(BF16).reshape(16, 16, 256)
        swap.send(half)
    outs += [load(mixed, mixed_out), load(probs, probs_out)]
    swap.wait()
    swap.place(second)
    outs.append(load(second, second_out))
    for copy in outs:
        copy.wait()


def first(clip_big, actions, tok, action_table, gain, shift, wq, wk, wv, wo, number):
    rows, width = tok.shape
    wide = shape_of((rows, width), BF16)
    probs = (rows // WIDE, 8, 2 * WIDE, KEYS)
    dma = pltpu.SemaphoreType.DMA
    full = pltpu.VMEM((rows, width), BF16)
    return pl.pallas_call(
        first_kernel,
        out_shape=[
            wide, wide, wide, wide, shape_of((2, rows, width), BF16), wide, shape_of(probs, BF16), wide,
            shape_of((rows, WIDE), BF16), shape_of((WIDE, width), BF16),
        ],
        in_specs=[IN_SMEM] * 2 + [WHOLE] * 4 + [IN_HBM] * 4,
        out_specs=[IN_HBM] * 8 + [WHOLE] * 2,
        scratch_shapes=[
            pltpu.VMEM((4, width, width), BF16), full, full, full, full,
            pltpu.VMEM((2, rows, width), BF16), full, pltpu.VMEM(probs, BF16), full,
            pltpu.VMEM((rows // 16, 16, width), BF16),
            pltpu.VMEM((7, 128, width), BF16),
            pltpu.VMEM((7, 128, width), BF16),
            dma((16,)), dma((2, 2)), dma((14,)), dma((14,)),
        ],
        compiler_params=params(collective_id=number, has_side_effects=True),
    )(clip_big, actions, tok, action_table, gain, shift, wq, wk, wv, wo)


def middle_kernel(
    clip_big, second, cot_in, gain_two, shift_two, gain, shift, bias_in, bias_out, wq, wk, wv, wo, win, wout,
    normed_out, query_out, key_out, value_out, probs_out, mixed_two_out, mixed_out, third_out, d_in, d_out, small,
    pool, probs, held, w_in, w_out, active, slope, third, normed_t, cot_t, turned,
    staged, came_cot, came_mixed, outgoing,
    loads, cot_sends, cot_recvs, mixed_sends, mixed_recvs, out_sems, prob_sems,
):
    rows, width = third.shape
    hidden = w_in.shape[1]
    chunks = hidden // CHUNK
    _clip, offset, is_big = where_am_i(clip_big)
    cot_swap = Swap(True, offset, is_big, turned, staged, came_cot, (cot_sends, cot_recvs))
    mixed_swap = Swap(False, offset, is_big, turned, staged, came_mixed, (mixed_sends, mixed_recvs))
    barrier = pltpu.get_barrier_semaphore()
    peers = cot_swap.greet(barrier)
    load = Loads(loads)
    cot_load = load(cot_in, turned)
    second_load = load(second, pool.at[0])
    weights = [load(source, held.at[at]) for at, source in enumerate((wq, wk, wv, wo))]
    weights += [load(win, w_in), load(wout, w_out)]
    cot_load.wait()
    pl.semaphore_wait(barrier, peers)
    cot_swap.send()
    second_load.wait()

    def norm_two(at, _):
        here = pl.ds(pl.multiple_of(at * 128, 128), 128)
        hat, _rate = normalise(pool[0, here, :].astype(F32))
        pool[4, here, :] = (hat * gain_two[...] + shift_two[...]).astype(BF16)
        return 0

    lax.fori_loop(0, rows // 128, norm_two, 0)
    outs = [load(pool.at[4], normed_out)]
    for at, out in enumerate((query_out, key_out, value_out)):
        weights[at].wait()
        for part in range(4):
            side = slice(part * 256, (part + 1) * 256)
            pool[1 + at, :, side] = dot(pool[4], held[at, :, side]).astype(BF16)
        outs.append(load(pool.at[1 + at], out))
    bias = temporal_bias(2 * KEYS)

    def probs_copy(at):
        return pltpu.make_async_copy(probs, probs_out.at[at], prob_sems.at[at])

    def group(at, _):
        @pl.when(at > 0)
        def _():
            probs_copy(0).wait()

        here = pl.ds(pl.multiple_of(at * KEYS, KEYS), KEYS)
        for two in range(8):
            side = pl.ds(two * WIDE, WIDE)
            prob, out = attend(pool[1, here, side], pool[2, here, side], pool[3, here, side], bias)
            probs[two] = prob
            pool[5, here, side] = out.astype(BF16)
        probs_copy(at).start()
        return 0

    lax.fori_loop(0, rows // KEYS, group, 0)
    outs += [load(pool.at[5], mixed_two_out)]
    weights[3].wait()
    for part in range(4):
        side = slice(part * 256, (part + 1) * 256)
        third[:, side] = pool[0, :, side].astype(F32) + dot(pool[5], held[3, :, side])
    outs[0].wait()

    def norm_three(at, _):
        here = pl.ds(pl.multiple_of(at * 128, 128), 128)
        hat, _rate = normalise(third[here, :])
        pool[4, here, :] = (hat * gain[...] + shift[...]).astype(BF16)
        return 0

    lax.fori_loop(0, rows // 128, norm_three, 0)
    normed_t[...] = pool[4].T
    weights[4].wait()

    def forward(at, _):
        side = pl.ds(pl.multiple_of(at * KEYS, KEYS), KEYS)
        inner = dot(pool[4], w_in[:, side]) + bias_in[:, side]
        square = inner * inner
        curve = jnp.tanh(ROOT * (inner + 0.044715 * inner * square))
        active[:, side] = (0.5 * inner * (1.0 + curve)).astype(BF16)
        slope[:, side] = (
            0.5 * (1.0 + curve)
            + (0.5 * ROOT) * inner * (1.0 - curve * curve) * (1.0 + (3 * 0.044715) * square)
        ).astype(BF16)
        return 0

    lax.fori_loop(0, hidden // KEYS, forward, 0)
    cot_swap.wait()
    cot_swap.place(pool.at[0])
    weights[5].wait()

    for part in range(width // KEYS):
        side = slice(part * KEYS, (part + 1) * KEYS)
        total = third[:, side] + bias_out[:, side] + dot(active[...], w_out[:, side])
        turned[:, :, side] = total.astype(BF16).reshape(rows // 16, 16, KEYS)
    mixed_swap.send()
    cot_t[...] = pool[0].T
    small[2:3, :] = jnp.sum(pool[0].astype(F32), axis=0, keepdims=True)

    def out_copies(at, slot):
        share = outgoing.shape[2]
        copies = [
            pltpu.make_async_copy(
                outgoing.at[slot],
                d_out.at[at // 4, :, pl.ds(lax.rem(at, 4) * share, share)],
                out_sems.at[slot, 0],
            )
        ]
        return copies

    def in_copies(at, slot):
        return [
            pltpu.make_async_copy(
                outgoing.at[2 + slot, pl.ds((which * 2 + part) * 4, 4)],
                d_in.at[which, at * 2 + part],
                out_sems.at[slot, 1 + which * 2 + part],
            )
            for which in range(2)
            for part in range(2)
        ]

    def backward(at, _):
        slot = lax.rem(at, 2)

        @pl.when(at >= 2)
        def _():
            for copy in out_copies(at - 2, slot) + in_copies(at - 2, slot):
                copy.wait()

        side = pl.ds(pl.multiple_of(at * CHUNK, CHUNK), CHUNK)
        wide = slope[:, side].astype(F32) * dot_nt(pool[0], w_out[side, :])
        grad_inner = wide.astype(BF16)
        slope[:, side] = grad_inner
        lanes = pl.ds(pl.multiple_of(lax.rem(at, 2) * CHUNK, CHUNK), CHUNK)
        small[pl.ds(3 + at // 2, 1), lanes] = jnp.sum(grad_inner.astype(F32), axis=0, keepdims=True)
        outgoing[slot] = dot(cot_t[...], active[:, side]).astype(BF16).reshape(outgoing.shape[1:])
        for top in range(4):
            block = dot(normed_t[top * 256 : (top + 1) * 256, :], grad_inner).astype(BF16)
            for part in range(2):
                first = ((top // 2) * 2 + part) * 4
                outgoing[
                    2 + slot, first : first + 4, :, (top % 2) * KEYS : (top % 2 + 1) * KEYS
                ] = block[:, part * KEYS : (part + 1) * KEYS].reshape(4, 64, KEYS)
        for copy in out_copies(at, slot) + in_copies(at, slot):
            copy.start()
        return 0

    lax.fori_loop(0, chunks, backward, 0)
    for copy in outs[1:]:
        copy.wait()
    probs_copy(1).wait()

    def back_rows(step, carry):
        here = pl.ds(pl.multiple_of(step * KEYS, KEYS), KEYS)
        hat, rate = normalise(third[here, :])
        grad = dot_nt(slope[here, :], w_in[...])
        pool[2, here, :] = (
            pool[0, here, :].astype(F32) + norm_backward(grad, hat, rate, gain[...])
        ).astype(BF16)
        return (
            carry[0] + jnp.sum(grad * hat, axis=0, keepdims=True),
            carry[1] + jnp.sum(grad, axis=0, keepdims=True),
        )

    zero = jnp.zeros((1, width), F32)
    sums = lax.fori_loop(0, rows // KEYS, back_rows, (zero, zero))
    small[0:1, :] = sums[0]
    small[1:2, :] = sums[1]
    small[7:8, :] = zero
    last = [load(pool.at[2], third_out)]
    mixed_swap.wait()
    mixed_swap.place(pool.at[1])
    last.append(load(pool.at[1], mixed_out))
    for at in (chunks - 2, chunks - 1):
        for copy in out_copies(at, at % 2) + in_copies(at, at % 2):
            copy.wait()
    for copy in last:
        copy.wait()


def middle(args, number):
    clip_big, second, cot = args[:3]
    win = args[13]
    rows, width = second.shape
    hidden = win.shape[1]
    wide = shape_of((rows, width), BF16)
    probs = (rows // KEYS, 8, 2 * KEYS, KEYS)
    dma = pltpu.SemaphoreType.DMA
    block = pltpu.VMEM((7, 128, width), BF16)
    args = list(args)
    args[2] = cot.reshape(rows // 16, 16, width)
    return pl.pallas_call(
        middle_kernel,
        out_shape=[
            wide, wide, wide, wide, shape_of(probs, BF16), wide, wide, wide,
            shape_of((2, hidden // KEYS, 4, 64, 2 * KEYS), BF16),
            shape_of((2, 16, KEYS, CHUNK), BF16),
            shape_of((8, width), F32),
        ],
        in_specs=[IN_SMEM, IN_HBM, IN_HBM] + [WHOLE] * 6 + [IN_HBM] * 6,
        out_specs=[IN_HBM] * 10 + [WHOLE],
        scratch_shapes=[
            pltpu.VMEM((6, rows, width), BF16),
            pltpu.VMEM(probs[1:], BF16),
            pltpu.VMEM((4, width, width), BF16),
            pltpu.VMEM((width, hidden), BF16),
            pltpu.VMEM((hidden, width), BF16),
            pltpu.VMEM((rows, hidden), BF16),
            pltpu.VMEM((rows, hidden), BF16),
            pltpu.VMEM((rows, width), F32),
            pltpu.VMEM((width, rows), BF16),
            pltpu.VMEM((width, rows), BF16),
            pltpu.VMEM((rows // 16, 16, width), BF16),
            block, block, block,
            pltpu.VMEM((4, 16, 64, CHUNK), BF16),
            dma((24,)), dma((7,)), dma((7,)), dma((7,)), dma((7,)), dma((2, 5)), dma((2,)),
        ],
        compiler_params=params(collective_id=number, has_side_effects=True),
    )(*args)


def on_device(
    tokens,
    cotangent,
    clip_big,
    actions,
    action_table,
    norm_gain,
    norm_bias,
    spatial_q,
    spatial_k,
    spatial_v,
    spatial_o,
    temporal_q,
    temporal_k,
    temporal_v,
    temporal_o,
    ffn_in,
    ffn_bias_in,
    ffn_out,
    ffn_bias_out,
):
    tok = tokens[0]
    rows, width = tok.shape
    me = lax.axis_index("seq")
    count = lax.axis_size("seq")
    gains = [norm_gain[at : at + 1] for at in range(3)]
    shifts = [norm_bias[at : at + 1] for at in range(3)]

    normed_one, query_one, key_one, value_one, pair_one, mixed_one, probs_one, second, hot, table = first(
        clip_big, actions, tok, action_table, gains[0], shifts[0],
        spatial_q, spatial_k, spatial_v, spatial_o, 1,
    )
    (normed_two, query_two, key_two, value_two, probs_two, mixed_two, mixed, grad_third, d_in, d_out,
     small_ffn) = middle(
        [
            clip_big, second, cotangent[0], gains[1], shifts[1], gains[2], shifts[2],
            ffn_bias_in, ffn_bias_out, temporal_q, temporal_k, temporal_v, temporal_o, ffn_in, ffn_out,
        ],
        2,
    )
    part = width // count
    finer = count // d_in.shape[1]
    if finer > 1:
        d_in = d_in.reshape(2, d_in.shape[1], KEYS, 2, finer, KEYS // finer).transpose(0, 1, 4, 2, 3, 5)
        d_out = d_out.reshape(2, d_out.shape[1], 4, finer, part, CHUNK).transpose(0, 1, 3, 2, 4, 5)
    d_in, d_out = (grads.reshape(2, count, 4 * part, CHUNK) for grads in (d_in, d_out))
    pieces = ffn_in.shape[1] // width
    token_grad, sum_out, sum_in, sum_temporal, sum_spatial, small = back(
        [
            clip_big, d_out, d_in, grad_third, second, mixed_two, query_two, key_two, value_two,
            normed_two, probs_two, temporal_q, temporal_k, temporal_v, temporal_o, mixed_one,
            query_one, key_one, value_one, pair_one, normed_one, probs_one, spatial_q, spatial_k,
            spatial_v, spatial_o, tok, hot, table, gains[0], gains[1], small_ffn,
        ],
        5,
    )
    hidden = ffn_in.shape[1]
    ffn_in_grad = (
        sum_in.reshape(2, KEYS, 2, hidden // count).transpose(0, 2, 1, 3).reshape(width, -1).astype(F32)
    )
    ffn_out_grad = (
        sum_out.reshape(2, 4, part, CHUNK).transpose(0, 1, 3, 2).reshape(hidden, part).astype(F32)
    )

    def finish(summed):
        joined = summed.reshape(2, 4, part, width // 2).transpose(0, 3, 1, 2).astype(F32)
        joined = joined.reshape(width, 4, part)
        return [joined[:, at] for at in range(4)]

    temporal_o_grad, temporal_q_grad, temporal_k_grad, temporal_v_grad = finish(sum_temporal)
    spatial_o_grad, spatial_q_grad, spatial_k_grad, spatial_v_grad = finish(sum_spatial)

    def mine(values):
        return lax.dynamic_slice_in_dim(values, me * part, part, 1)

    bias_in = small[19 : 19 + pieces].reshape(1, hidden)
    bias_in = lax.dynamic_slice_in_dim(bias_in, me * (hidden // count), hidden // count, 1)
    return (
        mixed[None],
        token_grad[None],
        mine(small[0:8]),
        mine(jnp.concatenate([small[8:10], small[16:17]], axis=0)),
        mine(jnp.concatenate([small[10:12], small[17:18]], axis=0)),
        spatial_q_grad,
        spatial_k_grad,
        spatial_v_grad,
        spatial_o_grad,
        temporal_q_grad,
        temporal_k_grad,
        temporal_v_grad,
        temporal_o_grad,
        ffn_in_grad,
        bias_in,
        ffn_out_grad,
        mine(small[18:19]),
    )


def solution(mesh):
    placed = (P("tile", "seq", None),) * 2 + (P(),) * 17
    return jax.shard_map(
        on_device,
        mesh=mesh,
        in_specs=placed,
        out_specs=(P("tile", "seq", None),) * 2 + (P(None, "seq"),) * 15,
        check_vma=False,
    )
```

```python
import functools

import jax
import jax.numpy as jnp
from jax import lax
from jax.experimental import pallas as pl
from jax.experimental.pallas import tpu as pltpu
from jax.sharding import PartitionSpec as P

HEAD_DIM = 64
FRAMES = 16
GRID_BIG = 16
GRID_SMALL = 8
WIDE = 128
KEYS = 256
CHUNK = 512
VMEM_BYTES = 62 * 2**20
FACTOR = HEAD_DIM**-0.5
ROOT = (2.0 / 3.141592653589793) ** 0.5

F32 = jnp.float32
BF16 = jnp.bfloat16
WHOLE = pl.BlockSpec(memory_space=pltpu.VMEM)
IN_HBM = pl.BlockSpec(memory_space=pl.ANY)
MESH = pl.DeviceIdType.MESH
IN_SMEM = pl.BlockSpec(memory_space=pltpu.SMEM)


def shape_of(dims, kind):
    return jax.ShapeDtypeStruct(dims, kind)


def params(**more):
    return pltpu.CompilerParams(vmem_limit_bytes=VMEM_BYTES, **more)


def dot(left, right):
    return jnp.dot(left, right, preferred_element_type=F32)


def dot_nt(left, right):
    return lax.dot_general(left, right, (((1,), (1,)), ((), ())), preferred_element_type=F32)


def dot_tn(left, right):
    return lax.dot_general(left, right, (((0,), (0,)), ((), ())), preferred_element_type=F32)


def normalise(values):
    centre = values - jnp.mean(values, axis=-1, keepdims=True)
    rate = lax.rsqrt(jnp.mean(centre * centre, axis=-1, keepdims=True) + 1e-05)
    return centre * rate, rate


def norm_backward(grad, hat, rate, gain):
    inner = grad * gain
    level = jnp.mean(inner, axis=-1, keepdims=True)
    slope = jnp.mean(inner * hat, axis=-1, keepdims=True)
    return rate * (inner - level - hat * slope)


def head_halves(block):
    lane = lax.broadcasted_iota(jnp.int32, block.shape, 1)
    zero = jnp.zeros_like(block)
    first = lane < HEAD_DIM
    return jnp.concatenate([jnp.where(first, block, zero), jnp.where(first, zero, block)], axis=0)


def join_halves(both):
    rows = both.shape[0] // 2
    lane = lax.broadcasted_iota(jnp.int32, (rows, both.shape[1]), 1)
    return jnp.where(lane < HEAD_DIM, both[:rows], both[rows:])


def attend(query, key, value, bias):
    scores = dot_nt(head_halves(query) * FACTOR, key) + bias
    top = jnp.max(scores, axis=1, keepdims=True)
    powers = jnp.exp(scores - top)
    prob = (powers * (1.0 / jnp.sum(powers, axis=1, keepdims=True))).astype(BF16)
    return prob, join_halves(dot(prob, value))


def attend_backward(prob, query, key, value, grad):
    grad_two = head_halves(grad)
    grad_prob = dot_nt(grad_two, value)
    prob_f = prob.astype(F32)
    delta = jnp.sum(prob_f * grad_prob, axis=1, keepdims=True)
    grad_score = (prob_f * (grad_prob - delta)).astype(BF16)
    grad_query = join_halves(dot(grad_score, key)) * FACTOR
    grad_key = dot_tn(grad_score, head_halves(query)) * FACTOR
    grad_value = dot_tn(prob, grad_two)
    return grad_query, grad_key, grad_value


def spatial_bias(is_big, rows):
    row = lax.broadcasted_iota(jnp.int32, (rows, KEYS), 0)
    column = lax.broadcasted_iota(jnp.int32, (rows, KEYS), 1)
    same = lax.rem(row, WIDE) // 32 == lax.rem(column, WIDE) // 32
    return jnp.where(same | (is_big == 1), 0.0, -1e30).astype(F32)


def temporal_bias(rows):
    row = lax.rem(lax.broadcasted_iota(jnp.int32, (rows, KEYS), 0), KEYS)
    column = lax.broadcasted_iota(jnp.int32, (rows, KEYS), 1)
    fits = (lax.rem(row, 16) == lax.rem(column, 16)) & (column <= row)
    return jnp.where(fits, 0.0, -1e30).astype(F32)


def weight_grad(target, at, grad, normed):
    grad_t = grad.T
    count, _rows, width = target.shape[1:]
    part = grad_t.shape[0] // count
    for which in range(2):
        block = dot(grad_t, normed[:, which * width : (which + 1) * width]).astype(BF16)
        target[which, :, at * part : (at + 1) * part, :] = block.reshape(count, part, width)


REACH = 3
STEPS = tuple(step for step in range(REACH, -REACH - 1, -1) if step != 0)


class Swap:
    def __init__(self, to_time, offset, is_big, source, staged, came, sems, parts=1):
        self.me, self.tile = lax.axis_index("seq"), lax.axis_index("tile")
        self.count = lax.axis_size("seq")
        self.to_time, self.offset, self.is_big = to_time, offset, is_big
        self.source, self.staged, self.came, self.sems = source, staged, came, sems
        self.parts = parts

    def peer(self, step):
        return (self.me + step, self.tile)

    def present(self, step):
        return (self.me + step >= 0) & (self.me + step < self.count)

    def greet(self, barrier):
        for step in STEPS:
            @pl.when(self.present(step))
            def _(step=step):
                pl.semaphore_signal(
                    barrier, inc=1, device_id=self.peer(step), device_id_type=MESH
                )
        return jnp.minimum(self.me, REACH) + jnp.minimum(self.count - 1 - self.me, REACH)

    def copy(self, step, part):
        slot, sem = REACH - step, (REACH - step) * self.parts + part
        source, target = self.staged.at[slot], self.came.at[slot]
        if self.parts > 1:
            rows = pl.ds(part * (128 // self.parts), 128 // self.parts)
            source, target = source.at[rows], target.at[rows]
        return remote(source, target, self.sems[0].at[sem], self.sems[1].at[sem], self.peer(step))

    def stage(self, step, part):
        which = jnp.clip(self.offset + step, 0, REACH)
        target = self.came if step == 0 else self.staged
        slot = REACH - step
        if self.to_time:
            frames = 4 // self.parts
            for frame in range(part * frames, (part + 1) * frames):
                block = self.source[pl.ds(which * 2 + frame * 8, 2)]
                target[slot, frame * 32 : frame * 32 + 32] = block.reshape(32, block.shape[2])
            return
        sides = 2 // self.parts
        for side in range(part * sides, (part + 1) * sides):
            block = self.source[pl.ds(which * 4 + side * 16, 4)]
            target[slot, side * 64 : side * 64 + 64] = block.reshape(64, block.shape[2])

    def send(self, part=0):
        for step in STEPS:
            self.stage(step, part)

            @pl.when(self.present(step))
            def _(step=step):
                self.copy(step, part).start()

        self.stage(0, part)

    def wait(self):
        for part in range(self.parts):
            for step in STEPS:
                @pl.when(self.present(step))
                def _(step=step, part=part):
                    self.copy(step, part).wait_send()

                @pl.when(self.present(-step))
                def _(step=step, part=part):
                    self.copy(step, part).wait_recv()

    def place(self, target):
        width = target.shape[-1]
        chosen = jnp.full((16, width), self.is_big, jnp.int32) == 1
        for at in range(REACH + 1):
            slot = REACH - self.offset + at
            for side in range(2):
                for frame in range(4):
                    low = frame * 32 + side * 16 if self.to_time else side * 64 + frame * 16
                    moved = self.came[pl.ds(slot, 1), low : low + 16][0]
                    if self.to_time:
                        here, mine = side * 256 + at * 64 + frame * 16, at * 8 + frame * 2 + side
                    else:
                        here, mine = frame * 128 + at * 32 + side * 16, side * 16 + frame * 4 + at
                    target[here : here + 16] = jnp.where(chosen, moved, self.source[mine])


def seq_dims(count):
    return {16: (2, 2, 2, 2), 64: (4, 4, 4)}.get(count, (1, 1, count))


def seq_orders(count):
    return {16: ((3, 1, 2, 0), (2, 1, 3, 0))}.get(count, ((2, 1, 0), (1, 2, 0)))


class Grid:
    def __init__(self):
        self.count = lax.axis_size("seq")
        self.dims = seq_dims(self.count)
        self.orders = seq_orders(self.count)
        self.axes = len(self.dims)
        self.me = lax.axis_index("seq")
        self.tile = lax.axis_index("tile")
        self.strides = [1]
        for size in self.dims[:0:-1]:
            self.strides.insert(0, self.strides[0] * size)
        self.places = [
            lax.rem(self.me // stride, size) for stride, size in zip(self.strides, self.dims)
        ]

    def along(self, axis, step):
        place = self.places[axis]
        there = lax.rem(place + step, self.dims[axis])
        return there, (self.me + (there - place) * self.strides[axis], self.tile)

    def other(self):
        return (self.me, 1 - self.tile)

    def peers(self, phase, order):
        if phase == 0:
            return [self.other()]
        axis = order[phase - 1]
        return [self.along(axis, step)[1] for step in range(1, self.dims[axis])]

    def greet(self, barrier):
        peers = [self.other()]
        for axis in range(self.axes):
            peers += [self.along(axis, step)[1] for step in range(1, self.dims[axis])]
        for peer in peers:
            pl.semaphore_signal(barrier, inc=1, device_id=peer, device_id_type=MESH)
        return len(peers)

    def split(self, flat, dims):
        where = []
        for size in dims[::-1]:
            where.insert(0, lax.rem(flat, size))
            flat = flat // size
        return tuple(where)


def remote(source, target, send_sem, recv_sem, device):
    return pltpu.make_async_remote_copy(
        src_ref=source,
        dst_ref=target,
        send_sem=send_sem,
        recv_sem=recv_sem,
        device_id=device,
        device_id_type=MESH,
    )


class Unit:
    def __init__(self, grid, order, rows, source, out, came, part, sems, free, number, reuse, again):
        self.grid, self.order = grid, order
        self.rows, self.part = rows, part
        self.away, self.own, self.fetched = source
        self.out, self.came = out, came
        self.sends, self.recvs = sems
        self.free, self.number, self.reuse, self.again = free, number, reuse, again
        self.last = grid.axes + 1

    def rest(self, phase):
        taken = self.order[:phase]
        return [axis for axis in range(self.grid.axes) if axis not in taken]

    def held(self, phase):
        lead = () if phase == 0 else (0,)
        return self.came[phase], lead

    def slab(self, phase, there):
        before = self.rest(phase - 1)
        where = [slice(None)] * len(before)
        where[before.index(self.order[phase - 1])] = there
        ref, lead = self.held(phase - 1)
        return ref.at[lead + tuple(where) + (self.part,)]

    def landing(self, phase, step):
        dims = len(self.rest(phase))
        return self.came[phase].at[(step,) + (slice(None),) * dims + (self.part,)]

    def copies(self, phase):
        number, grid = self.number, self.grid
        if phase == 0:
            if self.fetched is not None:
                return [pltpu.make_async_copy(self.fetched, self.start_of(), self.sends.at[number, 0, 0])]
            return [
                remote(
                    self.away, self.start_of(), self.sends.at[number, 0, 0],
                    self.recvs.at[number, 0, 0], grid.other(),
                )
            ]
        if phase == self.last:
            mine = self.out.at[grid.tile, self.rows]
            return [
                remote(
                    mine, mine, self.sends.at[number, phase, 0], self.recvs.at[number, phase, 0],
                    grid.other(),
                )
            ]
        axis = self.order[phase - 1]
        out = []
        for step in range(1, grid.dims[axis]):
            there, device = grid.along(axis, step)
            out.append(
                remote(
                    self.slab(phase, there), self.landing(phase, step - 1),
                    self.sends.at[number, phase, step - 1], self.recvs.at[number, phase, step - 1],
                    device,
                )
            )
        return out

    def start_of(self):
        return self.came[0].at[(slice(None),) * self.grid.axes + (self.part,)]

    def start(self, phase):
        if self.again and phase < self.last:
            amount = len(self.grid.peers(phase, self.order))
            pl.semaphore_wait(self.free.at[self.again - 1, phase], amount)
        for copy in self.copies(phase):
            copy.start()

    def release(self, phase):
        for number, order in self.reuse:
            for peer in self.grid.peers(phase, order):
                pl.semaphore_signal(
                    self.free.at[number, phase], inc=1, device_id=peer, device_id_type=MESH
                )

    def wait(self, phase):
        for copy in self.copies(phase):
            copy.wait()

    def turn(self, phase):
        self.wait(phase)
        grid = self.grid
        if phase == 0:
            def step(at, _):
                where = grid.split(at, grid.dims) + (self.part,)
                self.came[0][where] = self.came[0][where] + self.own(grid.split(at, grid.dims))
                return 0

            if self.fetched is None:
                lax.fori_loop(0, grid.count, step, 0)
                return
            self.own(None)
            for piece in range(4):
                base = piece * (grid.count // 4)
                self.own(piece)

                def step_kept(at, _, base=base):
                    where = grid.split(at + base, grid.dims) + (self.part,)
                    self.came[0][where] = self.came[0][where] + self.own(at)
                    return 0

                lax.fori_loop(0, grid.count // 4, step_kept, 0)
            return
        axis = self.order[phase - 1]
        own = self.slab(phase, grid.places[axis])
        size = grid.dims[axis]
        if phase == grid.axes:
            total = own[...].astype(F32)
            for at in range(size - 1):
                total = total + self.came[phase][at, self.part].astype(F32)
            self.out[grid.tile, self.rows] = total.astype(BF16)
            self.release(phase - 1)
            self.release(phase)
            return
        dims = tuple(grid.dims[axis] for axis in self.rest(phase))
        steps = 1
        for size_of in dims:
            steps *= size_of

        def step(at, _):
            where = grid.split(at, dims)
            total = own[where]
            for other in range(size - 1):
                total = total + self.came[phase][(other,) + where + (self.part,)]
            self.came[phase][(0,) + where + (self.part,)] = total
            return 0

        lax.fori_loop(0, steps, step, 0)
        self.release(phase - 1)

    def on(self, phase):
        if phase < self.last:
            self.turn(phase)
            self.start(phase + 1)


class Pair:
    def __init__(self, *units):
        self.units = units

    def __getattr__(self, name):
        def each(phase):
            for unit in self.units:
                getattr(unit, name)(phase)

        return each


class Total:
    def __init__(self, grid, value, came, sends, recvs):
        self.order = grid.orders[0]
        self.last = grid.axes
        self.grid, self.value, self.came, self.sends, self.recvs = grid, value, came, sends, recvs

    def copies(self, phase):
        first = sum(len(self.grid.peers(before, self.order)) for before in range(phase))
        return [
            remote(
                self.value, self.came.at[first + at], self.sends.at[first + at],
                self.recvs.at[first + at], peer,
            )
            for at, peer in enumerate(self.grid.peers(phase, self.order))
        ]

    def start(self, phase):
        for copy in self.copies(phase):
            copy.start()

    def on(self, phase):
        if phase > self.last:
            return
        copies = self.copies(phase)
        for copy in copies:
            copy.wait()
        total = self.value[...]
        first = sum(len(self.grid.peers(before, self.order)) for before in range(phase))
        for at in range(len(copies)):
            total = total + self.came[first + at]
        self.value[...] = total
        if phase < self.last:
            self.start(phase + 1)


def unit_scratch(rows, width, order, dims):
    left = list(range(len(dims)))
    out = [pltpu.VMEM(dims + (rows, width), BF16)]
    for axis in order:
        left.remove(axis)
        rest = tuple(dims[other] for other in left)
        out.append(pltpu.VMEM((max(dims[axis] - 1, 1),) + rest + (rows, width), BF16))
    return out


def back_kernel(
    clip_big, d_out, came_out, d_in, came_in, third, second, mixed_t, query_t, key_t, value_t, normed_t, probs_t,
    wq_t, wk_t, wv_t, wo_t, mixed_s, query_s, key_s, value_s, pair, normed_s, probs_s,
    wq_s, wk_s, wv_s, wo_s, tok, hot, table, gain_one, gain_two, small_ffn,
    token_grad, sum_out, sum_in, sum_time, sum_space, small,
    pool, turned, held, probs, d_weights, kept, came_key, came_value, swapped, *rest,
):
    grid = Grid()
    deep = grid.axes + 1
    unit_bufs, rest = rest[: 4 * deep], rest[4 * deep :]
    (totals, total_came, loads, unit_sends, unit_recvs, free, swap_sends, swap_recvs,
     total_sends, total_recvs, pair_sems) = rest
    rows, width = pool.shape[1:]
    _clip, offset, is_big = where_am_i(clip_big)
    swap = Swap(
        False, offset, is_big, turned, _Slots(pool, (11, 6)), swapped, (swap_sends, swap_recvs), 2
    )
    barrier = pltpu.get_barrier_semaphore()
    pl.semaphore_wait(barrier, grid.greet(barrier) + swap.greet(barrier))

    load = Loads(loads)
    orders = grid.orders
    share = d_out.shape[-2]
    every = (slice(None),) * grid.axes

    def buffers(group, which):
        first = (group % 2) * 2 * deep + which * deep
        return unit_bufs[first : first + deep]

    def fetched(group, which, keep, landed, out):
        half = share // 2
        rows_of = pl.ds(which * half, half)
        number = 2 * group + which
        first = (1, grid.dims[0] * grid.dims[1] // 4) if grid.dims[0] < 4 else (grid.dims[0] // 4, grid.dims[1])

        def own(at):
            if at is None:
                return None
            if isinstance(at, int):
                copy = pltpu.make_async_copy(
                    keep.at[
                        (
                            pl.ds(at * first[0] * first[1] // grid.dims[1], first[0]),
                            pl.ds(at * first[1] % grid.dims[1], first[1]),
                        )
                        + every[2:]
                        + (rows_of,)
                    ],
                    kept,
                    unit_sends.at[number, 0, 1],
                )
                copy.start()
                copy.wait()
                return None
            return kept[grid.split(at, first + grid.dims[2:])]

        reuse = [(4 * group + 2 * which + sub, orders[sub]) for sub in range(2)]
        return Unit(
            grid, orders[which], rows_of, (None, own, landed.at[every + (rows_of,)]), out,
            buffers(group, which), pl.ds(0, half), (unit_sends, unit_recvs), free, number, reuse, 0,
        )

    def made(group, which, out):
        quarter = share // 4
        rows_of = pl.ds(which * quarter, quarter)

        def own(where):
            return d_weights[(grid.tile,) + where + (rows_of,)]

        return Unit(
            grid, orders[which % 2], rows_of,
            (d_weights.at[(1 - grid.tile,) + every + (rows_of,)], own, None), out,
            buffers(group, which // 2), pl.ds((which % 2) * quarter, quarter),
            (unit_sends, unit_recvs), free, 4 + 4 * (group - 2) + which, [],
            4 * (group - 2) + which + 1,
        )

    p0 = Pair(*[fetched(0, which, d_out, came_out, sum_out) for which in range(2)])
    p1 = Pair(*[fetched(1, which, d_in, came_in, sum_in) for which in range(2)])
    p2 = Pair(*[made(2, which, sum_time) for which in range(4)])
    p3o, p3q, p3k, p3v = [made(3, which, sum_space) for which in range(4)]
    p0.start(0)
    p1.start(0)

    in_low = load(third, pool.at[0])
    in_mixed = load(mixed_t, pool.at[2])
    weights = [load(source, held.at[at]) for at, source in enumerate((wo_t, wq_t, wk_t, wv_t))]
    ins = [load(source, pool.at[3 + at]) for at, source in enumerate((query_t, key_t, value_t))]
    ins += [load(probs_t.at[at], probs.at[at]) for at in range(2)]
    late = [load(second, pool.at[1]), load(normed_t, pool.at[6])]
    p0.on(0)
    in_low.wait()
    in_mixed.wait()
    flat_weights = d_weights.reshape((2, grid.count) + d_weights.shape[-2:])
    weight_grad(flat_weights, 0, pool[0], pool.at[2])
    weights[0].wait()

    def mix_back(grad, target):
        for part in range(4):
            side = slice(part * 256, (part + 1) * 256)
            pool[target, :, side] = dot_nt(pool[grad], held[0, side, :]).astype(BF16)

    mix_back(0, 7)
    weights.append(load(wo_s, held.at[0]))
    for copy in ins:
        copy.wait()

    def time_group(at, _):
        here = pl.ds(pl.multiple_of(at * KEYS, KEYS), KEYS)
        for two in range(8):
            side = pl.ds(two * WIDE, WIDE)
            grads = attend_backward(
                probs[at, two], pool[3, here, side], pool[4, here, side], pool[5, here, side],
                pool[7, here, side],
            )
            for target, grad in enumerate(grads):
                pool[8 + target, here, side] = grad.astype(BF16)
        return 0

    lax.fori_loop(0, rows // KEYS, time_group, 0)
    ins = [
        load(source, pool.at[target])
        for source, target in (
            (query_s, 2), (key_s, 3), (value_s, 4), (pair.at[0], 5), (pair.at[1], 7)
        )
    ]
    ins += [
        load(probs_s.at[at], probs.at[at // 2, :, pl.ds(at % 2 * 2 * WIDE, 2 * WIDE)])
        for at in range(4)
    ]
    for copy in late:
        copy.wait()
    for at in range(3):
        weight_grad(flat_weights, at + 1, pool[8 + at], pool.at[6])
    for at in range(3):
        weights[at + 1].wait()

    def time_rows(step, carry):
        here = pl.ds(pl.multiple_of(step * 256, 256), 256)
        grad = (
            dot_nt(pool[8, here, :], held[1])
            + dot_nt(pool[9, here, :], held[2])
            + dot_nt(pool[10, here, :], held[3])
        )
        hat, rate = normalise(pool[1, here, :].astype(F32))
        total = pool[0, here, :].astype(F32) + norm_backward(grad, hat, rate, gain_two[...])
        turned[pl.ds(step * 16, 16)] = total.astype(BF16).reshape(16, 16, width)
        return (
            carry[0] + jnp.sum(grad * hat, axis=0, keepdims=True),
            carry[1] + jnp.sum(grad, axis=0, keepdims=True),
        )

    zero = jnp.zeros((1, width), F32)
    time_norm = (zero, zero)
    for side in range(2):
        time_norm = time_rows(side, time_norm)
        swap.send(side)
    weights += [load(source, held.at[at + 1]) for at, source in enumerate((wq_s, wk_s, wv_s))]
    in_mixed = load(mixed_s, pool.at[10])
    p0.on(1)
    p1.on(0)
    p2.start(0)
    swap.wait()
    swap.place(pool.at[1])
    in_normed = load(normed_s, pool.at[0])
    p2.turn(0)

    in_mixed.wait()
    weight_grad(flat_weights, 0, pool[1], pool.at[10])
    weights[4].wait()
    mix_back(1, 8)
    p0.on(2)
    p1.on(1)
    p2.start(1)
    p3o.start(0)
    for copy in ins:
        copy.wait()

    def space_group(at, _):
        here = pl.ds(pl.multiple_of(at * WIDE, WIDE), WIDE)
        lower = pl.ds(pl.multiple_of(lax.rem(at, 2) * 2 * WIDE, 2 * WIDE), 2 * WIDE)
        for two in range(8):
            side = pl.ds(two * WIDE, WIDE)
            keys = jnp.concatenate([pool[3, here, side], pool[5, here, side]], axis=0)
            values = jnp.concatenate([pool[4, here, side], pool[7, here, side]], axis=0)
            grad_query, grad_key, grad_value = attend_backward(
                probs[at // 2, two, lower], pool[2, here, side], keys, values, pool[8, here, side]
            )
            pool[9, here, side] = grad_query.astype(BF16)
            pool[10, here, side] = grad_key[:WIDE].astype(BF16)
            pool[11, here, side] = grad_value[:WIDE].astype(BF16)
            pool[6, here, side] = grad_key[WIDE:].astype(BF16)
            turned[pl.ds(at * 8, 8), :, side] = grad_value[WIDE:].astype(BF16).reshape(8, 16, WIDE)
        return 0

    lax.fori_loop(0, rows // (2 * WIDE), space_group, 0)
    p0.on(3)
    p1.on(2)
    p3o.on(0)
    lax.fori_loop(rows // (2 * WIDE), rows // WIDE, space_group, 0)
    across = [
        remote(
            source, target, pair_sems.at[0, at], pair_sems.at[1, at], grid.other(),
        )
        for at, (source, target) in enumerate(((pool.at[6], came_key), (turned, came_value)))
    ]
    for copy in across:
        copy.start()
    in_tok = load(tok, pool.at[2])
    in_normed.wait()
    weight_grad(flat_weights, 1, pool[9], pool.at[0])
    p3q.start(0)
    p2.on(1)
    for at, copy in enumerate(across):
        copy.wait()
        came = (came_key, came_value)[at][...].reshape(rows, width)
        pool[10 + at] = pool[10 + at] + came
        weight_grad(flat_weights, 2 + at, pool[10 + at], pool.at[0])
        (p3k, p3v)[at].start(0)
    p3q.on(0)
    p0.on(4)
    p1.on(3)
    for at in range(3):
        weights[5 + at].wait()
    in_tok.wait()

    def space_rows(step, carry):
        here = pl.ds(pl.multiple_of(step * 256, 256), 256)
        grad = (
            dot_nt(pool[9, here, :], held[1])
            + dot_nt(pool[10, here, :], held[2])
            + dot_nt(pool[11, here, :], held[3])
        )
        first = pool[2, here, :].astype(F32) + dot(hot[here, :], table[...])
        hat, rate = normalise(first)
        total = pool[1, here, :].astype(F32) + norm_backward(grad, hat, rate, gain_one[...])
        high = total.astype(BF16)
        pool[1, here, :] = high
        rest = (total - high.astype(F32)).astype(BF16)
        chosen = hot[here, :]
        return (
            carry[0] + jnp.sum(grad * hat, axis=0, keepdims=True),
            carry[1] + jnp.sum(grad, axis=0, keepdims=True),
            carry[2] + dot_tn(chosen, high)[:8] + dot_tn(chosen, rest)[:8],
        )

    p2.on(2)
    p3o.on(1)
    p3k.on(0)
    p3v.on(0)
    space_norm = lax.fori_loop(0, rows // 256, space_rows, (zero, zero, jnp.zeros((8, width), F32)))
    out_grad = load(pool.at[1], token_grad)
    totals[0:8] = space_norm[2]
    totals[8:16] = jnp.concatenate(
        [space_norm[0], time_norm[0], space_norm[1], time_norm[1], jnp.zeros((4, width), F32)], axis=0
    )
    totals[16:24] = small_ffn[...]
    total = Total(grid, totals, total_came, total_sends, total_recvs)
    total.start(0)
    p1.on(4)
    p2.on(3)
    p3o.on(2)
    p3q.on(1)
    total.on(0)
    p3k.on(1)
    p3v.on(1)
    p3o.on(3)
    p2.on(4)
    total.on(1)
    p3q.on(2)
    p3k.on(2)
    p3v.on(2)
    total.on(2)
    p3o.on(4)
    p3q.on(3)
    p3k.on(3)
    p3v.on(3)
    total.on(3)
    p3q.on(4)
    p3k.on(4)
    p3v.on(4)
    total.on(4)
    small[...] = totals[...]
    for unit in (p0, p1, p2, p3o, p3q, p3k, p3v):
        unit.wait(grid.axes + 1)
    out_grad.wait()


class _Slots:
    def __init__(self, pool, slots):
        self.pool, self.slots = pool, slots

    class _At:
        def __init__(self, slots):
            self.slots = slots

        def __getitem__(self, slot):
            return self.slots.pool.at[self.slots.slots[slot // 4], pl.ds(slot % 4 * 128, 128)]

    @property
    def at(self):
        return _Slots._At(self)

    def __setitem__(self, where, value):
        slot, rows = where
        first = slot % 4 * 128
        self.pool[self.slots[slot // 4], first + rows.start : first + rows.stop] = value


def back(args, number):
    args = list(args)
    rows, width = args[5].shape
    count = lax.axis_size("seq")
    dims = seq_dims(count)
    share, group = args[1].shape[-2:]
    dma = pltpu.SemaphoreType.DMA
    lead = (1, dims[0] * dims[1] // 4) if dims[0] < 4 else (dims[0] // 4, dims[1])
    scratch = [
        pltpu.VMEM((12, rows, width), BF16),
        pltpu.VMEM((rows // 16, 16, width), BF16),
        pltpu.VMEM((4, width, width), BF16),
        pltpu.VMEM((2, 8, 2 * KEYS, KEYS), BF16),
        pltpu.VMEM((2,) + dims + (share, group), BF16),
        pltpu.VMEM(lead + dims[2:] + (share // 2, group), BF16),
        pltpu.VMEM((rows, width), BF16),
        pltpu.VMEM((rows // 16, 16, width), BF16),
        pltpu.VMEM((7, 128, width), BF16),
    ]
    for _ in range(2):
        for order in seq_orders(count):
            scratch += unit_scratch(share // 2, group, order, dims)
    most = max(max(dims) - 1, 2)
    peers = 1 + sum(dims) - len(dims)
    scratch += [
        pltpu.VMEM((24, width), F32),
        pltpu.VMEM((peers, 24, width), F32),
        dma((40,)),
        dma((12, len(dims) + 2, most)),
        dma((12, len(dims) + 2, most)),
        pltpu.SemaphoreType.REGULAR((8, len(dims) + 1)),
        dma((14,)),
        dma((14,)),
        dma((peers,)),
        dma((peers,)),
        dma((2, 2)),
    ]
    for at in range(1, 5):
        args[at] = args[at].reshape(dims + (share, group))
    final = shape_of((2, share, group), BF16)
    return pl.pallas_call(
        back_kernel,
        out_shape=[shape_of((rows, width), BF16)] + [final] * 4 + [shape_of((24, width), F32)],
        in_specs=[IN_SMEM] + [IN_HBM] * 28 + [WHOLE] * 5,
        out_specs=[IN_HBM] + [WHOLE] * 5,
        scratch_shapes=scratch,
        compiler_params=params(collective_id=number, has_side_effects=True),
    )(*args)


def where_am_i(clip_big):
    me = lax.axis_index("seq")
    span = (GRID_BIG // GRID_SMALL) ** 2
    start, clip, offset, is_big = jnp.int32(0), jnp.int32(0), jnp.int32(0), jnp.int32(0)
    for at in range(clip_big.shape[0]):
        big = clip_big[at]
        size = jnp.where(big == 1, span, 1)
        inside = (me >= start) & (me < start + size)
        clip = jnp.where(inside, at, clip)
        offset = jnp.where(inside, me - start, offset)
        is_big = jnp.where(inside, big, is_big)
        start = start + size
    return clip, offset, is_big


class Loads:
    def __init__(self, sems):
        self.sems, self.used = sems, 0

    def __call__(self, source, target):
        copy = pltpu.make_async_copy(source, target, self.sems.at[self.used])
        self.used += 1
        copy.start()
        return copy


def first_kernel(
    clip_big, actions, tok, action_table, gain, shift, wq, wk, wv, wo,
    normed_out, query_out, key_out, value_out, pair_out, mixed_out, probs_out, second_out, hot, table,
    held, normed, query, key, value, pair, mixed, probs, second, turned, staged, came,
    loads, pair_sems, swap_sends, swap_recvs,
):
    rows, width = tok.shape
    clip, offset, is_big = where_am_i(clip_big)
    grid = Grid()
    swap = Swap(True, offset, is_big, turned, staged, came, (swap_sends, swap_recvs), 2)
    barrier = pltpu.get_barrier_semaphore()
    pl.semaphore_signal(barrier, inc=1, device_id=grid.other(), device_id_type=MESH)
    peers = 1 + swap.greet(barrier)
    load = Loads(loads)
    weights = [load(source, held.at[at]) for at, source in enumerate((wk, wv, wq, wo))]

    last = actions.shape[0] - 1
    base = clip * FRAMES + offset * (FRAMES // (REACH + 1))
    row = lax.broadcasted_iota(jnp.int32, (rows, WIDE), 0)
    frame_of = jnp.where(jnp.full((rows, WIDE), is_big, jnp.int32) == 1, row // WIDE, row // 32)
    action = jnp.zeros((rows, WIDE), jnp.int32)
    for frame in range(FRAMES):
        action = jnp.where(frame_of == frame, actions[jnp.minimum(base + frame, last)], action)
    lane = lax.broadcasted_iota(jnp.int32, (rows, WIDE), 1)
    hot[...] = jnp.where((action == lax.rem(lane, 8)) & (lane < 24), 1.0, 0.0).astype(BF16)
    exact = action_table[...]
    high = exact.astype(BF16)
    left = exact - high.astype(F32)
    middle = left.astype(BF16)
    low = left - middle.astype(F32)
    table[...] = jnp.concatenate(
        [high.astype(F32), middle.astype(F32), low, jnp.zeros((WIDE - 24, width), F32)], axis=0
    ).astype(BF16)

    def norm_rows(at, _):
        here = pl.ds(pl.multiple_of(at * 128, 128), 128)
        hat, _rate = normalise(tok[here, :].astype(F32) + dot(hot[here, :], table[...]))
        normed[here, :] = (hat * gain[...] + shift[...]).astype(BF16)
        return 0

    lax.fori_loop(0, rows // 128, norm_rows, 0)
    outs = [load(normed, normed_out)]
    across = []
    for at, (target, out) in enumerate(((key, key_out), (value, value_out), (query, query_out))):
        weights[at].wait()
        for part in range(4):
            side = pl.ds(part * 256, 256)
            target[:, side] = dot(normed[...], held[at, :, side]).astype(BF16)
        if at == 0:
            pl.semaphore_wait(barrier, peers)
        if at < 2:
            copy = remote(
                target, pair.at[at], pair_sems.at[0, at], pair_sems.at[1, at], grid.other()
            )
            copy.start()
            across.append(copy)
        outs.append(load(target, out))
    for copy in across:
        copy.wait()
    outs.append(load(pair, pair_out))
    weights[3].wait()
    bias = spatial_bias(is_big, 2 * WIDE)

    def group(at, _):
        here = pl.ds(pl.multiple_of(at * WIDE, WIDE), WIDE)
        for two in range(8):
            side = pl.ds(two * WIDE, WIDE)
            keys = jnp.concatenate([key[here, side], pair[0, here, side]], axis=0)
            values = jnp.concatenate([value[here, side], pair[1, here, side]], axis=0)
            prob, out = attend(query[here, side], keys, values, bias)
            probs[at, two] = prob
            mixed[here, side] = out.astype(BF16)
        return 0

    for half in range(2):
        lax.fori_loop(2 * half, 2 * half + 2, group, 0)
        here = slice(half * KEYS, (half + 1) * KEYS)
        blocks = slice(half * 16, (half + 1) * 16)
        for part in range(4):
            side = slice(part * 256, (part + 1) * 256)
            first = tok[here, side].astype(F32) + dot(hot[here, :], table[:, side])
            total = first + dot(mixed[here, :], held[3, :, side])
            turned[blocks, :, side] = total.astype(BF16).reshape(16, 16, 256)
        swap.send(half)
    outs += [load(mixed, mixed_out), load(probs, probs_out)]
    swap.wait()
    swap.place(second)
    outs.append(load(second, second_out))
    for copy in outs:
        copy.wait()


def first(clip_big, actions, tok, action_table, gain, shift, wq, wk, wv, wo, number):
    rows, width = tok.shape
    wide = shape_of((rows, width), BF16)
    probs = (rows // WIDE, 8, 2 * WIDE, KEYS)
    dma = pltpu.SemaphoreType.DMA
    full = pltpu.VMEM((rows, width), BF16)
    return pl.pallas_call(
        first_kernel,
        out_shape=[
            wide, wide, wide, wide, shape_of((2, rows, width), BF16), wide, shape_of(probs, BF16), wide,
            shape_of((rows, WIDE), BF16), shape_of((WIDE, width), BF16),
        ],
        in_specs=[IN_SMEM] * 2 + [WHOLE] * 4 + [IN_HBM] * 4,
        out_specs=[IN_HBM] * 8 + [WHOLE] * 2,
        scratch_shapes=[
            pltpu.VMEM((4, width, width), BF16), full, full, full, full,
            pltpu.VMEM((2, rows, width), BF16), full, pltpu.VMEM(probs, BF16), full,
            pltpu.VMEM((rows // 16, 16, width), BF16),
            pltpu.VMEM((7, 128, width), BF16),
            pltpu.VMEM((7, 128, width), BF16),
            dma((16,)), dma((2, 2)), dma((14,)), dma((14,)),
        ],
        compiler_params=params(collective_id=number, has_side_effects=True),
    )(clip_big, actions, tok, action_table, gain, shift, wq, wk, wv, wo)


def middle_kernel(
    clip_big, second, cot_in, gain_two, shift_two, gain, shift, bias_in, bias_out, wq, wk, wv, wo, win, wout,
    normed_out, query_out, key_out, value_out, probs_out, mixed_two_out, mixed_out, third_out,
    d_in, came_in, d_out, came_out, small,
    pool, probs, held, w_in, w_out, active, slope, third, normed_t, cot_t, turned,
    staged, came_cot, came_mixed, outgoing,
    loads, cot_sends, cot_recvs, mixed_sends, mixed_recvs, out_sems, grad_recvs, prob_sems,
):
    rows, width = third.shape
    hidden = w_in.shape[1]
    chunks = hidden // CHUNK
    _clip, offset, is_big = where_am_i(clip_big)
    cot_swap = Swap(True, offset, is_big, turned, staged, came_cot, (cot_sends, cot_recvs))
    mixed_swap = Swap(False, offset, is_big, turned, staged, came_mixed, (mixed_sends, mixed_recvs))
    barrier = pltpu.get_barrier_semaphore()
    tile = lax.axis_index("tile")
    other = (lax.axis_index("seq"), 1 - tile)
    pl.semaphore_signal(barrier, inc=1, device_id=other, device_id_type=MESH)
    peers = 1 + cot_swap.greet(barrier)
    load = Loads(loads)
    cot_load = load(cot_in, turned)
    second_load = load(second, pool.at[0])
    weights = [load(source, held.at[at]) for at, source in enumerate((wq, wk, wv, wo))]
    weights += [load(win, w_in), load(wout, w_out)]
    cot_load.wait()
    pl.semaphore_wait(barrier, peers)
    cot_swap.send()
    second_load.wait()

    def norm_two(at, _):
        here = pl.ds(pl.multiple_of(at * 128, 128), 128)
        hat, _rate = normalise(pool[0, here, :].astype(F32))
        pool[4, here, :] = (hat * gain_two[...] + shift_two[...]).astype(BF16)
        return 0

    lax.fori_loop(0, rows // 128, norm_two, 0)
    outs = [load(pool.at[4], normed_out)]
    for at, out in enumerate((query_out, key_out, value_out)):
        weights[at].wait()
        for part in range(4):
            side = slice(part * 256, (part + 1) * 256)
            pool[1 + at, :, side] = dot(pool[4], held[at, :, side]).astype(BF16)
        outs.append(load(pool.at[1 + at], out))
    bias = temporal_bias(2 * KEYS)

    def probs_copy(at):
        return pltpu.make_async_copy(probs, probs_out.at[at], prob_sems.at[at])

    def group(at, _):
        @pl.when(at > 0)
        def _():
            probs_copy(0).wait()

        here = pl.ds(pl.multiple_of(at * KEYS, KEYS), KEYS)
        for two in range(8):
            side = pl.ds(two * WIDE, WIDE)
            prob, out = attend(pool[1, here, side], pool[2, here, side], pool[3, here, side], bias)
            probs[two] = prob
            pool[5, here, side] = out.astype(BF16)
        probs_copy(at).start()
        return 0

    lax.fori_loop(0, rows // KEYS, group, 0)
    outs += [load(pool.at[5], mixed_two_out)]
    weights[3].wait()
    for part in range(4):
        side = slice(part * 256, (part + 1) * 256)
        third[:, side] = pool[0, :, side].astype(F32) + dot(pool[5], held[3, :, side])
    outs[0].wait()

    def norm_three(at, _):
        here = pl.ds(pl.multiple_of(at * 128, 128), 128)
        hat, _rate = normalise(third[here, :])
        pool[4, here, :] = (hat * gain[...] + shift[...]).astype(BF16)
        return 0

    lax.fori_loop(0, rows // 128, norm_three, 0)
    normed_t[...] = pool[4].T
    weights[4].wait()

    def forward(at, _):
        side = pl.ds(pl.multiple_of(at * KEYS, KEYS), KEYS)
        inner = dot(pool[4], w_in[:, side]) + bias_in[:, side]
        square = inner * inner
        curve = jnp.tanh(ROOT * (inner + 0.044715 * inner * square))
        active[:, side] = (0.5 * inner * (1.0 + curve)).astype(BF16)
        slope[:, side] = (
            0.5 * (1.0 + curve)
            + (0.5 * ROOT) * inner * (1.0 - curve * curve) * (1.0 + (3 * 0.044715) * square)
        ).astype(BF16)
        return 0

    lax.fori_loop(0, hidden // KEYS, forward, 0)
    cot_swap.wait()
    cot_swap.place(pool.at[0])
    weights[5].wait()

    for part in range(width // KEYS):
        side = slice(part * KEYS, (part + 1) * KEYS)
        total = third[:, side] + bias_out[:, side] + dot(active[...], w_out[:, side])
        turned[:, :, side] = total.astype(BF16).reshape(rows // 16, 16, KEYS)
    mixed_swap.send()
    cot_t[...] = pool[0].T
    small[2:3, :] = jnp.sum(pool[0].astype(F32), axis=0, keepdims=True)

    def out_copy(at, slot, away):
        share = outgoing.shape[2]
        where = (slice(None), pl.ds(lax.rem(at, 4) * share, share))
        source = outgoing.at[slot]
        if away:
            return remote(
                source, came_out.at[where], out_sems.at[slot, 0], grad_recvs.at[lax.rem(at, 4), 0], other
            )
        return pltpu.make_async_copy(source, d_out.at[where], out_sems.at[slot, 0])

    def in_copy(at, slot, part, away):
        which = 1 - tile if away else tile
        source = outgoing.at[2 + slot, pl.ds((which * 2 + part) * 4, 4)]
        if away:
            return remote(
                source, came_in.at[at * 2 + part], out_sems.at[slot, 1 + part],
                grad_recvs.at[at, 1 + part], other,
            )
        return pltpu.make_async_copy(source, d_in.at[at * 2 + part], out_sems.at[slot, 3 + part])

    def start_out(at, slot):
        @pl.when(at // 4 == tile)
        def _():
            out_copy(at, slot, False).start()

        @pl.when(at // 4 != tile)
        def _():
            out_copy(at, slot, True).start()

        for part in range(2):
            in_copy(at, slot, part, False).start()
            in_copy(at, slot, part, True).start()

    def sent_out(at, slot):
        @pl.when(at // 4 == tile)
        def _():
            out_copy(at, slot, False).wait()

        @pl.when(at // 4 != tile)
        def _():
            out_copy(at, slot, True).wait_send()

        for part in range(2):
            in_copy(at, slot, part, False).wait()
            in_copy(at, slot, part, True).wait_send()

    def backward(at, _):
        slot = lax.rem(at, 2)

        @pl.when(at >= 2)
        def _():
            sent_out(at - 2, slot)

        side = pl.ds(pl.multiple_of(at * CHUNK, CHUNK), CHUNK)
        wide = slope[:, side].astype(F32) * dot_nt(pool[0], w_out[side, :])
        grad_inner = wide.astype(BF16)
        slope[:, side] = grad_inner
        lanes = pl.ds(pl.multiple_of(lax.rem(at, 2) * CHUNK, CHUNK), CHUNK)
        small[pl.ds(3 + at // 2, 1), lanes] = jnp.sum(grad_inner.astype(F32), axis=0, keepdims=True)
        outgoing[slot] = dot(cot_t[...], active[:, side]).astype(BF16).reshape(outgoing.shape[1:])
        for top in range(4):
            block = dot(normed_t[top * 256 : (top + 1) * 256, :], grad_inner).astype(BF16)
            for part in range(2):
                first = ((top // 2) * 2 + part) * 4
                outgoing[
                    2 + slot, first : first + 4, :, (top % 2) * KEYS : (top % 2 + 1) * KEYS
                ] = block[:, part * KEYS : (part + 1) * KEYS].reshape(4, 64, KEYS)
        start_out(at, slot)
        return 0

    lax.fori_loop(0, chunks, backward, 0)
    for copy in outs[1:]:
        copy.wait()
    probs_copy(1).wait()

    def back_rows(step, carry):
        here = pl.ds(pl.multiple_of(step * KEYS, KEYS), KEYS)
        hat, rate = normalise(third[here, :])
        grad = dot_nt(slope[here, :], w_in[...])
        pool[2, here, :] = (
            pool[0, here, :].astype(F32) + norm_backward(grad, hat, rate, gain[...])
        ).astype(BF16)
        return (
            carry[0] + jnp.sum(grad * hat, axis=0, keepdims=True),
            carry[1] + jnp.sum(grad, axis=0, keepdims=True),
        )

    zero = jnp.zeros((1, width), F32)
    sums = lax.fori_loop(0, rows // KEYS, back_rows, (zero, zero))
    small[0:1, :] = sums[0]
    small[1:2, :] = sums[1]
    small[7:8, :] = zero
    last = [load(pool.at[2], third_out)]
    mixed_swap.wait()
    mixed_swap.place(pool.at[1])
    last.append(load(pool.at[1], mixed_out))
    for at in (chunks - 2, chunks - 1):
        sent_out(at, at % 2)
    for at in range(chunks):
        if at < 4:
            out_copy(at, 0, True).wait_recv()
        for part in range(2):
            in_copy(at, 0, part, True).wait_recv()
    for copy in last:
        copy.wait()


def middle(args, number):
    clip_big, second, cot = args[:3]
    win = args[13]
    rows, width = second.shape
    hidden = win.shape[1]
    wide = shape_of((rows, width), BF16)
    probs = (rows // KEYS, 8, 2 * KEYS, KEYS)
    dma = pltpu.SemaphoreType.DMA
    block = pltpu.VMEM((7, 128, width), BF16)
    args = list(args)
    args[2] = cot.reshape(rows // 16, 16, width)
    return pl.pallas_call(
        middle_kernel,
        out_shape=[
            wide, wide, wide, wide, shape_of(probs, BF16), wide, wide, wide,
            *[shape_of((hidden // KEYS, 4, 64, 2 * KEYS), BF16)] * 2,
            *[shape_of((16, KEYS, CHUNK), BF16)] * 2,
            shape_of((8, width), F32),
        ],
        in_specs=[IN_SMEM, IN_HBM, IN_HBM] + [WHOLE] * 6 + [IN_HBM] * 6,
        out_specs=[IN_HBM] * 12 + [WHOLE],
        scratch_shapes=[
            pltpu.VMEM((6, rows, width), BF16),
            pltpu.VMEM(probs[1:], BF16),
            pltpu.VMEM((4, width, width), BF16),
            pltpu.VMEM((width, hidden), BF16),
            pltpu.VMEM((hidden, width), BF16),
            pltpu.VMEM((rows, hidden), BF16),
            pltpu.VMEM((rows, hidden), BF16),
            pltpu.VMEM((rows, width), F32),
            pltpu.VMEM((width, rows), BF16),
            pltpu.VMEM((width, rows), BF16),
            pltpu.VMEM((rows // 16, 16, width), BF16),
            block, block, block,
            pltpu.VMEM((4, 16, 64, CHUNK), BF16),
            dma((24,)), dma((7,)), dma((7,)), dma((7,)), dma((7,)), dma((2, 5)), dma((8, 3)), dma((2,)),
        ],
        compiler_params=params(collective_id=number, has_side_effects=True),
    )(*args)


def on_device(
    tokens,
    cotangent,
    clip_big,
    actions,
    action_table,
    norm_gain,
    norm_bias,
    spatial_q,
    spatial_k,
    spatial_v,
    spatial_o,
    temporal_q,
    temporal_k,
    temporal_v,
    temporal_o,
    ffn_in,
    ffn_bias_in,
    ffn_out,
    ffn_bias_out,
):
    tok = tokens[0]
    rows, width = tok.shape
    me = lax.axis_index("seq")
    count = lax.axis_size("seq")
    gains = [norm_gain[at : at + 1] for at in range(3)]
    shifts = [norm_bias[at : at + 1] for at in range(3)]

    normed_one, query_one, key_one, value_one, pair_one, mixed_one, probs_one, second, hot, table = first(
        clip_big, actions, tok, action_table, gains[0], shifts[0],
        spatial_q, spatial_k, spatial_v, spatial_o, 1,
    )
    (normed_two, query_two, key_two, value_two, probs_two, mixed_two, mixed, grad_third, d_in, came_in,
     d_out, came_out, small_ffn) = middle(
        [
            clip_big, second, cotangent[0], gains[1], shifts[1], gains[2], shifts[2],
            ffn_bias_in, ffn_bias_out, temporal_q, temporal_k, temporal_v, temporal_o, ffn_in, ffn_out,
        ],
        2,
    )
    part = width // count
    finer = count // d_in.shape[0]

    def in_blocks(grads):
        if finer > 1:
            grads = grads.reshape(-1, KEYS, 2, finer, KEYS // finer).transpose(0, 3, 1, 2, 4)
        return grads.reshape(count, 4 * part, CHUNK)

    def out_blocks(grads):
        if finer > 1:
            grads = grads.reshape(-1, 4, finer, part, CHUNK).transpose(0, 2, 1, 3, 4)
        return grads.reshape(count, 4 * part, CHUNK)

    d_in, came_in, d_out, came_out = in_blocks(d_in), in_blocks(came_in), out_blocks(d_out), out_blocks(came_out)
    pieces = ffn_in.shape[1] // width
    token_grad, sum_out, sum_in, sum_temporal, sum_spatial, small = back(
        [
            clip_big, d_out, came_out, d_in, came_in, grad_third, second, mixed_two, query_two, key_two, value_two,
            normed_two, probs_two, temporal_q, temporal_k, temporal_v, temporal_o, mixed_one,
            query_one, key_one, value_one, pair_one, normed_one, probs_one, spatial_q, spatial_k,
            spatial_v, spatial_o, tok, hot, table, gains[0], gains[1], small_ffn,
        ],
        5,
    )
    hidden = ffn_in.shape[1]
    ffn_in_grad = (
        sum_in.reshape(2, KEYS, 2, hidden // count).transpose(0, 2, 1, 3).reshape(width, -1).astype(F32)
    )
    ffn_out_grad = (
        sum_out.reshape(2, 4, part, CHUNK).transpose(0, 1, 3, 2).reshape(hidden, part).astype(F32)
    )

    def finish(summed):
        joined = summed.reshape(2, 4, part, width // 2).transpose(0, 3, 1, 2).astype(F32)
        joined = joined.reshape(width, 4, part)
        return [joined[:, at] for at in range(4)]

    temporal_o_grad, temporal_q_grad, temporal_k_grad, temporal_v_grad = finish(sum_temporal)
    spatial_o_grad, spatial_q_grad, spatial_k_grad, spatial_v_grad = finish(sum_spatial)

    def mine(values):
        return lax.dynamic_slice_in_dim(values, me * part, part, 1)

    bias_in = small[19 : 19 + pieces].reshape(1, hidden)
    bias_in = lax.dynamic_slice_in_dim(bias_in, me * (hidden // count), hidden // count, 1)
    return (
        mixed[None],
        token_grad[None],
        mine(small[0:8]),
        mine(jnp.concatenate([small[8:10], small[16:17]], axis=0)),
        mine(jnp.concatenate([small[10:12], small[17:18]], axis=0)),
        spatial_q_grad,
        spatial_k_grad,
        spatial_v_grad,
        spatial_o_grad,
        temporal_q_grad,
        temporal_k_grad,
        temporal_v_grad,
        temporal_o_grad,
        ffn_in_grad,
        bias_in,
        ffn_out_grad,
        mine(small[18:19]),
    )


def solution(mesh):
    placed = (P("tile", "seq", None),) * 2 + (P(),) * 17
    return jax.shard_map(
        on_device,
        mesh=mesh,
        in_specs=placed,
        out_specs=(P("tile", "seq", None),) * 2 + (P(None, "seq"),) * 15,
        check_vma=False,
    )
```

```python
import functools

import jax
import jax.numpy as jnp
from jax import lax
from jax.experimental import pallas as pl
from jax.experimental.pallas import tpu as pltpu
from jax.sharding import PartitionSpec as P

HEAD_DIM = 64
FRAMES = 16
GRID_BIG = 16
GRID_SMALL = 8
WIDE = 128
KEYS = 256
CHUNK = 512
VMEM_BYTES = 62 * 2**20
FACTOR = HEAD_DIM**-0.5
ROOT = (2.0 / 3.141592653589793) ** 0.5

F32 = jnp.float32
BF16 = jnp.bfloat16
WHOLE = pl.BlockSpec(memory_space=pltpu.VMEM)
IN_HBM = pl.BlockSpec(memory_space=pl.ANY)
MESH = pl.DeviceIdType.MESH
IN_SMEM = pl.BlockSpec(memory_space=pltpu.SMEM)


def shape_of(dims, kind):
    return jax.ShapeDtypeStruct(dims, kind)


def params(**more):
    return pltpu.CompilerParams(vmem_limit_bytes=VMEM_BYTES, **more)


def dot(left, right):
    return jnp.dot(left, right, preferred_element_type=F32)


def dot_nt(left, right):
    return lax.dot_general(left, right, (((1,), (1,)), ((), ())), preferred_element_type=F32)


def dot_tn(left, right):
    return lax.dot_general(left, right, (((0,), (0,)), ((), ())), preferred_element_type=F32)


def normalise(values):
    centre = values - jnp.mean(values, axis=-1, keepdims=True)
    rate = lax.rsqrt(jnp.mean(centre * centre, axis=-1, keepdims=True) + 1e-05)
    return centre * rate, rate


def norm_backward(grad, hat, rate, gain):
    inner = grad * gain
    level = jnp.mean(inner, axis=-1, keepdims=True)
    slope = jnp.mean(inner * hat, axis=-1, keepdims=True)
    return rate * (inner - level - hat * slope)


def head_halves(block):
    lane = lax.broadcasted_iota(jnp.int32, block.shape, 1)
    zero = jnp.zeros_like(block)
    first = lane < HEAD_DIM
    return jnp.concatenate([jnp.where(first, block, zero), jnp.where(first, zero, block)], axis=0)


def join_halves(both):
    rows = both.shape[0] // 2
    lane = lax.broadcasted_iota(jnp.int32, (rows, both.shape[1]), 1)
    return jnp.where(lane < HEAD_DIM, both[:rows], both[rows:])


def attend(query, key, value, bias):
    scores = dot_nt(head_halves(query) * FACTOR, key) + bias
    top = jnp.max(scores, axis=1, keepdims=True)
    powers = jnp.exp(scores - top)
    prob = (powers * (1.0 / jnp.sum(powers, axis=1, keepdims=True))).astype(BF16)
    return prob, join_halves(dot(prob, value))


def attend_backward(prob, query, key, value, grad):
    grad_two = head_halves(grad)
    grad_prob = dot_nt(grad_two, value)
    prob_f = prob.astype(F32)
    delta = jnp.sum(prob_f * grad_prob, axis=1, keepdims=True)
    grad_score = (prob_f * (grad_prob - delta)).astype(BF16)
    grad_query = join_halves(dot(grad_score, key)) * FACTOR
    grad_key = dot_tn(grad_score, head_halves(query)) * FACTOR
    grad_value = dot_tn(prob, grad_two)
    return grad_query, grad_key, grad_value


def spatial_bias(is_big, rows):
    row = lax.broadcasted_iota(jnp.int32, (rows, KEYS), 0)
    column = lax.broadcasted_iota(jnp.int32, (rows, KEYS), 1)
    same = lax.rem(row, WIDE) // 32 == lax.rem(column, WIDE) // 32
    return jnp.where(same | (is_big == 1), 0.0, -1e30).astype(F32)


def temporal_bias(rows):
    row = lax.rem(lax.broadcasted_iota(jnp.int32, (rows, KEYS), 0), KEYS)
    column = lax.broadcasted_iota(jnp.int32, (rows, KEYS), 1)
    fits = (lax.rem(row, 16) == lax.rem(column, 16)) & (column <= row)
    return jnp.where(fits, 0.0, -1e30).astype(F32)


def weight_grad(target, at, grad, normed):
    grad_t = grad.T
    count, _rows, width = target.shape[1:]
    part = grad_t.shape[0] // count
    for which in range(2):
        block = dot(grad_t, normed[:, which * width : (which + 1) * width]).astype(BF16)
        target[which, :, at * part : (at + 1) * part, :] = block.reshape(count, part, width)


REACH = 3
STEPS = tuple(step for step in range(REACH, -REACH - 1, -1) if step != 0)


class Swap:
    def __init__(self, to_time, offset, is_big, source, staged, came, sems, parts=1):
        self.me, self.tile = lax.axis_index("seq"), lax.axis_index("tile")
        self.count = lax.axis_size("seq")
        self.to_time, self.offset, self.is_big = to_time, offset, is_big
        self.source, self.staged, self.came, self.sems = source, staged, came, sems
        self.parts = parts

    def peer(self, step):
        return (self.me + step, self.tile)

    def present(self, step):
        return (self.me + step >= 0) & (self.me + step < self.count)

    def greet(self, barrier):
        for step in STEPS:
            @pl.when(self.present(step))
            def _(step=step):
                pl.semaphore_signal(
                    barrier, inc=1, device_id=self.peer(step), device_id_type=MESH
                )
        return jnp.minimum(self.me, REACH) + jnp.minimum(self.count - 1 - self.me, REACH)

    def copy(self, step, part):
        slot, sem = REACH - step, (REACH - step) * self.parts + part
        source, target = self.staged.at[slot], self.came.at[slot]
        if self.parts > 1:
            rows = pl.ds(part * (128 // self.parts), 128 // self.parts)
            source, target = source.at[rows], target.at[rows]
        return remote(source, target, self.sems[0].at[sem], self.sems[1].at[sem], self.peer(step))

    def stage(self, step, part):
        which = jnp.clip(self.offset + step, 0, REACH)
        target = self.came if step == 0 else self.staged
        slot = REACH - step
        if self.to_time:
            frames = 4 // self.parts
            for frame in range(part * frames, (part + 1) * frames):
                block = self.source[pl.ds(which * 2 + frame * 8, 2)]
                target[slot, frame * 32 : frame * 32 + 32] = block.reshape(32, block.shape[2])
            return
        sides = 2 // self.parts
        for side in range(part * sides, (part + 1) * sides):
            block = self.source[pl.ds(which * 4 + side * 16, 4)]
            target[slot, side * 64 : side * 64 + 64] = block.reshape(64, block.shape[2])

    def send(self, part=0):
        for step in STEPS:
            self.stage(step, part)

            @pl.when(self.present(step))
            def _(step=step):
                self.copy(step, part).start()

        self.stage(0, part)

    def wait(self):
        for part in range(self.parts):
            for step in STEPS:
                @pl.when(self.present(step))
                def _(step=step, part=part):
                    self.copy(step, part).wait_send()

                @pl.when(self.present(-step))
                def _(step=step, part=part):
                    self.copy(step, part).wait_recv()

    def place(self, target):
        width = target.shape[-1]
        chosen = jnp.full((16, width), self.is_big, jnp.int32) == 1
        for at in range(REACH + 1):
            slot = REACH - self.offset + at
            for side in range(2):
                for frame in range(4):
                    low = frame * 32 + side * 16 if self.to_time else side * 64 + frame * 16
                    moved = self.came[pl.ds(slot, 1), low : low + 16][0]
                    if self.to_time:
                        here, mine = side * 256 + at * 64 + frame * 16, at * 8 + frame * 2 + side
                    else:
                        here, mine = frame * 128 + at * 32 + side * 16, side * 16 + frame * 4 + at
                    target[here : here + 16] = jnp.where(chosen, moved, self.source[mine])


def seq_dims(count):
    return {16: (2, 2, 2, 2), 64: (4, 4, 4)}.get(count, (1, 1, count))


def seq_orders(count):
    if count == 16:
        names = {"xy": (3, 2, 1, 0), "yx": (2, 3, 1, 0), "xz": (3, 1, 2, 0)}
        return names | {"yz": (2, 1, 3, 0), "zx": (1, 3, 2, 0), "zy": (1, 2, 3, 0)}
    names = {"xy": (2, 1, 0), "yx": (1, 2, 0), "xz": (2, 0, 1)}
    return names | {"yz": (1, 0, 2), "zx": (0, 2, 1), "zy": (0, 1, 2)}


class Grid:
    def __init__(self):
        self.count = lax.axis_size("seq")
        self.dims = seq_dims(self.count)
        self.orders = seq_orders(self.count)
        self.axes = len(self.dims)
        self.me = lax.axis_index("seq")
        self.tile = lax.axis_index("tile")
        self.strides = [1]
        for size in self.dims[:0:-1]:
            self.strides.insert(0, self.strides[0] * size)
        self.places = [
            lax.rem(self.me // stride, size) for stride, size in zip(self.strides, self.dims)
        ]

    def along(self, axis, step):
        place = self.places[axis]
        there = lax.rem(place + step, self.dims[axis])
        return there, (self.me + (there - place) * self.strides[axis], self.tile)

    def other(self):
        return (self.me, 1 - self.tile)

    def peers(self, phase, order):
        if phase == 0:
            return [self.other()]
        axis = order[phase - 1]
        return [self.along(axis, step)[1] for step in range(1, self.dims[axis])]

    def greet(self, barrier):
        peers = [self.other()]
        for axis in range(self.axes):
            peers += [self.along(axis, step)[1] for step in range(1, self.dims[axis])]
        for peer in peers:
            pl.semaphore_signal(barrier, inc=1, device_id=peer, device_id_type=MESH)
        return len(peers)

    def split(self, flat, dims):
        where = []
        for size in dims[::-1]:
            where.insert(0, lax.rem(flat, size))
            flat = flat // size
        return tuple(where)


def remote(source, target, send_sem, recv_sem, device):
    return pltpu.make_async_remote_copy(
        src_ref=source,
        dst_ref=target,
        send_sem=send_sem,
        recv_sem=recv_sem,
        device_id=device,
        device_id_type=MESH,
    )


class Unit:
    def __init__(self, grid, order, rows, source, out, came, part, sems, free, number, reuse, again):
        self.grid, self.order = grid, order
        self.rows, self.part = rows, part
        self.away, self.own, self.fetched = source
        self.out, self.came = out, came
        self.sends, self.recvs = sems
        self.free, self.number, self.reuse, self.again = free, number, reuse, again
        self.last = grid.axes + 1

    def rest(self, phase):
        taken = self.order[:phase]
        return [axis for axis in range(self.grid.axes) if axis not in taken]

    def held(self, phase):
        lead = () if phase == 0 else (0,)
        return self.came[phase], lead

    def slab(self, phase, there):
        before = self.rest(phase - 1)
        where = [slice(None)] * len(before)
        where[before.index(self.order[phase - 1])] = there
        ref, lead = self.held(phase - 1)
        return ref.at[lead + tuple(where) + (self.part,)]

    def landing(self, phase, step):
        dims = len(self.rest(phase))
        return self.came[phase].at[(step,) + (slice(None),) * dims + (self.part,)]

    def copies(self, phase):
        number, grid = self.number, self.grid
        if phase == 0:
            if self.fetched is not None:
                return [pltpu.make_async_copy(self.fetched, self.start_of(), self.sends.at[number, 0, 0])]
            return [
                remote(
                    self.away, self.start_of(), self.sends.at[number, 0, 0],
                    self.recvs.at[number, 0, 0], grid.other(),
                )
            ]
        if phase == self.last:
            mine = self.out.at[grid.tile, self.rows]
            return [
                remote(
                    mine, mine, self.sends.at[number, phase, 0], self.recvs.at[number, phase, 0],
                    grid.other(),
                )
            ]
        axis = self.order[phase - 1]
        out = []
        for step in range(1, grid.dims[axis]):
            there, device = grid.along(axis, step)
            out.append(
                remote(
                    self.slab(phase, there), self.landing(phase, step - 1),
                    self.sends.at[number, phase, step - 1], self.recvs.at[number, phase, step - 1],
                    device,
                )
            )
        return out

    def start_of(self):
        return self.came[0].at[(slice(None),) * self.grid.axes + (self.part,)]

    def start(self, phase):
        if self.again and phase < self.last:
            amount = len(self.grid.peers(phase, self.order))
            pl.semaphore_wait(self.free.at[self.again - 1, phase], amount)
        for copy in self.copies(phase):
            copy.start()

    def release(self, phase):
        for number, order in self.reuse:
            for peer in self.grid.peers(phase, order):
                pl.semaphore_signal(
                    self.free.at[number, phase], inc=1, device_id=peer, device_id_type=MESH
                )

    def wait(self, phase):
        for copy in self.copies(phase):
            copy.wait()

    def turn(self, phase):
        self.wait(phase)
        grid = self.grid
        if phase == 0:
            def step(at, _):
                where = grid.split(at, grid.dims) + (self.part,)
                self.came[0][where] = self.came[0][where] + self.own(grid.split(at, grid.dims))
                return 0

            if self.fetched is None:
                lax.fori_loop(0, grid.count, step, 0)
                return
            self.own(None)
            for piece in range(4):
                base = piece * (grid.count // 4)
                self.own(piece)

                def step_kept(at, _, base=base):
                    where = grid.split(at + base, grid.dims) + (self.part,)
                    self.came[0][where] = self.came[0][where] + self.own(at)
                    return 0

                lax.fori_loop(0, grid.count // 4, step_kept, 0)
            return
        axis = self.order[phase - 1]
        own = self.slab(phase, grid.places[axis])
        size = grid.dims[axis]
        if phase == grid.axes:
            total = own[...].astype(F32)
            for at in range(size - 1):
                total = total + self.came[phase][at, self.part].astype(F32)
            self.out[grid.tile, self.rows] = total.astype(BF16)
            self.release(phase - 1)
            self.release(phase)
            return
        dims = tuple(grid.dims[axis] for axis in self.rest(phase))
        steps = 1
        for size_of in dims:
            steps *= size_of

        def step(at, _):
            where = grid.split(at, dims)
            total = own[where]
            for other in range(size - 1):
                total = total + self.came[phase][(other,) + where + (self.part,)]
            self.came[phase][(0,) + where + (self.part,)] = total
            return 0

        lax.fori_loop(0, steps, step, 0)
        self.release(phase - 1)

    def on(self, phase):
        if phase < self.last:
            self.turn(phase)
            self.start(phase + 1)


class Pair:
    def __init__(self, *units):
        self.units = units

    def __getattr__(self, name):
        def each(phase):
            for unit in self.units:
                getattr(unit, name)(phase)

        return each


class Total:
    def __init__(self, grid, value, came, sends, recvs):
        self.order = grid.orders["xy"]
        self.last = grid.axes
        self.grid, self.value, self.came, self.sends, self.recvs = grid, value, came, sends, recvs

    def copies(self, phase):
        first = sum(len(self.grid.peers(before, self.order)) for before in range(phase))
        return [
            remote(
                self.value, self.came.at[first + at], self.sends.at[first + at],
                self.recvs.at[first + at], peer,
            )
            for at, peer in enumerate(self.grid.peers(phase, self.order))
        ]

    def start(self, phase):
        for copy in self.copies(phase):
            copy.start()

    def on(self, phase):
        if phase > self.last:
            return
        copies = self.copies(phase)
        for copy in copies:
            copy.wait()
        total = self.value[...]
        first = sum(len(self.grid.peers(before, self.order)) for before in range(phase))
        for at in range(len(copies)):
            total = total + self.came[first + at]
        self.value[...] = total
        if phase < self.last:
            self.start(phase + 1)


def unit_scratch(rows, width, order, dims):
    left = list(range(len(dims)))
    out = [pltpu.VMEM(dims + (rows, width), BF16)]
    for axis in order:
        left.remove(axis)
        rest = tuple(dims[other] for other in left)
        out.append(pltpu.VMEM((max(dims[axis] - 1, 1),) + rest + (rows, width), BF16))
    return out


def back_kernel(
    clip_big, d_out, came_out, d_in, came_in, third, second, mixed_t, query_t, key_t, value_t, normed_t, probs_t,
    wq_t, wk_t, wv_t, wo_t, mixed_s, query_s, key_s, value_s, pair, normed_s, probs_s,
    wq_s, wk_s, wv_s, wo_s, tok, hot, table, gain_one, gain_two, small_ffn,
    token_grad, sum_out, sum_in, sum_time, sum_space, small,
    pool, turned, held, probs, d_weights, kept, came_key, came_value, swapped, *rest,
):
    grid = Grid()
    deep = grid.axes + 1
    unit_bufs, rest = rest[: 4 * deep], rest[4 * deep :]
    (totals, total_came, loads, unit_sends, unit_recvs, free, swap_sends, swap_recvs,
     total_sends, total_recvs, pair_sems) = rest
    rows, width = pool.shape[1:]
    _clip, offset, is_big = where_am_i(clip_big)
    swap = Swap(
        False, offset, is_big, turned, _Slots(pool, (11, 6)), swapped, (swap_sends, swap_recvs), 2
    )
    barrier = pltpu.get_barrier_semaphore()
    pl.semaphore_wait(barrier, grid.greet(barrier) + swap.greet(barrier))

    load = Loads(loads)
    orders = grid.orders
    share = d_out.shape[-2]
    every = (slice(None),) * grid.axes

    ways = (("xy", "yx"), ("zx", "zy"), ("xz", "yz", "xz", "yz"), ("yx", "xy", "xy", "yx"))
    ways = [[orders[name] for name in group] for group in ways]

    def buffers(group, which):
        first = (group % 2) * 2 * deep + which * deep
        return unit_bufs[first : first + deep]

    def fetched(group, which, keep, landed, out):
        half = share // 2
        rows_of = pl.ds(which * half, half)
        number = 2 * group + which
        first = (1, grid.dims[0] * grid.dims[1] // 4) if grid.dims[0] < 4 else (grid.dims[0] // 4, grid.dims[1])

        def own(at):
            if at is None:
                return None
            if isinstance(at, int):
                copy = pltpu.make_async_copy(
                    keep.at[
                        (
                            pl.ds(at * first[0] * first[1] // grid.dims[1], first[0]),
                            pl.ds(at * first[1] % grid.dims[1], first[1]),
                        )
                        + every[2:]
                        + (rows_of,)
                    ],
                    kept,
                    unit_sends.at[number, 0, 1],
                )
                copy.start()
                copy.wait()
                return None
            return kept[grid.split(at, first + grid.dims[2:])]

        reuse = [
            (4 * group + 2 * which + sub, ways[group + 2][2 * which + sub]) for sub in range(2)
        ]
        return Unit(
            grid, ways[group][which], rows_of, (None, own, landed.at[every + (rows_of,)]), out,
            buffers(group, which), pl.ds(0, half), (unit_sends, unit_recvs), free, number, reuse, 0,
        )

    def made(group, which, out):
        quarter = share // 4
        rows_of = pl.ds(which * quarter, quarter)

        def own(where):
            return d_weights[(grid.tile,) + where + (rows_of,)]

        return Unit(
            grid, ways[group][which], rows_of,
            (d_weights.at[(1 - grid.tile,) + every + (rows_of,)], own, None), out,
            buffers(group, which // 2), pl.ds((which % 2) * quarter, quarter),
            (unit_sends, unit_recvs), free, 4 + 4 * (group - 2) + which, [],
            4 * (group - 2) + which + 1,
        )

    p0 = Pair(*[fetched(0, which, d_out, came_out, sum_out) for which in range(2)])
    p1 = Pair(*[fetched(1, which, d_in, came_in, sum_in) for which in range(2)])
    p2 = Pair(*[made(2, which, sum_time) for which in range(4)])
    p3o, p3q, p3k, p3v = [made(3, which, sum_space) for which in range(4)]
    p0.start(0)
    p1.start(0)

    in_low = load(third, pool.at[0])
    in_mixed = load(mixed_t, pool.at[2])
    weights = [load(source, held.at[at]) for at, source in enumerate((wo_t, wq_t, wk_t, wv_t))]
    ins = [load(source, pool.at[3 + at]) for at, source in enumerate((query_t, key_t, value_t))]
    ins += [load(probs_t.at[at], probs.at[at]) for at in range(2)]
    late = [load(second, pool.at[1]), load(normed_t, pool.at[6])]
    p0.on(0)
    p1.on(0)
    in_low.wait()
    in_mixed.wait()
    flat_weights = d_weights.reshape((2, grid.count) + d_weights.shape[-2:])
    weight_grad(flat_weights, 0, pool[0], pool.at[2])
    weights[0].wait()

    def mix_back(grad, target):
        for part in range(4):
            side = slice(part * 256, (part + 1) * 256)
            pool[target, :, side] = dot_nt(pool[grad], held[0, side, :]).astype(BF16)

    mix_back(0, 7)
    weights.append(load(wo_s, held.at[0]))
    for copy in ins:
        copy.wait()

    def time_group(at, _):
        here = pl.ds(pl.multiple_of(at * KEYS, KEYS), KEYS)
        for two in range(8):
            side = pl.ds(two * WIDE, WIDE)
            grads = attend_backward(
                probs[at, two], pool[3, here, side], pool[4, here, side], pool[5, here, side],
                pool[7, here, side],
            )
            for target, grad in enumerate(grads):
                pool[8 + target, here, side] = grad.astype(BF16)
        return 0

    lax.fori_loop(0, rows // KEYS, time_group, 0)
    ins = [
        load(source, pool.at[target])
        for source, target in (
            (query_s, 2), (key_s, 3), (value_s, 4), (pair.at[0], 5), (pair.at[1], 7)
        )
    ]
    ins += [
        load(probs_s.at[at], probs.at[at // 2, :, pl.ds(at % 2 * 2 * WIDE, 2 * WIDE)])
        for at in range(4)
    ]
    for copy in late:
        copy.wait()
    for at in range(3):
        weight_grad(flat_weights, at + 1, pool[8 + at], pool.at[6])
    for at in range(3):
        weights[at + 1].wait()

    def time_rows(step, carry):
        here = pl.ds(pl.multiple_of(step * 256, 256), 256)
        grad = (
            dot_nt(pool[8, here, :], held[1])
            + dot_nt(pool[9, here, :], held[2])
            + dot_nt(pool[10, here, :], held[3])
        )
        hat, rate = normalise(pool[1, here, :].astype(F32))
        total = pool[0, here, :].astype(F32) + norm_backward(grad, hat, rate, gain_two[...])
        turned[pl.ds(step * 16, 16)] = total.astype(BF16).reshape(16, 16, width)
        return (
            carry[0] + jnp.sum(grad * hat, axis=0, keepdims=True),
            carry[1] + jnp.sum(grad, axis=0, keepdims=True),
        )

    zero = jnp.zeros((1, width), F32)
    time_norm = (zero, zero)
    for side in range(2):
        time_norm = time_rows(side, time_norm)
        swap.send(side)
    weights += [load(source, held.at[at + 1]) for at, source in enumerate((wq_s, wk_s, wv_s))]
    in_mixed = load(mixed_s, pool.at[10])
    p0.on(1)
    p2.start(0)
    p2.turn(0)
    swap.wait()
    swap.place(pool.at[1])
    in_normed = load(normed_s, pool.at[0])
    p1.on(1)
    p0.on(2)
    p2.start(1)

    in_mixed.wait()
    weight_grad(flat_weights, 0, pool[1], pool.at[10])
    weights[4].wait()
    mix_back(1, 8)
    p3o.start(0)
    for copy in ins:
        copy.wait()

    def space_group(at, _):
        here = pl.ds(pl.multiple_of(at * WIDE, WIDE), WIDE)
        lower = pl.ds(pl.multiple_of(lax.rem(at, 2) * 2 * WIDE, 2 * WIDE), 2 * WIDE)
        for two in range(8):
            side = pl.ds(two * WIDE, WIDE)
            keys = jnp.concatenate([pool[3, here, side], pool[5, here, side]], axis=0)
            values = jnp.concatenate([pool[4, here, side], pool[7, here, side]], axis=0)
            grad_query, grad_key, grad_value = attend_backward(
                probs[at // 2, two, lower], pool[2, here, side], keys, values, pool[8, here, side]
            )
            pool[9, here, side] = grad_query.astype(BF16)
            pool[10, here, side] = grad_key[:WIDE].astype(BF16)
            pool[11, here, side] = grad_value[:WIDE].astype(BF16)
            pool[6, here, side] = grad_key[WIDE:].astype(BF16)
            turned[pl.ds(at * 8, 8), :, side] = grad_value[WIDE:].astype(BF16).reshape(8, 16, WIDE)
        return 0

    lax.fori_loop(0, rows // (2 * WIDE), space_group, 0)
    p0.on(3)
    p1.on(2)
    p3o.on(0)
    lax.fori_loop(rows // (2 * WIDE), rows // WIDE, space_group, 0)
    across = [
        remote(
            source, target, pair_sems.at[0, at], pair_sems.at[1, at], grid.other(),
        )
        for at, (source, target) in enumerate(((pool.at[6], came_key), (turned, came_value)))
    ]
    for copy in across:
        copy.start()
    in_tok = load(tok, pool.at[2])
    in_normed.wait()
    weight_grad(flat_weights, 1, pool[9], pool.at[0])
    p3q.start(0)
    for at, copy in enumerate(across):
        copy.wait()
        came = (came_key, came_value)[at][...].reshape(rows, width)
        pool[10 + at] = pool[10 + at] + came
        weight_grad(flat_weights, 2 + at, pool[10 + at], pool.at[0])
        (p3k, p3v)[at].start(0)
    p3q.on(0)
    p3k.on(0)
    p3v.on(0)
    p2.on(1)
    p0.on(4)
    p1.on(3)
    for at in range(3):
        weights[5 + at].wait()
    in_tok.wait()

    def space_rows(step, carry):
        here = pl.ds(pl.multiple_of(step * 256, 256), 256)
        grad = (
            dot_nt(pool[9, here, :], held[1])
            + dot_nt(pool[10, here, :], held[2])
            + dot_nt(pool[11, here, :], held[3])
        )
        first = pool[2, here, :].astype(F32) + dot(hot[here, :], table[...])
        hat, rate = normalise(first)
        total = pool[1, here, :].astype(F32) + norm_backward(grad, hat, rate, gain_one[...])
        high = total.astype(BF16)
        pool[1, here, :] = high
        rest = (total - high.astype(F32)).astype(BF16)
        chosen = hot[here, :]
        return (
            carry[0] + jnp.sum(grad * hat, axis=0, keepdims=True),
            carry[1] + jnp.sum(grad, axis=0, keepdims=True),
            carry[2] + dot_tn(chosen, high)[:8] + dot_tn(chosen, rest)[:8],
        )

    p3o.on(1)
    space_norm = lax.fori_loop(0, rows // 256, space_rows, (zero, zero, jnp.zeros((8, width), F32)))
    out_grad = load(pool.at[1], token_grad)
    totals[0:8] = space_norm[2]
    totals[8:16] = jnp.concatenate(
        [space_norm[0], time_norm[0], space_norm[1], time_norm[1], jnp.zeros((4, width), F32)], axis=0
    )
    totals[16:24] = small_ffn[...]
    total = Total(grid, totals, total_came, total_sends, total_recvs)
    total.start(0)
    p2.on(2)
    p3q.on(1)
    p1.on(4)
    p3o.on(2)
    total.on(0)
    p3v.on(1)
    p3k.on(1)
    p2.on(3)
    p3q.on(2)
    total.on(1)
    p3o.on(3)
    p3v.on(2)
    p3k.on(2)
    p3q.on(3)
    total.on(2)
    p2.on(4)
    p3v.on(3)
    p3k.on(3)
    total.on(3)
    p3o.on(4)
    p3q.on(4)
    p3v.on(4)
    p3k.on(4)
    total.on(4)
    small[...] = totals[...]
    for unit in (p0, p1, p2, p3o, p3q, p3k, p3v):
        unit.wait(grid.axes + 1)
    out_grad.wait()


class _Slots:
    def __init__(self, pool, slots):
        self.pool, self.slots = pool, slots

    class _At:
        def __init__(self, slots):
            self.slots = slots

        def __getitem__(self, slot):
            return self.slots.pool.at[self.slots.slots[slot // 4], pl.ds(slot % 4 * 128, 128)]

    @property
    def at(self):
        return _Slots._At(self)

    def __setitem__(self, where, value):
        slot, rows = where
        first = slot % 4 * 128
        self.pool[self.slots[slot // 4], first + rows.start : first + rows.stop] = value


def back(args, number):
    args = list(args)
    rows, width = args[5].shape
    count = lax.axis_size("seq")
    dims = seq_dims(count)
    share, group = args[1].shape[-2:]
    dma = pltpu.SemaphoreType.DMA
    lead = (1, dims[0] * dims[1] // 4) if dims[0] < 4 else (dims[0] // 4, dims[1])
    scratch = [
        pltpu.VMEM((12, rows, width), BF16),
        pltpu.VMEM((rows // 16, 16, width), BF16),
        pltpu.VMEM((4, width, width), BF16),
        pltpu.VMEM((2, 8, 2 * KEYS, KEYS), BF16),
        pltpu.VMEM((2,) + dims + (share, group), BF16),
        pltpu.VMEM(lead + dims[2:] + (share // 2, group), BF16),
        pltpu.VMEM((rows, width), BF16),
        pltpu.VMEM((rows // 16, 16, width), BF16),
        pltpu.VMEM((7, 128, width), BF16),
    ]
    for _ in range(2):
        for name in ("xy", "yx"):
            scratch += unit_scratch(share // 2, group, seq_orders(count)[name], dims)
    most = max(max(dims) - 1, 2)
    peers = 1 + sum(dims) - len(dims)
    scratch += [
        pltpu.VMEM((24, width), F32),
        pltpu.VMEM((peers, 24, width), F32),
        dma((40,)),
        dma((12, len(dims) + 2, most)),
        dma((12, len(dims) + 2, most)),
        pltpu.SemaphoreType.REGULAR((8, len(dims) + 1)),
        dma((14,)),
        dma((14,)),
        dma((peers,)),
        dma((peers,)),
        dma((2, 2)),
    ]
    for at in range(1, 5):
        args[at] = args[at].reshape(dims + (share, group))
    final = shape_of((2, share, group), BF16)
    return pl.pallas_call(
        back_kernel,
        out_shape=[shape_of((rows, width), BF16)] + [final] * 4 + [shape_of((24, width), F32)],
        in_specs=[IN_SMEM] + [IN_HBM] * 28 + [WHOLE] * 5,
        out_specs=[IN_HBM] + [WHOLE] * 5,
        scratch_shapes=scratch,
        compiler_params=params(collective_id=number, has_side_effects=True),
    )(*args)


def finish_kernel(sum_out, sum_in, sum_time, sum_space, small, *refs):
    table, gain, shift, inner, outer, bias_in, bias_out = refs[:7]
    weights, rolled = refs[7:-1], refs[-1]
    count = lax.axis_size("seq")
    me = lax.axis_index("seq")
    width = small.shape[1]
    part = width // count
    hidden = bias_in.shape[1]
    for half in range(2):
        for at in range(4):
            rows = slice(at * part, (at + 1) * part)
            first = half * (width // 2)
            for base, source in ((0, sum_space), (4, sum_time)):
                weights[base + at][:, first : first + width // 2] = source[half, rows].astype(F32)
            first = (half * 4 + at) * CHUNK
            outer[:, first : first + CHUNK] = sum_out[half, rows].astype(F32)
        if inner.shape[1] == KEYS:
            for at in range(2):
                first = half * 2 * KEYS + at * KEYS
                inner[first : first + KEYS, :] = sum_in[half, :, at * KEYS : (at + 1) * KEYS].astype(F32)
    rolled[...] = pltpu.roll(small[...], lax.rem(width - me * part, width), 1)
    table[...] = rolled[0:8, :part]
    gain[...] = jnp.concatenate([rolled[8:10, :part], rolled[16:17, :part]], axis=0)
    shift[...] = jnp.concatenate([rolled[10:12, :part], rolled[17:18, :part]], axis=0)
    bias_out[...] = rolled[18:19, :part]
    begin = me * hidden
    rolled[...] = pltpu.roll(small[...], lax.rem(width - lax.rem(begin, width), width), 1)
    for at in range(4):
        @pl.when(begin // width == at)
        def _(at=at):
            bias_in[...] = rolled[19 + at : 20 + at, :hidden]


def finish(sums, small, hidden):
    count = lax.axis_size("seq")
    width = small.shape[1]
    part = width // count
    outs = [
        shape_of((8, part), F32), shape_of((3, part), F32), shape_of((3, part), F32),
        shape_of((width, hidden // count), F32), shape_of((part, hidden), F32),
        shape_of((1, hidden // count), F32), shape_of((1, part), F32),
    ]
    out = pl.pallas_call(
        finish_kernel,
        out_shape=outs + [shape_of((part, width), F32)] * 8,
        in_specs=[WHOLE] * 5,
        out_specs=[WHOLE] * 15,
        scratch_shapes=[pltpu.VMEM(small.shape, F32)],
        compiler_params=params(),
    )(*sums, small)
    out = list(out)
    out[4] = out[4].T
    out[7:] = [value.T for value in out[7:]]
    if hidden // count != KEYS:
        inner = sums[1].reshape(2, KEYS, 2, hidden // count).transpose(0, 2, 1, 3)
        out[3] = inner.reshape(width, -1).astype(F32)
    return out


def where_am_i(clip_big):
    me = lax.axis_index("seq")
    span = (GRID_BIG // GRID_SMALL) ** 2
    start, clip, offset, is_big = jnp.int32(0), jnp.int32(0), jnp.int32(0), jnp.int32(0)
    for at in range(clip_big.shape[0]):
        big = clip_big[at]
        size = jnp.where(big == 1, span, 1)
        inside = (me >= start) & (me < start + size)
        clip = jnp.where(inside, at, clip)
        offset = jnp.where(inside, me - start, offset)
        is_big = jnp.where(inside, big, is_big)
        start = start + size
    return clip, offset, is_big


class Loads:
    def __init__(self, sems):
        self.sems, self.used = sems, 0

    def __call__(self, source, target):
        copy = pltpu.make_async_copy(source, target, self.sems.at[self.used])
        self.used += 1
        copy.start()
        return copy


def first_kernel(
    clip_big, actions, tok, action_table, gain, shift, wq, wk, wv, wo,
    normed_out, query_out, key_out, value_out, pair_out, mixed_out, probs_out, second_out, hot, table,
    held, normed, query, key, value, pair, mixed, probs, second, turned, staged, came,
    loads, pair_sems, swap_sends, swap_recvs,
):
    rows, width = tok.shape
    clip, offset, is_big = where_am_i(clip_big)
    grid = Grid()
    swap = Swap(True, offset, is_big, turned, staged, came, (swap_sends, swap_recvs), 2)
    barrier = pltpu.get_barrier_semaphore()
    pl.semaphore_signal(barrier, inc=1, device_id=grid.other(), device_id_type=MESH)
    peers = 1 + swap.greet(barrier)
    load = Loads(loads)
    weights = [load(source, held.at[at]) for at, source in enumerate((wk, wv, wq, wo))]

    last = actions.shape[0] - 1
    base = clip * FRAMES + offset * (FRAMES // (REACH + 1))
    row = lax.broadcasted_iota(jnp.int32, (rows, WIDE), 0)
    frame_of = jnp.where(jnp.full((rows, WIDE), is_big, jnp.int32) == 1, row // WIDE, row // 32)
    action = jnp.zeros((rows, WIDE), jnp.int32)
    for frame in range(FRAMES):
        action = jnp.where(frame_of == frame, actions[jnp.minimum(base + frame, last)], action)
    lane = lax.broadcasted_iota(jnp.int32, (rows, WIDE), 1)
    hot[...] = jnp.where((action == lax.rem(lane, 8)) & (lane < 24), 1.0, 0.0).astype(BF16)
    exact = action_table[...]
    high = exact.astype(BF16)
    left = exact - high.astype(F32)
    middle = left.astype(BF16)
    low = left - middle.astype(F32)
    table[...] = jnp.concatenate(
        [high.astype(F32), middle.astype(F32), low, jnp.zeros((WIDE - 24, width), F32)], axis=0
    ).astype(BF16)

    def norm_rows(at, _):
        here = pl.ds(pl.multiple_of(at * 128, 128), 128)
        hat, _rate = normalise(tok[here, :].astype(F32) + dot(hot[here, :], table[...]))
        normed[here, :] = (hat * gain[...] + shift[...]).astype(BF16)
        return 0

    lax.fori_loop(0, rows // 128, norm_rows, 0)
    outs = [load(normed, normed_out)]
    across = []
    for at, (target, out) in enumerate(((key, key_out), (value, value_out), (query, query_out))):
        weights[at].wait()
        for part in range(4):
            side = pl.ds(part * 256, 256)
            target[:, side] = dot(normed[...], held[at, :, side]).astype(BF16)
        if at == 0:
            pl.semaphore_wait(barrier, peers)
        if at < 2:
            copy = remote(
                target, pair.at[at], pair_sems.at[0, at], pair_sems.at[1, at], grid.other()
            )
            copy.start()
            across.append(copy)
        outs.append(load(target, out))
    for copy in across:
        copy.wait()
    outs.append(load(pair, pair_out))
    weights[3].wait()
    bias = spatial_bias(is_big, 2 * WIDE)

    def group(at, _):
        here = pl.ds(pl.multiple_of(at * WIDE, WIDE), WIDE)
        for two in range(8):
            side = pl.ds(two * WIDE, WIDE)
            keys = jnp.concatenate([key[here, side], pair[0, here, side]], axis=0)
            values = jnp.concatenate([value[here, side], pair[1, here, side]], axis=0)
            prob, out = attend(query[here, side], keys, values, bias)
            probs[at, two] = prob
            mixed[here, side] = out.astype(BF16)
        return 0

    for half in range(2):
        lax.fori_loop(2 * half, 2 * half + 2, group, 0)
        here = slice(half * KEYS, (half + 1) * KEYS)
        blocks = slice(half * 16, (half + 1) * 16)
        for part in range(4):
            side = slice(part * 256, (part + 1) * 256)
            first = tok[here, side].astype(F32) + dot(hot[here, :], table[:, side])
            total = first + dot(mixed[here, :], held[3, :, side])
            turned[blocks, :, side] = total.astype(BF16).reshape(16, 16, 256)
        swap.send(half)
    outs += [load(mixed, mixed_out), load(probs, probs_out)]
    swap.wait()
    swap.place(second)
    outs.append(load(second, second_out))
    for copy in outs:
        copy.wait()


def first(clip_big, actions, tok, action_table, gain, shift, wq, wk, wv, wo, number):
    rows, width = tok.shape
    wide = shape_of((rows, width), BF16)
    probs = (rows // WIDE, 8, 2 * WIDE, KEYS)
    dma = pltpu.SemaphoreType.DMA
    full = pltpu.VMEM((rows, width), BF16)
    return pl.pallas_call(
        first_kernel,
        out_shape=[
            wide, wide, wide, wide, shape_of((2, rows, width), BF16), wide, shape_of(probs, BF16), wide,
            shape_of((rows, WIDE), BF16), shape_of((WIDE, width), BF16),
        ],
        in_specs=[IN_SMEM] * 2 + [WHOLE] * 4 + [IN_HBM] * 4,
        out_specs=[IN_HBM] * 8 + [WHOLE] * 2,
        scratch_shapes=[
            pltpu.VMEM((4, width, width), BF16), full, full, full, full,
            pltpu.VMEM((2, rows, width), BF16), full, pltpu.VMEM(probs, BF16), full,
            pltpu.VMEM((rows // 16, 16, width), BF16),
            pltpu.VMEM((7, 128, width), BF16),
            pltpu.VMEM((7, 128, width), BF16),
            dma((16,)), dma((2, 2)), dma((14,)), dma((14,)),
        ],
        compiler_params=params(collective_id=number, has_side_effects=True),
    )(clip_big, actions, tok, action_table, gain, shift, wq, wk, wv, wo)


def middle_kernel(
    clip_big, second, cot_in, gain_two, shift_two, gain, shift, bias_in, bias_out, wq, wk, wv, wo, win, wout,
    normed_out, query_out, key_out, value_out, probs_out, mixed_two_out, mixed_out, third_out,
    d_in, came_in, d_out, came_out, small,
    pool, probs, held, w_in, w_out, active, slope, third, normed_t, cot_t, turned,
    staged, came_cot, came_mixed, outgoing,
    loads, cot_sends, cot_recvs, mixed_sends, mixed_recvs, out_sems, grad_recvs, prob_sems,
):
    rows, width = third.shape
    hidden = w_in.shape[1]
    chunks = hidden // CHUNK
    _clip, offset, is_big = where_am_i(clip_big)
    cot_swap = Swap(True, offset, is_big, turned, staged, came_cot, (cot_sends, cot_recvs))
    mixed_swap = Swap(False, offset, is_big, turned, staged, came_mixed, (mixed_sends, mixed_recvs))
    barrier = pltpu.get_barrier_semaphore()
    tile = lax.axis_index("tile")
    other = (lax.axis_index("seq"), 1 - tile)
    pl.semaphore_signal(barrier, inc=1, device_id=other, device_id_type=MESH)
    peers = 1 + cot_swap.greet(barrier)
    load = Loads(loads)
    cot_load = load(cot_in, turned)
    second_load = load(second, pool.at[0])
    weights = [load(source, held.at[at]) for at, source in enumerate((wq, wk, wv, wo))]
    weights += [load(win, w_in), load(wout, w_out)]
    cot_load.wait()
    pl.semaphore_wait(barrier, peers)
    cot_swap.send()
    second_load.wait()

    def norm_two(at, _):
        here = pl.ds(pl.multiple_of(at * 128, 128), 128)
        hat, _rate = normalise(pool[0, here, :].astype(F32))
        pool[4, here, :] = (hat * gain_two[...] + shift_two[...]).astype(BF16)
        return 0

    lax.fori_loop(0, rows // 128, norm_two, 0)
    outs = [load(pool.at[4], normed_out)]
    for at, out in enumerate((query_out, key_out, value_out)):
        weights[at].wait()
        for part in range(4):
            side = slice(part * 256, (part + 1) * 256)
            pool[1 + at, :, side] = dot(pool[4], held[at, :, side]).astype(BF16)
        outs.append(load(pool.at[1 + at], out))
    bias = temporal_bias(2 * KEYS)

    def probs_copy(at):
        return pltpu.make_async_copy(probs, probs_out.at[at], prob_sems.at[at])

    def group(at, _):
        @pl.when(at > 0)
        def _():
            probs_copy(0).wait()

        here = pl.ds(pl.multiple_of(at * KEYS, KEYS), KEYS)
        for two in range(8):
            side = pl.ds(two * WIDE, WIDE)
            prob, out = attend(pool[1, here, side], pool[2, here, side], pool[3, here, side], bias)
            probs[two] = prob
            pool[5, here, side] = out.astype(BF16)
        probs_copy(at).start()
        return 0

    lax.fori_loop(0, rows // KEYS, group, 0)
    outs += [load(pool.at[5], mixed_two_out)]
    weights[3].wait()
    for part in range(4):
        side = slice(part * 256, (part + 1) * 256)
        third[:, side] = pool[0, :, side].astype(F32) + dot(pool[5], held[3, :, side])
    outs[0].wait()

    def norm_three(at, _):
        here = pl.ds(pl.multiple_of(at * 128, 128), 128)
        hat, _rate = normalise(third[here, :])
        pool[4, here, :] = (hat * gain[...] + shift[...]).astype(BF16)
        return 0

    lax.fori_loop(0, rows // 128, norm_three, 0)
    normed_t[...] = pool[4].T
    weights[4].wait()

    def forward(at, _):
        side = pl.ds(pl.multiple_of(at * KEYS, KEYS), KEYS)
        inner = dot(pool[4], w_in[:, side]) + bias_in[:, side]
        square = inner * inner
        curve = jnp.tanh(ROOT * (inner + 0.044715 * inner * square))
        active[:, side] = (0.5 * inner * (1.0 + curve)).astype(BF16)
        slope[:, side] = (
            0.5 * (1.0 + curve)
            + (0.5 * ROOT) * inner * (1.0 - curve * curve) * (1.0 + (3 * 0.044715) * square)
        ).astype(BF16)
        return 0

    lax.fori_loop(0, hidden // KEYS, forward, 0)
    cot_swap.wait()
    cot_swap.place(pool.at[0])
    weights[5].wait()

    for part in range(width // KEYS):
        side = slice(part * KEYS, (part + 1) * KEYS)
        total = third[:, side] + bias_out[:, side] + dot(active[...], w_out[:, side])
        turned[:, :, side] = total.astype(BF16).reshape(rows // 16, 16, KEYS)
    mixed_swap.send()
    cot_t[...] = pool[0].T
    small[2:3, :] = jnp.sum(pool[0].astype(F32), axis=0, keepdims=True)

    def out_copy(at, slot, away):
        share = outgoing.shape[2]
        where = (slice(None), pl.ds(lax.rem(at, 4) * share, share))
        source = outgoing.at[slot]
        if away:
            return remote(
                source, came_out.at[where], out_sems.at[slot, 0], grad_recvs.at[lax.rem(at, 4), 0], other
            )
        return pltpu.make_async_copy(source, d_out.at[where], out_sems.at[slot, 0])

    def in_copy(at, slot, part, away):
        which = 1 - tile if away else tile
        source = outgoing.at[2 + slot, pl.ds((which * 2 + part) * 4, 4)]
        if away:
            return remote(
                source, came_in.at[at * 2 + part], out_sems.at[slot, 1 + part],
                grad_recvs.at[at, 1 + part], other,
            )
        return pltpu.make_async_copy(source, d_in.at[at * 2 + part], out_sems.at[slot, 3 + part])

    def start_out(at, slot):
        @pl.when(at // 4 == tile)
        def _():
            out_copy(at, slot, False).start()

        @pl.when(at // 4 != tile)
        def _():
            out_copy(at, slot, True).start()

        for part in range(2):
            in_copy(at, slot, part, False).start()
            in_copy(at, slot, part, True).start()

    def sent_out(at, slot):
        @pl.when(at // 4 == tile)
        def _():
            out_copy(at, slot, False).wait()

        @pl.when(at // 4 != tile)
        def _():
            out_copy(at, slot, True).wait_send()

        for part in range(2):
            in_copy(at, slot, part, False).wait()
            in_copy(at, slot, part, True).wait_send()

    def backward(at, _):
        slot = lax.rem(at, 2)

        @pl.when(at >= 2)
        def _():
            sent_out(at - 2, slot)

        side = pl.ds(pl.multiple_of(at * CHUNK, CHUNK), CHUNK)
        wide = slope[:, side].astype(F32) * dot_nt(pool[0], w_out[side, :])
        grad_inner = wide.astype(BF16)
        slope[:, side] = grad_inner
        lanes = pl.ds(pl.multiple_of(lax.rem(at, 2) * CHUNK, CHUNK), CHUNK)
        small[pl.ds(3 + at // 2, 1), lanes] = jnp.sum(grad_inner.astype(F32), axis=0, keepdims=True)
        outgoing[slot] = dot(cot_t[...], active[:, side]).astype(BF16).reshape(outgoing.shape[1:])
        for top in range(4):
            block = dot(normed_t[top * 256 : (top + 1) * 256, :], grad_inner).astype(BF16)
            for part in range(2):
                first = ((top // 2) * 2 + part) * 4
                outgoing[
                    2 + slot, first : first + 4, :, (top % 2) * KEYS : (top % 2 + 1) * KEYS
                ] = block[:, part * KEYS : (part + 1) * KEYS].reshape(4, 64, KEYS)
        start_out(at, slot)
        return 0

    lax.fori_loop(0, chunks, backward, 0)
    for copy in outs[1:]:
        copy.wait()
    probs_copy(1).wait()

    def back_rows(step, carry):
        here = pl.ds(pl.multiple_of(step * KEYS, KEYS), KEYS)
        hat, rate = normalise(third[here, :])
        grad = dot_nt(slope[here, :], w_in[...])
        pool[2, here, :] = (
            pool[0, here, :].astype(F32) + norm_backward(grad, hat, rate, gain[...])
        ).astype(BF16)
        return (
            carry[0] + jnp.sum(grad * hat, axis=0, keepdims=True),
            carry[1] + jnp.sum(grad, axis=0, keepdims=True),
        )

    zero = jnp.zeros((1, width), F32)
    sums = lax.fori_loop(0, rows // KEYS, back_rows, (zero, zero))
    small[0:1, :] = sums[0]
    small[1:2, :] = sums[1]
    small[7:8, :] = zero
    last = [load(pool.at[2], third_out)]
    mixed_swap.wait()
    mixed_swap.place(pool.at[1])
    last.append(load(pool.at[1], mixed_out))
    for at in (chunks - 2, chunks - 1):
        sent_out(at, at % 2)
    for at in range(chunks):
        if at < 4:
            out_copy(at, 0, True).wait_recv()
        for part in range(2):
            in_copy(at, 0, part, True).wait_recv()
    for copy in last:
        copy.wait()


def middle(args, number):
    clip_big, second, cot = args[:3]
    win = args[13]
    rows, width = second.shape
    hidden = win.shape[1]
    wide = shape_of((rows, width), BF16)
    probs = (rows // KEYS, 8, 2 * KEYS, KEYS)
    dma = pltpu.SemaphoreType.DMA
    block = pltpu.VMEM((7, 128, width), BF16)
    args = list(args)
    args[2] = cot.reshape(rows // 16, 16, width)
    return pl.pallas_call(
        middle_kernel,
        out_shape=[
            wide, wide, wide, wide, shape_of(probs, BF16), wide, wide, wide,
            *[shape_of((hidden // KEYS, 4, 64, 2 * KEYS), BF16)] * 2,
            *[shape_of((16, KEYS, CHUNK), BF16)] * 2,
            shape_of((8, width), F32),
        ],
        in_specs=[IN_SMEM, IN_HBM, IN_HBM] + [WHOLE] * 6 + [IN_HBM] * 6,
        out_specs=[IN_HBM] * 12 + [WHOLE],
        scratch_shapes=[
            pltpu.VMEM((6, rows, width), BF16),
            pltpu.VMEM(probs[1:], BF16),
            pltpu.VMEM((4, width, width), BF16),
            pltpu.VMEM((width, hidden), BF16),
            pltpu.VMEM((hidden, width), BF16),
            pltpu.VMEM((rows, hidden), BF16),
            pltpu.VMEM((rows, hidden), BF16),
            pltpu.VMEM((rows, width), F32),
            pltpu.VMEM((width, rows), BF16),
            pltpu.VMEM((width, rows), BF16),
            pltpu.VMEM((rows // 16, 16, width), BF16),
            block, block, block,
            pltpu.VMEM((4, 16, 64, CHUNK), BF16),
            dma((24,)), dma((7,)), dma((7,)), dma((7,)), dma((7,)), dma((2, 5)), dma((8, 3)), dma((2,)),
        ],
        compiler_params=params(collective_id=number, has_side_effects=True),
    )(*args)


def on_device(
    tokens,
    cotangent,
    clip_big,
    actions,
    action_table,
    norm_gain,
    norm_bias,
    spatial_q,
    spatial_k,
    spatial_v,
    spatial_o,
    temporal_q,
    temporal_k,
    temporal_v,
    temporal_o,
    ffn_in,
    ffn_bias_in,
    ffn_out,
    ffn_bias_out,
):
    tok = tokens[0]
    rows, width = tok.shape
    count = lax.axis_size("seq")
    gains = [norm_gain[at : at + 1] for at in range(3)]
    shifts = [norm_bias[at : at + 1] for at in range(3)]

    normed_one, query_one, key_one, value_one, pair_one, mixed_one, probs_one, second, hot, table = first(
        clip_big, actions, tok, action_table, gains[0], shifts[0],
        spatial_q, spatial_k, spatial_v, spatial_o, 1,
    )
    (normed_two, query_two, key_two, value_two, probs_two, mixed_two, mixed, grad_third, d_in, came_in,
     d_out, came_out, small_ffn) = middle(
        [
            clip_big, second, cotangent[0], gains[1], shifts[1], gains[2], shifts[2],
            ffn_bias_in, ffn_bias_out, temporal_q, temporal_k, temporal_v, temporal_o, ffn_in, ffn_out,
        ],
        2,
    )
    part = width // count
    finer = count // d_in.shape[0]

    def in_blocks(grads):
        if finer > 1:
            grads = grads.reshape(-1, KEYS, 2, finer, KEYS // finer).transpose(0, 3, 1, 2, 4)
        return grads.reshape(count, 4 * part, CHUNK)

    def out_blocks(grads):
        if finer > 1:
            grads = grads.reshape(-1, 4, finer, part, CHUNK).transpose(0, 2, 1, 3, 4)
        return grads.reshape(count, 4 * part, CHUNK)

    d_in, came_in, d_out, came_out = in_blocks(d_in), in_blocks(came_in), out_blocks(d_out), out_blocks(came_out)
    token_grad, sum_out, sum_in, sum_temporal, sum_spatial, small = back(
        [
            clip_big, d_out, came_out, d_in, came_in, grad_third, second, mixed_two, query_two, key_two, value_two,
            normed_two, probs_two, temporal_q, temporal_k, temporal_v, temporal_o, mixed_one,
            query_one, key_one, value_one, pair_one, normed_one, probs_one, spatial_q, spatial_k,
            spatial_v, spatial_o, tok, hot, table, gains[0], gains[1], small_ffn,
        ],
        5,
    )
    (table_grad, gain_grad, shift_grad, ffn_in_grad, ffn_out_grad, bias_in, bias_out, *weights) = finish(
        [sum_out, sum_in, sum_temporal, sum_spatial], small, ffn_in.shape[1]
    )
    return (
        mixed[None],
        token_grad[None],
        table_grad,
        gain_grad,
        shift_grad,
        *weights[1:4],
        weights[0],
        *weights[5:8],
        weights[4],
        ffn_in_grad,
        bias_in,
        ffn_out_grad,
        bias_out,
    )


def solution(mesh):
    placed = (P("tile", "seq", None),) * 2 + (P(),) * 17
    return jax.shard_map(
        on_device,
        mesh=mesh,
        in_specs=placed,
        out_specs=(P("tile", "seq", None),) * 2 + (P(None, "seq"),) * 15,
        check_vma=False,
    )
```

```python
import functools

import jax
import jax.numpy as jnp
from jax import lax
from jax.experimental import pallas as pl
from jax.experimental.pallas import tpu as pltpu
from jax.sharding import PartitionSpec as P

HEAD_DIM = 64
FRAMES = 16
GRID_BIG = 16
GRID_SMALL = 8
WIDE = 128
KEYS = 256
CHUNK = 512
VMEM_BYTES = 62 * 2**20
FACTOR = HEAD_DIM**-0.5
ROOT = (2.0 / 3.141592653589793) ** 0.5

F32 = jnp.float32
BF16 = jnp.bfloat16
WHOLE = pl.BlockSpec(memory_space=pltpu.VMEM)
IN_HBM = pl.BlockSpec(memory_space=pl.ANY)
MESH = pl.DeviceIdType.MESH
IN_SMEM = pl.BlockSpec(memory_space=pltpu.SMEM)


def shape_of(dims, kind):
    return jax.ShapeDtypeStruct(dims, kind)


def params(**more):
    return pltpu.CompilerParams(vmem_limit_bytes=VMEM_BYTES, **more)


def dot(left, right):
    return jnp.dot(left, right, preferred_element_type=F32)


def dot_nt(left, right):
    return lax.dot_general(left, right, (((1,), (1,)), ((), ())), preferred_element_type=F32)


def dot_tn(left, right):
    return lax.dot_general(left, right, (((0,), (0,)), ((), ())), preferred_element_type=F32)


def normalise(values):
    centre = values - jnp.mean(values, axis=-1, keepdims=True)
    rate = lax.rsqrt(jnp.mean(centre * centre, axis=-1, keepdims=True) + 1e-05)
    return centre * rate, rate


def norm_backward(grad, hat, rate, gain):
    inner = grad * gain
    level = jnp.mean(inner, axis=-1, keepdims=True)
    slope = jnp.mean(inner * hat, axis=-1, keepdims=True)
    return rate * (inner - level - hat * slope)


def head_halves(block):
    lane = lax.broadcasted_iota(jnp.int32, block.shape, 1)
    zero = jnp.zeros_like(block)
    first = lane < HEAD_DIM
    return jnp.concatenate([jnp.where(first, block, zero), jnp.where(first, zero, block)], axis=0)


def join_halves(both):
    rows = both.shape[0] // 2
    lane = lax.broadcasted_iota(jnp.int32, (rows, both.shape[1]), 1)
    return jnp.where(lane < HEAD_DIM, both[:rows], both[rows:])


def attend(query, key, value, bias):
    scores = dot_nt(head_halves(query) * FACTOR, key) + bias
    top = jnp.max(scores, axis=1, keepdims=True)
    powers = jnp.exp(scores - top)
    prob = (powers * (1.0 / jnp.sum(powers, axis=1, keepdims=True))).astype(BF16)
    return prob, join_halves(dot(prob, value))


def attend_backward(prob, query, key, value, grad):
    grad_two = head_halves(grad)
    grad_prob = dot_nt(grad_two, value)
    prob_f = prob.astype(F32)
    delta = jnp.sum(prob_f * grad_prob, axis=1, keepdims=True)
    grad_score = (prob_f * (grad_prob - delta)).astype(BF16)
    grad_query = join_halves(dot(grad_score, key)) * FACTOR
    grad_key = dot_tn(grad_score, head_halves(query)) * FACTOR
    grad_value = dot_tn(prob, grad_two)
    return grad_query, grad_key, grad_value


def spatial_bias(is_big, rows):
    row = lax.broadcasted_iota(jnp.int32, (rows, KEYS), 0)
    column = lax.broadcasted_iota(jnp.int32, (rows, KEYS), 1)
    same = lax.rem(row, WIDE) // 32 == lax.rem(column, WIDE) // 32
    return jnp.where(same | (is_big == 1), 0.0, -1e30).astype(F32)


def temporal_bias(rows):
    row = lax.rem(lax.broadcasted_iota(jnp.int32, (rows, KEYS), 0), KEYS)
    column = lax.broadcasted_iota(jnp.int32, (rows, KEYS), 1)
    fits = (lax.rem(row, 16) == lax.rem(column, 16)) & (column <= row)
    return jnp.where(fits, 0.0, -1e30).astype(F32)


def weight_grad(target, at, grad, normed):
    grad_t = grad.T
    count, _rows, width = target.shape[1:]
    part = grad_t.shape[0] // count
    for which in range(2):
        block = dot(grad_t, normed[:, which * width : (which + 1) * width]).astype(BF16)
        target[which, :, at * part : (at + 1) * part, :] = block.reshape(count, part, width)


REACH = 3
STEPS = tuple(step for step in range(REACH, -REACH - 1, -1) if step != 0)


class Swap:
    def __init__(self, to_time, offset, is_big, source, staged, came, sems, parts=1):
        self.me, self.tile = lax.axis_index("seq"), lax.axis_index("tile")
        self.count = lax.axis_size("seq")
        self.to_time, self.offset, self.is_big = to_time, offset, is_big
        self.source, self.staged, self.came, self.sems = source, staged, came, sems
        self.parts = parts

    def peer(self, step):
        return (self.me + step, self.tile)

    def present(self, step):
        return (self.me + step >= 0) & (self.me + step < self.count)

    def greet(self, barrier):
        for step in STEPS:
            @pl.when(self.present(step))
            def _(step=step):
                pl.semaphore_signal(
                    barrier, inc=1, device_id=self.peer(step), device_id_type=MESH
                )
        return jnp.minimum(self.me, REACH) + jnp.minimum(self.count - 1 - self.me, REACH)

    def copy(self, step, part):
        slot, sem = REACH - step, (REACH - step) * self.parts + part
        source, target = self.staged.at[slot], self.came.at[slot]
        if self.parts > 1:
            rows = pl.ds(part * (128 // self.parts), 128 // self.parts)
            source, target = source.at[rows], target.at[rows]
        return remote(source, target, self.sems[0].at[sem], self.sems[1].at[sem], self.peer(step))

    def stage(self, step, part):
        which = jnp.clip(self.offset + step, 0, REACH)
        target = self.came if step == 0 else self.staged
        slot = REACH - step
        if self.to_time:
            frames = 4 // self.parts
            for frame in range(part * frames, (part + 1) * frames):
                block = self.source[pl.ds(which * 2 + frame * 8, 2)]
                target[slot, frame * 32 : frame * 32 + 32] = block.reshape(32, block.shape[2])
            return
        sides = 2 // self.parts
        for side in range(part * sides, (part + 1) * sides):
            block = self.source[pl.ds(which * 4 + side * 16, 4)]
            target[slot, side * 64 : side * 64 + 64] = block.reshape(64, block.shape[2])

    def send(self, part=0):
        for step in STEPS:
            self.stage(step, part)

            @pl.when(self.present(step))
            def _(step=step):
                self.copy(step, part).start()

        self.stage(0, part)

    def wait(self, only=None):
        for part in range(self.parts) if only is None else (only,):
            for step in STEPS:
                @pl.when(self.present(step))
                def _(step=step, part=part):
                    self.copy(step, part).wait_send()

                @pl.when(self.present(-step))
                def _(step=step, part=part):
                    self.copy(step, part).wait_recv()

    def place(self, target):
        width = target.shape[-1]
        chosen = jnp.full((16, width), self.is_big, jnp.int32) == 1
        for at in range(REACH + 1):
            slot = REACH - self.offset + at
            for side in range(2):
                for frame in range(4):
                    low = frame * 32 + side * 16 if self.to_time else side * 64 + frame * 16
                    moved = self.came[pl.ds(slot, 1), low : low + 16][0]
                    if self.to_time:
                        here, mine = side * 256 + at * 64 + frame * 16, at * 8 + frame * 2 + side
                    else:
                        here, mine = frame * 128 + at * 32 + side * 16, side * 16 + frame * 4 + at
                    target[here : here + 16] = jnp.where(chosen, moved, self.source[mine])


def seq_dims(count):
    return {16: (2, 2, 2, 2), 64: (4, 4, 4)}.get(count, (1, 1, count))


def seq_orders(count):
    if count == 16:
        names = {"xy": (3, 2, 1, 0), "yx": (2, 3, 1, 0), "xz": (3, 1, 2, 0)}
        return names | {"yz": (2, 1, 3, 0), "zx": (1, 3, 2, 0), "zy": (1, 2, 3, 0)}
    names = {"xy": (2, 1, 0), "yx": (1, 2, 0), "xz": (2, 0, 1)}
    return names | {"yz": (1, 0, 2), "zx": (0, 2, 1), "zy": (0, 1, 2)}


class Grid:
    def __init__(self):
        self.count = lax.axis_size("seq")
        self.dims = seq_dims(self.count)
        self.orders = seq_orders(self.count)
        self.axes = len(self.dims)
        self.me = lax.axis_index("seq")
        self.tile = lax.axis_index("tile")
        self.strides = [1]
        for size in self.dims[:0:-1]:
            self.strides.insert(0, self.strides[0] * size)
        self.places = [
            lax.rem(self.me // stride, size) for stride, size in zip(self.strides, self.dims)
        ]

    def along(self, axis, step):
        place = self.places[axis]
        there = lax.rem(place + step, self.dims[axis])
        return there, (self.me + (there - place) * self.strides[axis], self.tile)

    def other(self):
        return (self.me, 1 - self.tile)

    def peers(self, phase, order):
        if phase == 0:
            return [self.other()]
        axis = order[phase - 1]
        return [self.along(axis, step)[1] for step in range(1, self.dims[axis])]

    def greet(self, barrier):
        peers = [self.other()]
        for axis in range(self.axes):
            peers += [self.along(axis, step)[1] for step in range(1, self.dims[axis])]
        for peer in peers:
            pl.semaphore_signal(barrier, inc=1, device_id=peer, device_id_type=MESH)
        return len(peers)

    def split(self, flat, dims):
        where = []
        for size in dims[::-1]:
            where.insert(0, lax.rem(flat, size))
            flat = flat // size
        return tuple(where)


def remote(source, target, send_sem, recv_sem, device):
    return pltpu.make_async_remote_copy(
        src_ref=source,
        dst_ref=target,
        send_sem=send_sem,
        recv_sem=recv_sem,
        device_id=device,
        device_id_type=MESH,
    )


class Unit:
    def __init__(self, grid, order, rows, source, out, came, part, sems, free, number, reuse, again):
        self.grid, self.order = grid, order
        self.rows, self.part = rows, part
        self.away, self.own, self.fetched = source
        self.out, self.came = out, came
        self.sends, self.recvs = sems
        self.free, self.number, self.reuse, self.again = free, number, reuse, again
        self.last = grid.axes + 1

    def rest(self, phase):
        taken = self.order[:phase]
        return [axis for axis in range(self.grid.axes) if axis not in taken]

    def held(self, phase):
        lead = () if phase == 0 else (0,)
        return self.came[phase], lead

    def slab(self, phase, there):
        before = self.rest(phase - 1)
        where = [slice(None)] * len(before)
        where[before.index(self.order[phase - 1])] = there
        ref, lead = self.held(phase - 1)
        return ref.at[lead + tuple(where) + (self.part,)]

    def landing(self, phase, step):
        dims = len(self.rest(phase))
        return self.came[phase].at[(step,) + (slice(None),) * dims + (self.part,)]

    def copies(self, phase):
        number, grid = self.number, self.grid
        if phase == 0:
            if self.fetched is not None:
                return [pltpu.make_async_copy(self.fetched, self.start_of(), self.sends.at[number, 0, 0])]
            return [
                remote(
                    self.away, self.start_of(), self.sends.at[number, 0, 0],
                    self.recvs.at[number, 0, 0], grid.other(),
                )
            ]
        if phase == self.last:
            mine = self.out.at[grid.tile, self.rows]
            return [
                remote(
                    mine, mine, self.sends.at[number, phase, 0], self.recvs.at[number, phase, 0],
                    grid.other(),
                )
            ]
        axis = self.order[phase - 1]
        out = []
        for step in range(1, grid.dims[axis]):
            there, device = grid.along(axis, step)
            out.append(
                remote(
                    self.slab(phase, there), self.landing(phase, step - 1),
                    self.sends.at[number, phase, step - 1], self.recvs.at[number, phase, step - 1],
                    device,
                )
            )
        return out

    def start_of(self):
        return self.came[0].at[(slice(None),) * self.grid.axes + (self.part,)]

    def start(self, phase):
        if self.again and phase < self.last:
            amount = len(self.grid.peers(phase, self.order))
            pl.semaphore_wait(self.free.at[self.again - 1, phase], amount)
        for copy in self.copies(phase):
            copy.start()

    def release(self, phase):
        for number, order in self.reuse:
            for peer in self.grid.peers(phase, order):
                pl.semaphore_signal(
                    self.free.at[number, phase], inc=1, device_id=peer, device_id_type=MESH
                )

    def wait(self, phase):
        for copy in self.copies(phase):
            copy.wait()

    def turn(self, phase):
        self.wait(phase)
        grid = self.grid
        if phase == 0:
            def step(at, _):
                where = grid.split(at, grid.dims) + (self.part,)
                self.came[0][where] = self.came[0][where] + self.own(grid.split(at, grid.dims))
                return 0

            if self.fetched is None:
                lax.fori_loop(0, grid.count, step, 0)
                return
            self.own(None)
            for piece in range(4):
                base = piece * (grid.count // 4)
                self.own(piece)

                def step_kept(at, _, base=base):
                    where = grid.split(at + base, grid.dims) + (self.part,)
                    self.came[0][where] = self.came[0][where] + self.own(at)
                    return 0

                lax.fori_loop(0, grid.count // 4, step_kept, 0)
            return
        axis = self.order[phase - 1]
        own = self.slab(phase, grid.places[axis])
        size = grid.dims[axis]
        if phase == grid.axes:
            total = own[...].astype(F32)
            for at in range(size - 1):
                total = total + self.came[phase][at, self.part].astype(F32)
            self.out[grid.tile, self.rows] = total.astype(BF16)
            self.release(phase - 1)
            self.release(phase)
            return
        dims = tuple(grid.dims[axis] for axis in self.rest(phase))
        steps = 1
        for size_of in dims:
            steps *= size_of

        def step(at, _):
            where = grid.split(at, dims)
            total = own[where]
            for other in range(size - 1):
                total = total + self.came[phase][(other,) + where + (self.part,)]
            self.came[phase][(0,) + where + (self.part,)] = total
            return 0

        lax.fori_loop(0, steps, step, 0)
        self.release(phase - 1)

    def on(self, phase):
        if phase < self.last:
            self.turn(phase)
            self.start(phase + 1)


class Pair:
    def __init__(self, *units):
        self.units = units

    def __getattr__(self, name):
        def each(phase):
            for unit in self.units:
                getattr(unit, name)(phase)

        return each


class Total:
    def __init__(self, grid, value, came, sends, recvs):
        self.order = grid.orders["xy"]
        self.last = grid.axes
        self.grid, self.value, self.came, self.sends, self.recvs = grid, value, came, sends, recvs

    def copies(self, phase):
        first = sum(len(self.grid.peers(before, self.order)) for before in range(phase))
        return [
            remote(
                self.value, self.came.at[first + at], self.sends.at[first + at],
                self.recvs.at[first + at], peer,
            )
            for at, peer in enumerate(self.grid.peers(phase, self.order))
        ]

    def start(self, phase):
        for copy in self.copies(phase):
            copy.start()

    def on(self, phase):
        if phase > self.last:
            return
        copies = self.copies(phase)
        for copy in copies:
            copy.wait()
        total = self.value[...]
        first = sum(len(self.grid.peers(before, self.order)) for before in range(phase))
        for at in range(len(copies)):
            total = total + self.came[first + at]
        self.value[...] = total
        if phase < self.last:
            self.start(phase + 1)


def unit_scratch(rows, width, order, dims):
    left = list(range(len(dims)))
    out = [pltpu.VMEM(dims + (rows, width), BF16)]
    for axis in order:
        left.remove(axis)
        rest = tuple(dims[other] for other in left)
        out.append(pltpu.VMEM((max(dims[axis] - 1, 1),) + rest + (rows, width), BF16))
    return out


def back_kernel(
    clip_big, d_out, came_out, d_in, came_in, third, second, mixed_t, query_t, key_t, value_t, normed_t, probs_t,
    wq_t, wk_t, wv_t, wo_t, mixed_s, query_s, key_s, value_s, pair, normed_s, probs_s,
    wq_s, wk_s, wv_s, wo_s, tok, hot, table, gain_one, gain_two, small_ffn,
    token_grad, sum_out, sum_in, sum_time, sum_space, small,
    pool, turned, held, probs, d_weights, kept, came_key, came_value, swapped, *rest,
):
    grid = Grid()
    deep = grid.axes + 1
    unit_bufs, rest = rest[: 4 * deep], rest[4 * deep :]
    (totals, total_came, loads, unit_sends, unit_recvs, free, swap_sends, swap_recvs,
     total_sends, total_recvs, pair_sems) = rest
    rows, width = pool.shape[1:]
    _clip, offset, is_big = where_am_i(clip_big)
    swap = Swap(
        False, offset, is_big, turned, _Slots(pool, (11, 6)), swapped, (swap_sends, swap_recvs), 2
    )
    barrier = pltpu.get_barrier_semaphore()
    pl.semaphore_wait(barrier, grid.greet(barrier) + swap.greet(barrier))

    load = Loads(loads)
    orders = grid.orders
    share = d_out.shape[-2]
    every = (slice(None),) * grid.axes

    ways = (("xy", "yx"), ("zx", "zy"), ("xz", "yz", "xz", "yz"), ("yx", "xy", "xy", "yx"))
    ways = [[orders[name] for name in group] for group in ways]

    def buffers(group, which):
        first = (group % 2) * 2 * deep + which * deep
        return unit_bufs[first : first + deep]

    def fetched(group, which, keep, landed, out):
        half = share // 2
        rows_of = pl.ds(which * half, half)
        number = 2 * group + which
        first = (1, grid.dims[0] * grid.dims[1] // 4) if grid.dims[0] < 4 else (grid.dims[0] // 4, grid.dims[1])

        def own(at):
            if at is None:
                return None
            if isinstance(at, int):
                copy = pltpu.make_async_copy(
                    keep.at[
                        (
                            pl.ds(at * first[0] * first[1] // grid.dims[1], first[0]),
                            pl.ds(at * first[1] % grid.dims[1], first[1]),
                        )
                        + every[2:]
                        + (rows_of,)
                    ],
                    kept,
                    unit_sends.at[number, 0, 1],
                )
                copy.start()
                copy.wait()
                return None
            return kept[grid.split(at, first + grid.dims[2:])]

        reuse = [
            (4 * group + 2 * which + sub, ways[group + 2][2 * which + sub]) for sub in range(2)
        ]
        return Unit(
            grid, ways[group][which], rows_of, (None, own, landed.at[every + (rows_of,)]), out,
            buffers(group, which), pl.ds(0, half), (unit_sends, unit_recvs), free, number, reuse, 0,
        )

    def made(group, which, out):
        quarter = share // 4
        rows_of = pl.ds(which * quarter, quarter)

        def own(where):
            return d_weights[(grid.tile,) + where + (rows_of,)]

        return Unit(
            grid, ways[group][which], rows_of,
            (d_weights.at[(1 - grid.tile,) + every + (rows_of,)], own, None), out,
            buffers(group, which // 2), pl.ds((which % 2) * quarter, quarter),
            (unit_sends, unit_recvs), free, 4 + 4 * (group - 2) + which, [],
            4 * (group - 2) + which + 1,
        )

    p0 = Pair(*[fetched(0, which, d_out, came_out, sum_out) for which in range(2)])
    p1 = Pair(*[fetched(1, which, d_in, came_in, sum_in) for which in range(2)])
    p2 = Pair(*[made(2, which, sum_time) for which in range(4)])
    p3o, p3q, p3k, p3v = [made(3, which, sum_space) for which in range(4)]
    p0.start(0)
    p1.start(0)

    in_low = load(third, pool.at[0])
    in_mixed = load(mixed_t, pool.at[2])
    weights = [load(source, held.at[at]) for at, source in enumerate((wo_t, wq_t, wk_t, wv_t))]
    ins = [load(source, pool.at[3 + at]) for at, source in enumerate((query_t, key_t, value_t))]
    ins += [load(probs_t.at[at], probs.at[at]) for at in range(2)]
    late = [load(second, pool.at[1]), load(normed_t, pool.at[6])]
    p0.on(0)
    p1.on(0)
    in_low.wait()
    in_mixed.wait()
    flat_weights = d_weights.reshape((2, grid.count) + d_weights.shape[-2:])
    weight_grad(flat_weights, 0, pool[0], pool.at[2])
    weights[0].wait()

    def mix_back(grad, target):
        for part in range(4):
            side = slice(part * 256, (part + 1) * 256)
            pool[target, :, side] = dot_nt(pool[grad], held[0, side, :]).astype(BF16)

    mix_back(0, 7)
    weights.append(load(wo_s, held.at[0]))
    for copy in ins:
        copy.wait()

    def time_group(at, _):
        here = pl.ds(pl.multiple_of(at * KEYS, KEYS), KEYS)
        for two in range(8):
            side = pl.ds(two * WIDE, WIDE)
            grads = attend_backward(
                probs[at, two], pool[3, here, side], pool[4, here, side], pool[5, here, side],
                pool[7, here, side],
            )
            for target, grad in enumerate(grads):
                pool[8 + target, here, side] = grad.astype(BF16)
        return 0

    lax.fori_loop(0, rows // KEYS, time_group, 0)
    ins = [
        load(source, pool.at[target])
        for source, target in (
            (query_s, 2), (key_s, 3), (value_s, 4), (pair.at[0], 5), (pair.at[1], 7)
        )
    ]
    ins += [
        load(probs_s.at[at], probs.at[at // 2, :, pl.ds(at % 2 * 2 * WIDE, 2 * WIDE)])
        for at in range(4)
    ]
    for copy in late:
        copy.wait()
    for at in range(3):
        weight_grad(flat_weights, at + 1, pool[8 + at], pool.at[6])
    for at in range(3):
        weights[at + 1].wait()

    def time_rows(step, carry):
        here = pl.ds(pl.multiple_of(step * 256, 256), 256)
        grad = (
            dot_nt(pool[8, here, :], held[1])
            + dot_nt(pool[9, here, :], held[2])
            + dot_nt(pool[10, here, :], held[3])
        )
        hat, rate = normalise(pool[1, here, :].astype(F32))
        total = pool[0, here, :].astype(F32) + norm_backward(grad, hat, rate, gain_two[...])
        turned[pl.ds(step * 16, 16)] = total.astype(BF16).reshape(16, 16, width)
        return (
            carry[0] + jnp.sum(grad * hat, axis=0, keepdims=True),
            carry[1] + jnp.sum(grad, axis=0, keepdims=True),
        )

    zero = jnp.zeros((1, width), F32)
    time_norm = (zero, zero)
    for side in range(2):
        time_norm = time_rows(side, time_norm)
        swap.send(side)
    weights += [load(source, held.at[at + 1]) for at, source in enumerate((wq_s, wk_s, wv_s))]
    in_mixed = load(mixed_s, pool.at[10])
    p0.on(1)
    p2.start(0)
    p2.turn(0)
    p1.on(1)
    swap.wait()
    swap.place(pool.at[1])
    in_normed = load(normed_s, pool.at[0])
    p0.on(2)
    p2.start(1)

    in_mixed.wait()
    weight_grad(flat_weights, 0, pool[1], pool.at[10])
    weights[4].wait()
    mix_back(1, 8)
    p3o.start(0)
    for copy in ins:
        copy.wait()

    def space_group(at, _):
        here = pl.ds(pl.multiple_of(at * WIDE, WIDE), WIDE)
        lower = pl.ds(pl.multiple_of(lax.rem(at, 2) * 2 * WIDE, 2 * WIDE), 2 * WIDE)
        for two in range(8):
            side = pl.ds(two * WIDE, WIDE)
            keys = jnp.concatenate([pool[3, here, side], pool[5, here, side]], axis=0)
            values = jnp.concatenate([pool[4, here, side], pool[7, here, side]], axis=0)
            grad_query, grad_key, grad_value = attend_backward(
                probs[at // 2, two, lower], pool[2, here, side], keys, values, pool[8, here, side]
            )
            pool[9, here, side] = grad_query.astype(BF16)
            pool[10, here, side] = grad_key[:WIDE].astype(BF16)
            pool[11, here, side] = grad_value[:WIDE].astype(BF16)
            pool[6, here, side] = grad_key[WIDE:].astype(BF16)
            turned[pl.ds(at * 8, 8), :, side] = grad_value[WIDE:].astype(BF16).reshape(8, 16, WIDE)
        return 0

    lax.fori_loop(0, rows // (2 * WIDE), space_group, 0)
    p0.on(3)
    p1.on(2)
    p3o.on(0)
    lax.fori_loop(rows // (2 * WIDE), rows // WIDE, space_group, 0)
    across = [
        remote(
            source, target, pair_sems.at[0, at], pair_sems.at[1, at], grid.other(),
        )
        for at, (source, target) in enumerate(((pool.at[6], came_key), (turned, came_value)))
    ]
    for copy in across:
        copy.start()
    in_tok = load(tok, pool.at[2])
    in_normed.wait()
    weight_grad(flat_weights, 1, pool[9], pool.at[0])
    p3q.start(0)
    for at, copy in enumerate(across):
        copy.wait()
        came = (came_key, came_value)[at][...].reshape(rows, width)
        pool[10 + at] = pool[10 + at] + came
        weight_grad(flat_weights, 2 + at, pool[10 + at], pool.at[0])
        (p3k, p3v)[at].start(0)
    p3q.on(0)
    p3k.on(0)
    p3v.on(0)
    p2.on(1)
    p0.on(4)
    p1.on(3)
    for at in range(3):
        weights[5 + at].wait()
    in_tok.wait()

    def space_rows(step, carry):
        here = pl.ds(pl.multiple_of(step * 256, 256), 256)
        grad = (
            dot_nt(pool[9, here, :], held[1])
            + dot_nt(pool[10, here, :], held[2])
            + dot_nt(pool[11, here, :], held[3])
        )
        first = pool[2, here, :].astype(F32) + dot(hot[here, :], table[...])
        hat, rate = normalise(first)
        total = pool[1, here, :].astype(F32) + norm_backward(grad, hat, rate, gain_one[...])
        high = total.astype(BF16)
        pool[1, here, :] = high
        rest = (total - high.astype(F32)).astype(BF16)
        chosen = hot[here, :]
        return (
            carry[0] + jnp.sum(grad * hat, axis=0, keepdims=True),
            carry[1] + jnp.sum(grad, axis=0, keepdims=True),
            carry[2] + dot_tn(chosen, high)[:8] + dot_tn(chosen, rest)[:8],
        )

    p3o.on(1)
    space_norm = lax.fori_loop(0, rows // 256, space_rows, (zero, zero, jnp.zeros((8, width), F32)))
    out_grad = load(pool.at[1], token_grad)
    totals[0:8] = space_norm[2]
    totals[8:16] = jnp.concatenate(
        [space_norm[0], time_norm[0], space_norm[1], time_norm[1], jnp.zeros((4, width), F32)], axis=0
    )
    totals[16:24] = small_ffn[...]
    total = Total(grid, totals, total_came, total_sends, total_recvs)
    total.start(0)
    p2.on(2)
    p3q.on(1)
    p1.on(4)
    p3o.on(2)
    total.on(0)
    p3v.on(1)
    p3k.on(1)
    p2.on(3)
    p3q.on(2)
    total.on(1)
    p3o.on(3)
    p3v.on(2)
    p3k.on(2)
    p3q.on(3)
    total.on(2)
    p2.on(4)
    p3v.on(3)
    p3k.on(3)
    total.on(3)
    p3o.on(4)
    p3q.on(4)
    p3v.on(4)
    p3k.on(4)
    total.on(4)
    small[...] = totals[...]
    for unit in (p0, p1, p2, p3o, p3q, p3k, p3v):
        unit.wait(grid.axes + 1)
    out_grad.wait()


class _Slots:
    def __init__(self, pool, slots):
        self.pool, self.slots = pool, slots

    class _At:
        def __init__(self, slots):
            self.slots = slots

        def __getitem__(self, slot):
            return self.slots.pool.at[self.slots.slots[slot // 4], pl.ds(slot % 4 * 128, 128)]

    @property
    def at(self):
        return _Slots._At(self)

    def __setitem__(self, where, value):
        slot, rows = where
        first = slot % 4 * 128
        self.pool[self.slots[slot // 4], first + rows.start : first + rows.stop] = value


def back(args, number):
    args = list(args)
    rows, width = args[5].shape
    count = lax.axis_size("seq")
    dims = seq_dims(count)
    share, group = args[1].shape[-2:]
    dma = pltpu.SemaphoreType.DMA
    lead = (1, dims[0] * dims[1] // 4) if dims[0] < 4 else (dims[0] // 4, dims[1])
    scratch = [
        pltpu.VMEM((12, rows, width), BF16),
        pltpu.VMEM((rows // 16, 16, width), BF16),
        pltpu.VMEM((4, width, width), BF16),
        pltpu.VMEM((2, 8, 2 * KEYS, KEYS), BF16),
        pltpu.VMEM((2,) + dims + (share, group), BF16),
        pltpu.VMEM(lead + dims[2:] + (share // 2, group), BF16),
        pltpu.VMEM((rows, width), BF16),
        pltpu.VMEM((rows // 16, 16, width), BF16),
        pltpu.VMEM((7, 128, width), BF16),
    ]
    for _ in range(2):
        for name in ("xy", "yx"):
            scratch += unit_scratch(share // 2, group, seq_orders(count)[name], dims)
    most = max(max(dims) - 1, 2)
    peers = 1 + sum(dims) - len(dims)
    scratch += [
        pltpu.VMEM((24, width), F32),
        pltpu.VMEM((peers, 24, width), F32),
        dma((40,)),
        dma((12, len(dims) + 2, most)),
        dma((12, len(dims) + 2, most)),
        pltpu.SemaphoreType.REGULAR((8, len(dims) + 1)),
        dma((14,)),
        dma((14,)),
        dma((peers,)),
        dma((peers,)),
        dma((2, 2)),
    ]
    for at in range(1, 5):
        args[at] = args[at].reshape(dims + (share, group))
    final = shape_of((2, share, group), BF16)
    return pl.pallas_call(
        back_kernel,
        out_shape=[shape_of((rows, width), BF16)] + [final] * 4 + [shape_of((24, width), F32)],
        in_specs=[IN_SMEM] + [IN_HBM] * 28 + [WHOLE] * 5,
        out_specs=[IN_HBM] + [WHOLE] * 5,
        scratch_shapes=scratch,
        compiler_params=params(collective_id=number, has_side_effects=True),
    )(*args)


def finish_kernel(sum_out, sum_in, sum_time, sum_space, small, *refs):
    table, gain, shift, inner, outer, bias_in, bias_out = refs[:7]
    weights, rolled = refs[7:-1], refs[-1]
    count = lax.axis_size("seq")
    me = lax.axis_index("seq")
    width = small.shape[1]
    part = width // count
    hidden = bias_in.shape[1]
    for half in range(2):
        for at in range(4):
            rows = slice(at * part, (at + 1) * part)
            first = half * (width // 2)
            for base, source in ((0, sum_space), (4, sum_time)):
                weights[base + at][:, first : first + width // 2] = source[half, rows].astype(F32)
            first = (half * 4 + at) * CHUNK
            outer[:, first : first + CHUNK] = sum_out[half, rows].astype(F32)
        if inner.shape[1] == KEYS:
            for at in range(2):
                first = half * 2 * KEYS + at * KEYS
                inner[first : first + KEYS, :] = sum_in[half, :, at * KEYS : (at + 1) * KEYS].astype(F32)
    rolled[...] = pltpu.roll(small[...], lax.rem(width - me * part, width), 1)
    table[...] = rolled[0:8, :part]
    gain[...] = jnp.concatenate([rolled[8:10, :part], rolled[16:17, :part]], axis=0)
    shift[...] = jnp.concatenate([rolled[10:12, :part], rolled[17:18, :part]], axis=0)
    bias_out[...] = rolled[18:19, :part]
    begin = me * hidden
    rolled[...] = pltpu.roll(small[...], lax.rem(width - lax.rem(begin, width), width), 1)
    for at in range(4):
        @pl.when(begin // width == at)
        def _(at=at):
            bias_in[...] = rolled[19 + at : 20 + at, :hidden]


def finish(sums, small, hidden):
    count = lax.axis_size("seq")
    width = small.shape[1]
    part = width // count
    outs = [
        shape_of((8, part), F32), shape_of((3, part), F32), shape_of((3, part), F32),
        shape_of((width, hidden // count), F32), shape_of((part, hidden), F32),
        shape_of((1, hidden // count), F32), shape_of((1, part), F32),
    ]
    out = pl.pallas_call(
        finish_kernel,
        out_shape=outs + [shape_of((part, width), F32)] * 8,
        in_specs=[WHOLE] * 5,
        out_specs=[WHOLE] * 15,
        scratch_shapes=[pltpu.VMEM(small.shape, F32)],
        compiler_params=params(),
    )(*sums, small)
    out = list(out)
    out[4] = out[4].T
    out[7:] = [value.T for value in out[7:]]
    if hidden // count != KEYS:
        inner = sums[1].reshape(2, KEYS, 2, hidden // count).transpose(0, 2, 1, 3)
        out[3] = inner.reshape(width, -1).astype(F32)
    return out


def where_am_i(clip_big):
    me = lax.axis_index("seq")
    span = (GRID_BIG // GRID_SMALL) ** 2
    start, clip, offset, is_big = jnp.int32(0), jnp.int32(0), jnp.int32(0), jnp.int32(0)
    for at in range(clip_big.shape[0]):
        big = clip_big[at]
        size = jnp.where(big == 1, span, 1)
        inside = (me >= start) & (me < start + size)
        clip = jnp.where(inside, at, clip)
        offset = jnp.where(inside, me - start, offset)
        is_big = jnp.where(inside, big, is_big)
        start = start + size
    return clip, offset, is_big


class Loads:
    def __init__(self, sems):
        self.sems, self.used = sems, 0

    def __call__(self, source, target):
        copy = pltpu.make_async_copy(source, target, self.sems.at[self.used])
        self.used += 1
        copy.start()
        return copy


def first_kernel(
    clip_big, actions, tok, action_table, gain, shift, cot, wq, wk, wv, wo,
    normed_out, query_out, key_out, value_out, pair_out, mixed_out, probs_out, second_out, cot_out, hot, table,
    held, normed, query, key, value, pair, mixed, probs, second, turned, staged, came, cot_staged, cot_came,
    loads, pair_sems, swap_sends, swap_recvs, cot_sends, cot_recvs,
):
    rows, width = tok.shape
    clip, offset, is_big = where_am_i(clip_big)
    grid = Grid()
    swap = Swap(True, offset, is_big, turned, staged, came, (swap_sends, swap_recvs), 2)
    cot_swap = Swap(True, offset, is_big, cot, cot_staged, cot_came, (cot_sends, cot_recvs), 2)
    barrier = pltpu.get_barrier_semaphore()
    pl.semaphore_signal(barrier, inc=1, device_id=grid.other(), device_id_type=MESH)
    peers = 1 + swap.greet(barrier)
    load = Loads(loads)
    weights = [load(source, held.at[at]) for at, source in enumerate((wk, wv, wq, wo))]
    pl.semaphore_wait(barrier, peers)
    cot_swap.send(0)

    last = actions.shape[0] - 1
    base = clip * FRAMES + offset * (FRAMES // (REACH + 1))
    row = lax.broadcasted_iota(jnp.int32, (rows, WIDE), 0)
    frame_of = jnp.where(jnp.full((rows, WIDE), is_big, jnp.int32) == 1, row // WIDE, row // 32)
    action = jnp.zeros((rows, WIDE), jnp.int32)
    for frame in range(FRAMES):
        action = jnp.where(frame_of == frame, actions[jnp.minimum(base + frame, last)], action)
    lane = lax.broadcasted_iota(jnp.int32, (rows, WIDE), 1)
    hot[...] = jnp.where((action == lax.rem(lane, 8)) & (lane < 24), 1.0, 0.0).astype(BF16)
    exact = action_table[...]
    high = exact.astype(BF16)
    left = exact - high.astype(F32)
    middle = left.astype(BF16)
    low = left - middle.astype(F32)
    table[...] = jnp.concatenate(
        [high.astype(F32), middle.astype(F32), low, jnp.zeros((WIDE - 24, width), F32)], axis=0
    ).astype(BF16)

    def norm_rows(at, _):
        here = pl.ds(pl.multiple_of(at * 128, 128), 128)
        hat, _rate = normalise(tok[here, :].astype(F32) + dot(hot[here, :], table[...]))
        normed[here, :] = (hat * gain[...] + shift[...]).astype(BF16)
        return 0

    lax.fori_loop(0, rows // 128, norm_rows, 0)
    outs = [load(normed, normed_out)]
    across = []
    for at, (target, out) in enumerate(((key, key_out), (value, value_out), (query, query_out))):
        weights[at].wait()
        for part in range(4):
            side = pl.ds(part * 256, 256)
            target[:, side] = dot(normed[...], held[at, :, side]).astype(BF16)
        if at < 2:
            copy = remote(
                target, pair.at[at], pair_sems.at[0, at], pair_sems.at[1, at], grid.other()
            )
            copy.start()
            across.append(copy)
        outs.append(load(target, out))
    for copy in across:
        copy.wait()
    outs.append(load(pair, pair_out))
    weights[3].wait()
    bias = spatial_bias(is_big, 2 * WIDE)

    def group(at, _):
        here = pl.ds(pl.multiple_of(at * WIDE, WIDE), WIDE)
        for two in range(8):
            side = pl.ds(two * WIDE, WIDE)
            keys = jnp.concatenate([key[here, side], pair[0, here, side]], axis=0)
            values = jnp.concatenate([value[here, side], pair[1, here, side]], axis=0)
            prob, out = attend(query[here, side], keys, values, bias)
            probs[at, two] = prob
            mixed[here, side] = out.astype(BF16)
        return 0

    for half in range(2):
        lax.fori_loop(2 * half, 2 * half + 2, group, 0)
        here = slice(half * KEYS, (half + 1) * KEYS)
        blocks = slice(half * 16, (half + 1) * 16)
        for part in range(4):
            side = slice(part * 256, (part + 1) * 256)
            first = tok[here, side].astype(F32) + dot(hot[here, :], table[:, side])
            total = first + dot(mixed[here, :], held[3, :, side])
            turned[blocks, :, side] = total.astype(BF16).reshape(16, 16, 256)
        swap.send(half)
    outs += [load(mixed, mixed_out), load(probs, probs_out)]
    cot_swap.wait(0)
    half = pl.ds(0, cot_out.shape[1])
    outs.append(load(cot_came.at[:, half], cot_out))
    swap.wait()
    swap.place(second)
    outs.append(load(second, second_out))
    for copy in outs:
        copy.wait()


def first(clip_big, actions, tok, action_table, gain, shift, cot, wq, wk, wv, wo, number):
    rows, width = tok.shape
    wide = shape_of((rows, width), BF16)
    probs = (rows // WIDE, 8, 2 * WIDE, KEYS)
    dma = pltpu.SemaphoreType.DMA
    full = pltpu.VMEM((rows, width), BF16)
    return pl.pallas_call(
        first_kernel,
        out_shape=[
            wide, wide, wide, wide, shape_of((2, rows, width), BF16), wide, shape_of(probs, BF16), wide,
            shape_of((7, 64, width), BF16), shape_of((rows, WIDE), BF16), shape_of((WIDE, width), BF16),
        ],
        in_specs=[IN_SMEM] * 2 + [WHOLE] * 5 + [IN_HBM] * 4,
        out_specs=[IN_HBM] * 9 + [WHOLE] * 2,
        scratch_shapes=[
            pltpu.VMEM((4, width, width), BF16), full, full, full, full,
            pltpu.VMEM((2, rows, width), BF16), full, pltpu.VMEM(probs, BF16), full,
            pltpu.VMEM((rows // 16, 16, width), BF16),
            *[pltpu.VMEM((7, 128, width), BF16)] * 4,
            dma((16,)), dma((2, 2)), *[dma((14,))] * 4,
        ],
        compiler_params=params(collective_id=number, has_side_effects=True),
    )(
        clip_big, actions, tok, action_table, gain, shift, cot.reshape(rows // 16, 16, width),
        wq, wk, wv, wo,
    )


def middle_kernel(
    clip_big, second, cot_in, cot_half, gain_two, shift_two, gain, shift, bias_in, bias_out, wq, wk, wv, wo, win, wout,
    normed_out, query_out, key_out, value_out, probs_out, mixed_two_out, mixed_out, third_out,
    d_in, came_in, d_out, came_out, small,
    pool, probs, held, w_in, w_out, active, slope, third, normed_t, cot_t, turned,
    staged, came_cot, came_mixed, outgoing,
    loads, cot_sends, cot_recvs, mixed_sends, mixed_recvs, out_sems, grad_recvs, prob_sems,
):
    rows, width = third.shape
    hidden = w_in.shape[1]
    chunks = hidden // CHUNK
    _clip, offset, is_big = where_am_i(clip_big)
    cot_swap = Swap(True, offset, is_big, turned, staged, came_cot, (cot_sends, cot_recvs), 2)
    mixed_swap = Swap(False, offset, is_big, turned, staged, came_mixed, (mixed_sends, mixed_recvs), 2)
    barrier = pltpu.get_barrier_semaphore()
    tile = lax.axis_index("tile")
    other = (lax.axis_index("seq"), 1 - tile)
    pl.semaphore_signal(barrier, inc=1, device_id=other, device_id_type=MESH)
    peers = 1 + cot_swap.greet(barrier)
    load = Loads(loads)
    cot_load = load(cot_in, turned)
    second_load = load(second, pool.at[0])
    weights = [load(source, held.at[at]) for at, source in enumerate((wq, wk, wv, wo))]
    weights += [load(win, w_in), load(wout, w_out)]
    cot_load.wait()
    pl.semaphore_wait(barrier, peers)
    cot_swap.send(1)
    cot_load = load(cot_half, came_cot.at[:, pl.ds(0, cot_half.shape[1])])
    second_load.wait()

    def norm_two(at, _):
        here = pl.ds(pl.multiple_of(at * 128, 128), 128)
        hat, _rate = normalise(pool[0, here, :].astype(F32))
        pool[4, here, :] = (hat * gain_two[...] + shift_two[...]).astype(BF16)
        return 0

    lax.fori_loop(0, rows // 128, norm_two, 0)
    outs = [load(pool.at[4], normed_out)]
    for at, out in enumerate((query_out, key_out, value_out)):
        weights[at].wait()
        for part in range(4):
            side = slice(part * 256, (part + 1) * 256)
            pool[1 + at, :, side] = dot(pool[4], held[at, :, side]).astype(BF16)
        outs.append(load(pool.at[1 + at], out))
    bias = temporal_bias(2 * KEYS)

    def probs_copy(at):
        return pltpu.make_async_copy(probs, probs_out.at[at], prob_sems.at[at])

    def group(at, _):
        @pl.when(at > 0)
        def _():
            probs_copy(0).wait()

        here = pl.ds(pl.multiple_of(at * KEYS, KEYS), KEYS)
        for two in range(8):
            side = pl.ds(two * WIDE, WIDE)
            prob, out = attend(pool[1, here, side], pool[2, here, side], pool[3, here, side], bias)
            probs[two] = prob
            pool[5, here, side] = out.astype(BF16)
        probs_copy(at).start()
        return 0

    lax.fori_loop(0, rows // KEYS, group, 0)
    outs += [load(pool.at[5], mixed_two_out)]
    weights[3].wait()
    for part in range(4):
        side = slice(part * 256, (part + 1) * 256)
        third[:, side] = pool[0, :, side].astype(F32) + dot(pool[5], held[3, :, side])
    outs[0].wait()

    def norm_three(at, _):
        here = pl.ds(pl.multiple_of(at * 128, 128), 128)
        hat, _rate = normalise(third[here, :])
        pool[4, here, :] = (hat * gain[...] + shift[...]).astype(BF16)
        return 0

    lax.fori_loop(0, rows // 128, norm_three, 0)
    normed_t[...] = pool[4].T
    weights[4].wait()

    def forward(at, _):
        side = pl.ds(pl.multiple_of(at * KEYS, KEYS), KEYS)
        inner = dot(pool[4], w_in[:, side]) + bias_in[:, side]
        square = inner * inner
        curve = jnp.tanh(ROOT * (inner + 0.044715 * inner * square))
        active[:, side] = (0.5 * inner * (1.0 + curve)).astype(BF16)
        slope[:, side] = (
            0.5 * (1.0 + curve)
            + (0.5 * ROOT) * inner * (1.0 - curve * curve) * (1.0 + (3 * 0.044715) * square)
        ).astype(BF16)
        return 0

    lax.fori_loop(0, hidden // KEYS, forward, 0)
    cot_load.wait()
    cot_swap.wait(1)
    cot_swap.place(pool.at[0])
    weights[5].wait()

    for half in range(2):
        here, blocks = pl.ds(half * KEYS, KEYS), slice(half * 16, (half + 1) * 16)
        for part in range(width // KEYS):
            side = slice(part * KEYS, (part + 1) * KEYS)
            total = third[here, side] + bias_out[:, side] + dot(active[here, :], w_out[:, side])
            turned[blocks, :, side] = total.astype(BF16).reshape(16, 16, KEYS)
        mixed_swap.send(half)
    cot_t[...] = pool[0].T
    small[2:3, :] = jnp.sum(pool[0].astype(F32), axis=0, keepdims=True)

    def out_copy(at, slot, away):
        share = outgoing.shape[2]
        where = (slice(None), pl.ds(lax.rem(at, 4) * share, share))
        source = outgoing.at[slot]
        if away:
            return remote(
                source, came_out.at[where], out_sems.at[slot, 0], grad_recvs.at[lax.rem(at, 4), 0], other
            )
        return pltpu.make_async_copy(source, d_out.at[where], out_sems.at[slot, 0])

    def in_copy(at, slot, part, away):
        which = 1 - tile if away else tile
        source = outgoing.at[2 + slot, pl.ds((which * 2 + part) * 4, 4)]
        if away:
            return remote(
                source, came_in.at[at * 2 + part], out_sems.at[slot, 1 + part],
                grad_recvs.at[at, 1 + part], other,
            )
        return pltpu.make_async_copy(source, d_in.at[at * 2 + part], out_sems.at[slot, 3 + part])

    def start_out(at, slot):
        @pl.when(at // 4 == tile)
        def _():
            out_copy(at, slot, False).start()

        @pl.when(at // 4 != tile)
        def _():
            out_copy(at, slot, True).start()

        for part in range(2):
            in_copy(at, slot, part, False).start()
            in_copy(at, slot, part, True).start()

    def sent_out(at, slot):
        @pl.when(at // 4 == tile)
        def _():
            out_copy(at, slot, False).wait()

        @pl.when(at // 4 != tile)
        def _():
            out_copy(at, slot, True).wait_send()

        for part in range(2):
            in_copy(at, slot, part, False).wait()
            in_copy(at, slot, part, True).wait_send()

    def backward(at, _):
        slot = lax.rem(at, 2)

        @pl.when(at >= 2)
        def _():
            sent_out(at - 2, slot)

        side = pl.ds(pl.multiple_of(at * CHUNK, CHUNK), CHUNK)
        wide = slope[:, side].astype(F32) * dot_nt(pool[0], w_out[side, :])
        grad_inner = wide.astype(BF16)
        slope[:, side] = grad_inner
        lanes = pl.ds(pl.multiple_of(lax.rem(at, 2) * CHUNK, CHUNK), CHUNK)
        small[pl.ds(3 + at // 2, 1), lanes] = jnp.sum(grad_inner.astype(F32), axis=0, keepdims=True)
        outgoing[slot] = dot(cot_t[...], active[:, side]).astype(BF16).reshape(outgoing.shape[1:])
        for top in range(4):
            block = dot(normed_t[top * 256 : (top + 1) * 256, :], grad_inner).astype(BF16)
            for part in range(2):
                first = ((top // 2) * 2 + part) * 4
                outgoing[
                    2 + slot, first : first + 4, :, (top % 2) * KEYS : (top % 2 + 1) * KEYS
                ] = block[:, part * KEYS : (part + 1) * KEYS].reshape(4, 64, KEYS)
        start_out(at, slot)
        return 0

    lax.fori_loop(0, chunks, backward, 0)
    for copy in outs[1:]:
        copy.wait()
    probs_copy(1).wait()

    def back_rows(step, carry):
        here = pl.ds(pl.multiple_of(step * KEYS, KEYS), KEYS)
        hat, rate = normalise(third[here, :])
        grad = dot_nt(slope[here, :], w_in[...])
        pool[2, here, :] = (
            pool[0, here, :].astype(F32) + norm_backward(grad, hat, rate, gain[...])
        ).astype(BF16)
        return (
            carry[0] + jnp.sum(grad * hat, axis=0, keepdims=True),
            carry[1] + jnp.sum(grad, axis=0, keepdims=True),
        )

    zero = jnp.zeros((1, width), F32)
    sums = lax.fori_loop(0, rows // KEYS, back_rows, (zero, zero))
    small[0:1, :] = sums[0]
    small[1:2, :] = sums[1]
    small[7:8, :] = zero
    last = [load(pool.at[2], third_out)]
    mixed_swap.wait()
    mixed_swap.place(pool.at[1])
    last.append(load(pool.at[1], mixed_out))
    for at in (chunks - 2, chunks - 1):
        sent_out(at, at % 2)
    for at in range(chunks):
        if at < 4:
            out_copy(at, 0, True).wait_recv()
        for part in range(2):
            in_copy(at, 0, part, True).wait_recv()
    for copy in last:
        copy.wait()


def middle(args, number):
    clip_big, second, cot = args[:3]
    win = args[14]
    rows, width = second.shape
    hidden = win.shape[1]
    wide = shape_of((rows, width), BF16)
    probs = (rows // KEYS, 8, 2 * KEYS, KEYS)
    dma = pltpu.SemaphoreType.DMA
    block = pltpu.VMEM((7, 128, width), BF16)
    args = list(args)
    args[2] = cot.reshape(rows // 16, 16, width)
    return pl.pallas_call(
        middle_kernel,
        out_shape=[
            wide, wide, wide, wide, shape_of(probs, BF16), wide, wide, wide,
            *[shape_of((hidden // KEYS, 4, 64, 2 * KEYS), BF16)] * 2,
            *[shape_of((16, KEYS, CHUNK), BF16)] * 2,
            shape_of((8, width), F32),
        ],
        in_specs=[IN_SMEM] + [IN_HBM] * 3 + [WHOLE] * 6 + [IN_HBM] * 6,
        out_specs=[IN_HBM] * 12 + [WHOLE],
        scratch_shapes=[
            pltpu.VMEM((6, rows, width), BF16),
            pltpu.VMEM(probs[1:], BF16),
            pltpu.VMEM((4, width, width), BF16),
            pltpu.VMEM((width, hidden), BF16),
            pltpu.VMEM((hidden, width), BF16),
            pltpu.VMEM((rows, hidden), BF16),
            pltpu.VMEM((rows, hidden), BF16),
            pltpu.VMEM((rows, width), F32),
            pltpu.VMEM((width, rows), BF16),
            pltpu.VMEM((width, rows), BF16),
            pltpu.VMEM((rows // 16, 16, width), BF16),
            block, block, block,
            pltpu.VMEM((4, 16, 64, CHUNK), BF16),
            dma((24,)), *[dma((14,))] * 4, dma((2, 5)), dma((8, 3)), dma((2,)),
        ],
        compiler_params=params(collective_id=number, has_side_effects=True),
    )(*args)


def on_device(
    tokens,
    cotangent,
    clip_big,
    actions,
    action_table,
    norm_gain,
    norm_bias,
    spatial_q,
    spatial_k,
    spatial_v,
    spatial_o,
    temporal_q,
    temporal_k,
    temporal_v,
    temporal_o,
    ffn_in,
    ffn_bias_in,
    ffn_out,
    ffn_bias_out,
):
    tok = tokens[0]
    rows, width = tok.shape
    count = lax.axis_size("seq")
    gains = [norm_gain[at : at + 1] for at in range(3)]
    shifts = [norm_bias[at : at + 1] for at in range(3)]

    normed_one, query_one, key_one, value_one, pair_one, mixed_one, probs_one, second, cot_half, hot, table = first(
        clip_big, actions, tok, action_table, gains[0], shifts[0], cotangent[0],
        spatial_q, spatial_k, spatial_v, spatial_o, 1,
    )
    (normed_two, query_two, key_two, value_two, probs_two, mixed_two, mixed, grad_third, d_in, came_in,
     d_out, came_out, small_ffn) = middle(
        [
            clip_big, second, cotangent[0], cot_half, gains[1], shifts[1], gains[2], shifts[2],
            ffn_bias_in, ffn_bias_out, temporal_q, temporal_k, temporal_v, temporal_o, ffn_in, ffn_out,
        ],
        2,
    )
    part = width // count
    finer = count // d_in.shape[0]

    def in_blocks(grads):
        if finer > 1:
            grads = grads.reshape(-1, KEYS, 2, finer, KEYS // finer).transpose(0, 3, 1, 2, 4)
        return grads.reshape(count, 4 * part, CHUNK)

    def out_blocks(grads):
        if finer > 1:
            grads = grads.reshape(-1, 4, finer, part, CHUNK).transpose(0, 2, 1, 3, 4)
        return grads.reshape(count, 4 * part, CHUNK)

    d_in, came_in, d_out, came_out = in_blocks(d_in), in_blocks(came_in), out_blocks(d_out), out_blocks(came_out)
    token_grad, sum_out, sum_in, sum_temporal, sum_spatial, small = back(
        [
            clip_big, d_out, came_out, d_in, came_in, grad_third, second, mixed_two, query_two, key_two, value_two,
            normed_two, probs_two, temporal_q, temporal_k, temporal_v, temporal_o, mixed_one,
            query_one, key_one, value_one, pair_one, normed_one, probs_one, spatial_q, spatial_k,
            spatial_v, spatial_o, tok, hot, table, gains[0], gains[1], small_ffn,
        ],
        5,
    )
    (table_grad, gain_grad, shift_grad, ffn_in_grad, ffn_out_grad, bias_in, bias_out, *weights) = finish(
        [sum_out, sum_in, sum_temporal, sum_spatial], small, ffn_in.shape[1]
    )
    return (
        mixed[None],
        token_grad[None],
        table_grad,
        gain_grad,
        shift_grad,
        *weights[1:4],
        weights[0],
        *weights[5:8],
        weights[4],
        ffn_in_grad,
        bias_in,
        ffn_out_grad,
        bias_out,
    )


def solution(mesh):
    placed = (P("tile", "seq", None),) * 2 + (P(),) * 17
    return jax.shard_map(
        on_device,
        mesh=mesh,
        in_specs=placed,
        out_specs=(P("tile", "seq", None),) * 2 + (P(None, "seq"),) * 15,
        check_vma=False,
    )
```

```python
import functools

import jax
import jax.numpy as jnp
from jax import lax
from jax.experimental import pallas as pl
from jax.experimental.pallas import tpu as pltpu
from jax.sharding import PartitionSpec as P

HEAD_DIM = 64
FRAMES = 16
GRID_BIG = 16
GRID_SMALL = 8
WIDE = 128
KEYS = 256
CHUNK = 512
VMEM_BYTES = 62 * 2**20
FACTOR = HEAD_DIM**-0.5
ROOT = (2.0 / 3.141592653589793) ** 0.5

F32 = jnp.float32
BF16 = jnp.bfloat16
WHOLE = pl.BlockSpec(memory_space=pltpu.VMEM)
IN_HBM = pl.BlockSpec(memory_space=pl.ANY)
MESH = pl.DeviceIdType.MESH
IN_SMEM = pl.BlockSpec(memory_space=pltpu.SMEM)


def shape_of(dims, kind):
    return jax.ShapeDtypeStruct(dims, kind)


def params(**more):
    return pltpu.CompilerParams(vmem_limit_bytes=VMEM_BYTES, **more)


def dot(left, right):
    return jnp.dot(left, right, preferred_element_type=F32)


def dot_nt(left, right):
    return lax.dot_general(left, right, (((1,), (1,)), ((), ())), preferred_element_type=F32)


def dot_tn(left, right):
    return lax.dot_general(left, right, (((0,), (0,)), ((), ())), preferred_element_type=F32)


def normalise(values):
    centre = values - jnp.mean(values, axis=-1, keepdims=True)
    rate = lax.rsqrt(jnp.mean(centre * centre, axis=-1, keepdims=True) + 1e-05)
    return centre * rate, rate


def norm_backward(grad, hat, rate, gain):
    inner = grad * gain
    level = jnp.mean(inner, axis=-1, keepdims=True)
    slope = jnp.mean(inner * hat, axis=-1, keepdims=True)
    return rate * (inner - level - hat * slope)


def head_halves(block):
    lane = lax.broadcasted_iota(jnp.int32, block.shape, 1)
    zero = jnp.zeros_like(block)
    first = lane < HEAD_DIM
    return jnp.concatenate([jnp.where(first, block, zero), jnp.where(first, zero, block)], axis=0)


def join_halves(both):
    rows = both.shape[0] // 2
    lane = lax.broadcasted_iota(jnp.int32, (rows, both.shape[1]), 1)
    return jnp.where(lane < HEAD_DIM, both[:rows], both[rows:])


def attend(query, key, value, bias):
    scores = dot_nt(head_halves(query) * FACTOR, key) + bias
    top = jnp.max(scores, axis=1, keepdims=True)
    powers = jnp.exp(scores - top)
    prob = (powers * (1.0 / jnp.sum(powers, axis=1, keepdims=True))).astype(BF16)
    return prob, join_halves(dot(prob, value))


def attend_backward(prob, query, key, value, grad):
    grad_two = head_halves(grad)
    grad_prob = dot_nt(grad_two, value)
    prob_f = prob.astype(F32)
    delta = jnp.sum(prob_f * grad_prob, axis=1, keepdims=True)
    grad_score = (prob_f * (grad_prob - delta)).astype(BF16)
    grad_query = join_halves(dot(grad_score, key)) * FACTOR
    grad_key = dot_tn(grad_score, head_halves(query)) * FACTOR
    grad_value = dot_tn(prob, grad_two)
    return grad_query, grad_key, grad_value


def spatial_bias(is_big, rows):
    row = lax.broadcasted_iota(jnp.int32, (rows, KEYS), 0)
    column = lax.broadcasted_iota(jnp.int32, (rows, KEYS), 1)
    same = lax.rem(row, WIDE) // 32 == lax.rem(column, WIDE) // 32
    return jnp.where(same | (is_big == 1), 0.0, -1e30).astype(F32)


def temporal_bias(rows):
    row = lax.rem(lax.broadcasted_iota(jnp.int32, (rows, KEYS), 0), KEYS)
    column = lax.broadcasted_iota(jnp.int32, (rows, KEYS), 1)
    fits = (lax.rem(row, 16) == lax.rem(column, 16)) & (column <= row)
    return jnp.where(fits, 0.0, -1e30).astype(F32)


def weight_grad(target, at, grad, normed):
    grad_t = grad.T
    count, _rows, width = target.shape[1:]
    part = grad_t.shape[0] // count
    for which in range(2):
        block = dot(grad_t, normed[:, which * width : (which + 1) * width]).astype(BF16)
        target[which, :, at * part : (at + 1) * part, :] = block.reshape(count, part, width)


REACH = 3
STEPS = tuple(step for step in range(REACH, -REACH - 1, -1) if step != 0)


class Swap:
    def __init__(self, to_time, offset, is_big, source, staged, came, sems, parts=1):
        self.me, self.tile = lax.axis_index("seq"), lax.axis_index("tile")
        self.count = lax.axis_size("seq")
        self.to_time, self.offset, self.is_big = to_time, offset, is_big
        self.source, self.staged, self.came, self.sems = source, staged, came, sems
        self.parts = parts

    def peer(self, step):
        return (self.me + step, self.tile)

    def present(self, step):
        return (self.me + step >= 0) & (self.me + step < self.count)

    def greet(self, barrier):
        for step in STEPS:
            @pl.when(self.present(step))
            def _(step=step):
                pl.semaphore_signal(
                    barrier, inc=1, device_id=self.peer(step), device_id_type=MESH
                )
        return jnp.minimum(self.me, REACH) + jnp.minimum(self.count - 1 - self.me, REACH)

    def copy(self, step, part):
        slot, sem = REACH - step, (REACH - step) * self.parts + part
        source, target = self.staged.at[slot], self.came.at[slot]
        if self.parts > 1:
            rows = pl.ds(part * (128 // self.parts), 128 // self.parts)
            source, target = source.at[rows], target.at[rows]
        return remote(source, target, self.sems[0].at[sem], self.sems[1].at[sem], self.peer(step))

    def stage(self, step, part):
        which = jnp.clip(self.offset + step, 0, REACH)
        target = self.came if step == 0 else self.staged
        slot = REACH - step
        if self.to_time:
            frames = 4 // self.parts
            for frame in range(part * frames, (part + 1) * frames):
                block = self.source[pl.ds(which * 2 + frame * 8, 2)]
                target[slot, frame * 32 : frame * 32 + 32] = block.reshape(32, block.shape[2])
            return
        sides = 2 // self.parts
        for side in range(part * sides, (part + 1) * sides):
            block = self.source[pl.ds(which * 4 + side * 16, 4)]
            target[slot, side * 64 : side * 64 + 64] = block.reshape(64, block.shape[2])

    def send(self, part=0):
        for step in STEPS:
            self.stage(step, part)

            @pl.when(self.present(step))
            def _(step=step):
                self.copy(step, part).start()

        self.stage(0, part)

    def wait(self, only=None):
        for part in range(self.parts) if only is None else (only,):
            for step in STEPS:
                @pl.when(self.present(step))
                def _(step=step, part=part):
                    self.copy(step, part).wait_send()

                @pl.when(self.present(-step))
                def _(step=step, part=part):
                    self.copy(step, part).wait_recv()

    def place(self, target):
        width = target.shape[-1]
        chosen = jnp.full((16, width), self.is_big, jnp.int32) == 1
        for at in range(REACH + 1):
            slot = REACH - self.offset + at
            for side in range(2):
                for frame in range(4):
                    low = frame * 32 + side * 16 if self.to_time else side * 64 + frame * 16
                    moved = self.came[pl.ds(slot, 1), low : low + 16][0]
                    if self.to_time:
                        here, mine = side * 256 + at * 64 + frame * 16, at * 8 + frame * 2 + side
                    else:
                        here, mine = frame * 128 + at * 32 + side * 16, side * 16 + frame * 4 + at
                    target[here : here + 16] = jnp.where(chosen, moved, self.source[mine])


def seq_dims(count):
    return {16: (2, 2, 2, 2), 64: (4, 4, 4)}.get(count, (1, 1, count))


def seq_orders(count):
    if count == 16:
        names = {"xy": (3, 2, 1, 0), "yx": (2, 3, 1, 0), "xz": (3, 1, 2, 0)}
        return names | {"yz": (2, 1, 3, 0), "zx": (1, 3, 2, 0), "zy": (1, 2, 3, 0)}
    names = {"xy": (2, 1, 0), "yx": (1, 2, 0), "xz": (2, 0, 1)}
    return names | {"yz": (1, 0, 2), "zx": (0, 2, 1), "zy": (0, 1, 2)}


class Grid:
    def __init__(self):
        self.count = lax.axis_size("seq")
        self.dims = seq_dims(self.count)
        self.orders = seq_orders(self.count)
        self.axes = len(self.dims)
        self.me = lax.axis_index("seq")
        self.tile = lax.axis_index("tile")
        self.strides = [1]
        for size in self.dims[:0:-1]:
            self.strides.insert(0, self.strides[0] * size)
        self.places = [
            lax.rem(self.me // stride, size) for stride, size in zip(self.strides, self.dims)
        ]

    def along(self, axis, step):
        place = self.places[axis]
        there = lax.rem(place + step, self.dims[axis])
        return there, (self.me + (there - place) * self.strides[axis], self.tile)

    def other(self):
        return (self.me, 1 - self.tile)

    def peers(self, phase, order):
        if phase == 0:
            return [self.other()]
        axis = order[phase - 1]
        return [self.along(axis, step)[1] for step in range(1, self.dims[axis])]

    def greet(self, barrier):
        peers = [self.other()]
        for axis in range(self.axes):
            peers += [self.along(axis, step)[1] for step in range(1, self.dims[axis])]
        for peer in peers:
            pl.semaphore_signal(barrier, inc=1, device_id=peer, device_id_type=MESH)
        return len(peers)

    def split(self, flat, dims):
        where = []
        for size in dims[::-1]:
            where.insert(0, lax.rem(flat, size))
            flat = flat // size
        return tuple(where)


def remote(source, target, send_sem, recv_sem, device):
    return pltpu.make_async_remote_copy(
        src_ref=source,
        dst_ref=target,
        send_sem=send_sem,
        recv_sem=recv_sem,
        device_id=device,
        device_id_type=MESH,
    )


class Unit:
    def __init__(self, grid, order, rows, source, out, came, part, sems, free, number, reuse, again):
        self.grid, self.order = grid, order
        self.rows, self.part = rows, part
        self.away, self.own, self.fetched = source
        self.out, self.came = out, came
        self.sends, self.recvs = sems
        self.free, self.number, self.reuse, self.again = free, number, reuse, again
        self.last = grid.axes + 1

    def rest(self, phase):
        taken = self.order[:phase]
        return [axis for axis in range(self.grid.axes) if axis not in taken]

    def held(self, phase):
        lead = () if phase == 0 else (0,)
        return self.came[phase], lead

    def slab(self, phase, there):
        before = self.rest(phase - 1)
        where = [slice(None)] * len(before)
        where[before.index(self.order[phase - 1])] = there
        ref, lead = self.held(phase - 1)
        return ref.at[lead + tuple(where) + (self.part,)]

    def landing(self, phase, step):
        dims = len(self.rest(phase))
        return self.came[phase].at[(step,) + (slice(None),) * dims + (self.part,)]

    def copies(self, phase):
        number, grid = self.number, self.grid
        if phase == 0:
            if self.fetched is not None:
                return [pltpu.make_async_copy(self.fetched, self.start_of(), self.sends.at[number, 0, 0])]
            return [
                remote(
                    self.away, self.start_of(), self.sends.at[number, 0, 0],
                    self.recvs.at[number, 0, 0], grid.other(),
                )
            ]
        if phase == self.last:
            mine = self.out.at[grid.tile, self.rows]
            return [
                remote(
                    mine, mine, self.sends.at[number, phase, 0], self.recvs.at[number, phase, 0],
                    grid.other(),
                )
            ]
        axis = self.order[phase - 1]
        out = []
        for step in range(1, grid.dims[axis]):
            there, device = grid.along(axis, step)
            out.append(
                remote(
                    self.slab(phase, there), self.landing(phase, step - 1),
                    self.sends.at[number, phase, step - 1], self.recvs.at[number, phase, step - 1],
                    device,
                )
            )
        return out

    def start_of(self):
        return self.came[0].at[(slice(None),) * self.grid.axes + (self.part,)]

    def start(self, phase):
        if self.again and phase < self.last:
            amount = len(self.grid.peers(phase, self.order))
            pl.semaphore_wait(self.free.at[self.again - 1, phase], amount)
        for copy in self.copies(phase):
            copy.start()

    def release(self, phase):
        for number, order in self.reuse:
            for peer in self.grid.peers(phase, order):
                pl.semaphore_signal(
                    self.free.at[number, phase], inc=1, device_id=peer, device_id_type=MESH
                )

    def wait(self, phase):
        for copy in self.copies(phase):
            copy.wait()

    def turn(self, phase):
        self.wait(phase)
        grid = self.grid
        if phase == 0:
            def step(at, _):
                where = grid.split(at, grid.dims) + (self.part,)
                self.came[0][where] = self.came[0][where] + self.own(grid.split(at, grid.dims))
                return 0

            if self.fetched is None:
                lax.fori_loop(0, grid.count, step, 0)
                return
            self.own(None)
            for piece in range(4):
                base = piece * (grid.count // 4)
                self.own(piece)

                def step_kept(at, _, base=base):
                    where = grid.split(at + base, grid.dims) + (self.part,)
                    self.came[0][where] = self.came[0][where] + self.own(at)
                    return 0

                lax.fori_loop(0, grid.count // 4, step_kept, 0)
            return
        axis = self.order[phase - 1]
        own = self.slab(phase, grid.places[axis])
        size = grid.dims[axis]
        if phase == grid.axes:
            total = own[...].astype(F32)
            for at in range(size - 1):
                total = total + self.came[phase][at, self.part].astype(F32)
            self.out[grid.tile, self.rows] = total.astype(BF16)
            self.release(phase - 1)
            self.release(phase)
            return
        dims = tuple(grid.dims[axis] for axis in self.rest(phase))
        steps = 1
        for size_of in dims:
            steps *= size_of

        def step(at, _):
            where = grid.split(at, dims)
            total = own[where]
            for other in range(size - 1):
                total = total + self.came[phase][(other,) + where + (self.part,)]
            self.came[phase][(0,) + where + (self.part,)] = total
            return 0

        lax.fori_loop(0, steps, step, 0)
        self.release(phase - 1)

    def on(self, phase):
        if phase < self.last:
            self.turn(phase)
            self.start(phase + 1)


class Pair:
    def __init__(self, *units):
        self.units = units

    def __getattr__(self, name):
        def each(phase):
            for unit in self.units:
                getattr(unit, name)(phase)

        return each


class Total:
    def __init__(self, grid, value, came, sends, recvs):
        self.order = grid.orders["xy"]
        self.last = grid.axes
        self.grid, self.value, self.came, self.sends, self.recvs = grid, value, came, sends, recvs

    def copies(self, phase):
        first = sum(len(self.grid.peers(before, self.order)) for before in range(phase))
        return [
            remote(
                self.value, self.came.at[first + at], self.sends.at[first + at],
                self.recvs.at[first + at], peer,
            )
            for at, peer in enumerate(self.grid.peers(phase, self.order))
        ]

    def start(self, phase):
        for copy in self.copies(phase):
            copy.start()

    def on(self, phase):
        if phase > self.last:
            return
        copies = self.copies(phase)
        for copy in copies:
            copy.wait()
        total = self.value[...]
        first = sum(len(self.grid.peers(before, self.order)) for before in range(phase))
        for at in range(len(copies)):
            total = total + self.came[first + at]
        self.value[...] = total
        if phase < self.last:
            self.start(phase + 1)


def unit_scratch(rows, width, order, dims):
    left = list(range(len(dims)))
    out = [pltpu.VMEM(dims + (rows, width), BF16)]
    for axis in order:
        left.remove(axis)
        rest = tuple(dims[other] for other in left)
        out.append(pltpu.VMEM((max(dims[axis] - 1, 1),) + rest + (rows, width), BF16))
    return out


def back_kernel(
    clip_big, d_out, came_out, d_in, came_in, third, second, mixed_t, query_t, key_t, value_t, normed_t, probs_t,
    wq_t, wk_t, wv_t, wo_t, mixed_s, query_s, key_s, value_s, pair, normed_s, probs_s,
    wq_s, wk_s, wv_s, wo_s, tok, hot, table, gain_one, gain_two, small_ffn,
    token_grad, sum_out, sum_in, sum_time, sum_space, small,
    pool, turned, held, probs, d_weights, kept, came_key, came_value, swapped, *rest,
):
    grid = Grid()
    deep = grid.axes + 1
    unit_bufs, rest = rest[: 4 * deep], rest[4 * deep :]
    (totals, total_came, loads, unit_sends, unit_recvs, free, swap_sends, swap_recvs,
     total_sends, total_recvs, pair_sems) = rest
    rows, width = pool.shape[1:]
    _clip, offset, is_big = where_am_i(clip_big)
    swap = Swap(
        False, offset, is_big, turned, _Slots(pool, (11, 6)), swapped, (swap_sends, swap_recvs), 2
    )
    barrier = pltpu.get_barrier_semaphore()
    pl.semaphore_wait(barrier, grid.greet(barrier) + swap.greet(barrier))

    load = Loads(loads)
    orders = grid.orders
    share = d_out.shape[-2]
    every = (slice(None),) * grid.axes

    ways = (("xy", "yx"), ("zx", "zy"), ("xz", "yz", "xz", "yz"), ("yx", "xy", "xy", "yx"))
    ways = [[orders[name] for name in group] for group in ways]

    def buffers(group, which):
        first = (group % 2) * 2 * deep + which * deep
        return unit_bufs[first : first + deep]

    def fetched(group, which, keep, landed, out):
        half = share // 2
        rows_of = pl.ds(which * half, half)
        number = 2 * group + which
        first = (1, grid.dims[0] * grid.dims[1] // 4) if grid.dims[0] < 4 else (grid.dims[0] // 4, grid.dims[1])

        def own(at):
            if at is None:
                return None
            if isinstance(at, int):
                copy = pltpu.make_async_copy(
                    keep.at[
                        (
                            pl.ds(at * first[0] * first[1] // grid.dims[1], first[0]),
                            pl.ds(at * first[1] % grid.dims[1], first[1]),
                        )
                        + every[2:]
                        + (rows_of,)
                    ],
                    kept,
                    unit_sends.at[number, 0, 1],
                )
                copy.start()
                copy.wait()
                return None
            return kept[grid.split(at, first + grid.dims[2:])]

        reuse = [
            (4 * group + 2 * which + sub, ways[group + 2][2 * which + sub]) for sub in range(2)
        ]
        return Unit(
            grid, ways[group][which], rows_of, (None, own, landed.at[every + (rows_of,)]), out,
            buffers(group, which), pl.ds(0, half), (unit_sends, unit_recvs), free, number, reuse, 0,
        )

    def made(group, which, out):
        quarter = share // 4
        rows_of = pl.ds(which * quarter, quarter)

        def own(where):
            return d_weights[(grid.tile,) + where + (rows_of,)]

        return Unit(
            grid, ways[group][which], rows_of,
            (d_weights.at[(1 - grid.tile,) + every + (rows_of,)], own, None), out,
            buffers(group, which // 2), pl.ds((which % 2) * quarter, quarter),
            (unit_sends, unit_recvs), free, 4 + 4 * (group - 2) + which, [],
            4 * (group - 2) + which + 1,
        )

    p0 = Pair(*[fetched(0, which, d_out, came_out, sum_out) for which in range(2)])
    p1 = Pair(*[fetched(1, which, d_in, came_in, sum_in) for which in range(2)])
    p2 = Pair(*[made(2, which, sum_time) for which in range(4)])
    p3o, p3q, p3k, p3v = [made(3, which, sum_space) for which in range(4)]
    p0.start(0)
    p1.start(0)

    in_low = load(third, pool.at[0])
    in_mixed = load(mixed_t, pool.at[2])
    weights = [load(source, held.at[at]) for at, source in enumerate((wo_t, wq_t, wk_t, wv_t))]
    ins = [load(source, pool.at[3 + at]) for at, source in enumerate((query_t, key_t, value_t))]
    ins += [load(probs_t.at[at], probs.at[at]) for at in range(2)]
    late = [load(second, pool.at[1]), load(normed_t, pool.at[6])]
    p0.on(0)
    p1.on(0)
    in_low.wait()
    in_mixed.wait()
    flat_weights = d_weights.reshape((2, grid.count) + d_weights.shape[-2:])
    weight_grad(flat_weights, 0, pool[0], pool.at[2])
    weights[0].wait()

    def mix_back(grad, target):
        for part in range(4):
            side = slice(part * 256, (part + 1) * 256)
            pool[target, :, side] = dot_nt(pool[grad], held[0, side, :]).astype(BF16)

    mix_back(0, 7)
    weights.append(load(wo_s, held.at[0]))
    for copy in ins:
        copy.wait()

    def time_group(at, _):
        here = pl.ds(pl.multiple_of(at * KEYS, KEYS), KEYS)
        for two in range(8):
            side = pl.ds(two * WIDE, WIDE)
            grads = attend_backward(
                probs[at, two], pool[3, here, side], pool[4, here, side], pool[5, here, side],
                pool[7, here, side],
            )
            for target, grad in enumerate(grads):
                pool[8 + target, here, side] = grad.astype(BF16)
        return 0

    lax.fori_loop(0, rows // KEYS, time_group, 0)
    ins = [
        load(source, pool.at[target])
        for source, target in (
            (query_s, 2), (key_s, 3), (value_s, 4), (pair.at[0], 5), (pair.at[1], 7)
        )
    ]
    ins += [
        load(probs_s.at[at], probs.at[at // 2, :, pl.ds(at % 2 * 2 * WIDE, 2 * WIDE)])
        for at in range(4)
    ]
    for copy in late:
        copy.wait()
    for at in range(3):
        weight_grad(flat_weights, at + 1, pool[8 + at], pool.at[6])
    for at in range(3):
        weights[at + 1].wait()

    def time_rows(step, carry):
        here = pl.ds(pl.multiple_of(step * 256, 256), 256)
        grad = (
            dot_nt(pool[8, here, :], held[1])
            + dot_nt(pool[9, here, :], held[2])
            + dot_nt(pool[10, here, :], held[3])
        )
        hat, rate = normalise(pool[1, here, :].astype(F32))
        total = pool[0, here, :].astype(F32) + norm_backward(grad, hat, rate, gain_two[...])
        turned[pl.ds(step * 16, 16)] = total.astype(BF16).reshape(16, 16, width)
        return (
            carry[0] + jnp.sum(grad * hat, axis=0, keepdims=True),
            carry[1] + jnp.sum(grad, axis=0, keepdims=True),
        )

    zero = jnp.zeros((1, width), F32)
    time_norm = (zero, zero)
    for side in range(2):
        time_norm = time_rows(side, time_norm)
        swap.send(side)
    weights += [load(source, held.at[at + 1]) for at, source in enumerate((wq_s, wk_s, wv_s))]
    in_mixed = load(mixed_s, pool.at[10])
    p0.on(1)
    p2.start(0)
    p2.turn(0)
    p1.on(1)
    swap.wait()
    swap.place(pool.at[1])
    in_normed = load(normed_s, pool.at[0])
    p0.on(2)
    p2.start(1)

    in_mixed.wait()
    weight_grad(flat_weights, 0, pool[1], pool.at[10])
    weights[4].wait()
    mix_back(1, 8)
    p3o.start(0)
    for copy in ins:
        copy.wait()

    def space_group(at, _):
        here = pl.ds(pl.multiple_of(at * WIDE, WIDE), WIDE)
        lower = pl.ds(pl.multiple_of(lax.rem(at, 2) * 2 * WIDE, 2 * WIDE), 2 * WIDE)
        for two in range(8):
            side = pl.ds(two * WIDE, WIDE)
            keys = jnp.concatenate([pool[3, here, side], pool[5, here, side]], axis=0)
            values = jnp.concatenate([pool[4, here, side], pool[7, here, side]], axis=0)
            grad_query, grad_key, grad_value = attend_backward(
                probs[at // 2, two, lower], pool[2, here, side], keys, values, pool[8, here, side]
            )
            pool[9, here, side] = grad_query.astype(BF16)
            pool[10, here, side] = grad_key[:WIDE].astype(BF16)
            pool[11, here, side] = grad_value[:WIDE].astype(BF16)
            pool[6, here, side] = grad_key[WIDE:].astype(BF16)
            turned[pl.ds(at * 8, 8), :, side] = grad_value[WIDE:].astype(BF16).reshape(8, 16, WIDE)
        return 0

    lax.fori_loop(0, rows // (2 * WIDE), space_group, 0)
    p0.on(3)
    p1.on(2)
    p3o.on(0)
    lax.fori_loop(rows // (2 * WIDE), rows // WIDE, space_group, 0)
    across = [
        remote(
            source, target, pair_sems.at[0, at], pair_sems.at[1, at], grid.other(),
        )
        for at, (source, target) in enumerate(((pool.at[6], came_key), (turned, came_value)))
    ]
    for copy in across:
        copy.start()
    in_tok = load(tok, pool.at[2])
    in_normed.wait()
    weight_grad(flat_weights, 1, pool[9], pool.at[0])
    p3q.start(0)
    p2.on(1)
    for at, copy in enumerate(across):
        copy.wait()
        came = (came_key, came_value)[at][...].reshape(rows, width)
        pool[10 + at] = pool[10 + at] + came
        weight_grad(flat_weights, 2 + at, pool[10 + at], pool.at[0])
        (p3k, p3v)[at].start(0)
    p3q.on(0)
    p3k.on(0)
    p3v.on(0)
    p0.on(4)
    p1.on(3)
    for at in range(3):
        weights[5 + at].wait()
    in_tok.wait()

    def space_rows(step, carry):
        here = pl.ds(pl.multiple_of(step * 256, 256), 256)
        grad = (
            dot_nt(pool[9, here, :], held[1])
            + dot_nt(pool[10, here, :], held[2])
            + dot_nt(pool[11, here, :], held[3])
        )
        first = pool[2, here, :].astype(F32) + dot(hot[here, :], table[...])
        hat, rate = normalise(first)
        total = pool[1, here, :].astype(F32) + norm_backward(grad, hat, rate, gain_one[...])
        high = total.astype(BF16)
        pool[1, here, :] = high
        rest = (total - high.astype(F32)).astype(BF16)
        chosen = hot[here, :]
        return (
            carry[0] + jnp.sum(grad * hat, axis=0, keepdims=True),
            carry[1] + jnp.sum(grad, axis=0, keepdims=True),
            carry[2] + dot_tn(chosen, high)[:8] + dot_tn(chosen, rest)[:8],
        )

    p3o.on(1)
    space_norm = lax.fori_loop(0, rows // 256, space_rows, (zero, zero, jnp.zeros((8, width), F32)))
    out_grad = load(pool.at[1], token_grad)
    totals[0:8] = space_norm[2]
    totals[8:16] = jnp.concatenate(
        [space_norm[0], time_norm[0], space_norm[1], time_norm[1], jnp.zeros((4, width), F32)], axis=0
    )
    totals[16:24] = small_ffn[...]
    total = Total(grid, totals, total_came, total_sends, total_recvs)
    total.start(0)
    p2.on(2)
    p3q.on(1)
    p1.on(4)
    p3o.on(2)
    total.on(0)
    p3v.on(1)
    p3k.on(1)
    p2.on(3)
    p3q.on(2)
    total.on(1)
    p3o.on(3)
    p3v.on(2)
    p3k.on(2)
    p3q.on(3)
    total.on(2)
    p2.on(4)
    p3v.on(3)
    p3k.on(3)
    total.on(3)
    p3o.on(4)
    p3q.on(4)
    p3v.on(4)
    p3k.on(4)
    total.on(4)
    small[...] = totals[...]
    for unit in (p0, p1, p2, p3o, p3q, p3k, p3v):
        unit.wait(grid.axes + 1)
    out_grad.wait()


class _Slots:
    def __init__(self, pool, slots):
        self.pool, self.slots = pool, slots

    class _At:
        def __init__(self, slots):
            self.slots = slots

        def __getitem__(self, slot):
            return self.slots.pool.at[self.slots.slots[slot // 4], pl.ds(slot % 4 * 128, 128)]

    @property
    def at(self):
        return _Slots._At(self)

    def __setitem__(self, where, value):
        slot, rows = where
        first = slot % 4 * 128
        self.pool[self.slots[slot // 4], first + rows.start : first + rows.stop] = value


def back(args, number):
    args = list(args)
    rows, width = args[5].shape
    count = lax.axis_size("seq")
    dims = seq_dims(count)
    share, group = args[1].shape[-2:]
    dma = pltpu.SemaphoreType.DMA
    lead = (1, dims[0] * dims[1] // 4) if dims[0] < 4 else (dims[0] // 4, dims[1])
    scratch = [
        pltpu.VMEM((12, rows, width), BF16),
        pltpu.VMEM((rows // 16, 16, width), BF16),
        pltpu.VMEM((4, width, width), BF16),
        pltpu.VMEM((2, 8, 2 * KEYS, KEYS), BF16),
        pltpu.VMEM((2,) + dims + (share, group), BF16),
        pltpu.VMEM(lead + dims[2:] + (share // 2, group), BF16),
        pltpu.VMEM((rows, width), BF16),
        pltpu.VMEM((rows // 16, 16, width), BF16),
        pltpu.VMEM((7, 128, width), BF16),
    ]
    for _ in range(2):
        for name in ("xy", "yx"):
            scratch += unit_scratch(share // 2, group, seq_orders(count)[name], dims)
    most = max(max(dims) - 1, 2)
    peers = 1 + sum(dims) - len(dims)
    scratch += [
        pltpu.VMEM((24, width), F32),
        pltpu.VMEM((peers, 24, width), F32),
        dma((40,)),
        dma((12, len(dims) + 2, most)),
        dma((12, len(dims) + 2, most)),
        pltpu.SemaphoreType.REGULAR((8, len(dims) + 1)),
        dma((14,)),
        dma((14,)),
        dma((peers,)),
        dma((peers,)),
        dma((2, 2)),
    ]
    for at in range(1, 5):
        args[at] = args[at].reshape(dims + (share, group))
    final = shape_of((2, share, group), BF16)
    return pl.pallas_call(
        back_kernel,
        out_shape=[shape_of((rows, width), BF16)] + [final] * 4 + [shape_of((24, width), F32)],
        in_specs=[IN_SMEM] + [IN_HBM] * 28 + [WHOLE] * 5,
        out_specs=[IN_HBM] + [WHOLE] * 5,
        scratch_shapes=scratch,
        compiler_params=params(collective_id=number, has_side_effects=True),
    )(*args)


def finish_kernel(sum_out, sum_in, sum_time, sum_space, small, *refs):
    table, gain, shift, inner, outer, bias_in, bias_out = refs[:7]
    weights, rolled = refs[7:-1], refs[-1]
    count = lax.axis_size("seq")
    me = lax.axis_index("seq")
    width = small.shape[1]
    part = width // count
    hidden = bias_in.shape[1]
    for half in range(2):
        for at in range(4):
            rows = slice(at * part, (at + 1) * part)
            first = half * (width // 2)
            for base, source in ((0, sum_space), (4, sum_time)):
                weights[base + at][:, first : first + width // 2] = source[half, rows].astype(F32)
            first = (half * 4 + at) * CHUNK
            outer[:, first : first + CHUNK] = sum_out[half, rows].astype(F32)
        if inner.shape[1] == KEYS:
            for at in range(2):
                first = half * 2 * KEYS + at * KEYS
                inner[first : first + KEYS, :] = sum_in[half, :, at * KEYS : (at + 1) * KEYS].astype(F32)
    rolled[...] = pltpu.roll(small[...], lax.rem(width - me * part, width), 1)
    table[...] = rolled[0:8, :part]
    gain[...] = jnp.concatenate([rolled[8:10, :part], rolled[16:17, :part]], axis=0)
    shift[...] = jnp.concatenate([rolled[10:12, :part], rolled[17:18, :part]], axis=0)
    bias_out[...] = rolled[18:19, :part]
    begin = me * hidden
    rolled[...] = pltpu.roll(small[...], lax.rem(width - lax.rem(begin, width), width), 1)
    for at in range(4):
        @pl.when(begin // width == at)
        def _(at=at):
            bias_in[...] = rolled[19 + at : 20 + at, :hidden]


def finish(sums, small, hidden):
    count = lax.axis_size("seq")
    width = small.shape[1]
    part = width // count
    outs = [
        shape_of((8, part), F32), shape_of((3, part), F32), shape_of((3, part), F32),
        shape_of((width, hidden // count), F32), shape_of((part, hidden), F32),
        shape_of((1, hidden // count), F32), shape_of((1, part), F32),
    ]
    out = pl.pallas_call(
        finish_kernel,
        out_shape=outs + [shape_of((part, width), F32)] * 8,
        in_specs=[WHOLE] * 5,
        out_specs=[WHOLE] * 15,
        scratch_shapes=[pltpu.VMEM(small.shape, F32)],
        compiler_params=params(),
    )(*sums, small)
    out = list(out)
    out[4] = out[4].T
    out[7:] = [value.T for value in out[7:]]
    if hidden // count != KEYS:
        inner = sums[1].reshape(2, KEYS, 2, hidden // count).transpose(0, 2, 1, 3)
        out[3] = inner.reshape(width, -1).astype(F32)
    return out


def where_am_i(clip_big):
    me = lax.axis_index("seq")
    span = (GRID_BIG // GRID_SMALL) ** 2
    start, clip, offset, is_big = jnp.int32(0), jnp.int32(0), jnp.int32(0), jnp.int32(0)
    for at in range(clip_big.shape[0]):
        big = clip_big[at]
        size = jnp.where(big == 1, span, 1)
        inside = (me >= start) & (me < start + size)
        clip = jnp.where(inside, at, clip)
        offset = jnp.where(inside, me - start, offset)
        is_big = jnp.where(inside, big, is_big)
        start = start + size
    return clip, offset, is_big


class Loads:
    def __init__(self, sems):
        self.sems, self.used = sems, 0

    def __call__(self, source, target):
        copy = pltpu.make_async_copy(source, target, self.sems.at[self.used])
        self.used += 1
        copy.start()
        return copy


def first_kernel(
    clip_big, actions, tok, action_table, gain, shift, cot, wq, wk, wv, wo,
    normed_out, query_out, key_out, value_out, pair_out, mixed_out, probs_out, second_out, cot_out, hot, table,
    held, normed, query, key, value, pair, mixed, probs, second, turned, staged, came, cot_staged, cot_came,
    loads, pair_sems, swap_sends, swap_recvs, cot_sends, cot_recvs,
):
    rows, width = tok.shape
    clip, offset, is_big = where_am_i(clip_big)
    grid = Grid()
    swap = Swap(True, offset, is_big, turned, staged, came, (swap_sends, swap_recvs), 2)
    cot_swap = Swap(True, offset, is_big, cot, cot_staged, cot_came, (cot_sends, cot_recvs), 2)
    barrier = pltpu.get_barrier_semaphore()
    pl.semaphore_signal(barrier, inc=1, device_id=grid.other(), device_id_type=MESH)
    peers = 1 + swap.greet(barrier)
    load = Loads(loads)
    weights = [load(source, held.at[at]) for at, source in enumerate((wk, wv, wq, wo))]
    pl.semaphore_wait(barrier, peers)
    cot_swap.send(0)

    last = actions.shape[0] - 1
    base = clip * FRAMES + offset * (FRAMES // (REACH + 1))
    row = lax.broadcasted_iota(jnp.int32, (rows, WIDE), 0)
    frame_of = jnp.where(jnp.full((rows, WIDE), is_big, jnp.int32) == 1, row // WIDE, row // 32)
    action = jnp.zeros((rows, WIDE), jnp.int32)
    for frame in range(FRAMES):
        action = jnp.where(frame_of == frame, actions[jnp.minimum(base + frame, last)], action)
    lane = lax.broadcasted_iota(jnp.int32, (rows, WIDE), 1)
    hot[...] = jnp.where((action == lax.rem(lane, 8)) & (lane < 24), 1.0, 0.0).astype(BF16)
    exact = action_table[...]
    high = exact.astype(BF16)
    left = exact - high.astype(F32)
    middle = left.astype(BF16)
    low = left - middle.astype(F32)
    table[...] = jnp.concatenate(
        [high.astype(F32), middle.astype(F32), low, jnp.zeros((WIDE - 24, width), F32)], axis=0
    ).astype(BF16)

    def norm_rows(at, _):
        here = pl.ds(pl.multiple_of(at * 128, 128), 128)
        hat, _rate = normalise(tok[here, :].astype(F32) + dot(hot[here, :], table[...]))
        normed[here, :] = (hat * gain[...] + shift[...]).astype(BF16)
        return 0

    lax.fori_loop(0, rows // 128, norm_rows, 0)
    outs = [load(normed, normed_out)]
    across = []
    for at, (target, out) in enumerate(((key, key_out), (value, value_out), (query, query_out))):
        weights[at].wait()
        for part in range(4):
            side = pl.ds(part * 256, 256)
            target[:, side] = dot(normed[...], held[at, :, side]).astype(BF16)
        if at < 2:
            copy = remote(
                target, pair.at[at], pair_sems.at[0, at], pair_sems.at[1, at], grid.other()
            )
            copy.start()
            across.append(copy)
        outs.append(load(target, out))
    for copy in across:
        copy.wait()
    outs.append(load(pair, pair_out))
    weights[3].wait()
    bias = spatial_bias(is_big, 2 * WIDE)

    def group(at, _):
        here = pl.ds(pl.multiple_of(at * WIDE, WIDE), WIDE)
        for two in range(8):
            side = pl.ds(two * WIDE, WIDE)
            keys = jnp.concatenate([key[here, side], pair[0, here, side]], axis=0)
            values = jnp.concatenate([value[here, side], pair[1, here, side]], axis=0)
            prob, out = attend(query[here, side], keys, values, bias)
            probs[at, two] = prob
            mixed[here, side] = out.astype(BF16)
        return 0

    for half in range(2):
        lax.fori_loop(2 * half, 2 * half + 2, group, 0)
        here = slice(half * KEYS, (half + 1) * KEYS)
        blocks = slice(half * 16, (half + 1) * 16)
        for part in range(4):
            side = slice(part * 256, (part + 1) * 256)
            first = tok[here, side].astype(F32) + dot(hot[here, :], table[:, side])
            total = first + dot(mixed[here, :], held[3, :, side])
            turned[blocks, :, side] = total.astype(BF16).reshape(16, 16, 256)
        swap.send(half)
    outs += [load(mixed, mixed_out), load(probs, probs_out)]
    cot_swap.wait(0)
    half = pl.ds(0, cot_out.shape[1])
    outs.append(load(cot_came.at[:, half], cot_out))
    swap.wait()
    swap.place(second)
    outs.append(load(second, second_out))
    for copy in outs:
        copy.wait()


def first(clip_big, actions, tok, action_table, gain, shift, cot, wq, wk, wv, wo, number):
    rows, width = tok.shape
    wide = shape_of((rows, width), BF16)
    probs = (rows // WIDE, 8, 2 * WIDE, KEYS)
    dma = pltpu.SemaphoreType.DMA
    full = pltpu.VMEM((rows, width), BF16)
    return pl.pallas_call(
        first_kernel,
        out_shape=[
            wide, wide, wide, wide, shape_of((2, rows, width), BF16), wide, shape_of(probs, BF16), wide,
            shape_of((7, 64, width), BF16), shape_of((rows, WIDE), BF16), shape_of((WIDE, width), BF16),
        ],
        in_specs=[IN_SMEM] * 2 + [WHOLE] * 5 + [IN_HBM] * 4,
        out_specs=[IN_HBM] * 9 + [WHOLE] * 2,
        scratch_shapes=[
            pltpu.VMEM((4, width, width), BF16), full, full, full, full,
            pltpu.VMEM((2, rows, width), BF16), full, pltpu.VMEM(probs, BF16), full,
            pltpu.VMEM((rows // 16, 16, width), BF16),
            *[pltpu.VMEM((7, 128, width), BF16)] * 4,
            dma((16,)), dma((2, 2)), *[dma((14,))] * 4,
        ],
        compiler_params=params(collective_id=number, has_side_effects=True),
    )(
        clip_big, actions, tok, action_table, gain, shift, cot.reshape(rows // 16, 16, width),
        wq, wk, wv, wo,
    )


def middle_kernel(
    clip_big, second, cot_in, cot_half, gain_two, shift_two, gain, shift, bias_in, bias_out, wq, wk, wv, wo, win, wout,
    normed_out, query_out, key_out, value_out, probs_out, mixed_two_out, mixed_out, third_out,
    d_in, came_in, d_out, came_out, small,
    pool, probs, held, w_in, w_out, active, slope, third, normed_t, cot_t, turned,
    staged, came_cot, came_mixed, outgoing,
    loads, cot_sends, cot_recvs, mixed_sends, mixed_recvs, out_sems, grad_recvs, prob_sems,
):
    rows, width = third.shape
    hidden = w_in.shape[1]
    chunks = hidden // CHUNK
    _clip, offset, is_big = where_am_i(clip_big)
    cot_swap = Swap(True, offset, is_big, turned, staged, came_cot, (cot_sends, cot_recvs), 2)
    mixed_swap = Swap(False, offset, is_big, turned, staged, came_mixed, (mixed_sends, mixed_recvs), 2)
    barrier = pltpu.get_barrier_semaphore()
    tile = lax.axis_index("tile")
    other = (lax.axis_index("seq"), 1 - tile)
    pl.semaphore_signal(barrier, inc=1, device_id=other, device_id_type=MESH)
    peers = 1 + cot_swap.greet(barrier)
    load = Loads(loads)
    cot_load = load(cot_in, turned)
    second_load = load(second, pool.at[0])
    weights = [load(source, held.at[at]) for at, source in enumerate((wq, wk, wv, wo))]
    weights += [load(win, w_in), load(wout, w_out)]
    cot_load.wait()
    pl.semaphore_wait(barrier, peers)
    cot_swap.send(1)
    cot_load = load(cot_half, came_cot.at[:, pl.ds(0, cot_half.shape[1])])
    second_load.wait()

    def norm_two(at, _):
        here = pl.ds(pl.multiple_of(at * 128, 128), 128)
        hat, _rate = normalise(pool[0, here, :].astype(F32))
        pool[4, here, :] = (hat * gain_two[...] + shift_two[...]).astype(BF16)
        return 0

    lax.fori_loop(0, rows // 128, norm_two, 0)
    outs = [load(pool.at[4], normed_out)]
    for at, out in enumerate((query_out, key_out, value_out)):
        weights[at].wait()
        for part in range(4):
            side = slice(part * 256, (part + 1) * 256)
            pool[1 + at, :, side] = dot(pool[4], held[at, :, side]).astype(BF16)
        outs.append(load(pool.at[1 + at], out))
    bias = temporal_bias(2 * KEYS)

    def probs_copy(at):
        return pltpu.make_async_copy(probs, probs_out.at[at], prob_sems.at[at])

    def group(at, _):
        @pl.when(at > 0)
        def _():
            probs_copy(0).wait()

        here = pl.ds(pl.multiple_of(at * KEYS, KEYS), KEYS)
        for two in range(8):
            side = pl.ds(two * WIDE, WIDE)
            prob, out = attend(pool[1, here, side], pool[2, here, side], pool[3, here, side], bias)
            probs[two] = prob
            pool[5, here, side] = out.astype(BF16)
        probs_copy(at).start()
        return 0

    lax.fori_loop(0, rows // KEYS, group, 0)
    outs += [load(pool.at[5], mixed_two_out)]
    weights[3].wait()
    for part in range(4):
        side = slice(part * 256, (part + 1) * 256)
        third[:, side] = pool[0, :, side].astype(F32) + dot(pool[5], held[3, :, side])
    outs[0].wait()

    def norm_three(at, _):
        here = pl.ds(pl.multiple_of(at * 128, 128), 128)
        hat, _rate = normalise(third[here, :])
        pool[4, here, :] = (hat * gain[...] + shift[...]).astype(BF16)
        return 0

    lax.fori_loop(0, rows // 128, norm_three, 0)
    normed_t[...] = pool[4].T
    weights[4].wait()

    def forward(at, _):
        side = pl.ds(pl.multiple_of(at * KEYS, KEYS), KEYS)
        inner = dot(pool[4], w_in[:, side]) + bias_in[:, side]
        square = inner * inner
        curve = jnp.tanh(ROOT * (inner + 0.044715 * inner * square))
        active[:, side] = (0.5 * inner * (1.0 + curve)).astype(BF16)
        slope[:, side] = (
            0.5 * (1.0 + curve)
            + (0.5 * ROOT) * inner * (1.0 - curve * curve) * (1.0 + (3 * 0.044715) * square)
        ).astype(BF16)
        return 0

    lax.fori_loop(0, hidden // KEYS, forward, 0)
    cot_load.wait()
    cot_swap.wait(1)
    cot_swap.place(pool.at[0])
    weights[5].wait()

    for half in range(2):
        here, blocks = pl.ds(half * KEYS, KEYS), slice(half * 16, (half + 1) * 16)
        for part in range(width // KEYS):
            side = slice(part * KEYS, (part + 1) * KEYS)
            total = third[here, side] + bias_out[:, side] + dot(active[here, :], w_out[:, side])
            turned[blocks, :, side] = total.astype(BF16).reshape(16, 16, KEYS)
        mixed_swap.send(half)
    cot_t[...] = pool[0].T
    small[2:3, :] = jnp.sum(pool[0].astype(F32), axis=0, keepdims=True)

    def out_copy(at, slot, away):
        share = outgoing.shape[2]
        where = (slice(None), pl.ds(lax.rem(at, 4) * share, share))
        source = outgoing.at[slot]
        if away:
            return remote(
                source, came_out.at[where], out_sems.at[slot, 0], grad_recvs.at[lax.rem(at, 4), 0], other
            )
        return pltpu.make_async_copy(source, d_out.at[where], out_sems.at[slot, 0])

    def in_copy(at, slot, part, away):
        which = 1 - tile if away else tile
        source = outgoing.at[2 + slot, pl.ds((which * 2 + part) * 4, 4)]
        if away:
            return remote(
                source, came_in.at[at * 2 + part], out_sems.at[slot, 1 + part],
                grad_recvs.at[at, 1 + part], other,
            )
        return pltpu.make_async_copy(source, d_in.at[at * 2 + part], out_sems.at[slot, 3 + part])

    def start_out(at, slot):
        @pl.when(at // 4 == tile)
        def _():
            out_copy(at, slot, False).start()

        @pl.when(at // 4 != tile)
        def _():
            out_copy(at, slot, True).start()

        for part in range(2):
            in_copy(at, slot, part, False).start()
            in_copy(at, slot, part, True).start()

    def sent_out(at, slot):
        @pl.when(at // 4 == tile)
        def _():
            out_copy(at, slot, False).wait()

        @pl.when(at // 4 != tile)
        def _():
            out_copy(at, slot, True).wait_send()

        for part in range(2):
            in_copy(at, slot, part, False).wait()
            in_copy(at, slot, part, True).wait_send()

    def backward(at, _):
        slot = lax.rem(at, 2)

        @pl.when(at >= 2)
        def _():
            sent_out(at - 2, slot)

        side = pl.ds(pl.multiple_of(at * CHUNK, CHUNK), CHUNK)
        wide = slope[:, side].astype(F32) * dot_nt(pool[0], w_out[side, :])
        grad_inner = wide.astype(BF16)
        slope[:, side] = grad_inner
        lanes = pl.ds(pl.multiple_of(lax.rem(at, 2) * CHUNK, CHUNK), CHUNK)
        small[pl.ds(3 + at // 2, 1), lanes] = jnp.sum(grad_inner.astype(F32), axis=0, keepdims=True)
        outgoing[slot] = dot(cot_t[...], active[:, side]).astype(BF16).reshape(outgoing.shape[1:])
        for top in range(4):
            block = dot(normed_t[top * 256 : (top + 1) * 256, :], grad_inner).astype(BF16)
            for part in range(2):
                first = ((top // 2) * 2 + part) * 4
                outgoing[
                    2 + slot, first : first + 4, :, (top % 2) * KEYS : (top % 2 + 1) * KEYS
                ] = block[:, part * KEYS : (part + 1) * KEYS].reshape(4, 64, KEYS)
        start_out(at, slot)
        return 0

    lax.fori_loop(0, chunks, backward, 0)
    for copy in outs[1:]:
        copy.wait()
    probs_copy(1).wait()

    def back_rows(step, carry):
        here = pl.ds(pl.multiple_of(step * KEYS, KEYS), KEYS)
        hat, rate = normalise(third[here, :])
        grad = dot_nt(slope[here, :], w_in[...])
        pool[2, here, :] = (
            pool[0, here, :].astype(F32) + norm_backward(grad, hat, rate, gain[...])
        ).astype(BF16)
        return (
            carry[0] + jnp.sum(grad * hat, axis=0, keepdims=True),
            carry[1] + jnp.sum(grad, axis=0, keepdims=True),
        )

    zero = jnp.zeros((1, width), F32)
    sums = lax.fori_loop(0, rows // KEYS, back_rows, (zero, zero))
    small[0:1, :] = sums[0]
    small[1:2, :] = sums[1]
    small[7:8, :] = zero
    last = [load(pool.at[2], third_out)]
    mixed_swap.wait()
    mixed_swap.place(pool.at[1])
    last.append(load(pool.at[1], mixed_out))
    for at in (chunks - 2, chunks - 1):
        sent_out(at, at % 2)
    for at in range(chunks):
        if at < 4:
            out_copy(at, 0, True).wait_recv()
        for part in range(2):
            in_copy(at, 0, part, True).wait_recv()
    for copy in last:
        copy.wait()


def middle(args, number):
    clip_big, second, cot = args[:3]
    win = args[14]
    rows, width = second.shape
    hidden = win.shape[1]
    wide = shape_of((rows, width), BF16)
    probs = (rows // KEYS, 8, 2 * KEYS, KEYS)
    dma = pltpu.SemaphoreType.DMA
    block = pltpu.VMEM((7, 128, width), BF16)
    args = list(args)
    args[2] = cot.reshape(rows // 16, 16, width)
    return pl.pallas_call(
        middle_kernel,
        out_shape=[
            wide, wide, wide, wide, shape_of(probs, BF16), wide, wide, wide,
            *[shape_of((hidden // KEYS, 4, 64, 2 * KEYS), BF16)] * 2,
            *[shape_of((16, KEYS, CHUNK), BF16)] * 2,
            shape_of((8, width), F32),
        ],
        in_specs=[IN_SMEM] + [IN_HBM] * 3 + [WHOLE] * 6 + [IN_HBM] * 6,
        out_specs=[IN_HBM] * 12 + [WHOLE],
        scratch_shapes=[
            pltpu.VMEM((6, rows, width), BF16),
            pltpu.VMEM(probs[1:], BF16),
            pltpu.VMEM((4, width, width), BF16),
            pltpu.VMEM((width, hidden), BF16),
            pltpu.VMEM((hidden, width), BF16),
            pltpu.VMEM((rows, hidden), BF16),
            pltpu.VMEM((rows, hidden), BF16),
            pltpu.VMEM((rows, width), F32),
            pltpu.VMEM((width, rows), BF16),
            pltpu.VMEM((width, rows), BF16),
            pltpu.VMEM((rows // 16, 16, width), BF16),
            block, block, block,
            pltpu.VMEM((4, 16, 64, CHUNK), BF16),
            dma((24,)), *[dma((14,))] * 4, dma((2, 5)), dma((8, 3)), dma((2,)),
        ],
        compiler_params=params(collective_id=number, has_side_effects=True),
    )(*args)


def on_device(
    tokens,
    cotangent,
    clip_big,
    actions,
    action_table,
    norm_gain,
    norm_bias,
    spatial_q,
    spatial_k,
    spatial_v,
    spatial_o,
    temporal_q,
    temporal_k,
    temporal_v,
    temporal_o,
    ffn_in,
    ffn_bias_in,
    ffn_out,
    ffn_bias_out,
):
    tok = tokens[0]
    rows, width = tok.shape
    count = lax.axis_size("seq")
    gains = [norm_gain[at : at + 1] for at in range(3)]
    shifts = [norm_bias[at : at + 1] for at in range(3)]

    normed_one, query_one, key_one, value_one, pair_one, mixed_one, probs_one, second, cot_half, hot, table = first(
        clip_big, actions, tok, action_table, gains[0], shifts[0], cotangent[0],
        spatial_q, spatial_k, spatial_v, spatial_o, 1,
    )
    (normed_two, query_two, key_two, value_two, probs_two, mixed_two, mixed, grad_third, d_in, came_in,
     d_out, came_out, small_ffn) = middle(
        [
            clip_big, second, cotangent[0], cot_half, gains[1], shifts[1], gains[2], shifts[2],
            ffn_bias_in, ffn_bias_out, temporal_q, temporal_k, temporal_v, temporal_o, ffn_in, ffn_out,
        ],
        2,
    )
    part = width // count
    finer = count // d_in.shape[0]

    def in_blocks(grads):
        if finer > 1:
            grads = grads.reshape(-1, KEYS, 2, finer, KEYS // finer).transpose(0, 3, 1, 2, 4)
        return grads.reshape(count, 4 * part, CHUNK)

    def out_blocks(grads):
        if finer > 1:
            grads = grads.reshape(-1, 4, finer, part, CHUNK).transpose(0, 2, 1, 3, 4)
        return grads.reshape(count, 4 * part, CHUNK)

    d_in, came_in, d_out, came_out = in_blocks(d_in), in_blocks(came_in), out_blocks(d_out), out_blocks(came_out)
    token_grad, sum_out, sum_in, sum_temporal, sum_spatial, small = back(
        [
            clip_big, d_out, came_out, d_in, came_in, grad_third, second, mixed_two, query_two, key_two, value_two,
            normed_two, probs_two, temporal_q, temporal_k, temporal_v, temporal_o, mixed_one,
            query_one, key_one, value_one, pair_one, normed_one, probs_one, spatial_q, spatial_k,
            spatial_v, spatial_o, tok, hot, table, gains[0], gains[1], small_ffn,
        ],
        5,
    )
    (table_grad, gain_grad, shift_grad, ffn_in_grad, ffn_out_grad, bias_in, bias_out, *weights) = finish(
        [sum_out, sum_in, sum_temporal, sum_spatial], small, ffn_in.shape[1]
    )
    return (
        mixed[None],
        token_grad[None],
        table_grad,
        gain_grad,
        shift_grad,
        *weights[1:4],
        weights[0],
        *weights[5:8],
        weights[4],
        ffn_in_grad,
        bias_in,
        ffn_out_grad,
        bias_out,
    )


def solution(mesh):
    placed = (P("tile", "seq", None),) * 2 + (P(),) * 17
    return jax.shard_map(
        on_device,
        mesh=mesh,
        in_specs=placed,
        out_specs=(P("tile", "seq", None),) * 2 + (P(None, "seq"),) * 15,
        check_vma=False,
    )
```

```python
import functools

import jax
import jax.numpy as jnp
from jax import lax
from jax.experimental import pallas as pl
from jax.experimental.pallas import tpu as pltpu
from jax.sharding import PartitionSpec as P

HEAD_DIM = 64
FRAMES = 16
GRID_BIG = 16
GRID_SMALL = 8
WIDE = 128
KEYS = 256
CHUNK = 512
VMEM_BYTES = 62 * 2**20
FACTOR = HEAD_DIM**-0.5
ROOT = (2.0 / 3.141592653589793) ** 0.5

F32 = jnp.float32
BF16 = jnp.bfloat16
WHOLE = pl.BlockSpec(memory_space=pltpu.VMEM)
IN_HBM = pl.BlockSpec(memory_space=pl.ANY)
MESH = pl.DeviceIdType.MESH
IN_SMEM = pl.BlockSpec(memory_space=pltpu.SMEM)


def shape_of(dims, kind):
    return jax.ShapeDtypeStruct(dims, kind)


def params(**more):
    return pltpu.CompilerParams(vmem_limit_bytes=VMEM_BYTES, **more)


def dot(left, right):
    return jnp.dot(left, right, preferred_element_type=F32)


def dot_nt(left, right):
    return lax.dot_general(left, right, (((1,), (1,)), ((), ())), preferred_element_type=F32)


def dot_tn(left, right):
    return lax.dot_general(left, right, (((0,), (0,)), ((), ())), preferred_element_type=F32)


def normalise(values):
    centre = values - jnp.mean(values, axis=-1, keepdims=True)
    rate = lax.rsqrt(jnp.mean(centre * centre, axis=-1, keepdims=True) + 1e-05)
    return centre * rate, rate


def norm_backward(grad, hat, rate, gain):
    inner = grad * gain
    level = jnp.mean(inner, axis=-1, keepdims=True)
    slope = jnp.mean(inner * hat, axis=-1, keepdims=True)
    return rate * (inner - level - hat * slope)


def head_halves(block):
    lane = lax.broadcasted_iota(jnp.int32, block.shape, 1)
    zero = jnp.zeros_like(block)
    first = lane < HEAD_DIM
    return jnp.concatenate([jnp.where(first, block, zero), jnp.where(first, zero, block)], axis=0)


def join_halves(both):
    rows = both.shape[0] // 2
    lane = lax.broadcasted_iota(jnp.int32, (rows, both.shape[1]), 1)
    return jnp.where(lane < HEAD_DIM, both[:rows], both[rows:])


def attend(query, key, value, bias):
    scores = dot_nt(head_halves(query) * FACTOR, key) + bias
    top = jnp.max(scores, axis=1, keepdims=True)
    powers = jnp.exp(scores - top)
    prob = (powers * (1.0 / jnp.sum(powers, axis=1, keepdims=True))).astype(BF16)
    return prob, join_halves(dot(prob, value))


def attend_backward(prob, query, key, value, grad):
    grad_two = head_halves(grad)
    grad_prob = dot_nt(grad_two, value)
    prob_f = prob.astype(F32)
    delta = jnp.sum(prob_f * grad_prob, axis=1, keepdims=True)
    grad_score = (prob_f * (grad_prob - delta)).astype(BF16)
    grad_query = join_halves(dot(grad_score, key)) * FACTOR
    grad_key = dot_tn(grad_score, head_halves(query)) * FACTOR
    grad_value = dot_tn(prob, grad_two)
    return grad_query, grad_key, grad_value


def spatial_bias(is_big, rows):
    row = lax.broadcasted_iota(jnp.int32, (rows, KEYS), 0)
    column = lax.broadcasted_iota(jnp.int32, (rows, KEYS), 1)
    same = lax.rem(row, WIDE) // 32 == lax.rem(column, WIDE) // 32
    return jnp.where(same | (is_big == 1), 0.0, -1e30).astype(F32)


def temporal_bias(rows):
    row = lax.rem(lax.broadcasted_iota(jnp.int32, (rows, KEYS), 0), KEYS)
    column = lax.broadcasted_iota(jnp.int32, (rows, KEYS), 1)
    fits = (lax.rem(row, 16) == lax.rem(column, 16)) & (column <= row)
    return jnp.where(fits, 0.0, -1e30).astype(F32)


def weight_grad(target, at, grad, normed):
    grad_t = grad.T
    count, _rows, width = target.shape[1:]
    part = grad_t.shape[0] // count
    for which in range(2):
        block = dot(grad_t, normed[:, which * width : (which + 1) * width]).astype(BF16)
        target[which, :, at * part : (at + 1) * part, :] = block.reshape(count, part, width)


REACH = 3
STEPS = tuple(step for step in range(REACH, -REACH - 1, -1) if step != 0)


class Swap:
    def __init__(self, to_time, offset, is_big, source, staged, came, sems, parts=1):
        self.me, self.tile = lax.axis_index("seq"), lax.axis_index("tile")
        self.count = lax.axis_size("seq")
        self.to_time, self.offset, self.is_big = to_time, offset, is_big
        self.source, self.staged, self.came, self.sems = source, staged, came, sems
        self.parts = parts

    def peer(self, step):
        return (self.me + step, self.tile)

    def present(self, step):
        return (self.me + step >= 0) & (self.me + step < self.count)

    def greet(self, barrier):
        for step in STEPS:
            @pl.when(self.present(step))
            def _(step=step):
                pl.semaphore_signal(
                    barrier, inc=1, device_id=self.peer(step), device_id_type=MESH
                )
        return jnp.minimum(self.me, REACH) + jnp.minimum(self.count - 1 - self.me, REACH)

    def copy(self, step, part):
        slot, sem = REACH - step, (REACH - step) * self.parts + part
        source, target = self.staged.at[slot], self.came.at[slot]
        if self.parts > 1:
            rows = pl.ds(part * (128 // self.parts), 128 // self.parts)
            source, target = source.at[rows], target.at[rows]
        return remote(source, target, self.sems[0].at[sem], self.sems[1].at[sem], self.peer(step))

    def stage(self, step, part):
        which = jnp.clip(self.offset + step, 0, REACH)
        target = self.came if step == 0 else self.staged
        slot = REACH - step
        if self.to_time:
            frames = 4 // self.parts
            for frame in range(part * frames, (part + 1) * frames):
                block = self.source[pl.ds(which * 2 + frame * 8, 2)]
                target[slot, frame * 32 : frame * 32 + 32] = block.reshape(32, block.shape[2])
            return
        sides = 2 // self.parts
        for side in range(part * sides, (part + 1) * sides):
            block = self.source[pl.ds(which * 4 + side * 16, 4)]
            target[slot, side * 64 : side * 64 + 64] = block.reshape(64, block.shape[2])

    def send(self, part=0):
        for step in STEPS:
            self.stage(step, part)

            @pl.when(self.present(step))
            def _(step=step):
                self.copy(step, part).start()

        self.stage(0, part)

    def wait(self, only=None):
        for part in range(self.parts) if only is None else (only,):
            for step in STEPS:
                @pl.when(self.present(step))
                def _(step=step, part=part):
                    self.copy(step, part).wait_send()

                @pl.when(self.present(-step))
                def _(step=step, part=part):
                    self.copy(step, part).wait_recv()

    def place(self, target):
        width = target.shape[-1]
        chosen = jnp.full((16, width), self.is_big, jnp.int32) == 1
        for at in range(REACH + 1):
            slot = REACH - self.offset + at
            for side in range(2):
                for frame in range(4):
                    low = frame * 32 + side * 16 if self.to_time else side * 64 + frame * 16
                    moved = self.came[pl.ds(slot, 1), low : low + 16][0]
                    if self.to_time:
                        here, mine = side * 256 + at * 64 + frame * 16, at * 8 + frame * 2 + side
                    else:
                        here, mine = frame * 128 + at * 32 + side * 16, side * 16 + frame * 4 + at
                    target[here : here + 16] = jnp.where(chosen, moved, self.source[mine])


def seq_dims(count):
    return {16: (2, 2, 2, 2), 64: (4, 4, 4)}.get(count, (1, 1, count))


def seq_orders(count):
    if count == 16:
        names = {"xy": (3, 2, 1, 0), "yx": (2, 3, 1, 0), "xz": (3, 1, 2, 0)}
        return names | {"yz": (2, 1, 3, 0), "zx": (1, 3, 2, 0), "zy": (1, 2, 3, 0)}
    names = {"xy": (2, 1, 0), "yx": (1, 2, 0), "xz": (2, 0, 1)}
    return names | {"yz": (1, 0, 2), "zx": (0, 2, 1), "zy": (0, 1, 2)}


class Grid:
    def __init__(self):
        self.count = lax.axis_size("seq")
        self.dims = seq_dims(self.count)
        self.orders = seq_orders(self.count)
        self.axes = len(self.dims)
        self.me = lax.axis_index("seq")
        self.tile = lax.axis_index("tile")
        self.strides = [1]
        for size in self.dims[:0:-1]:
            self.strides.insert(0, self.strides[0] * size)
        self.places = [
            lax.rem(self.me // stride, size) for stride, size in zip(self.strides, self.dims)
        ]

    def along(self, axis, step):
        place = self.places[axis]
        there = lax.rem(place + step, self.dims[axis])
        return there, (self.me + (there - place) * self.strides[axis], self.tile)

    def other(self):
        return (self.me, 1 - self.tile)

    def peers(self, phase, order):
        if phase == 0:
            return [self.other()]
        axis = order[phase - 1]
        return [self.along(axis, step)[1] for step in range(1, self.dims[axis])]

    def greet(self, barrier):
        peers = [self.other()]
        for axis in range(self.axes):
            peers += [self.along(axis, step)[1] for step in range(1, self.dims[axis])]
        for peer in peers:
            pl.semaphore_signal(barrier, inc=1, device_id=peer, device_id_type=MESH)
        return len(peers)

    def split(self, flat, dims):
        where = []
        for size in dims[::-1]:
            where.insert(0, lax.rem(flat, size))
            flat = flat // size
        return tuple(where)


def remote(source, target, send_sem, recv_sem, device):
    return pltpu.make_async_remote_copy(
        src_ref=source,
        dst_ref=target,
        send_sem=send_sem,
        recv_sem=recv_sem,
        device_id=device,
        device_id_type=MESH,
    )


class Unit:
    def __init__(self, grid, order, rows, source, out, came, part, sems, free, number, reuse, again):
        self.grid, self.order = grid, order
        self.rows, self.part = rows, part
        self.away, self.own, self.fetched = source
        self.out, self.came = out, came
        self.sends, self.recvs = sems
        self.free, self.number, self.reuse, self.again = free, number, reuse, again
        self.last = grid.axes + 1

    def rest(self, phase):
        taken = self.order[:phase]
        return [axis for axis in range(self.grid.axes) if axis not in taken]

    def held(self, phase):
        lead = () if phase == 0 else (0,)
        return self.came[phase], lead

    def slab(self, phase, there):
        before = self.rest(phase - 1)
        where = [slice(None)] * len(before)
        where[before.index(self.order[phase - 1])] = there
        ref, lead = self.held(phase - 1)
        return ref.at[lead + tuple(where) + (self.part,)]

    def landing(self, phase, step):
        dims = len(self.rest(phase))
        return self.came[phase].at[(step,) + (slice(None),) * dims + (self.part,)]

    def copies(self, phase):
        number, grid = self.number, self.grid
        if phase == 0:
            if self.fetched is not None:
                return [pltpu.make_async_copy(self.fetched, self.start_of(), self.sends.at[number, 0, 0])]
            return [
                remote(
                    self.away, self.start_of(), self.sends.at[number, 0, 0],
                    self.recvs.at[number, 0, 0], grid.other(),
                )
            ]
        if phase == self.last:
            mine = self.out.at[grid.tile, self.rows]
            return [
                remote(
                    mine, mine, self.sends.at[number, phase, 0], self.recvs.at[number, phase, 0],
                    grid.other(),
                )
            ]
        axis = self.order[phase - 1]
        out = []
        for step in range(1, grid.dims[axis]):
            there, device = grid.along(axis, step)
            out.append(
                remote(
                    self.slab(phase, there), self.landing(phase, step - 1),
                    self.sends.at[number, phase, step - 1], self.recvs.at[number, phase, step - 1],
                    device,
                )
            )
        return out

    def start_of(self):
        return self.came[0].at[(slice(None),) * self.grid.axes + (self.part,)]

    def start(self, phase):
        if self.again and phase < self.last:
            amount = len(self.grid.peers(phase, self.order))
            pl.semaphore_wait(self.free.at[self.again - 1, phase], amount)
        for copy in self.copies(phase):
            copy.start()

    def release(self, phase):
        for number, order in self.reuse:
            for peer in self.grid.peers(phase, order):
                pl.semaphore_signal(
                    self.free.at[number, phase], inc=1, device_id=peer, device_id_type=MESH
                )

    def wait(self, phase):
        for copy in self.copies(phase):
            copy.wait()

    def turn(self, phase):
        self.wait(phase)
        grid = self.grid
        if phase == 0:
            def step(at, _):
                where = grid.split(at, grid.dims) + (self.part,)
                self.came[0][where] = self.came[0][where] + self.own(grid.split(at, grid.dims))
                return 0

            if self.fetched is None:
                lax.fori_loop(0, grid.count, step, 0)
                return
            self.own(None)
            for piece in range(4):
                base = piece * (grid.count // 4)
                self.own(piece)

                def step_kept(at, _, base=base):
                    where = grid.split(at + base, grid.dims) + (self.part,)
                    self.came[0][where] = self.came[0][where] + self.own(at)
                    return 0

                lax.fori_loop(0, grid.count // 4, step_kept, 0)
            return
        axis = self.order[phase - 1]
        own = self.slab(phase, grid.places[axis])
        size = grid.dims[axis]
        if phase == grid.axes:
            total = own[...].astype(F32)
            for at in range(size - 1):
                total = total + self.came[phase][at, self.part].astype(F32)
            self.out[grid.tile, self.rows] = total.astype(BF16)
            self.release(phase - 1)
            self.release(phase)
            return
        dims = tuple(grid.dims[axis] for axis in self.rest(phase))
        steps = 1
        for size_of in dims:
            steps *= size_of

        def step(at, _):
            where = grid.split(at, dims)
            total = own[where]
            for other in range(size - 1):
                total = total + self.came[phase][(other,) + where + (self.part,)]
            self.came[phase][(0,) + where + (self.part,)] = total
            return 0

        lax.fori_loop(0, steps, step, 0)
        self.release(phase - 1)

    def on(self, phase):
        if phase < self.last:
            self.turn(phase)
            self.start(phase + 1)


class Pair:
    def __init__(self, *units):
        self.units = units

    def __getattr__(self, name):
        def each(phase):
            for unit in self.units:
                getattr(unit, name)(phase)

        return each


class Total:
    def __init__(self, grid, value, came, sends, recvs):
        self.order = grid.orders["xy"]
        self.last = grid.axes
        self.grid, self.value, self.came, self.sends, self.recvs = grid, value, came, sends, recvs

    def copies(self, phase):
        first = sum(len(self.grid.peers(before, self.order)) for before in range(phase))
        return [
            remote(
                self.value, self.came.at[first + at], self.sends.at[first + at],
                self.recvs.at[first + at], peer,
            )
            for at, peer in enumerate(self.grid.peers(phase, self.order))
        ]

    def start(self, phase):
        for copy in self.copies(phase):
            copy.start()

    def on(self, phase):
        if phase > self.last:
            return
        copies = self.copies(phase)
        for copy in copies:
            copy.wait()
        total = self.value[...]
        first = sum(len(self.grid.peers(before, self.order)) for before in range(phase))
        for at in range(len(copies)):
            total = total + self.came[first + at]
        self.value[...] = total
        if phase < self.last:
            self.start(phase + 1)


def unit_scratch(rows, width, order, dims):
    left = list(range(len(dims)))
    out = [pltpu.VMEM(dims + (rows, width), BF16)]
    for axis in order:
        left.remove(axis)
        rest = tuple(dims[other] for other in left)
        out.append(pltpu.VMEM((max(dims[axis] - 1, 1),) + rest + (rows, width), BF16))
    return out


def back_kernel(
    clip_big, d_out, came_out, d_in, came_in, third, second, mixed_t, query_t, key_t, value_t, normed_t, probs_t,
    wq_t, wk_t, wv_t, wo_t, mixed_s, query_s, key_s, value_s, pair, normed_s, probs_s,
    wq_s, wk_s, wv_s, wo_s, tok, hot, table, gain_one, gain_two, small_ffn,
    token_grad, sum_out, sum_in, sum_time, sum_space, small,
    pool, turned, held, probs, d_weights, kept, came_key, came_value, swapped, *rest,
):
    grid = Grid()
    deep = grid.axes + 1
    unit_bufs, rest = rest[: 4 * deep], rest[4 * deep :]
    (totals, total_came, loads, unit_sends, unit_recvs, free, swap_sends, swap_recvs,
     total_sends, total_recvs, pair_sems) = rest
    rows, width = pool.shape[1:]
    _clip, offset, is_big = where_am_i(clip_big)
    swap = Swap(
        False, offset, is_big, turned, _Slots(pool, (11, 6)), swapped, (swap_sends, swap_recvs), 2
    )
    barrier = pltpu.get_barrier_semaphore()
    pl.semaphore_wait(barrier, grid.greet(barrier) + swap.greet(barrier))

    load = Loads(loads)
    orders = grid.orders
    share = d_out.shape[-2]
    every = (slice(None),) * grid.axes

    ways = (("xy", "yx"), ("zx", "zy"), ("xz", "yz", "xz", "yz"), ("yx", "xy", "xy", "yx"))
    ways = [[orders[name] for name in group] for group in ways]

    def buffers(group, which):
        first = (group % 2) * 2 * deep + which * deep
        return unit_bufs[first : first + deep]

    def fetched(group, which, keep, landed, out):
        half = share // 2
        rows_of = pl.ds(which * half, half)
        number = 2 * group + which
        first = (1, grid.dims[0] * grid.dims[1] // 4) if grid.dims[0] < 4 else (grid.dims[0] // 4, grid.dims[1])

        def own(at):
            if at is None:
                return None
            if isinstance(at, int):
                copy = pltpu.make_async_copy(
                    keep.at[
                        (
                            pl.ds(at * first[0] * first[1] // grid.dims[1], first[0]),
                            pl.ds(at * first[1] % grid.dims[1], first[1]),
                        )
                        + every[2:]
                        + (rows_of,)
                    ],
                    kept,
                    unit_sends.at[number, 0, 1],
                )
                copy.start()
                copy.wait()
                return None
            return kept[grid.split(at, first + grid.dims[2:])]

        reuse = [
            (4 * group + 2 * which + sub, ways[group + 2][2 * which + sub]) for sub in range(2)
        ]
        return Unit(
            grid, ways[group][which], rows_of, (None, own, landed.at[every + (rows_of,)]), out,
            buffers(group, which), pl.ds(0, half), (unit_sends, unit_recvs), free, number, reuse, 0,
        )

    def made(group, which, out):
        quarter = share // 4
        rows_of = pl.ds(which * quarter, quarter)

        def own(where):
            return d_weights[(grid.tile,) + where + (rows_of,)]

        return Unit(
            grid, ways[group][which], rows_of,
            (d_weights.at[(1 - grid.tile,) + every + (rows_of,)], own, None), out,
            buffers(group, which // 2), pl.ds((which % 2) * quarter, quarter),
            (unit_sends, unit_recvs), free, 4 + 4 * (group - 2) + which, [],
            4 * (group - 2) + which + 1,
        )

    p0 = Pair(*[fetched(0, which, d_out, came_out, sum_out) for which in range(2)])
    p1 = Pair(*[fetched(1, which, d_in, came_in, sum_in) for which in range(2)])
    p2 = Pair(*[made(2, which, sum_time) for which in range(4)])
    p3o, p3q, p3k, p3v = [made(3, which, sum_space) for which in range(4)]
    p0.start(0)
    p1.start(0)

    in_low = load(third, pool.at[0])
    in_mixed = load(mixed_t, pool.at[2])
    weights = [load(source, held.at[at]) for at, source in enumerate((wo_t, wq_t, wk_t, wv_t))]
    ins = [load(source, pool.at[3 + at]) for at, source in enumerate((query_t, key_t, value_t))]
    ins += [load(probs_t.at[at], probs.at[at]) for at in range(2)]
    late = [load(second, pool.at[1]), load(normed_t, pool.at[6])]
    p0.on(0)
    p1.on(0)
    in_low.wait()
    in_mixed.wait()
    flat_weights = d_weights.reshape((2, grid.count) + d_weights.shape[-2:])
    weight_grad(flat_weights, 0, pool[0], pool.at[2])
    weights[0].wait()

    def mix_back(grad, target):
        for part in range(4):
            side = slice(part * 256, (part + 1) * 256)
            pool[target, :, side] = dot_nt(pool[grad], held[0, side, :]).astype(BF16)

    mix_back(0, 7)
    weights.append(load(wo_s, held.at[0]))
    for copy in ins:
        copy.wait()

    def time_group(at, _):
        here = pl.ds(pl.multiple_of(at * KEYS, KEYS), KEYS)
        for two in range(8):
            side = pl.ds(two * WIDE, WIDE)
            grads = attend_backward(
                probs[at, two], pool[3, here, side], pool[4, here, side], pool[5, here, side],
                pool[7, here, side],
            )
            for target, grad in enumerate(grads):
                pool[8 + target, here, side] = grad.astype(BF16)
        return 0

    lax.fori_loop(0, rows // KEYS, time_group, 0)
    ins = [
        load(source, pool.at[target])
        for source, target in (
            (query_s, 2), (key_s, 3), (value_s, 4), (pair.at[0], 5), (pair.at[1], 7)
        )
    ]
    ins += [
        load(probs_s.at[at], probs.at[at // 2, :, pl.ds(at % 2 * 2 * WIDE, 2 * WIDE)])
        for at in range(4)
    ]
    for copy in late:
        copy.wait()
    for at in range(3):
        weight_grad(flat_weights, at + 1, pool[8 + at], pool.at[6])
    for at in range(3):
        weights[at + 1].wait()

    def time_rows(step, carry):
        here = pl.ds(pl.multiple_of(step * 256, 256), 256)
        grad = (
            dot_nt(pool[8, here, :], held[1])
            + dot_nt(pool[9, here, :], held[2])
            + dot_nt(pool[10, here, :], held[3])
        )
        hat, rate = normalise(pool[1, here, :].astype(F32))
        total = pool[0, here, :].astype(F32) + norm_backward(grad, hat, rate, gain_two[...])
        turned[pl.ds(step * 16, 16)] = total.astype(BF16).reshape(16, 16, width)
        return (
            carry[0] + jnp.sum(grad * hat, axis=0, keepdims=True),
            carry[1] + jnp.sum(grad, axis=0, keepdims=True),
        )

    zero = jnp.zeros((1, width), F32)
    time_norm = (zero, zero)
    for side in range(2):
        time_norm = time_rows(side, time_norm)
        swap.send(side)
    weights += [load(source, held.at[at + 1]) for at, source in enumerate((wq_s, wk_s, wv_s))]
    in_mixed = load(mixed_s, pool.at[10])
    p0.on(1)
    p2.start(0)
    p2.turn(0)
    p1.on(1)
    p0.on(2)
    swap.wait()
    swap.place(pool.at[1])
    in_normed = load(normed_s, pool.at[0])
    p2.start(1)

    in_mixed.wait()
    weight_grad(flat_weights, 0, pool[1], pool.at[10])
    weights[4].wait()
    mix_back(1, 8)
    p3o.start(0)
    for copy in ins:
        copy.wait()

    def space_group(at, _):
        here = pl.ds(pl.multiple_of(at * WIDE, WIDE), WIDE)
        lower = pl.ds(pl.multiple_of(lax.rem(at, 2) * 2 * WIDE, 2 * WIDE), 2 * WIDE)
        for two in range(8):
            side = pl.ds(two * WIDE, WIDE)
            keys = jnp.concatenate([pool[3, here, side], pool[5, here, side]], axis=0)
            values = jnp.concatenate([pool[4, here, side], pool[7, here, side]], axis=0)
            grad_query, grad_key, grad_value = attend_backward(
                probs[at // 2, two, lower], pool[2, here, side], keys, values, pool[8, here, side]
            )
            pool[9, here, side] = grad_query.astype(BF16)
            pool[10, here, side] = grad_key[:WIDE].astype(BF16)
            pool[11, here, side] = grad_value[:WIDE].astype(BF16)
            pool[6, here, side] = grad_key[WIDE:].astype(BF16)
            turned[pl.ds(at * 8, 8), :, side] = grad_value[WIDE:].astype(BF16).reshape(8, 16, WIDE)
        return 0

    lax.fori_loop(0, rows // (2 * WIDE), space_group, 0)
    p0.on(3)
    p1.on(2)
    p3o.on(0)
    lax.fori_loop(rows // (2 * WIDE), rows // WIDE, space_group, 0)
    across = [
        remote(
            source, target, pair_sems.at[0, at], pair_sems.at[1, at], grid.other(),
        )
        for at, (source, target) in enumerate(((pool.at[6], came_key), (turned, came_value)))
    ]
    for copy in across:
        copy.start()
    in_tok = load(tok, pool.at[2])
    in_normed.wait()
    weight_grad(flat_weights, 1, pool[9], pool.at[0])
    p3q.start(0)
    p2.on(1)
    for at, copy in enumerate(across):
        copy.wait()
        came = (came_key, came_value)[at][...].reshape(rows, width)
        pool[10 + at] = pool[10 + at] + came
        weight_grad(flat_weights, 2 + at, pool[10 + at], pool.at[0])
        (p3k, p3v)[at].start(0)
    p3q.on(0)
    p3k.on(0)
    p3v.on(0)
    p0.on(4)
    p1.on(3)
    for at in range(3):
        weights[5 + at].wait()
    in_tok.wait()

    def space_rows(step, carry):
        here = pl.ds(pl.multiple_of(step * 256, 256), 256)
        grad = (
            dot_nt(pool[9, here, :], held[1])
            + dot_nt(pool[10, here, :], held[2])
            + dot_nt(pool[11, here, :], held[3])
        )
        first = pool[2, here, :].astype(F32) + dot(hot[here, :], table[...])
        hat, rate = normalise(first)
        total = pool[1, here, :].astype(F32) + norm_backward(grad, hat, rate, gain_one[...])
        high = total.astype(BF16)
        pool[1, here, :] = high
        rest = (total - high.astype(F32)).astype(BF16)
        chosen = hot[here, :]
        return (
            carry[0] + jnp.sum(grad * hat, axis=0, keepdims=True),
            carry[1] + jnp.sum(grad, axis=0, keepdims=True),
            carry[2] + dot_tn(chosen, high)[:8] + dot_tn(chosen, rest)[:8],
        )

    p3o.on(1)
    space_norm = lax.fori_loop(0, rows // 256, space_rows, (zero, zero, jnp.zeros((8, width), F32)))
    out_grad = load(pool.at[1], token_grad)
    totals[0:8] = space_norm[2]
    totals[8:16] = jnp.concatenate(
        [space_norm[0], time_norm[0], space_norm[1], time_norm[1], jnp.zeros((4, width), F32)], axis=0
    )
    totals[16:24] = small_ffn[...]
    total = Total(grid, totals, total_came, total_sends, total_recvs)
    total.start(0)
    p2.on(2)
    p3q.on(1)
    p1.on(4)
    p3o.on(2)
    total.on(0)
    p3v.on(1)
    p3k.on(1)
    p2.on(3)
    p3q.on(2)
    total.on(1)
    p3o.on(3)
    p3v.on(2)
    p3k.on(2)
    p3q.on(3)
    total.on(2)
    p2.on(4)
    p3v.on(3)
    p3k.on(3)
    total.on(3)
    p3o.on(4)
    p3q.on(4)
    p3v.on(4)
    p3k.on(4)
    total.on(4)
    small[...] = totals[...]
    for unit in (p0, p1, p2, p3o, p3q, p3k, p3v):
        unit.wait(grid.axes + 1)
    out_grad.wait()


class _Slots:
    def __init__(self, pool, slots):
        self.pool, self.slots = pool, slots

    class _At:
        def __init__(self, slots):
            self.slots = slots

        def __getitem__(self, slot):
            return self.slots.pool.at[self.slots.slots[slot // 4], pl.ds(slot % 4 * 128, 128)]

    @property
    def at(self):
        return _Slots._At(self)

    def __setitem__(self, where, value):
        slot, rows = where
        first = slot % 4 * 128
        self.pool[self.slots[slot // 4], first + rows.start : first + rows.stop] = value


def back(args, number):
    args = list(args)
    rows, width = args[5].shape
    count = lax.axis_size("seq")
    dims = seq_dims(count)
    share, group = args[1].shape[-2:]
    dma = pltpu.SemaphoreType.DMA
    lead = (1, dims[0] * dims[1] // 4) if dims[0] < 4 else (dims[0] // 4, dims[1])
    scratch = [
        pltpu.VMEM((12, rows, width), BF16),
        pltpu.VMEM((rows // 16, 16, width), BF16),
        pltpu.VMEM((4, width, width), BF16),
        pltpu.VMEM((2, 8, 2 * KEYS, KEYS), BF16),
        pltpu.VMEM((2,) + dims + (share, group), BF16),
        pltpu.VMEM(lead + dims[2:] + (share // 2, group), BF16),
        pltpu.VMEM((rows, width), BF16),
        pltpu.VMEM((rows // 16, 16, width), BF16),
        pltpu.VMEM((7, 128, width), BF16),
    ]
    for _ in range(2):
        for name in ("xy", "yx"):
            scratch += unit_scratch(share // 2, group, seq_orders(count)[name], dims)
    most = max(max(dims) - 1, 2)
    peers = 1 + sum(dims) - len(dims)
    scratch += [
        pltpu.VMEM((24, width), F32),
        pltpu.VMEM((peers, 24, width), F32),
        dma((40,)),
        dma((12, len(dims) + 2, most)),
        dma((12, len(dims) + 2, most)),
        pltpu.SemaphoreType.REGULAR((8, len(dims) + 1)),
        dma((14,)),
        dma((14,)),
        dma((peers,)),
        dma((peers,)),
        dma((2, 2)),
    ]
    for at in range(1, 5):
        args[at] = args[at].reshape(dims + (share, group))
    final = shape_of((2, share, group), BF16)
    return pl.pallas_call(
        back_kernel,
        out_shape=[shape_of((rows, width), BF16)] + [final] * 4 + [shape_of((24, width), F32)],
        in_specs=[IN_SMEM] + [IN_HBM] * 28 + [WHOLE] * 5,
        out_specs=[IN_HBM] + [WHOLE] * 5,
        scratch_shapes=scratch,
        compiler_params=params(collective_id=number, has_side_effects=True),
    )(*args)


def finish_kernel(sum_out, sum_in, sum_time, sum_space, small, *refs):
    table, gain, shift, inner, outer, bias_in, bias_out = refs[:7]
    weights, rolled = refs[7:-1], refs[-1]
    count = lax.axis_size("seq")
    me = lax.axis_index("seq")
    width = small.shape[1]
    part = width // count
    hidden = bias_in.shape[1]
    for half in range(2):
        for at in range(4):
            rows = slice(at * part, (at + 1) * part)
            first = half * (width // 2)
            for base, source in ((0, sum_space), (4, sum_time)):
                weights[base + at][:, first : first + width // 2] = source[half, rows].astype(F32)
            first = (half * 4 + at) * CHUNK
            outer[:, first : first + CHUNK] = sum_out[half, rows].astype(F32)
        if inner.shape[1] == KEYS:
            for at in range(2):
                first = half * 2 * KEYS + at * KEYS
                inner[first : first + KEYS, :] = sum_in[half, :, at * KEYS : (at + 1) * KEYS].astype(F32)
    rolled[...] = pltpu.roll(small[...], lax.rem(width - me * part, width), 1)
    table[...] = rolled[0:8, :part]
    gain[...] = jnp.concatenate([rolled[8:10, :part], rolled[16:17, :part]], axis=0)
    shift[...] = jnp.concatenate([rolled[10:12, :part], rolled[17:18, :part]], axis=0)
    bias_out[...] = rolled[18:19, :part]
    begin = me * hidden
    rolled[...] = pltpu.roll(small[...], lax.rem(width - lax.rem(begin, width), width), 1)
    for at in range(4):
        @pl.when(begin // width == at)
        def _(at=at):
            bias_in[...] = rolled[19 + at : 20 + at, :hidden]


def finish(sums, small, hidden):
    count = lax.axis_size("seq")
    width = small.shape[1]
    part = width // count
    outs = [
        shape_of((8, part), F32), shape_of((3, part), F32), shape_of((3, part), F32),
        shape_of((width, hidden // count), F32), shape_of((part, hidden), F32),
        shape_of((1, hidden // count), F32), shape_of((1, part), F32),
    ]
    out = pl.pallas_call(
        finish_kernel,
        out_shape=outs + [shape_of((part, width), F32)] * 8,
        in_specs=[WHOLE] * 5,
        out_specs=[WHOLE] * 15,
        scratch_shapes=[pltpu.VMEM(small.shape, F32)],
        compiler_params=params(),
    )(*sums, small)
    out = list(out)
    out[4] = out[4].T
    out[7:] = [value.T for value in out[7:]]
    if hidden // count != KEYS:
        inner = sums[1].reshape(2, KEYS, 2, hidden // count).transpose(0, 2, 1, 3)
        out[3] = inner.reshape(width, -1).astype(F32)
    return out


def where_am_i(clip_big):
    me = lax.axis_index("seq")
    span = (GRID_BIG // GRID_SMALL) ** 2
    start, clip, offset, is_big = jnp.int32(0), jnp.int32(0), jnp.int32(0), jnp.int32(0)
    for at in range(clip_big.shape[0]):
        big = clip_big[at]
        size = jnp.where(big == 1, span, 1)
        inside = (me >= start) & (me < start + size)
        clip = jnp.where(inside, at, clip)
        offset = jnp.where(inside, me - start, offset)
        is_big = jnp.where(inside, big, is_big)
        start = start + size
    return clip, offset, is_big


class Loads:
    def __init__(self, sems):
        self.sems, self.used = sems, 0

    def __call__(self, source, target):
        copy = pltpu.make_async_copy(source, target, self.sems.at[self.used])
        self.used += 1
        copy.start()
        return copy


def first_kernel(
    clip_big, actions, tok, action_table, gain, shift, cot, wq, wk, wv, wo,
    normed_out, query_out, key_out, value_out, pair_out, mixed_out, probs_out, second_out, cot_out, hot, table,
    held, normed, query, key, value, pair, mixed, probs, second, turned, staged, came, cot_staged, cot_came,
    loads, pair_sems, swap_sends, swap_recvs, cot_sends, cot_recvs,
):
    rows, width = tok.shape
    clip, offset, is_big = where_am_i(clip_big)
    grid = Grid()
    swap = Swap(True, offset, is_big, turned, staged, came, (swap_sends, swap_recvs), 2)
    cot_swap = Swap(True, offset, is_big, cot, cot_staged, cot_came, (cot_sends, cot_recvs), 2)
    barrier = pltpu.get_barrier_semaphore()
    pl.semaphore_signal(barrier, inc=1, device_id=grid.other(), device_id_type=MESH)
    peers = 1 + swap.greet(barrier)
    load = Loads(loads)
    weights = [load(source, held.at[at]) for at, source in enumerate((wk, wv, wq, wo))]
    pl.semaphore_wait(barrier, peers)
    cot_swap.send(0)

    last = actions.shape[0] - 1
    base = clip * FRAMES + offset * (FRAMES // (REACH + 1))
    row = lax.broadcasted_iota(jnp.int32, (rows, WIDE), 0)
    frame_of = jnp.where(jnp.full((rows, WIDE), is_big, jnp.int32) == 1, row // WIDE, row // 32)
    action = jnp.zeros((rows, WIDE), jnp.int32)
    for frame in range(FRAMES):
        action = jnp.where(frame_of == frame, actions[jnp.minimum(base + frame, last)], action)
    lane = lax.broadcasted_iota(jnp.int32, (rows, WIDE), 1)
    hot[...] = jnp.where((action == lax.rem(lane, 8)) & (lane < 24), 1.0, 0.0).astype(BF16)
    exact = action_table[...]
    high = exact.astype(BF16)
    left = exact - high.astype(F32)
    middle = left.astype(BF16)
    low = left - middle.astype(F32)
    table[...] = jnp.concatenate(
        [high.astype(F32), middle.astype(F32), low, jnp.zeros((WIDE - 24, width), F32)], axis=0
    ).astype(BF16)

    def norm_rows(at, _):
        here = pl.ds(pl.multiple_of(at * 128, 128), 128)
        hat, _rate = normalise(tok[here, :].astype(F32) + dot(hot[here, :], table[...]))
        normed[here, :] = (hat * gain[...] + shift[...]).astype(BF16)
        return 0

    lax.fori_loop(0, rows // 128, norm_rows, 0)
    outs = [load(normed, normed_out)]
    across = []
    for at, (target, out) in enumerate(((key, key_out), (value, value_out), (query, query_out))):
        weights[at].wait()
        for part in range(4):
            side = pl.ds(part * 256, 256)
            target[:, side] = dot(normed[...], held[at, :, side]).astype(BF16)
        if at < 2:
            copy = remote(
                target, pair.at[at], pair_sems.at[0, at], pair_sems.at[1, at], grid.other()
            )
            copy.start()
            across.append(copy)
        outs.append(load(target, out))
    for copy in across:
        copy.wait()
    outs.append(load(pair, pair_out))
    weights[3].wait()
    bias = spatial_bias(is_big, 2 * WIDE)

    def group(at, _):
        here = pl.ds(pl.multiple_of(at * WIDE, WIDE), WIDE)
        for two in range(8):
            side = pl.ds(two * WIDE, WIDE)
            keys = jnp.concatenate([key[here, side], pair[0, here, side]], axis=0)
            values = jnp.concatenate([value[here, side], pair[1, here, side]], axis=0)
            prob, out = attend(query[here, side], keys, values, bias)
            probs[at, two] = prob
            mixed[here, side] = out.astype(BF16)
        return 0

    for half in range(2):
        lax.fori_loop(2 * half, 2 * half + 2, group, 0)
        here = slice(half * KEYS, (half + 1) * KEYS)
        blocks = slice(half * 16, (half + 1) * 16)
        for part in range(4):
            side = slice(part * 256, (part + 1) * 256)
            first = tok[here, side].astype(F32) + dot(hot[here, :], table[:, side])
            total = first + dot(mixed[here, :], held[3, :, side])
            turned[blocks, :, side] = total.astype(BF16).reshape(16, 16, 256)
        swap.send(half)
    outs += [load(mixed, mixed_out), load(probs, probs_out)]
    cot_swap.wait(0)
    half = pl.ds(0, cot_out.shape[1])
    outs.append(load(cot_came.at[:, half], cot_out))
    swap.wait()
    swap.place(second)
    outs.append(load(second, second_out))
    for copy in outs:
        copy.wait()


def first(clip_big, actions, tok, action_table, gain, shift, cot, wq, wk, wv, wo, number):
    rows, width = tok.shape
    wide = shape_of((rows, width), BF16)
    probs = (rows // WIDE, 8, 2 * WIDE, KEYS)
    dma = pltpu.SemaphoreType.DMA
    full = pltpu.VMEM((rows, width), BF16)
    return pl.pallas_call(
        first_kernel,
        out_shape=[
            wide, wide, wide, wide, shape_of((2, rows, width), BF16), wide, shape_of(probs, BF16), wide,
            shape_of((7, 64, width), BF16), shape_of((rows, WIDE), BF16), shape_of((WIDE, width), BF16),
        ],
        in_specs=[IN_SMEM] * 2 + [WHOLE] * 5 + [IN_HBM] * 4,
        out_specs=[IN_HBM] * 9 + [WHOLE] * 2,
        scratch_shapes=[
            pltpu.VMEM((4, width, width), BF16), full, full, full, full,
            pltpu.VMEM((2, rows, width), BF16), full, pltpu.VMEM(probs, BF16), full,
            pltpu.VMEM((rows // 16, 16, width), BF16),
            *[pltpu.VMEM((7, 128, width), BF16)] * 4,
            dma((16,)), dma((2, 2)), *[dma((14,))] * 4,
        ],
        compiler_params=params(collective_id=number, has_side_effects=True),
    )(
        clip_big, actions, tok, action_table, gain, shift, cot.reshape(rows // 16, 16, width),
        wq, wk, wv, wo,
    )


def middle_kernel(
    clip_big, second, cot_in, cot_half, gain_two, shift_two, gain, shift, bias_in, bias_out, wq, wk, wv, wo, win, wout,
    normed_out, query_out, key_out, value_out, probs_out, mixed_two_out, mixed_out, third_out,
    d_in, came_in, d_out, came_out, small,
    pool, probs, held, w_in, w_out, active, slope, third, normed_t, cot_t, turned, lifted,
    staged, came_cot, came_mixed, outgoing,
    loads, cot_sends, cot_recvs, mixed_sends, mixed_recvs, out_sems, grad_recvs, prob_sems,
):
    rows, width = third.shape
    hidden = w_in.shape[1]
    chunks = hidden // CHUNK
    _clip, offset, is_big = where_am_i(clip_big)
    cot_swap = Swap(True, offset, is_big, turned, staged, came_cot, (cot_sends, cot_recvs), 2)
    mixed_swap = Swap(False, offset, is_big, lifted, staged, came_mixed, (mixed_sends, mixed_recvs), 2)
    barrier = pltpu.get_barrier_semaphore()
    tile = lax.axis_index("tile")
    other = (lax.axis_index("seq"), 1 - tile)
    pl.semaphore_signal(barrier, inc=1, device_id=other, device_id_type=MESH)
    peers = 1 + cot_swap.greet(barrier)
    load = Loads(loads)
    cot_load = load(cot_in, turned)
    second_load = load(second, pool.at[0])
    weights = [load(source, held.at[at]) for at, source in enumerate((wq, wk, wv, wo))]
    weights += [load(win, w_in), load(wout, w_out)]
    half_load = load(cot_half, came_cot.at[:, pl.ds(0, cot_half.shape[1])])
    second_load.wait()

    def norm_two(at, _):
        here = pl.ds(pl.multiple_of(at * 128, 128), 128)
        hat, _rate = normalise(pool[0, here, :].astype(F32))
        pool[4, here, :] = (hat * gain_two[...] + shift_two[...]).astype(BF16)
        return 0

    lax.fori_loop(0, rows // 128, norm_two, 0)
    outs = [load(pool.at[4], normed_out)]
    for at, out in enumerate((query_out, key_out, value_out)):
        weights[at].wait()
        for part in range(4):
            side = slice(part * 256, (part + 1) * 256)
            pool[1 + at, :, side] = dot(pool[4], held[at, :, side]).astype(BF16)
        outs.append(load(pool.at[1 + at], out))
    pl.semaphore_wait(barrier, peers)
    cot_load.wait()
    cot_swap.send(1)
    bias = temporal_bias(2 * KEYS)

    def probs_copy(at):
        return pltpu.make_async_copy(probs, probs_out.at[at], prob_sems.at[at])

    def group(at, _):
        @pl.when(at > 0)
        def _():
            probs_copy(0).wait()

        here = pl.ds(pl.multiple_of(at * KEYS, KEYS), KEYS)
        for two in range(8):
            side = pl.ds(two * WIDE, WIDE)
            prob, out = attend(pool[1, here, side], pool[2, here, side], pool[3, here, side], bias)
            probs[two] = prob
            pool[5, here, side] = out.astype(BF16)
        probs_copy(at).start()
        return 0

    lax.fori_loop(0, rows // KEYS, group, 0)
    outs += [load(pool.at[5], mixed_two_out)]
    weights[3].wait()
    for part in range(4):
        side = slice(part * 256, (part + 1) * 256)
        third[:, side] = pool[0, :, side].astype(F32) + dot(pool[5], held[3, :, side])
    outs[0].wait()

    def norm_three(at, _):
        here = pl.ds(pl.multiple_of(at * 128, 128), 128)
        hat, _rate = normalise(third[here, :])
        pool[4, here, :] = (hat * gain[...] + shift[...]).astype(BF16)
        return 0

    lax.fori_loop(0, rows // 128, norm_three, 0)
    weights[4].wait()

    def forward(at, _):
        side = pl.ds(pl.multiple_of(at * KEYS, KEYS), KEYS)
        inner = dot(pool[4], w_in[:, side]) + bias_in[:, side]
        square = inner * inner
        curve = jnp.tanh(ROOT * (inner + 0.044715 * inner * square))
        active[:, side] = (0.5 * inner * (1.0 + curve)).astype(BF16)
        slope[:, side] = (
            0.5 * (1.0 + curve)
            + (0.5 * ROOT) * inner * (1.0 - curve * curve) * (1.0 + (3 * 0.044715) * square)
        ).astype(BF16)
        return 0

    lax.fori_loop(0, hidden // KEYS, forward, 0)
    half_load.wait()
    cot_swap.wait(1)
    weights[5].wait()

    for half in range(2):
        here, blocks = pl.ds(half * KEYS, KEYS), slice(half * 16, (half + 1) * 16)
        for part in range(width // KEYS):
            side = slice(part * KEYS, (part + 1) * KEYS)
            total = third[here, side] + bias_out[:, side] + dot(active[here, :], w_out[:, side])
            lifted[blocks, :, side] = total.astype(BF16).reshape(16, 16, KEYS)
        mixed_swap.send(half)
    cot_swap.place(pool.at[0])
    normed_t[...] = pool[4].T
    cot_t[...] = pool[0].T
    small[2:3, :] = jnp.sum(pool[0].astype(F32), axis=0, keepdims=True)

    def out_copy(at, slot, away):
        share = outgoing.shape[2]
        where = (slice(None), pl.ds(lax.rem(at, 4) * share, share))
        source = outgoing.at[slot]
        if away:
            return remote(
                source, came_out.at[where], out_sems.at[slot, 0], grad_recvs.at[lax.rem(at, 4), 0], other
            )
        return pltpu.make_async_copy(source, d_out.at[where], out_sems.at[slot, 0])

    def in_copy(at, slot, part, away):
        which = 1 - tile if away else tile
        source = outgoing.at[2 + slot, pl.ds((which * 2 + part) * 4, 4)]
        if away:
            return remote(
                source, came_in.at[at * 2 + part], out_sems.at[slot, 1 + part],
                grad_recvs.at[at, 1 + part], other,
            )
        return pltpu.make_async_copy(source, d_in.at[at * 2 + part], out_sems.at[slot, 3 + part])

    def start_out(at, slot):
        @pl.when(at // 4 == tile)
        def _():
            out_copy(at, slot, False).start()

        @pl.when(at // 4 != tile)
        def _():
            out_copy(at, slot, True).start()

        for part in range(2):
            in_copy(at, slot, part, False).start()
            in_copy(at, slot, part, True).start()

    def sent_out(at, slot):
        @pl.when(at // 4 == tile)
        def _():
            out_copy(at, slot, False).wait()

        @pl.when(at // 4 != tile)
        def _():
            out_copy(at, slot, True).wait_send()

        for part in range(2):
            in_copy(at, slot, part, False).wait()
            in_copy(at, slot, part, True).wait_send()

    def backward(at, _):
        slot = lax.rem(at, 2)

        @pl.when(at >= 2)
        def _():
            sent_out(at - 2, slot)

        side = pl.ds(pl.multiple_of(at * CHUNK, CHUNK), CHUNK)
        wide = slope[:, side].astype(F32) * dot_nt(pool[0], w_out[side, :])
        grad_inner = wide.astype(BF16)
        slope[:, side] = grad_inner
        lanes = pl.ds(pl.multiple_of(lax.rem(at, 2) * CHUNK, CHUNK), CHUNK)
        small[pl.ds(3 + at // 2, 1), lanes] = jnp.sum(grad_inner.astype(F32), axis=0, keepdims=True)
        outgoing[slot] = dot(cot_t[...], active[:, side]).astype(BF16).reshape(outgoing.shape[1:])
        for top in range(4):
            block = dot(normed_t[top * 256 : (top + 1) * 256, :], grad_inner).astype(BF16)
            for part in range(2):
                first = ((top // 2) * 2 + part) * 4
                outgoing[
                    2 + slot, first : first + 4, :, (top % 2) * KEYS : (top % 2 + 1) * KEYS
                ] = block[:, part * KEYS : (part + 1) * KEYS].reshape(4, 64, KEYS)
        start_out(at, slot)
        return 0

    lax.fori_loop(0, chunks, backward, 0)
    for copy in outs[1:]:
        copy.wait()
    probs_copy(1).wait()

    def back_rows(step, carry):
        here = pl.ds(pl.multiple_of(step * KEYS, KEYS), KEYS)
        hat, rate = normalise(third[here, :])
        grad = dot_nt(slope[here, :], w_in[...])
        pool[2, here, :] = (
            pool[0, here, :].astype(F32) + norm_backward(grad, hat, rate, gain[...])
        ).astype(BF16)
        return (
            carry[0] + jnp.sum(grad * hat, axis=0, keepdims=True),
            carry[1] + jnp.sum(grad, axis=0, keepdims=True),
        )

    zero = jnp.zeros((1, width), F32)
    sums = lax.fori_loop(0, rows // KEYS, back_rows, (zero, zero))
    small[0:1, :] = sums[0]
    small[1:2, :] = sums[1]
    small[7:8, :] = zero
    last = [load(pool.at[2], third_out)]
    mixed_swap.wait()
    mixed_swap.place(pool.at[1])
    last.append(load(pool.at[1], mixed_out))
    for at in (chunks - 2, chunks - 1):
        sent_out(at, at % 2)
    for at in range(chunks):
        if at < 4:
            out_copy(at, 0, True).wait_recv()
        for part in range(2):
            in_copy(at, 0, part, True).wait_recv()
    for copy in last:
        copy.wait()


def middle(args, number):
    clip_big, second, cot = args[:3]
    win = args[14]
    rows, width = second.shape
    hidden = win.shape[1]
    wide = shape_of((rows, width), BF16)
    probs = (rows // KEYS, 8, 2 * KEYS, KEYS)
    dma = pltpu.SemaphoreType.DMA
    block = pltpu.VMEM((7, 128, width), BF16)
    args = list(args)
    args[2] = cot.reshape(rows // 16, 16, width)
    return pl.pallas_call(
        middle_kernel,
        out_shape=[
            wide, wide, wide, wide, shape_of(probs, BF16), wide, wide, wide,
            *[shape_of((hidden // KEYS, 4, 64, 2 * KEYS), BF16)] * 2,
            *[shape_of((16, KEYS, CHUNK), BF16)] * 2,
            shape_of((8, width), F32),
        ],
        in_specs=[IN_SMEM] + [IN_HBM] * 3 + [WHOLE] * 6 + [IN_HBM] * 6,
        out_specs=[IN_HBM] * 12 + [WHOLE],
        scratch_shapes=[
            pltpu.VMEM((6, rows, width), BF16),
            pltpu.VMEM(probs[1:], BF16),
            pltpu.VMEM((4, width, width), BF16),
            pltpu.VMEM((width, hidden), BF16),
            pltpu.VMEM((hidden, width), BF16),
            pltpu.VMEM((rows, hidden), BF16),
            pltpu.VMEM((rows, hidden), BF16),
            pltpu.VMEM((rows, width), F32),
            pltpu.VMEM((width, rows), BF16),
            pltpu.VMEM((width, rows), BF16),
            *[pltpu.VMEM((rows // 16, 16, width), BF16)] * 2,
            block, block, block,
            pltpu.VMEM((4, 16, 64, CHUNK), BF16),
            dma((24,)), *[dma((14,))] * 4, dma((2, 5)), dma((8, 3)), dma((2,)),
        ],
        compiler_params=params(collective_id=number, has_side_effects=True),
    )(*args)


def on_device(
    tokens,
    cotangent,
    clip_big,
    actions,
    action_table,
    norm_gain,
    norm_bias,
    spatial_q,
    spatial_k,
    spatial_v,
    spatial_o,
    temporal_q,
    temporal_k,
    temporal_v,
    temporal_o,
    ffn_in,
    ffn_bias_in,
    ffn_out,
    ffn_bias_out,
):
    tok = tokens[0]
    rows, width = tok.shape
    count = lax.axis_size("seq")
    gains = [norm_gain[at : at + 1] for at in range(3)]
    shifts = [norm_bias[at : at + 1] for at in range(3)]

    normed_one, query_one, key_one, value_one, pair_one, mixed_one, probs_one, second, cot_half, hot, table = first(
        clip_big, actions, tok, action_table, gains[0], shifts[0], cotangent[0],
        spatial_q, spatial_k, spatial_v, spatial_o, 1,
    )
    (normed_two, query_two, key_two, value_two, probs_two, mixed_two, mixed, grad_third, d_in, came_in,
     d_out, came_out, small_ffn) = middle(
        [
            clip_big, second, cotangent[0], cot_half, gains[1], shifts[1], gains[2], shifts[2],
            ffn_bias_in, ffn_bias_out, temporal_q, temporal_k, temporal_v, temporal_o, ffn_in, ffn_out,
        ],
        2,
    )
    part = width // count
    finer = count // d_in.shape[0]

    def in_blocks(grads):
        if finer > 1:
            grads = grads.reshape(-1, KEYS, 2, finer, KEYS // finer).transpose(0, 3, 1, 2, 4)
        return grads.reshape(count, 4 * part, CHUNK)

    def out_blocks(grads):
        if finer > 1:
            grads = grads.reshape(-1, 4, finer, part, CHUNK).transpose(0, 2, 1, 3, 4)
        return grads.reshape(count, 4 * part, CHUNK)

    d_in, came_in, d_out, came_out = in_blocks(d_in), in_blocks(came_in), out_blocks(d_out), out_blocks(came_out)
    token_grad, sum_out, sum_in, sum_temporal, sum_spatial, small = back(
        [
            clip_big, d_out, came_out, d_in, came_in, grad_third, second, mixed_two, query_two, key_two, value_two,
            normed_two, probs_two, temporal_q, temporal_k, temporal_v, temporal_o, mixed_one,
            query_one, key_one, value_one, pair_one, normed_one, probs_one, spatial_q, spatial_k,
            spatial_v, spatial_o, tok, hot, table, gains[0], gains[1], small_ffn,
        ],
        5,
    )
    (table_grad, gain_grad, shift_grad, ffn_in_grad, ffn_out_grad, bias_in, bias_out, *weights) = finish(
        [sum_out, sum_in, sum_temporal, sum_spatial], small, ffn_in.shape[1]
    )
    return (
        mixed[None],
        token_grad[None],
        table_grad,
        gain_grad,
        shift_grad,
        *weights[1:4],
        weights[0],
        *weights[5:8],
        weights[4],
        ffn_in_grad,
        bias_in,
        ffn_out_grad,
        bias_out,
    )


def solution(mesh):
    placed = (P("tile", "seq", None),) * 2 + (P(),) * 17
    return jax.shard_map(
        on_device,
        mesh=mesh,
        in_specs=placed,
        out_specs=(P("tile", "seq", None),) * 2 + (P(None, "seq"),) * 15,
        check_vma=False,
    )
```
